32 devices in a mesh: gx: 2 (over x), gy: 4 (over y, core), gz: 4 (over z).
Axes of the slice: x: 2, y: 2, z: 4, core: 2. Of those that a mesh axis runs over, the one named last changes fastest.
Arguments:
- right_side: float32 [48, 128, 512], P('gx', 'gy', 'gz'), may hold values from -6 to 6
- conductance: float32 [48, 128, 512], P('gx', 'gy', 'gz'), may hold values from 0.05 to 10
- absorption: float32 [48, 128, 512], P('gx', 'gy', 'gz'), may hold values from 0.002 to 0.02
- block_agg: int32 [24, 64, 256], P('gx', 'gy', 'gz'), may hold values from 0 to 127, as said below
Outputs:
- solution: float32 [48, 128, 512], P('gx', 'gy', 'gz')
The draws below stay inside these ranges and needn't reach their ends.
Inputs may be any that keep to these rules, and one draw needn't show every extreme that they name: `block_agg`: aggregates never leave their brick; in every brick each number 0 to 127 names at least one block.
All inputs are finite; a program needn't handle non-finite values.
Results may differ from the reference program's by a relative error of at most 0.0003.
Values sent between devices are 32-bit elements; how exact they have to be, the bound alone decides.
No kernel may reach another device: no remote copies, remote signals or barrier semaphores. Data moves between devices by JAX's collectives and lax.ppermute only.
A program may use at most 128 MiB of HBM per device.

```python
import math
import jax
import jax.numpy as jnp

CX = 24
CY = 32
CZ = 128
RXY = 4
RZ = 8
AGG = 128
PRE = 2
POST = 4
KC = 8
NX = 48
NY = 128
NZ = 512
N_GX = 2
N_GY = 4
N_GZ = 4


def draw_block_agg(key, part):
    span_y = CY // 2
    span_z = CZ // 2
    bands_z = RXY * RZ
    jitter = jax.random.randint(key, (2, NX // 2, NY // 2, NZ // 2), -1, 2, dtype=jnp.int32)
    local_x = (jnp.arange(NX // 2, dtype=jnp.int32) % (CX // 2))[:, None, None]
    local_y = (jnp.arange(NY // 2, dtype=jnp.int32) % span_y)[None, :, None]
    local_z = (jnp.arange(NZ // 2, dtype=jnp.int32) % span_z)[None, None, :]
    keep_plane = (local_x == 0).astype(jnp.int32)
    shift_y = jitter[0] * (1 - keep_plane)
    shift_z = jitter[1] * (1 - keep_plane)
    region_y = jnp.clip(local_y + shift_y, 0, span_y - 1) * RXY // span_y
    region_z = jnp.clip(local_z + shift_z, 0, span_z - 1) * bands_z // span_z
    return (region_y * bands_z + region_z).astype(jnp.int32)


def draw_conductance(key, part):
    key_lines = jax.random.fold_in(key, 11)
    key_fibre = jax.random.fold_in(key, 12)
    key_matrix = jax.random.fold_in(key, 13)
    lines = jax.random.randint(key_lines, (1, NY, NZ), 0, 10, dtype=jnp.int32) < 3
    fibre = jnp.exp(jax.random.uniform(key_fibre, (NX, NY, NZ), jnp.float32, math.log(2.0), math.log(10.0)))
    matrix = jnp.exp(jax.random.uniform(key_matrix, (NX, NY, NZ), jnp.float32, math.log(0.05), math.log(0.2)))
    return jnp.clip(jnp.where(lines, fibre, matrix), 0.05, 10.0).astype(jnp.float32)


def level_of(own_key, dims, split, least, high):
    loudness = 1.0
    for position, shards_of in split:
        draws = jax.random.uniform(jax.random.fold_in(jax.random.fold_in(own_key, 6), position), (shards_of,), jnp.float32, least / len(split), high / len(split))
        loudness = loudness * jnp.repeat(jnp.exp(draws), dims[position] // shards_of).reshape((-1,) + (1,) * (len(dims) - 1 - position))
    return loudness


def gaussian(own_key, extent, scale, limit, shards=(), kind=jnp.bfloat16):
    values = scale * jax.random.normal(own_key, extent, jnp.float32)
    if shards:
        values = values * level_of(own_key, extent, shards, -0.22, 0.18)
    return jnp.clip(values, -limit, limit).astype(kind)


def setup_inputs(seed: int = 0) -> dict:
    keys = jax.random.split(jax.random.key(seed), 5)
    right_side = gaussian(keys[0], (NX, NY, NZ), 1.0, 6.0, ((0, 2), (1, 4), (2, 4)), jnp.float32)
    conductance = draw_conductance(jax.random.fold_in(keys[4], 71), 0)
    absorption = jnp.clip(jnp.exp(math.log(0.02) - 2.30258502 * jax.random.uniform(keys[2], (NX, NY, NZ), jnp.float32) ** level_of(keys[2], (NX, NY, NZ), ((0, 2), (1, 4), (2, 4)), -0.2, 0.2)), 0.002, 0.02)
    block_agg = draw_block_agg(jax.random.fold_in(keys[4], 71), 0)
    return dict(right_side=right_side, conductance=conductance, absorption=absorption, block_agg=block_agg)


OMEGA_FINE = 0.8
OMEGA_COARSE = 0.7


def harmonic(one_side, other_side):
    return 2.0 * (one_side * other_side) / (one_side + other_side)


def block_sum(values):
    size_a, size_b, size_c = values.shape
    return values.reshape(size_a // 2, 2, size_b // 2, 2, size_c // 2, 2).sum(axis=(1, 3, 5))


def upsample(values):
    size_a, size_b, size_c = values.shape
    spread = jnp.broadcast_to(values[:, None, :, None, :, None], (size_a, 2, size_b, 2, size_c, 2))
    return spread.reshape(2 * size_a, 2 * size_b, 2 * size_c)


def neighbour_sum(values, face_x, face_y, face_z):
    padded = jnp.pad(values, 1)
    beside = face_x[1:] * padded[2:, 1:-1, 1:-1] + face_x[:-1] * padded[:-2, 1:-1, 1:-1]
    beside = beside + face_y[:, 1:] * padded[1:-1, 2:, 1:-1] + face_y[:, :-1] * padded[1:-1, :-2, 1:-1]
    beside = beside + face_z[:, :, 1:] * padded[1:-1, 1:-1, 2:] + face_z[:, :, :-1] * padded[1:-1, 1:-1, :-2]
    return beside


def reference(right_side, conductance, absorption, block_agg):
    pad_x = jnp.pad(conductance, ((1, 1), (0, 0), (0, 0)))
    pad_y = jnp.pad(conductance, ((0, 0), (1, 1), (0, 0)))
    pad_z = jnp.pad(conductance, ((0, 0), (0, 0), (1, 1)))
    face_x = harmonic(pad_x[:-1], pad_x[1:])
    face_y = harmonic(pad_y[:, :-1], pad_y[:, 1:])
    face_z = harmonic(pad_z[:, :, :-1], pad_z[:, :, 1:])
    cell_diag = absorption + face_x[:-1] + face_x[1:] + face_y[:, :-1] + face_y[:, 1:] + face_z[:, :, :-1] + face_z[:, :, 1:]

    def fine_apply(values):
        return cell_diag * values - neighbour_sum(values, face_x, face_y, face_z)

    def smooth(values, sweeps):
        for repeat_no in range(sweeps):
            values = values + OMEGA_FINE * (right_side - fine_apply(values)) / cell_diag
        return values

    presmoothed = smooth(jnp.zeros_like(right_side), PRE)
    residual = right_side - fine_apply(presmoothed)

    blocks_x, blocks_y, blocks_z = block_agg.shape
    brick_x = jnp.arange(blocks_x, dtype=jnp.int32) // (CX // 2)
    brick_y = jnp.arange(blocks_y, dtype=jnp.int32) // (CY // 2)
    brick_z = jnp.arange(blocks_z, dtype=jnp.int32) // (CZ // 2)
    brick_ids = (brick_x[:, None, None] * N_GY + brick_y[None, :, None]) * N_GZ + brick_z[None, None, :]
    global_ids = (brick_ids * AGG + block_agg).astype(jnp.int32)
    coarse_count = AGG * N_GX * N_GY * N_GZ

    def aggregate_sum(values, labels):
        return jax.ops.segment_sum(values.reshape(-1), labels.reshape(-1), num_segments=coarse_count)

    block_x = face_x[0::2].reshape(blocks_x + 1, blocks_y, 2, blocks_z, 2).sum(axis=(2, 4))
    block_y = face_y[:, 0::2].reshape(blocks_x, 2, blocks_y + 1, blocks_z, 2).sum(axis=(1, 4))
    block_z = face_z[:, :, 0::2].reshape(blocks_x, 2, blocks_y, 2, blocks_z + 1).sum(axis=(1, 3))
    block_absorb = block_sum(absorption)
    block_diag = block_absorb + block_x[:-1] + block_x[1:] + block_y[:, :-1] + block_y[:, 1:] + block_z[:, :, :-1] + block_z[:, :, 1:]

    coarse_diag = aggregate_sum(block_absorb, global_ids)
    pairs = [(global_ids[:-1], global_ids[1:], block_x[1:-1]),
             (global_ids[:, :-1], global_ids[:, 1:], block_y[:, 1:-1]),
             (global_ids[:, :, :-1], global_ids[:, :, 1:], block_z[:, :, 1:-1])]
    for low_ids, high_ids, cut_weights in pairs:
        crossing = jnp.where(low_ids != high_ids, cut_weights, 0.0)
        coarse_diag = coarse_diag + aggregate_sum(crossing, low_ids) + aggregate_sum(crossing, high_ids)

    def coarse_apply(coarse_vec):
        block_vec = coarse_vec[global_ids]
        applied = block_diag * block_vec - neighbour_sum(block_vec, block_x, block_y, block_z)
        return aggregate_sum(applied, global_ids)

    coarse_rhs = aggregate_sum(block_sum(residual), global_ids)
    correction = jnp.zeros((coarse_count,), jnp.float32)
    for turn_no in range(KC):
        correction = correction + OMEGA_COARSE * (coarse_rhs - coarse_apply(correction)) / coarse_diag
    corrected = presmoothed + upsample(correction[global_ids])
    return smooth(corrected, POST)
```

```python
import functools

import jax
import jax.numpy as jnp
from jax import lax
from jax.experimental import pallas as pl
from jax.experimental.pallas import tpu as pltpu
from jax.sharding import PartitionSpec as P

AGG = 128
LANES = 128
HALO = 4
BLOCK_HALO = HALO // 2
POST = 4
KC = 8
OMEGA_FINE = 0.8
OMEGA_COARSE = 0.7
F32 = jnp.float32
BF16 = jnp.bfloat16
SMEM = pl.BlockSpec(memory_space=pltpu.SMEM)
VMEM = pl.BlockSpec(memory_space=pltpu.VMEM)
IX, PARITY, X_LOW, X_HIGH, Y_LOW, Y_HIGH, Z_LOW, Z_HIGH = range(8)


def call(kernel, outs, scratch=(), limit=16, flops=10**6):
    def run(flags, *arrays):
        return pl.pallas_call(
            kernel,
            out_shape=outs,
            in_specs=[SMEM] + [VMEM] * len(arrays),
            out_specs=jax.tree.map(lambda _: VMEM, outs),
            scratch_shapes=list(scratch),
            compiler_params=pltpu.CompilerParams(vmem_limit_bytes=limit * 2**20),
            cost_estimate=pl.CostEstimate(flops=flops, bytes_accessed=10**5, transcendentals=0),
        )(flags, *arrays)

    return run


def shaped(*shape):
    return jax.ShapeDtypeStruct(shape, F32)


def lane_no(shape):
    return lax.broadcasted_iota(jnp.int32, shape, len(shape) - 1)


def row_no(shape):
    return lax.broadcasted_iota(jnp.int32, shape, len(shape) - 2)


def turned(values, shift, axis):
    shift = shift % values.shape[axis]
    return values if shift == 0 else pltpu.roll(values, shift, axis)


def picked(values, index):
    return jnp.take_along_axis(values, index, axis=1, mode="promise_in_bounds")


def pack_x_kernel(count, fields, labels, flags, *refs):
    ins, outs = refs[: fields + labels], refs[fields + labels :]
    nx = ins[0].shape[0]

    def fill(out, fine_at, block_at):
        for f in range(fields):
            out[HALO * f : HALO * (f + 1)] = ins[f][pl.ds(fine_at, HALO)]
        if labels:
            last = HALO * fields
            out[last] = jnp.zeros(out.shape[1:], F32)
            rows = ins[-1].shape[1]
            for b in range(BLOCK_HALO):
                out[last, rows * b : rows * (b + 1), : ins[-1].shape[2]] = ins[-1][block_at + b].astype(F32)

    if count == 2:
        first = flags[IX] == 0
        fill(outs[0], jnp.where(first, nx - HALO, 0), jnp.where(first, nx // 2 - BLOCK_HALO, 0))
    else:
        fill(outs[0], nx - HALO, nx // 2 - BLOCK_HALO)
        fill(outs[1], 0, 0)


def slab_of(own, low, high, f, x):
    nx = own.shape[0]
    if x < HALO:
        return low[HALO * f + x]
    if x < HALO + nx:
        return own[x - HALO]
    return high[HALO * f + x - HALO - nx]


def label_slab(own, low, high, f, b):
    nb, rows, width = own.shape
    if b < BLOCK_HALO:
        return low[HALO * f, rows * b : rows * (b + 1), :width]
    if b < BLOCK_HALO + nb:
        return own[b - BLOCK_HALO].astype(F32)
    at = b - BLOCK_HALO - nb
    return high[HALO * f, rows * at : rows * (at + 1), :width]


def pack_y_kernel(fields, labels, flags, *refs):
    ins = refs[: fields + labels]
    low, high = refs[fields + labels : fields + labels + 2]
    to_high, to_low = refs[fields + labels + 2 :]
    nx, ny = ins[0].shape[0], ins[0].shape[1]
    wide = nx + 2 * HALO
    for f in range(fields):
        for x in range(wide):
            slab = slab_of(ins[f], low, high, f, x)
            at = (f * wide + x) * HALO
            to_high[at : at + HALO] = slab[ny - HALO :]
            to_low[at : at + HALO] = slab[:HALO]
    if labels:
        base = fields * wide * HALO
        nb, rows, width = ins[-1].shape
        to_high[base:] = jnp.zeros((to_high.shape[0] - base, LANES), F32)
        to_low[base:] = jnp.zeros((to_low.shape[0] - base, LANES), F32)
        for b in range(nb + 2 * BLOCK_HALO):
            slab = label_slab(ins[-1], low, high, fields, b)
            at = base + BLOCK_HALO * b
            to_high[at : at + BLOCK_HALO, :width] = slab[rows - BLOCK_HALO :]
            to_low[at : at + BLOCK_HALO, :width] = slab[:BLOCK_HALO]


def pack_z_kernel(fields, labels, flags, *refs):
    ins = refs[: fields + labels]
    x_low, x_high, y_low, y_high = refs[fields + labels : fields + labels + 4]
    outs = refs[fields + labels + 4 :]
    wide_ref, send = outs[0], outs[1]
    nx, ny = ins[0].shape[0], ins[0].shape[1]
    wide, tall = nx + 2 * HALO, ny + 2 * HALO
    group = LANES // (2 * HALO)
    lane = lane_no((tall, LANES))
    for f in range(fields):
        for g in range(wide // group):
            packed = jnp.zeros((tall, LANES), F32)
            for k in range(group):
                x = g * group + k
                at = (f * wide + x) * HALO
                wide_ref[f, x, HALO : HALO + ny] = slab_of(ins[f], x_low, x_high, f, x)
                wide_ref[f, x, :HALO] = y_low[at : at + HALO]
                wide_ref[f, x, HALO + ny :] = y_high[at : at + HALO]
                moved = turned(wide_ref[f, x], 2 * HALO * k + HALO, 1)
                packed = jnp.where(lane // (2 * HALO) == k, moved, packed)
            at = (f * (wide // group) + g) * tall
            send[at : at + tall] = packed
    if labels:
        base = fields * (wide // group) * tall
        label_ref = outs[2]
        nb, rows, width = ins[-1].shape
        span = rows + 2 * BLOCK_HALO
        label_ref[...] = jnp.zeros(label_ref.shape, F32)
        lane = lane_no((span, LANES))
        packed = jnp.zeros((span, LANES), F32)
        for b in range(nb + 2 * BLOCK_HALO):
            at = fields * wide * HALO + BLOCK_HALO * b
            label_ref[b, BLOCK_HALO : BLOCK_HALO + rows, :width] = label_slab(ins[-1], x_low, x_high, fields, b)
            label_ref[b, :BLOCK_HALO] = y_low[at : at + BLOCK_HALO]
            label_ref[b, BLOCK_HALO + rows : span] = y_high[at : at + BLOCK_HALO]
            slab = label_ref[b, :span]
            slab = jnp.where(lane < width, slab, turned(slab, width, 1))
            moved = turned(slab, 2 * BLOCK_HALO * b + BLOCK_HALO - width, 1)
            packed = jnp.where(lane // (2 * BLOCK_HALO) == b, moved, packed)
        send[base:] = jnp.zeros((send.shape[0] - base, LANES), F32)
        send[base : base + span] = packed


def permuted(values, axes, pairs):
    return lax.ppermute(values, axes, pairs)


class Links:
    def __init__(self, mesh):
        self.sizes = [mesh.shape[a] for a in ("gx", "gy", "gz")]
        n_x, n_y, n_z = self.sizes
        self.ring_x = [(i, (i + 1) % n_x) for i in range(n_x)]
        self.ring_y = [(i, (i + 1) % n_y) for i in range(n_y)]
        self.snake = []
        for i in range(n_x):
            for j in range(0, n_y, 2):
                nodes = [(i * n_y + j) * n_z + k for k in range(n_z)]
                nodes += [(i * n_y + j + 1) * n_z + k for k in reversed(range(n_z))]
                self.snake += [(nodes[m], nodes[(m + 1) % len(nodes)]) for m in range(len(nodes))]

    @staticmethod
    def back(pairs):
        return [(b, a) for a, b in pairs]

    def x(self, sends):
        if self.sizes[0] == 2:
            got = permuted(sends[0], "gx", self.ring_x)
            return got, got
        return permuted(sends[0], "gx", self.ring_x), permuted(sends[-1], "gx", self.back(self.ring_x))

    def y(self, to_high, to_low):
        return permuted(to_high, "gy", self.ring_y), permuted(to_low, "gy", self.back(self.ring_y))

    def z(self, send):
        axes = ("gx", "gy", "gz")
        return permuted(send, axes, self.snake), permuted(send, axes, self.back(self.snake))


def widened(links, flags, fields, labels=()):
    count = len(fields)
    has = len(labels)
    nx, ny, nz = fields[0].shape
    wide, tall = nx + 2 * HALO, ny + 2 * HALO
    blocks = nx // 2 + 2 * BLOCK_HALO
    arrays = tuple(fields) + tuple(labels)
    n_send = 1 if links.sizes[0] == 2 else 2
    sends = call(
        functools.partial(pack_x_kernel, links.sizes[0], count, has),
        [shaped(HALO * count + has, ny, nz)] * n_send,
    )(flags, *arrays)
    x_low, x_high = links.x(sends)
    rows = count * wide * HALO + has * blocks * BLOCK_HALO
    to_high, to_low = call(
        functools.partial(pack_y_kernel, count, has), [shaped(rows, nz)] * 2
    )(flags, *arrays, x_low, x_high)
    y_low, y_high = links.y(to_high, to_low)
    groups = wide // (LANES // (2 * HALO))
    rows = count * groups * tall + has * 24
    outs = [shaped(count, wide, tall, nz), shaped(rows, nz)]
    if has:
        outs.append(shaped(blocks, 24, LANES))
    got = call(functools.partial(pack_z_kernel, count, has), outs)(
        flags, *arrays, x_low, x_high, y_low, y_high
    )
    forth, back = links.z(got[1])
    return got[0], forth, back, (got[2] if has else None)


def lane_halo(flags, forth, back, at, rows):
    lane = lane_no((rows, LANES))
    one, two = forth[at : at + rows], back[at : at + rows]
    even = flags[PARITY] == 0
    low, high = jnp.where(even, one, two), jnp.where(even, two, one)
    return jnp.where(lane % (2 * HALO) < HALO, low, high)


def spread_lanes(flags, forth, back, wide_ref, f, out):
    wide, tall = out.shape[0], out.shape[2]
    group = LANES // (2 * HALO)
    for g in range(wide // group):
        packed = lane_halo(flags, forth, back, (f * (wide // group) + g) * tall, tall)
        for k in range(group):
            x = g * group + k
            out[x, 0] = wide_ref[f, x]
            out[x, 1] = turned(packed, -(2 * HALO * k + HALO), 1)


def get(ref, x):
    return jnp.concatenate([ref[x, 0], ref[x, 1]], axis=1)


def put(ref, x, values):
    ref[x, 0] = values[:, :LANES]
    ref[x, 1] = values[:, LANES:]


def weight(one, two):
    return 2.0 * (one * two) / (one + two)


def beside(field, x, wx, wy, wz):
    here, face_y, face_z = get(field, x), get(wy, x), get(wz, x)
    total = get(wx, x) * get(field, x + 1) + get(wx, x - 1) * get(field, x - 1)
    total = total + face_y * turned(here, -1, 0) + turned(face_y * here, 1, 0)
    return total + face_z * turned(here, -1, 1) + turned(face_z * here, 1, 1)


def pack_rows(values):
    half = values.shape[0] // 2
    lane = lane_no((half, LANES))
    return jnp.where(lane < LANES // 2, values[:half], turned(values[half:], LANES // 2, 1))


def fine_kernel(flags, wide_ref, forth, back, label_ref, *refs):
    (inv_diag, start, wx, wy, wz, pre, block_label, block_near, block_weight, face_label, face_near, face_weight,
     scaled_rhs, scale, cond, rhs, absorb, diag, once, res, side_rows, side_lanes) = refs
    wide, _, tall, _ = inv_diag.shape
    both = 2 * LANES
    nx, ny = pre.shape[0], pre.shape[1]
    last = HALO + nx
    for f, out in enumerate((cond, rhs, absorb)):
        spread_lanes(flags, forth, back, wide_ref, f, out)
    row, lane = row_no((tall, both)), lane_no((tall, both))
    keep_y = jnp.where(
        row == HALO - 1, flags[Y_LOW], jnp.where(row == HALO + ny - 1, flags[Y_HIGH], 1)
    ).astype(F32)
    keep_z = jnp.where(
        lane == both - 1, flags[Z_LOW], jnp.where(lane == LANES - 1, flags[Z_HIGH], 1)
    ).astype(F32)

    def fields(x, before):
        here = get(cond, x)
        keep = jnp.where(x == HALO - 1, flags[X_LOW], jnp.where(x == last - 1, flags[X_HIGH], 1)).astype(F32)
        face_x = keep * weight(here, get(cond, jnp.minimum(x + 1, wide - 1)))
        face_y = keep_y * weight(here, turned(here, -1, 0))
        face_z = keep_z * weight(here, turned(here, -1, 1))
        total = get(absorb, x) + face_x + before
        total = total + face_y + turned(face_y, 1, 0) + face_z + turned(face_z, 1, 1)
        inverse = OMEGA_FINE / total
        for ref, values in ((wx, face_x), (wy, face_y), (wz, face_z), (diag, total), (inv_diag, inverse)):
            put(ref, x, values)
        put(start, x, inverse * get(rhs, x))
        return face_x

    lax.fori_loop(0, wide, fields, jnp.zeros((tall, both), F32))

    @pl.loop(HALO - 1, last + 1)
    def _(x):
        put(once, x, (2.0 - OMEGA_FINE) * get(start, x) + get(inv_diag, x) * beside(start, x, wx, wy, wz))

    @pl.loop(HALO, last)
    def _(x):
        full = get(rhs, x) - get(diag, x) * get(once, x) + beside(once, x, wx, wy, wz)
        res[x, 0] = full[:, :LANES]
        pre[x - HALO] = once[x, 0, HALO : HALO + ny]

    nb, half, width = nx // 2, ny // 2, LANES // 2
    lane = lane_no((half, LANES))
    row = row_no((half, LANES))
    even = 2 * (lane % width)
    odd = even + 1
    iota = row_no((AGG, LANES)).astype(F32)
    side_rows[...] = jnp.zeros(side_rows.shape, F32)
    side_lanes[...] = jnp.zeros(side_lanes.shape, F32)

    def rows_at(ref, x, off):
        return ref[x, 0, pl.ds(off, half, stride=2)]

    def four(ref, x):
        return sum(rows_at(ref, x + a, HALO + b) for a in range(2) for b in range(2))

    def in_pairs(values):
        return picked(values + turned(values, -1, 1), even)

    def edge_x(x):
        return in_pairs(rows_at(wx, x, HALO) + rows_at(wx, x, HALO + 1))

    def block_step(b, carry):
        low_x, acc_r, acc_q = carry
        x = HALO + 2 * b
        at = b + BLOCK_HALO
        rows = pl.ds(BLOCK_HALO, half)
        own = label_ref[at, rows]
        near_x, past_x = label_ref[at + 1, rows], label_ref[at - 1, rows]
        high_x = edge_x(x + 1)
        high_y = in_pairs(rows_at(wy, x, HALO + 1) + rows_at(wy, x + 1, HALO + 1))
        low_y = in_pairs(rows_at(wy, x, HALO - 1) + rows_at(wy, x + 1, HALO - 1))
        side = four(wz, x)
        high_z = picked(side, odd)
        end = sum(
            wz[x + a, 1, pl.ds(HALO + c, half, stride=2)] for a in range(2) for c in range(2)
        )
        low_z = picked(jnp.where(lane == 0, turned(end, 1, 1), turned(side, 1, 1)), even)
        near_y, past_y = turned(own, -1, 0), turned(own, 1, 0)
        near_z, past_z = turned(own, -1, 1), turned(own, 1, 1)
        end_x, end_y, end_z = b == nb - 1, row == half - 1, lane == width - 1
        total = in_pairs(four(absorb, x))
        total = total + jnp.where((near_x != own) | end_x, high_x, 0.0)
        total = total + jnp.where((past_x != own) | (b == 0), low_x, 0.0)
        total = total + jnp.where((near_y != own) | end_y, high_y, 0.0)
        total = total + jnp.where((past_y != own) | (row == 0), low_y, 0.0)
        total = total + jnp.where((near_z != own) | end_z, high_z, 0.0)
        total = total + jnp.where((past_z != own) | (lane == 0), low_z, 0.0)
        packed = pack_rows(own)
        block_label[b] = packed
        block_near[0, b], block_near[1, b], block_near[2, b] = pack_rows(near_x), pack_rows(near_y), pack_rows(near_z)
        block_weight[0, b] = pack_rows(jnp.where(end_x, 0.0, high_x))
        block_weight[1, b] = pack_rows(jnp.where(end_y, 0.0, high_y))
        block_weight[2, b] = pack_rows(jnp.where(end_z, 0.0, high_z))
        sums, total = pack_rows(in_pairs(four(res, x))), pack_rows(total)
        for r in range(half // 2):
            hit = packed[r : r + 1] == iota
            acc_r = acc_r + jnp.where(hit, sums[r : r + 1], 0.0)
            acc_q = acc_q + jnp.where(hit, total[r : r + 1], 0.0)

        @pl.when(b == 0)
        def _():
            face_label[0] = packed
            face_near[0] = pack_rows(past_x)
            face_weight[0] = pack_rows(low_x)

        @pl.when(end_x)
        def _():
            face_label[1] = packed
            face_near[1] = pack_rows(near_x)
            face_weight[1] = pack_rows(high_x)

        here = pl.ds(b, 1)
        side_rows[0, here], side_rows[1, here] = own[:1], own[half - 1 :]
        side_rows[2, here] = label_ref[at, pl.ds(BLOCK_HALO - 1, 1)]
        side_rows[3, here] = label_ref[at, pl.ds(BLOCK_HALO + half, 1)]
        side_rows[4, here], side_rows[5, here] = low_y[:1], high_y[half - 1 :]
        mine = lane == b
        for s, (values, at_lane) in enumerate(((own, 0), (own, width - 1), (low_z, 0), (high_z, width - 1))):
            one = jnp.broadcast_to(values[:, at_lane : at_lane + 1], (half, LANES))
            side_lanes[s] = jnp.where(mine, one, side_lanes[s])
        return high_x, acc_r, acc_q

    nothing = jnp.zeros((AGG, LANES), F32)
    _, acc_r, acc_q = lax.fori_loop(0, nb, block_step, (edge_x(HALO - 1), nothing, nothing))
    for s in range(2):
        face_label[2 + s] = pack_rows(side_rows[s])
        face_near[2 + s] = pack_rows(side_rows[2 + s])
        face_weight[2 + s] = pack_rows(jnp.where(lane < width, side_rows[4 + s], 0.0))
        face_label[4 + s] = pack_rows(side_lanes[s])
        face_weight[4 + s] = pack_rows(side_lanes[2 + s])
    base = 3 * (wide // (LANES // (2 * HALO))) * tall
    even_place = flags[PARITY] == 0
    one, two = forth[pl.ds(base + BLOCK_HALO, half)], back[pl.ds(base + BLOCK_HALO, half)]
    below, above = jnp.where(even_place, one, two), jnp.where(even_place, two, one)
    span = 2 * BLOCK_HALO
    spot = span * jnp.minimum(lane + BLOCK_HALO, LANES // span - 1)
    face_near[4] = pack_rows(picked(below, spot + BLOCK_HALO - 1))
    face_near[5] = pack_rows(picked(above, spot + BLOCK_HALO))

    def lane_total(values):
        ones = jnp.ones((8, LANES), F32)
        return lax.dot_general(
            ones, values, (((1,), (1,)), ((), ())), precision=lax.Precision.HIGHEST, preferred_element_type=F32
        )

    scale[...] = OMEGA_COARSE / lane_total(acc_q)
    scaled_rhs[...] = scale[...] * lane_total(acc_r)


def tiles_kernel(flags, block_label, block_near, block_weight, face_label, face_near, face_weight, out, left, right):
    iota = row_no((AGG, LANES)).astype(F32)
    depth = block_label.shape[1]

    def product(labels, pairs):
        for r in range(depth):
            lanes = pl.ds(r * LANES, LANES)
            left[:, lanes] = jnp.where(labels[r : r + 1] == iota, 1.0, 0.0).astype(BF16)
            held = sum(jnp.where(near[r : r + 1] == iota, w[r : r + 1], 0.0) for near, w in pairs)
            high = held.astype(BF16)
            right[:AGG, lanes] = high
            right[AGG:, lanes] = (held - high.astype(F32)).astype(BF16)
        return lax.dot_general(
            left[...], right[...], (((1,), (1,)), ((), ())), preferred_element_type=F32
        )

    def own_step(b, total):
        return total + product(block_label[b], [(block_near[d, b], block_weight[d, b]) for d in range(3)])

    own = lax.fori_loop(0, block_label.shape[0], own_step, jnp.zeros((AGG, 2 * AGG), F32))
    own = own[:, :AGG] + own[:, AGG:]
    own = jnp.where(row_no((AGG, AGG)) == lane_no((AGG, AGG)), 0.0, own + own.T)

    def keep(t, tile):
        high = tile.astype(BF16)
        out[pl.ds(t * AGG, AGG), :AGG] = high
        out[pl.ds(t * AGG, AGG), AGG:] = (tile - high.astype(F32)).astype(BF16)

    keep(0, own)

    @pl.loop(0, 6)
    def _(s):
        tile = product(face_near[s], [(face_label[s], face_weight[s])])
        keep(s + 1, tile[:, :AGG] + tile[:, AGG:])


def turn_kernel(flags, tiles, scaled_rhs, scale, own, x_low, x_high, y_low, y_high, forth, back, out):
    even = flags[PARITY] == 0
    one, two = forth[...], back[...]
    vectors = [own[...], x_low[...], x_high[...], y_low[...], y_high[...]]
    vectors += [jnp.where(even, one, two), jnp.where(even, two, one)]
    row = row_no((8, AGG))
    parts = []
    for v in vectors:
        high = v.astype(BF16).astype(F32)
        parts.append(jnp.where(row == 0, high, jnp.where(row == 1, v - high, 0.0)).astype(BF16))
    got = jnp.dot(jnp.concatenate(parts, axis=1), tiles[...], preferred_element_type=F32)
    applied = jnp.sum(got[:, :AGG] + got[:, AGG:], axis=0, keepdims=True)
    out[...] = (1.0 - OMEGA_COARSE) * own[...] + scaled_rhs[...] + scale[...] * applied


def correct_kernel(flags, pre, label_ref, coarse, out):
    nb, half = pre.shape[0] // 2, pre.shape[1] // 2
    to_block = lane_no((half, LANES)) // 2
    table = jnp.broadcast_to(coarse[:1], (half, LANES))

    @pl.loop(0, nb)
    def _(b):
        labels = picked(label_ref[b + BLOCK_HALO, pl.ds(BLOCK_HALO, half)], to_block)
        values = picked(table, labels.astype(jnp.int32))
        for a in range(2):
            for c in range(2):
                rows = pl.ds(c, half, stride=2)
                out[2 * b + a, rows] = pre[2 * b + a, rows] + values


def post_kernel(flags, wide_ref, forth, back, inv_diag, start, wx, wy, wz, out, one, two):
    spread_lanes(flags, forth, back, wide_ref, 0, one)
    wide = one.shape[0]
    nx, ny = out.shape[0], out.shape[1]

    def sweep(src, x):
        kept = (1.0 - OMEGA_FINE) * get(src, x) + get(start, x)
        return kept + get(inv_diag, x) * beside(src, x, wx, wy, wz)

    buffers = (one, two)
    for s in range(POST - 1):
        src, dst = buffers[s % 2], buffers[(s + 1) % 2]

        @pl.loop(s + 1, wide - s - 1)
        def _(x):
            put(dst, x, sweep(src, x))

    src = buffers[(POST - 1) % 2]

    @pl.loop(HALO, HALO + nx)
    def _(x):
        out[x - HALO] = sweep(src, x)[HALO : HALO + ny, :LANES]


def body(links, right_side, conductance, absorption, block_agg):
    nx, ny, nz = right_side.shape
    wide, tall = nx + 2 * HALO, ny + 2 * HALO
    nb = nx // 2
    ix, iy, iz = (lax.axis_index(a) for a in ("gx", "gy", "gz"))
    n_x, n_y, n_z = links.sizes
    flags = jnp.stack(
        [ix, iy % 2, ix > 0, ix < n_x - 1, iy > 0, iy < n_y - 1, iz > 0, iz < n_z - 1]
    ).astype(jnp.int32)
    wide_fields, forth, back, labels = widened(links, flags, (conductance, right_side, absorption), (block_agg,))
    big = shaped(wide, 2, tall, nz)
    outs = [big] * 5 + [shaped(nx, ny, nz)]
    outs += [shaped(nb, 8, LANES), shaped(3, nb, 8, LANES), shaped(3, nb, 8, LANES)]
    outs += [shaped(6, 8, LANES)] * 3 + [shaped(8, AGG)] * 2
    scratch = [pltpu.VMEM((wide, 2, tall, nz), F32)] * 5 + [pltpu.VMEM((wide, 1, tall, nz), F32)]
    scratch += [pltpu.VMEM((6, 16, LANES), F32), pltpu.VMEM((4, 16, LANES), F32)]
    got = call(fine_kernel, outs, scratch, limit=40)(flags, wide_fields, forth, back, labels)
    inv_diag, start, wx, wy, wz, pre = got[:6]
    scaled_rhs, scale = got[12:]
    tiles = call(
        tiles_kernel,
        jax.ShapeDtypeStruct((7 * AGG, 2 * AGG), BF16),
        [pltpu.VMEM((AGG, 8 * LANES), BF16), pltpu.VMEM((2 * AGG, 8 * LANES), BF16)],
    )(flags, *got[6:12])
    coarse = scaled_rhs
    for _ in range(KC - 1):
        near = links.x([coarse] * (1 if n_x == 2 else 2)) + links.y(coarse, coarse) + links.z(coarse)
        coarse = call(turn_kernel, shaped(8, AGG))(flags, tiles, scaled_rhs, scale, coarse, *near)
    corrected = call(correct_kernel, shaped(nx, ny, nz))(flags, pre, labels, coarse)
    wide_iter, forth, back, _ = widened(links, flags, (corrected,))
    return call(post_kernel, shaped(nx, ny, nz), [pltpu.VMEM((wide, 2, tall, nz), F32)] * 2, limit=24)(
        flags, wide_iter, forth, back, inv_diag, start, wx, wy, wz
    )


def solution(mesh):
    spec = P("gx", "gy", "gz")
    return jax.shard_map(
        functools.partial(body, Links(mesh)), mesh=mesh, in_specs=(spec,) * 4, out_specs=spec, check_vma=False
    )
```

```python
import functools

import jax
import jax.numpy as jnp
from jax import lax
from jax.experimental import pallas as pl
from jax.experimental.pallas import tpu as pltpu
from jax.sharding import PartitionSpec as P

AGG = 128
LANES = 128
SUB = 8
HALO = 4
WIDTHS = (4, 3, 3)
POST = 4
KC = 8
OMEGA_FINE = 0.8
OMEGA_COARSE = 0.7
F32 = jnp.float32
BF16 = jnp.bfloat16
SMEM = pl.BlockSpec(memory_space=pltpu.SMEM)
VMEM = pl.BlockSpec(memory_space=pltpu.VMEM)
IX, PARITY, X_LOW, X_HIGH, Y_LOW, Y_HIGH, Z_LOW, Z_HIGH = range(8)


def call(kernel, outs, scratch=(), limit=16, flops=10**6, in_specs=None):
    def run(flags, *arrays):
        return pl.pallas_call(
            kernel,
            out_shape=outs,
            in_specs=[SMEM] + (in_specs or [VMEM] * len(arrays)),
            out_specs=jax.tree.map(lambda _: VMEM, outs),
            scratch_shapes=list(scratch),
            compiler_params=pltpu.CompilerParams(vmem_limit_bytes=limit * 2**20),
            cost_estimate=pl.CostEstimate(flops=flops, bytes_accessed=10**5, transcendentals=0),
        )(flags, *arrays)

    return run


def shaped(*shape):
    return jax.ShapeDtypeStruct(shape, F32)


def lane_no(shape):
    return lax.broadcasted_iota(jnp.int32, shape, len(shape) - 1)


def row_no(shape):
    return lax.broadcasted_iota(jnp.int32, shape, len(shape) - 2)


def turned(values, shift, axis):
    if isinstance(shift, int):
        shift = shift % values.shape[axis]
        if shift == 0:
            return values
    return pltpu.roll(values, shift, axis)


def picked(values, index):
    return jnp.take_along_axis(values, index, axis=1, mode="promise_in_bounds")


class Frame:
    def __init__(self, nx, ny):
        self.nx, self.ny = nx, ny
        self.wide, self.tall = nx + 2 * HALO, ny + 2 * HALO
        self.rows = self.tall + 2 * SUB
        self.span = pl.ds(SUB, self.tall)
        self.own = SUB + HALO
        self.main = (self.wide, self.rows, LANES)
        self.ends = (2, self.rows, LANES)


def bases(widths):
    return [sum(widths[:f]) for f in range(len(widths) + 1)]


def pack_x_kernel(count, widths, flags, *refs):
    fields = len(widths)
    ins, labels, outs = refs[:fields], refs[fields], refs[fields + 1 : -2]
    near, sems = refs[-2:]
    nx, ny = ins[0].shape[0], ins[0].shape[1]
    base = bases(widths)
    copies = []
    for s, out in enumerate(outs):
        for f, (ref, width) in enumerate(zip(ins, widths)):
            if count == 2:
                at = jnp.where(flags[IX] == 0, nx - width, 0)
            else:
                at = (nx - width, 0)[s]
            copies.append(
                pltpu.make_async_copy(
                    ref.at[pl.ds(at, width)], out.at[pl.ds(base[f], width)], sems.at[len(copies)]
                )
            )
        if count == 2:
            at = jnp.where(flags[IX] == 0, nx // 2 - 1, 0)
        else:
            at = (nx // 2 - 1, 0)[s]
        copies.append(pltpu.make_async_copy(labels.at[at], near.at[s], sems.at[len(copies)]))
    for copy in copies:
        copy.start()
    for copy in copies:
        copy.wait()
    for s, out in enumerate(outs):
        out[base[-1]] = jnp.zeros(out.shape[1:], F32)
        out[base[-1], : ny // 2, : near.shape[2]] = near[s].astype(F32)


def slab_of(own, low, high, base, width, x):
    nx = own.shape[0]
    if HALO <= x < HALO + nx:
        return own[x - HALO]
    if x < HALO:
        at = x - (HALO - width)
        return low[base + at] if at >= 0 else None
    at = x - HALO - nx
    return high[base + at] if at < width else None


def pack_y_kernel(widths, labels, flags, *refs):
    fields = len(widths)
    ins = refs[:fields]
    low, high = refs[fields + labels : fields + labels + 2]
    to_high, to_low = refs[fields + labels + 2 :]
    nx, ny = ins[0].shape[0], ins[0].shape[1]
    frame = Frame(nx, ny)
    base = bases(widths)
    for f in range(fields):
        for x in range(frame.wide):
            slab = slab_of(ins[f], low, high, base[f], widths[f], x)
            at = (f * frame.wide + x) * HALO
            if slab is None:
                slab = jnp.ones((ny, LANES), F32)
            to_high[at : at + HALO] = slab[ny - HALO :]
            to_low[at : at + HALO] = slab[:HALO]
    if labels:
        at = fields * frame.wide * HALO
        nb, rows, width = refs[fields].shape
        for out, row in ((to_high, rows - 1), (to_low, 0)):
            out[at:] = jnp.zeros((out.shape[0] - at, LANES), F32)
            for b in range(nb):
                out[at + b : at + b + 1, :width] = refs[fields][b, row : row + 1].astype(F32)


def pack_z_kernel(widths, labels, flags, *refs):
    fields = len(widths)
    ins = refs[:fields]
    x_low, x_high, y_low, y_high = refs[fields + labels : fields + labels + 4]
    wide_ref, send_forth, send_back = refs[fields + labels + 4 :]
    nx, ny = ins[0].shape[0], ins[0].shape[1]
    frame = Frame(nx, ny)
    base = bases(widths)
    tall, own = frame.tall, frame.own
    even = flags[PARITY] == 0

    def send(at, count, to_high, to_low):
        send_forth[at : at + count] = jnp.where(even, to_high, to_low)
        send_back[at : at + count] = jnp.where(even, to_low, to_high)

    group = lane_no((tall, LANES)) // HALO
    spare = jnp.ones((SUB, LANES), F32)
    for f in range(fields):
        to_high = to_low = jnp.ones((tall, LANES), F32)
        for x in range(frame.wide):
            at = (f * frame.wide + x) * HALO
            slab = slab_of(ins[f], x_low, x_high, base[f], widths[f], x)
            wide_ref[f, x, own : own + ny] = jnp.ones((ny, LANES), F32) if slab is None else slab
            wide_ref[f, x, SUB:own] = y_low[at : at + HALO]
            wide_ref[f, x, own + ny : own + ny + HALO] = y_high[at : at + HALO]
            wide_ref[f, x, :SUB] = spare
            wide_ref[f, x, SUB + tall :] = spare
            moved = turned(wide_ref[f, x, SUB : SUB + tall], HALO * (x + 1), 1)
            to_high = jnp.where(group == x, moved, to_high)
            to_low = jnp.where(group == (x + 1) % frame.wide, moved, to_low)
        send(f * tall, tall, to_high, turned(to_low, -HALO, 1))
    if labels:
        nb, rows, width = refs[fields].shape
        lane = lane_no((rows, LANES))
        to_high = to_low = jnp.zeros((rows, LANES), F32)
        for b in range(nb):
            slab = refs[fields][b].astype(F32)
            to_high = jnp.where(lane == b, slab[:, width - 1 :], to_high)
            to_low = jnp.where(lane == b, slab[:, :1], to_low)
        send(fields * tall, rows, to_high, to_low)


class Links:
    def __init__(self, mesh):
        self.sizes = [mesh.shape[a] for a in ("gx", "gy", "gz")]
        n_x, n_y, n_z = self.sizes
        self.ring_x = [(i, (i + 1) % n_x) for i in range(n_x)]
        self.ring_y = [(i, (i + 1) % n_y) for i in range(n_y)]
        self.snake = []
        for i in range(n_x):
            for j in range(0, n_y, 2):
                nodes = [(i * n_y + j) * n_z + k for k in range(n_z)]
                nodes += [(i * n_y + j + 1) * n_z + k for k in reversed(range(n_z))]
                self.snake += [(nodes[m], nodes[(m + 1) % len(nodes)]) for m in range(len(nodes))]

    @staticmethod
    def back(pairs):
        return [(b, a) for a, b in pairs]

    def x(self, sends):
        if self.sizes[0] == 2:
            got = lax.ppermute(sends[0], "gx", self.ring_x)
            return got, got
        return lax.ppermute(sends[0], "gx", self.ring_x), lax.ppermute(sends[-1], "gx", self.back(self.ring_x))

    def y(self, to_high, to_low):
        return lax.ppermute(to_high, "gy", self.ring_y), lax.ppermute(to_low, "gy", self.back(self.ring_y))

    def z(self, forth, back):
        axes = ("gx", "gy", "gz")
        return lax.ppermute(forth, axes, self.snake), lax.ppermute(back, axes, self.back(self.snake))


def widened(links, flags, widths, arrays, from_x):
    fields, labels = len(widths), len(arrays) - len(widths)
    nx, ny, nz = arrays[0].shape
    frame = Frame(nx, ny)
    rows = fields * frame.wide * HALO + labels * ny // 2
    sends = call(functools.partial(pack_y_kernel, widths, labels), [shaped(rows, nz)] * 2)(flags, *arrays, *from_x)
    from_y = links.y(*sends)
    rows = fields * frame.tall + labels * ny // 2
    wide, *sends = call(
        functools.partial(pack_z_kernel, widths, labels), [shaped(fields, *frame.main)] + [shaped(rows, nz)] * 2
    )(flags, *arrays, *from_x, *from_y)
    return (wide, *links.z(*sends)), from_y


def sides(flags, forth, back):
    even = flags[PARITY] == 0
    return jnp.where(even, forth, back), jnp.where(even, back, forth)


def weight(one, two):
    return 2.0 * (one * two) / (one + two)


def lane_mask(x):
    return ((lane_no((1, LANES)) - (HALO * x + HALO - 1)) & (LANES - 1)) < 2


def edge_step(here, x, edges):
    return jnp.where(lane_mask(x), turned(here, HALO * x + HALO, 1), edges)


def joined(below, above):
    lane = lane_no(below.shape)
    return jnp.where(lane % HALO == HALO - 1, below, turned(above, HALO, 1))


def next_and_last(here, join, x):
    lane = lane_no((1, LANES))
    edge = turned(join, (LANES - HALO) - HALO * x, 1)
    upper = turned(jnp.where(lane == 0, edge, here), -1, 1)
    lower = turned(jnp.where(lane == LANES - 1, edge, here), 1, 1)
    return upper, lower


def ends_near(below, above, edges):
    layer = lane_no((1, LANES)) % HALO
    return (
        jnp.where(layer == HALO - 1, turned(edges, -1, 1), turned(below, -1, 1)),
        turned(below, 1, 1),
        turned(above, -1, 1),
        jnp.where(layer == 0, turned(edges, 1 - HALO, 1), turned(above, 1, 1)),
    )


def main_sum(frame, field, x, join, wx, wy, wz_up, wz_low):
    span = frame.span
    upper, lower = next_and_last(field[x, span], join, x)
    total = wx[x, span] * field[x + 1, span] + wx[x - 1, span] * field[x - 1, span]
    total = total + wy[x, span] * field[x, pl.ds(SUB + 1, frame.tall)]
    down = pl.ds(SUB - 1, frame.tall)
    total = total + wy[x, down] * field[x, down]
    return total + wz_up[x, span] * upper + wz_low[x, span] * lower


def ends_sum(frame, ends, s, upper, lower, wx, wy, wz_up, wz_low):
    span, down = frame.span, pl.ds(SUB - 1, frame.tall)
    here = ends[s, span]
    total = wx[s, span] * turned(here, -HALO, 1) + turned(wx[s, span] * here, HALO, 1)
    total = total + wy[s, span] * ends[s, pl.ds(SUB + 1, frame.tall)] + wy[s, down] * ends[s, down]
    return total + wz_up[s, span] * upper + wz_low[s, span] * lower


def clear_spares(ref, frame):
    for x in range(ref.shape[0]):
        ref[x, :SUB] = jnp.zeros((SUB, LANES), F32)
        ref[x, SUB + frame.tall :] = jnp.zeros((SUB, LANES), F32)


def pack_rows(values):
    half = values.shape[0] // 2
    lane = lane_no((half, LANES))
    return jnp.where(lane < LANES // 2, values[:half], turned(values[half:], LANES // 2, 1))


def lane_total(values):
    ones = jnp.ones((SUB, LANES), F32)
    return lax.dot_general(
        ones, values, (((1,), (1,)), ((), ())), precision=lax.Precision.HIGHEST, preferred_element_type=F32
    )


def paired(values):
    even = 2 * (lane_no(values.shape) % (LANES // 2))
    return picked(values + turned(values, -1, 1), even)


def fine_kernel(flags, wide_ref, forth, back, from_x_low, from_x_high, from_y_low, from_y_high, block_label,
                face_label, inner_diag, *refs):
    main, ends = refs[:6], refs[6:12]
    pre, face_near, face_weight, scaled_rhs, scale, once, once_ends, res = refs[12:]
    wx, wy, wz_up, wz_low, inv_diag, start = main
    ex, ey, ez_up, ez_low, inv_ends, start_ends = ends
    nx, ny = pre.shape[0], pre.shape[1]
    frame = Frame(nx, ny)
    wide, tall, span = frame.wide, frame.tall, frame.span
    last = HALO + nx
    got = [sides(flags, forth[f * tall : (f + 1) * tall], back[f * tall : (f + 1) * tall]) for f in range(3)]
    (cond_below, cond_above), rhs_ends, absorb_ends = got
    for ref in (wy, start, once):
        clear_spares(ref, frame)
    for ref in (ey, start_ends, once_ends):
        clear_spares(ref, frame)

    row = row_no((tall, LANES))
    lane = lane_no((1, LANES))
    keep_y = jnp.where(
        row == HALO - 1, flags[Y_LOW], jnp.where(row == HALO + ny - 1, flags[Y_HIGH], 1)
    ).astype(F32)
    keep_low, keep_high = flags[Z_LOW].astype(F32), flags[Z_HIGH].astype(F32)

    def cond_edges(x, edges):
        return edge_step(wide_ref[0, x, span], x, edges)

    edges = lax.fori_loop(0, wide, cond_edges, jnp.ones((tall, LANES), F32), unroll=4)
    near = ends_near(cond_below, cond_above, edges)
    slab = lane // HALO
    keep_x = jnp.where(
        slab == HALO - 1, flags[X_LOW], jnp.where(slab == last - 1, flags[X_HIGH], 1)
    ).astype(F32)
    layer = lane % HALO
    for s, here in enumerate((cond_below, cond_above)):
        up, low = weight(here, near[2 * s]), weight(here, near[2 * s + 1])
        if s == 0:
            up = up * jnp.where(layer == HALO - 1, keep_low, 1.0)
        else:
            low = low * jnp.where(layer == 0, keep_high, 1.0)
        face_x = keep_x * weight(here, turned(here, -HALO, 1))
        face_y = keep_y * weight(here, turned(here, -1, 0))
        ex[s, span], ey[s, span], ez_up[s, span], ez_low[s, span] = face_x, face_y, up, low
        total = absorb_ends[s] + face_x + turned(face_x, HALO, 1) + face_y + turned(face_y, 1, 0) + up + low
        inverse = OMEGA_FINE / total
        inv_ends[s, span] = inverse
        start_ends[s, span] = inverse * rhs_ends[s]

    join = joined(cond_below, cond_above)
    wz_under = ez_up[0, span]

    def fields(x, carry):
        before, edges = carry
        here = wide_ref[0, x, span]
        keep = jnp.where(x == HALO - 1, flags[X_LOW], jnp.where(x == last - 1, flags[X_HIGH], 1)).astype(F32)
        edge = turned(join, (LANES - HALO) - HALO * x, 1)
        upper = turned(jnp.where(lane == 0, edge, here), -1, 1)
        face_x = keep * weight(here, wide_ref[0, jnp.minimum(x + 1, wide - 1), span])
        face_y = keep_y * weight(here, wide_ref[0, x, pl.ds(SUB + 1, tall)])
        up = weight(here, upper) * jnp.where(lane == LANES - 1, keep_high, 1.0)
        under = turned(wz_under, (LANES - HALO) - HALO * x, 1)
        low = turned(jnp.where(lane == LANES - 1, under, up), 1, 1)
        total = wide_ref[2, x, span] + face_x + before + face_y + turned(face_y, 1, 0) + up + low
        inverse = OMEGA_FINE / total
        begin = inverse * wide_ref[1, x, span]
        for ref, values in zip(main, (face_x, face_y, up, low, inverse, begin)):
            ref[x, span] = values
        return face_x, edge_step(begin, x, edges)

    nothing = jnp.zeros((tall, LANES), F32)
    _, edges = lax.fori_loop(0, wide, fields, (nothing, nothing))

    join = joined(start_ends[0, span], start_ends[1, span])
    near = ends_near(start_ends[0, span], start_ends[1, span], edges)
    for s in range(2):
        total = ends_sum(frame, start_ends, s, near[2 * s], near[2 * s + 1], ex, ey, ez_up, ez_low)
        once_ends[s, span] = (2.0 - OMEGA_FINE) * start_ends[s, span] + inv_ends[s, span] * total

    @pl.loop(HALO - 1, last + 1)
    def _(x):
        total = main_sum(frame, start, x, join, wx, wy, wz_up, wz_low)
        once[x, span] = (2.0 - OMEGA_FINE) * start[x, span] + inv_diag[x, span] * total

    join2 = joined(once_ends[0, span], once_ends[1, span])

    @pl.loop(HALO, last)
    def _(x):
        total = main_sum(frame, once, x, join2, wx, wy, wz_up, wz_low)
        full = wide_ref[1, x, span] - (OMEGA_FINE / inv_diag[x, span]) * once[x, span] + total
        res[x - HALO, span] = full
        pre[x - HALO] = once[x, pl.ds(frame.own, ny)]

    nb, half, width = nx // 2, ny // 2, LANES // 2
    iota = row_no((AGG, LANES)).astype(F32)

    def rows_at(ref, x, off):
        return ref[x, pl.ds(frame.own + off, half, stride=2)]

    def add_rows(total, labels, values, rows):
        for r in range(rows):
            total = total + jnp.where(labels[r : r + 1] == iota, values[r : r + 1], 0.0)
        return total

    def restrict(b, total):
        four = sum(rows_at(res, 2 * b + a, c) for a in range(2) for c in range(2))
        return add_rows(total, block_label[b], pack_rows(paired(four)), SUB)

    zeros = jnp.zeros((AGG, LANES), F32)
    sums = lax.fori_loop(0, nb, restrict, zeros)

    blank = jnp.zeros((half - nb, LANES), F32)
    low_at, high_at = pl.ds(frame.own - 1, 1), pl.ds(frame.own + ny - 1, 1)
    face_weight[0] = pack_rows(paired(rows_at(wx, HALO - 1, 0) + rows_at(wx, HALO - 1, 1)))
    face_weight[1] = pack_rows(paired(rows_at(wx, last - 1, 0) + rows_at(wx, last - 1, 1)))
    for s, at in ((2, low_at), (3, high_at)):
        lines = [wy[HALO + 2 * b, at] + wy[HALO + 2 * b + 1, at] for b in range(nb)]
        face_weight[s] = pack_rows(paired(jnp.concatenate(lines + [blank], axis=0)))
    lane = lane_no((half, LANES))
    for s, (ref, side, layer_at) in ((4, (ez_up, 0, HALO - 1)), (5, (ez_low, 1, 0))):
        values = rows_at(ref, side, 0) + rows_at(ref, side, 1)
        values = values + turned(values, -HALO, 1)
        spot = jnp.minimum(2 * HALO * lane + HALO * HALO + layer_at, LANES - 1)
        face_weight[s] = pack_rows(jnp.where(lane < nb, picked(values, spot), 0.0))
    around = zeros
    for s in range(6):
        around = add_rows(around, face_label[s], face_weight[s], SUB)
    scale[...] = OMEGA_COARSE / (inner_diag[...] + lane_total(around))
    scaled_rhs[...] = scale[...] * lane_total(sums)

    at = sum(WIDTHS)
    face_near[0] = pack_rows(from_x_low[at, :half])
    face_near[1] = pack_rows(from_x_high[at, :half])
    at = 3 * wide * HALO
    face_near[2] = pack_rows(from_y_low[at : at + half])
    face_near[3] = pack_rows(from_y_high[at : at + half])
    below, above = sides(flags, forth[3 * tall : 3 * tall + half], back[3 * tall : 3 * tall + half])
    face_near[4] = pack_rows(below)
    face_near[5] = pack_rows(above)


def tile_product(left, right, labels, pairs):
    iota = row_no((AGG, LANES)).astype(F32)
    for r in range(SUB):
        lanes = pl.ds(r * LANES, LANES)
        left[:, lanes] = jnp.where(labels[r : r + 1] == iota, 1.0, 0.0).astype(BF16)
        held = sum(jnp.where(near[r : r + 1] == iota, w[r : r + 1], 0.0) for near, w in pairs)
        high = held.astype(BF16)
        right[:AGG, lanes] = high
        right[AGG:, lanes] = (held - high.astype(F32)).astype(BF16)
    return lax.dot_general(left[...], right[...], (((1,), (1,)), ((), ())), preferred_element_type=F32)


def keep_tile(out, at, tile):
    high = tile.astype(BF16)
    out[pl.ds(at, AGG), :AGG] = high
    out[pl.ds(at, AGG), AGG:] = (tile - high.astype(F32)).astype(BF16)


def own_kernel(flags, cond, absorb, block_agg, out, block_label, face_label, inner_diag, part, line, left, right):
    nx, ny = cond.shape[0], cond.shape[1]
    nb, half, width = nx // 2, ny // 2, LANES // 2
    lane, row = lane_no((half, LANES)), row_no((half, LANES))
    even = 2 * (lane % width)
    iota = row_no((AGG, LANES)).astype(F32)
    line[...] = jnp.zeros(line.shape, F32)

    def halves(values, slot):
        part[slot] = values
        return part[slot, pl.ds(0, half, stride=2)], part[slot, pl.ds(1, half, stride=2)]

    def label_at(b):
        values = block_agg[b].astype(F32)
        return jnp.concatenate([values, values], axis=1)

    def step(b, carry):
        low_x, tile, around = carry
        x = 2 * b
        one, two, three = cond[x], cond[x + 1], cond[jnp.minimum(x + 2, nx - 1)]
        faces_x = sum(halves(weight(two, three), 0))
        both_y = weight(one, turned(one, -1, 0)) + weight(two, turned(two, -1, 0))
        both_z = weight(one, turned(one, -1, 1)) + weight(two, turned(two, -1, 1))
        end_x, end_y, end_z = b == nb - 1, row == half - 1, lane % width == width - 1
        high_x = jnp.where(end_x, 0.0, paired(faces_x))
        high_y = jnp.where(end_y, 0.0, paired(halves(both_y, 1)[1]))
        high_z = jnp.where(end_z, 0.0, picked(sum(halves(both_z, 2)), even + 1))
        low_y = turned(high_y, 1, 0)
        low_z = turned(high_z, 1, 1)
        own = label_at(b)
        near_x, past_x = label_at(jnp.minimum(b + 1, nb - 1)), label_at(jnp.maximum(b - 1, 0))
        near_y, past_y = turned(own, -1, 0), turned(own, 1, 0)
        near_z, past_z = turned(own, -1, 1), turned(own, 1, 1)
        total = paired(sum(halves(absorb[x] + absorb[x + 1], 3)))
        for near, values in (
            (near_x, high_x), (past_x, low_x), (near_y, high_y), (past_y, low_y), (near_z, high_z), (past_z, low_z)
        ):
            total = total + jnp.where(near != own, values, 0.0)
        packed, total = pack_rows(own), pack_rows(total)
        block_label[b] = packed
        pairs = [
            (pack_rows(near_x), pack_rows(high_x)),
            (pack_rows(near_y), pack_rows(high_y)),
            (pack_rows(near_z), pack_rows(high_z)),
        ]
        tile = tile + tile_product(left, right, packed, pairs)
        for r in range(SUB):
            around = around + jnp.where(packed[r : r + 1] == iota, total[r : r + 1], 0.0)
        line[0, pl.ds(b, 1)], line[1, pl.ds(b, 1)] = own[:1], own[half - 1 :]
        line[2] = jnp.where(lane == b, own[:, :1], line[2])
        line[3] = jnp.where(lane == b, own[:, width - 1 : width], line[3])
        return high_x, tile, around

    nothing = jnp.zeros((half, LANES), F32)
    _, tile, around = lax.fori_loop(
        0, nb, step, (nothing, jnp.zeros((AGG, 2 * AGG), F32), jnp.zeros((AGG, LANES), F32))
    )
    tile = tile[:, :AGG] + tile[:, AGG:]
    keep_tile(out, 0, jnp.where(row_no((AGG, AGG)) == lane_no((AGG, AGG)), 0.0, tile + tile.T))
    inner_diag[...] = lane_total(around)
    face_label[0], face_label[1] = block_label[0], block_label[nb - 1]
    for s in range(4):
        face_label[2 + s] = pack_rows(line[s])


def faces_kernel(flags, own, face_label, face_near, face_weight, out, left, right):
    out[:AGG] = own[...]

    @pl.loop(0, 6)
    def _(s):
        tile = tile_product(left, right, face_near[s], [(face_label[s], face_weight[s])])
        keep_tile(out, (s + 1) * AGG, tile[:, :AGG] + tile[:, AGG:])


def turn_kernel(flags, tiles, scaled_rhs, scale, own, x_low, x_high, y_low, y_high, forth, back, out):
    vectors = [own[...], x_low[...], x_high[...], y_low[...], y_high[...], *sides(flags, forth[...], back[...])]
    row = row_no((SUB, AGG))
    parts = []
    for v in vectors:
        high = v.astype(BF16).astype(F32)
        parts.append(jnp.where(row == 0, high, jnp.where(row == 1, v - high, 0.0)).astype(BF16))
    got = jnp.dot(jnp.concatenate(parts, axis=1), tiles[...], preferred_element_type=F32)
    applied = jnp.sum(got[:, :AGG] + got[:, AGG:], axis=0, keepdims=True)
    out[...] = (1.0 - OMEGA_COARSE) * own[...] + scaled_rhs[...] + scale[...] * applied


def lifted(pre, block_agg, table, out, b, at):
    half = pre.shape[1] // 2
    labels = block_agg[b]
    labels = jnp.concatenate([labels, labels], axis=1)
    labels = picked(labels, lane_no((half, LANES)) // 2)
    values = picked(table, labels)
    for a in range(2):
        for c in range(2):
            rows = pl.ds(c, half, stride=2)
            out[at + a, rows] = pre[2 * b + a, rows] + values


def send_kernel(count, flags, pre, block_agg, coarse, *outs):
    nb, half = pre.shape[0] // 2, pre.shape[1] // 2
    table = jnp.broadcast_to(coarse[:1], (half, LANES))
    for s, out in enumerate(outs):
        for h in range(HALO // 2):
            if count == 2:
                b = jnp.where(flags[IX] == 0, nb - HALO // 2 + h, h)
            else:
                b = (nb - HALO // 2 + h, h)[s]
            lifted(pre, block_agg, table, out, b, 2 * h)


def correct_kernel(flags, pre, block_agg, coarse, out):
    table = jnp.broadcast_to(coarse[:1], (pre.shape[1] // 2, LANES))

    @pl.loop(0, pre.shape[0] // 2)
    def _(b):
        lifted(pre, block_agg, table, out, b, 2 * b)


def post_kernel(flags, wide_ref, forth, back, *refs):
    main, ends = refs[:6], refs[6:12]
    out, one, two, one_ends, two_ends = refs[12:]
    nx, ny = out.shape[0], out.shape[1]
    frame = Frame(nx, ny)
    wide, tall, span = frame.wide, frame.tall, frame.span
    wx, wy, wz_up, wz_low, inv_diag, start = main
    ex, ey, ez_up, ez_low, inv_ends, start_ends = ends
    for ref in (one, two, one_ends, two_ends):
        clear_spares(ref, frame)
    below, above = sides(flags, forth[...], back[...])
    two_ends[0, span], two_ends[1, span] = below, above
    kept = 1.0 - OMEGA_FINE
    buffers = ((wide_ref.at[0], two_ends), (one, one_ends), (two, two_ends), (one, one_ends))
    for s in range(POST):
        src, src_ends = buffers[s]
        join = joined(src_ends[0, span], src_ends[1, span])
        final = s == POST - 1
        dst, dst_ends = (None, None) if final else buffers[s + 1]

        def step(x, edges, src=src, join=join, dst=dst, final=final):
            here = src[x, span]
            total = main_sum(frame, src, x, join, wx, wy, wz_up, wz_low)
            new = kept * here + start[x, span] + inv_diag[x, span] * total
            if final:
                out[x - HALO] = new[HALO : HALO + ny]
                return edges
            dst[x, span] = new
            return edge_step(here, x, edges)

        edges = jnp.zeros((tall, LANES), F32)
        edges = lax.fori_loop(s + 1, wide - s - 1, step, edges)
        if not final:
            near = ends_near(src_ends[0, span], src_ends[1, span], edges)
            news = []
            for e in range(2):
                total = ends_sum(frame, src_ends, e, near[2 * e], near[2 * e + 1], ex, ey, ez_up, ez_low)
                news.append(kept * src_ends[e, span] + start_ends[e, span] + inv_ends[e, span] * total)
            dst_ends[0, span], dst_ends[1, span] = news


def body(links, right_side, conductance, absorption, block_agg):
    nx, ny, nz = right_side.shape
    frame = Frame(nx, ny)
    nb = nx // 2
    ix, iy, iz = (lax.axis_index(a) for a in ("gx", "gy", "gz"))
    n_x, n_y, n_z = links.sizes
    flags = jnp.stack(
        [ix, iy % 2, ix > 0, ix < n_x - 1, iy > 0, iy < n_y - 1, iz > 0, iz < n_z - 1]
    ).astype(jnp.int32)
    arrays = (conductance, right_side, absorption, block_agg)
    n_send = 1 if n_x == 2 else 2
    x_sends = call(
        functools.partial(pack_x_kernel, n_x, WIDTHS),
        [shaped(sum(WIDTHS) + 1, ny, nz)] * n_send,
        [pltpu.VMEM((n_send, ny // 2, nz // 2), jnp.int32), pltpu.SemaphoreType.DMA((n_send * 4,))],
        in_specs=[pl.BlockSpec(memory_space=pl.ANY)] * 4,
    )(flags, *arrays)
    from_x = links.x(x_sends)
    pair = [pltpu.VMEM((AGG, SUB * LANES), BF16), pltpu.VMEM((2 * AGG, SUB * LANES), BF16)]
    own_tile, block_label, face_label, inner_diag = call(
        own_kernel,
        [jax.ShapeDtypeStruct((AGG, 2 * AGG), BF16), shaped(nb, SUB, LANES), shaped(6, SUB, LANES), shaped(SUB, AGG)],
        [pltpu.VMEM((4, ny, LANES), F32), pltpu.VMEM((4, ny // 2, LANES), F32)] + pair,
    )(flags, conductance, absorption, block_agg)
    halo, from_y = widened(links, flags, WIDTHS, arrays, from_x)
    outs = [shaped(*frame.main)] * 6 + [shaped(*frame.ends)] * 6 + [shaped(nx, ny, nz)]
    outs += [shaped(6, SUB, LANES)] * 2 + [shaped(SUB, AGG)] * 2
    scratch = [pltpu.VMEM(frame.main, F32), pltpu.VMEM(frame.ends, F32), pltpu.VMEM((nx, frame.rows, LANES), F32)]
    got = call(fine_kernel, outs, scratch, limit=28)(
        flags, *halo, *from_x, *from_y, block_label, face_label, inner_diag
    )
    fields, pre = got[:12], got[12]
    face_near, face_weight, scaled_rhs, scale = got[13:]
    tiles = call(faces_kernel, jax.ShapeDtypeStruct((7 * AGG, 2 * AGG), BF16), pair)(
        flags, own_tile, face_label, face_near, face_weight
    )
    coarse = scaled_rhs
    for _ in range(KC - 1):
        near = links.x([coarse] * n_send) + links.y(coarse, coarse) + links.z(coarse, coarse)
        coarse = call(turn_kernel, shaped(SUB, AGG))(flags, tiles, scaled_rhs, scale, coarse, *near)
    x_sends = call(functools.partial(send_kernel, n_x), [shaped(HALO, ny, nz)] * n_send)(
        flags, pre, block_agg, coarse
    )
    from_x = links.x(x_sends)
    corrected = call(correct_kernel, shaped(nx, ny, nz))(flags, pre, block_agg, coarse)
    halo, _ = widened(links, flags, (HALO,), (corrected,), from_x)
    scratch = [pltpu.VMEM(frame.main, F32)] * 2 + [pltpu.VMEM(frame.ends, F32)] * 2
    return call(post_kernel, shaped(nx, ny, nz), scratch, limit=24)(flags, *halo, *fields)


def solution(mesh):
    spec = P("gx", "gy", "gz")
    return jax.shard_map(
        functools.partial(body, Links(mesh)), mesh=mesh, in_specs=(spec,) * 4, out_specs=spec, check_vma=False
    )
```

```python
import functools

import jax
import jax.numpy as jnp
from jax import lax
from jax.experimental import pallas as pl
from jax.experimental.pallas import tpu as pltpu
from jax.sharding import PartitionSpec as P

AGG = 128
LANES = 128
SUB = 8
HALO = 4
WIDTHS = (4, 3, 3)
POST = 4
KC = 8
OMEGA_FINE = 0.8
OMEGA_COARSE = 0.7
F32 = jnp.float32
BF16 = jnp.bfloat16
SMEM = pl.BlockSpec(memory_space=pltpu.SMEM)
VMEM = pl.BlockSpec(memory_space=pltpu.VMEM)
IX, PARITY, X_LOW, X_HIGH, Y_LOW, Y_HIGH, Z_LOW, Z_HIGH = range(8)


def call(kernel, outs, scratch=(), limit=16, flops=10**6, in_specs=None):
    def run(flags, *arrays):
        return pl.pallas_call(
            kernel,
            out_shape=outs,
            in_specs=[SMEM] + (in_specs or [VMEM] * len(arrays)),
            out_specs=jax.tree.map(lambda _: VMEM, outs),
            scratch_shapes=list(scratch),
            compiler_params=pltpu.CompilerParams(vmem_limit_bytes=limit * 2**20),
            cost_estimate=pl.CostEstimate(flops=flops, bytes_accessed=10**5, transcendentals=0),
        )(flags, *arrays)

    return run


def shaped(*shape):
    return jax.ShapeDtypeStruct(shape, F32)


def lane_no(shape):
    return lax.broadcasted_iota(jnp.int32, shape, len(shape) - 1)


def row_no(shape):
    return lax.broadcasted_iota(jnp.int32, shape, len(shape) - 2)


def turned(values, shift, axis):
    if isinstance(shift, int):
        shift = shift % values.shape[axis]
        if shift == 0:
            return values
    return pltpu.roll(values, shift, axis)


def batched(low, high, step, carry, size=6):
    def some(i, carry):
        return step([low + i * size + k for k in range(size)], carry)

    carry = lax.fori_loop(0, (high - low) // size, some, carry)
    rest = (high - low) % size
    return step(list(range(high - rest, high)), carry) if rest else carry


def picked(values, index):
    return jnp.take_along_axis(values, index, axis=1, mode="promise_in_bounds")


class Frame:
    def __init__(self, nx, ny):
        self.nx, self.ny = nx, ny
        self.wide, self.tall = nx + 2 * HALO, ny + 2 * HALO
        self.rows = self.tall + 2 * SUB
        self.span = pl.ds(SUB, self.tall)
        self.own = SUB + HALO
        self.main = (self.wide, self.rows, LANES)
        self.ends = (2, self.rows, LANES)


def bases(widths):
    return [sum(widths[:f]) for f in range(len(widths) + 1)]


def pack_x_kernel(count, widths, flags, *refs):
    fields = len(widths)
    ins, labels, outs = refs[:fields], refs[fields], refs[fields + 1 : -2]
    near, sems = refs[-2:]
    nx, ny = ins[0].shape[0], ins[0].shape[1]
    base = bases(widths)
    copies = []
    for s, out in enumerate(outs):
        for f, (ref, width) in enumerate(zip(ins, widths)):
            if count == 2:
                at = jnp.where(flags[IX] == 0, nx - width, 0)
            else:
                at = (nx - width, 0)[s]
            copies.append(
                pltpu.make_async_copy(
                    ref.at[pl.ds(at, width)], out.at[pl.ds(base[f], width)], sems.at[len(copies)]
                )
            )
        if count == 2:
            at = jnp.where(flags[IX] == 0, nx // 2 - 1, 0)
        else:
            at = (nx // 2 - 1, 0)[s]
        copies.append(pltpu.make_async_copy(labels.at[at], near.at[s], sems.at[len(copies)]))
    for copy in copies:
        copy.start()
    for copy in copies:
        copy.wait()
    for s, out in enumerate(outs):
        out[base[-1]] = jnp.zeros(out.shape[1:], F32)
        out[base[-1], : ny // 2, : near.shape[2]] = near[s].astype(F32)


def slab_of(own, low, high, base, width, x):
    nx = own.shape[0]
    if HALO <= x < HALO + nx:
        return own[x - HALO]
    if x < HALO:
        at = x - (HALO - width)
        return low[base + at] if at >= 0 else None
    at = x - HALO - nx
    return high[base + at] if at < width else None


def pack_y_kernel(widths, labels, flags, *refs):
    fields = len(widths)
    ins = refs[:fields]
    low, high = refs[fields + labels : fields + labels + 2]
    to_high, to_low = refs[fields + labels + 2 :]
    nx, ny = ins[0].shape[0], ins[0].shape[1]
    frame = Frame(nx, ny)
    base = bases(widths)
    for f in range(fields):
        for x in range(frame.wide):
            slab = slab_of(ins[f], low, high, base[f], widths[f], x)
            at = (f * frame.wide + x) * HALO
            if slab is None:
                slab = jnp.ones((ny, LANES), F32)
            to_high[at : at + HALO] = slab[ny - HALO :]
            to_low[at : at + HALO] = slab[:HALO]
    if labels:
        at = fields * frame.wide * HALO
        nb, rows, width = refs[fields].shape
        for out, row in ((to_high, rows - 1), (to_low, 0)):
            out[at:] = jnp.zeros((out.shape[0] - at, LANES), F32)
            for b in range(nb):
                out[at + b : at + b + 1, :width] = refs[fields][b, row : row + 1].astype(F32)


def pack_z_kernel(widths, labels, flags, *refs):
    fields = len(widths)
    ins = refs[:fields]
    x_low, x_high, y_low, y_high = refs[fields + labels : fields + labels + 4]
    wide_ref, send_forth, send_back = refs[fields + labels + 4 :]
    nx, ny = ins[0].shape[0], ins[0].shape[1]
    frame = Frame(nx, ny)
    base = bases(widths)
    tall, own = frame.tall, frame.own
    even = flags[PARITY] == 0

    def send(at, count, to_high, to_low):
        send_forth[at : at + count] = jnp.where(even, to_high, to_low)
        send_back[at : at + count] = jnp.where(even, to_low, to_high)

    group = lane_no((tall, LANES)) // HALO
    spare = jnp.ones((SUB, LANES), F32)
    for f in range(fields):
        to_high = to_low = jnp.ones((tall, LANES), F32)
        for x in range(frame.wide):
            at = (f * frame.wide + x) * HALO
            slab = slab_of(ins[f], x_low, x_high, base[f], widths[f], x)
            wide_ref[f, x, own : own + ny] = jnp.ones((ny, LANES), F32) if slab is None else slab
            wide_ref[f, x, SUB:own] = y_low[at : at + HALO]
            wide_ref[f, x, own + ny : own + ny + HALO] = y_high[at : at + HALO]
            wide_ref[f, x, :SUB] = spare
            wide_ref[f, x, SUB + tall :] = spare
            moved = turned(wide_ref[f, x, SUB : SUB + tall], HALO * (x + 1), 1)
            to_high = jnp.where(group == x, moved, to_high)
            to_low = jnp.where(group == (x + 1) % frame.wide, moved, to_low)
        send(f * tall, tall, to_high, turned(to_low, -HALO, 1))
    if labels:
        nb, rows, width = refs[fields].shape
        lane = lane_no((rows, LANES))
        to_high = to_low = jnp.zeros((rows, LANES), F32)
        for b in range(nb):
            slab = refs[fields][b].astype(F32)
            to_high = jnp.where(lane == b, slab[:, width - 1 :], to_high)
            to_low = jnp.where(lane == b, slab[:, :1], to_low)
        send(fields * tall, rows, to_high, to_low)


class Links:
    def __init__(self, mesh):
        self.sizes = [mesh.shape[a] for a in ("gx", "gy", "gz")]
        n_x, n_y, n_z = self.sizes
        self.ring_x = [(i, (i + 1) % n_x) for i in range(n_x)]
        self.ring_y = [(i, (i + 1) % n_y) for i in range(n_y)]
        self.snake = []
        for i in range(n_x):
            for j in range(0, n_y, 2):
                nodes = [(i * n_y + j) * n_z + k for k in range(n_z)]
                nodes += [(i * n_y + j + 1) * n_z + k for k in reversed(range(n_z))]
                self.snake += [(nodes[m], nodes[(m + 1) % len(nodes)]) for m in range(len(nodes))]

    @staticmethod
    def back(pairs):
        return [(b, a) for a, b in pairs]

    def x(self, sends):
        if self.sizes[0] == 2:
            got = lax.ppermute(sends[0], "gx", self.ring_x)
            return got, got
        return lax.ppermute(sends[0], "gx", self.ring_x), lax.ppermute(sends[-1], "gx", self.back(self.ring_x))

    def y(self, to_high, to_low):
        return lax.ppermute(to_high, "gy", self.ring_y), lax.ppermute(to_low, "gy", self.back(self.ring_y))

    def z(self, forth, back):
        axes = ("gx", "gy", "gz")
        return lax.ppermute(forth, axes, self.snake), lax.ppermute(back, axes, self.back(self.snake))


def widened(links, flags, widths, arrays, from_x, beside_y=None, beside_z=None):
    fields, labels = len(widths), len(arrays) - len(widths)
    nx, ny, nz = arrays[0].shape
    frame = Frame(nx, ny)
    rows = fields * frame.wide * HALO + labels * ny // 2
    sends = call(functools.partial(pack_y_kernel, widths, labels), [shaped(rows, nz)] * 2)(flags, *arrays, *from_x)
    work = beside_y(sends[0]) if beside_y else ()
    from_y = links.y(*sends)
    from_y = lax.optimization_barrier((*from_y, *work))[:2] if work else from_y
    rows = fields * frame.tall + labels * ny // 2
    wide, *sends = call(
        functools.partial(pack_z_kernel, widths, labels), [shaped(fields, *frame.main)] + [shaped(rows, nz)] * 2
    )(flags, *arrays, *from_x, *from_y)
    if beside_z:
        beside_z(sends[0])
    return (wide, *links.z(*sends)), from_y


def sides(flags, forth, back):
    even = flags[PARITY] == 0
    return jnp.where(even, forth, back), jnp.where(even, back, forth)


def weight(one, two):
    return 2.0 * (one * two) / (one + two)


def lane_mask(x):
    return ((lane_no((1, LANES)) - (HALO * x + HALO - 1)) & (LANES - 1)) < 2


def edge_step(here, x, edges):
    return jnp.where(lane_mask(x), turned(here, HALO * x + HALO, 1), edges)


def joined(below, above):
    lane = lane_no(below.shape)
    return jnp.where(lane % HALO == HALO - 1, turned(above, HALO - 1, 1), turned(below, 1, 1))


def next_and_last(here, join, x):
    lane = lane_no((1, LANES))
    edge = turned(join, (LANES - HALO) - HALO * x, 1)
    upper = jnp.where(lane == LANES - 1, edge, turned(here, -1, 1))
    lower = jnp.where(lane == 0, edge, turned(here, 1, 1))
    return upper, lower


def ends_near(below, above, edges):
    layer = lane_no((1, LANES)) % HALO
    return (
        jnp.where(layer == HALO - 1, turned(edges, -1, 1), turned(below, -1, 1)),
        turned(below, 1, 1),
        turned(above, -1, 1),
        jnp.where(layer == 0, turned(edges, 1 - HALO, 1), turned(above, 1, 1)),
    )


def main_sum(frame, field, x, join, wx, wy, wz_up, wz_low):
    span = frame.span
    upper, lower = next_and_last(field[x, span], join, x)
    total = wx[x, span] * field[x + 1, span] + wx[x - 1, span] * field[x - 1, span]
    total = total + wy[x, span] * field[x, pl.ds(SUB + 1, frame.tall)]
    down = pl.ds(SUB - 1, frame.tall)
    total = total + wy[x, down] * field[x, down]
    return total + wz_up[x, span] * upper + wz_low[x, span] * lower


def ends_sum(frame, ends, s, upper, lower, wx, wy, wz_up, wz_low):
    span, down = frame.span, pl.ds(SUB - 1, frame.tall)
    here = ends[s, span]
    total = wx[s, span] * turned(here, -HALO, 1) + turned(wx[s, span] * here, HALO, 1)
    total = total + wy[s, span] * ends[s, pl.ds(SUB + 1, frame.tall)] + wy[s, down] * ends[s, down]
    return total + wz_up[s, span] * upper + wz_low[s, span] * lower


def clear_spares(ref, frame):
    for x in range(ref.shape[0]):
        ref[x, :SUB] = jnp.zeros((SUB, LANES), F32)
        ref[x, SUB + frame.tall :] = jnp.zeros((SUB, LANES), F32)


def pack_rows(values):
    half = values.shape[0] // 2
    lane = lane_no((half, LANES))
    return jnp.where(lane < LANES // 2, values[:half], turned(values[half:], LANES // 2, 1))


def lane_total(values):
    ones = jnp.ones((SUB, LANES), F32)
    return lax.dot_general(
        ones, values, (((1,), (1,)), ((), ())), precision=lax.Precision.HIGHEST, preferred_element_type=F32
    )


def paired(values):
    even = 2 * (lane_no(values.shape) % (LANES // 2))
    return picked(values + turned(values, -1, 1), even)


def fine_kernel(flags, wide_ref, forth, back, from_x_low, from_x_high, from_y_low, from_y_high, block_label,
                face_label, inner_diag, *refs):
    main, ends = refs[:6], refs[6:12]
    pre, face_near, face_weight, scaled_rhs, scale, once, once_ends, res, diag = refs[12:]
    wx, wy, wz_up, wz_low, inv_diag, start = main
    ex, ey, ez_up, ez_low, inv_ends, start_ends = ends
    nx, ny = pre.shape[0], pre.shape[1]
    frame = Frame(nx, ny)
    wide, tall, span = frame.wide, frame.tall, frame.span
    last = HALO + nx
    got = [sides(flags, forth[f * tall : (f + 1) * tall], back[f * tall : (f + 1) * tall]) for f in range(3)]
    (cond_below, cond_above), rhs_ends, absorb_ends = got
    for ref in (wy, start, once):
        clear_spares(ref, frame)
    for ref in (ey, start_ends, once_ends):
        clear_spares(ref, frame)

    row = row_no((tall, LANES))
    lane = lane_no((1, LANES))
    keep_y = jnp.where(
        row == HALO - 1, flags[Y_LOW], jnp.where(row == HALO + ny - 1, flags[Y_HIGH], 1)
    ).astype(F32)
    keep_low, keep_high = flags[Z_LOW].astype(F32), flags[Z_HIGH].astype(F32)

    def cond_edges(xs, edges):
        for x in xs:
            edges = edge_step(wide_ref[0, x, span], x, edges)
        return edges

    edges = batched(0, wide, cond_edges, jnp.ones((tall, LANES), F32), 8)
    near = ends_near(cond_below, cond_above, edges)
    slab = lane // HALO
    keep_x = jnp.where(
        slab == HALO - 1, flags[X_LOW], jnp.where(slab == last - 1, flags[X_HIGH], 1)
    ).astype(F32)
    layer = lane % HALO
    for s, here in enumerate((cond_below, cond_above)):
        up, low = weight(here, near[2 * s]), weight(here, near[2 * s + 1])
        if s == 0:
            up = up * jnp.where(layer == HALO - 1, keep_low, 1.0)
        else:
            low = low * jnp.where(layer == 0, keep_high, 1.0)
        face_x = keep_x * weight(here, turned(here, -HALO, 1))
        face_y = keep_y * weight(here, turned(here, -1, 0))
        ex[s, span], ey[s, span], ez_up[s, span], ez_low[s, span] = face_x, face_y, up, low
        total = absorb_ends[s] + face_x + turned(face_x, HALO, 1) + face_y + turned(face_y, 1, 0) + up + low
        inverse = OMEGA_FINE / total
        inv_ends[s, span] = inverse
        start_ends[s, span] = inverse * rhs_ends[s]

    join = joined(cond_below, cond_above)
    wz_under = ez_up[0, span]

    def fields(xs, carry):
        before, edges = carry
        stores = []
        for x in xs:
            here = wide_ref[0, x, span]
            keep = jnp.where(x == HALO - 1, flags[X_LOW], jnp.where(x == last - 1, flags[X_HIGH], 1)).astype(F32)
            upper = next_and_last(here, join, x)[0]
            face_x = keep * weight(here, wide_ref[0, jnp.minimum(x + 1, wide - 1), span])
            face_y = keep_y * weight(here, wide_ref[0, x, pl.ds(SUB + 1, tall)])
            up = weight(here, upper) * jnp.where(lane == LANES - 1, keep_high, 1.0)
            under = turned(wz_under, (LANES - HALO + 1) - HALO * x, 1)
            low = jnp.where(lane == 0, under, turned(up, 1, 1))
            total = wide_ref[2, x, span] + face_x + before + face_y + turned(face_y, 1, 0) + up + low
            inverse = OMEGA_FINE / total
            begin = inverse * wide_ref[1, x, span]
            stores.append((x, (face_x, face_y, up, low, inverse, begin, total)))
            edges = edge_step(begin, x, edges)
            before = face_x
        for x, values in stores:
            for ref, value in zip((*main, diag), values):
                ref[x, span] = value
        return before, edges

    nothing = jnp.zeros((tall, LANES), F32)
    _, edges = batched(0, wide, fields, (nothing, nothing), 4)

    join = joined(start_ends[0, span], start_ends[1, span])
    near = ends_near(start_ends[0, span], start_ends[1, span], edges)
    for s in range(2):
        total = ends_sum(frame, start_ends, s, near[2 * s], near[2 * s + 1], ex, ey, ez_up, ez_low)
        once_ends[s, span] = (2.0 - OMEGA_FINE) * start_ends[s, span] + inv_ends[s, span] * total

    def second(xs, carry):
        news = []
        for x in xs:
            total = main_sum(frame, start, x, join, wx, wy, wz_up, wz_low)
            news.append((2.0 - OMEGA_FINE) * start[x, span] + inv_diag[x, span] * total)
        for x, new in zip(xs, news):
            once[x, span] = new
        return carry

    batched(HALO - 1, last + 1, second, 0)
    join2 = joined(once_ends[0, span], once_ends[1, span])

    def remainder(xs, carry):
        news = []
        for x in xs:
            total = main_sum(frame, once, x, join2, wx, wy, wz_up, wz_low)
            news.append(wide_ref[1, x, span] - diag[x, span] * once[x, span] + total)
        for x, new in zip(xs, news):
            res[x - HALO, span] = new
        for x in xs:
            pre[x - HALO] = once[x, pl.ds(frame.own, ny)]
        return carry

    batched(HALO, last, remainder, 0)

    nb, half, width = nx // 2, ny // 2, LANES // 2
    iota = row_no((AGG, LANES)).astype(F32)

    def rows_at(ref, x, off):
        return ref[x, pl.ds(frame.own + off, half, stride=2)]

    def add_rows(total, labels, values, rows):
        for r in range(rows):
            total = total + jnp.where(labels[r : r + 1] == iota, values[r : r + 1], 0.0)
        return total

    def restrict(b, total):
        four = sum(rows_at(res, 2 * b + a, c) for a in range(2) for c in range(2))
        return add_rows(total, block_label[b], pack_rows(paired(four)), SUB)

    zeros = jnp.zeros((AGG, LANES), F32)
    sums = lax.fori_loop(0, nb, restrict, zeros)

    blank = jnp.zeros((half - nb, LANES), F32)
    low_at, high_at = pl.ds(frame.own - 1, 1), pl.ds(frame.own + ny - 1, 1)
    face_weight[0] = pack_rows(paired(rows_at(wx, HALO - 1, 0) + rows_at(wx, HALO - 1, 1)))
    face_weight[1] = pack_rows(paired(rows_at(wx, last - 1, 0) + rows_at(wx, last - 1, 1)))
    for s, at in ((2, low_at), (3, high_at)):
        lines = [wy[HALO + 2 * b, at] + wy[HALO + 2 * b + 1, at] for b in range(nb)]
        face_weight[s] = pack_rows(paired(jnp.concatenate(lines + [blank], axis=0)))
    lane = lane_no((half, LANES))
    for s, (ref, side, layer_at) in ((4, (ez_up, 0, HALO - 1)), (5, (ez_low, 1, 0))):
        values = rows_at(ref, side, 0) + rows_at(ref, side, 1)
        values = values + turned(values, -HALO, 1)
        spot = jnp.minimum(2 * HALO * lane + HALO * HALO + layer_at, LANES - 1)
        face_weight[s] = pack_rows(jnp.where(lane < nb, picked(values, spot), 0.0))
    around = zeros
    for s in range(6):
        around = add_rows(around, face_label[s], face_weight[s], SUB)
    scale[...] = OMEGA_COARSE / (inner_diag[...] + lane_total(around))
    scaled_rhs[...] = scale[...] * lane_total(sums)

    at = sum(WIDTHS)
    face_near[0] = pack_rows(from_x_low[at, :half])
    face_near[1] = pack_rows(from_x_high[at, :half])
    at = 3 * wide * HALO
    face_near[2] = pack_rows(from_y_low[at : at + half])
    face_near[3] = pack_rows(from_y_high[at : at + half])
    below, above = sides(flags, forth[3 * tall : 3 * tall + half], back[3 * tall : 3 * tall + half])
    face_near[4] = pack_rows(below)
    face_near[5] = pack_rows(above)


def tile_product(left, right, labels, pairs):
    iota = row_no((AGG, LANES)).astype(F32)
    for r in range(SUB):
        lanes = pl.ds(r * LANES, LANES)
        left[:, lanes] = jnp.where(labels[r : r + 1] == iota, 1.0, 0.0).astype(BF16)
        held = sum(jnp.where(near[r : r + 1] == iota, w[r : r + 1], 0.0) for near, w in pairs)
        high = held.astype(BF16)
        right[:AGG, lanes] = high
        right[AGG:, lanes] = (held - high.astype(F32)).astype(BF16)
    return lax.dot_general(left[...], right[...], (((1,), (1,)), ((), ())), preferred_element_type=F32)


def keep_tile(out, at, tile):
    high = tile.astype(BF16)
    out[pl.ds(at, AGG), :AGG] = high
    out[pl.ds(at, AGG), AGG:] = (tile - high.astype(F32)).astype(BF16)


def own_kernel(first, count, last, flags, cond, absorb, block_agg, *refs):
    if last:
        tile_in, around_in, _, out, block_label, face_label, inner_diag, part, line, left, right = refs
    elif first:
        tile_in, around_in, _, tile_out, around_out, part, line, left, right = refs
    else:
        _, tile_out, around_out, part, line, left, right = refs
    nx, ny = cond.shape[0], cond.shape[1]
    nb, half, width = nx // 2, ny // 2, LANES // 2
    lane, row = lane_no((half, LANES)), row_no((half, LANES))
    even = 2 * (lane % width)
    iota = row_no((AGG, LANES)).astype(F32)

    def halves(values, slot):
        part[slot] = values
        return part[slot, pl.ds(0, half, stride=2)], part[slot, pl.ds(1, half, stride=2)]

    def label_at(b):
        values = block_agg[b].astype(F32)
        return jnp.concatenate([values, values], axis=1)

    def upper_x(b):
        x = 2 * b
        faces = weight(cond[x + 1], cond[jnp.minimum(x + 2, nx - 1)])
        return jnp.where(b == nb - 1, 0.0, paired(sum(halves(faces, 0))))

    def step(b, carry):
        low_x, tile, around = carry
        x = 2 * b
        one, two = cond[x], cond[x + 1]
        both_y = weight(one, turned(one, -1, 0)) + weight(two, turned(two, -1, 0))
        both_z = weight(one, turned(one, -1, 1)) + weight(two, turned(two, -1, 1))
        high_x = upper_x(b)
        high_y = jnp.where(row == half - 1, 0.0, paired(halves(both_y, 1)[1]))
        high_z = jnp.where(lane % width == width - 1, 0.0, picked(sum(halves(both_z, 2)), even + 1))
        low_y = turned(high_y, 1, 0)
        low_z = turned(high_z, 1, 1)
        own = label_at(b)
        near_x, past_x = label_at(jnp.minimum(b + 1, nb - 1)), label_at(jnp.maximum(b - 1, 0))
        near_y, past_y = turned(own, -1, 0), turned(own, 1, 0)
        near_z, past_z = turned(own, -1, 1), turned(own, 1, 1)
        total = paired(sum(halves(absorb[x] + absorb[x + 1], 3)))
        for near, values in (
            (near_x, high_x), (past_x, low_x), (near_y, high_y), (past_y, low_y), (near_z, high_z), (past_z, low_z)
        ):
            total = total + jnp.where(near != own, values, 0.0)
        packed, total = pack_rows(own), pack_rows(total)
        pairs = [
            (pack_rows(near_x), pack_rows(high_x)),
            (pack_rows(near_y), pack_rows(high_y)),
            (pack_rows(near_z), pack_rows(high_z)),
        ]
        tile = tile + tile_product(left, right, packed, pairs)
        for r in range(SUB):
            around = around + jnp.where(packed[r : r + 1] == iota, total[r : r + 1], 0.0)
        return high_x, tile, around

    if first:
        start = (upper_x(first - 1), tile_in[...], around_in[...])
    else:
        start = tuple(jnp.zeros(shape, F32) for shape in ((half, LANES), (AGG, 2 * AGG), (AGG, LANES)))
    _, tile, around = lax.fori_loop(first, first + count, step, start)
    if not last:
        tile_out[...], around_out[...] = tile, around
        return
    tile = tile[:, :AGG] + tile[:, AGG:]
    keep_tile(out, 0, jnp.where(row_no((AGG, AGG)) == lane_no((AGG, AGG)), 0.0, tile + tile.T))
    inner_diag[...] = lane_total(around)
    line[...] = jnp.zeros(line.shape, F32)
    for b in range(nb):
        own = label_at(b)
        block_label[b] = pack_rows(own)
        line[0, b : b + 1], line[1, b : b + 1] = own[:1], own[half - 1 :]
        line[2] = jnp.where(lane == b, own[:, :1], line[2])
        line[3] = jnp.where(lane == b, own[:, width - 1 : width], line[3])
    face_label[0], face_label[1] = block_label[0], block_label[nb - 1]
    for s in range(4):
        face_label[2 + s] = pack_rows(line[s])


def faces_kernel(flags, own, face_label, face_near, face_weight, out, left, right):
    out[:AGG] = own[...]

    @pl.loop(0, 6)
    def _(s):
        tile = tile_product(left, right, face_near[s], [(face_label[s], face_weight[s])])
        keep_tile(out, (s + 1) * AGG, tile[:, :AGG] + tile[:, AGG:])


def turn_kernel(flags, tiles, scaled_rhs, scale, own, x_low, x_high, y_low, y_high, forth, back, out):
    vectors = [own[...], x_low[...], x_high[...], y_low[...], y_high[...], *sides(flags, forth[...], back[...])]
    row = row_no((SUB, AGG))
    parts = []
    for v in vectors:
        high = v.astype(BF16).astype(F32)
        parts.append(jnp.where(row == 0, high, jnp.where(row == 1, v - high, 0.0)).astype(BF16))
    got = jnp.dot(jnp.concatenate(parts, axis=1), tiles[...], preferred_element_type=F32)
    applied = jnp.sum(got[:, :AGG] + got[:, AGG:], axis=0, keepdims=True)
    out[...] = (1.0 - OMEGA_COARSE) * own[...] + scaled_rhs[...] + scale[...] * applied


def lifted(pre, block_agg, table, out, b, at):
    half = pre.shape[1] // 2
    labels = block_agg[b]
    labels = jnp.concatenate([labels, labels], axis=1)
    labels = picked(labels, lane_no((half, LANES)) // 2)
    values = picked(table, labels)
    for a in range(2):
        for c in range(2):
            rows = pl.ds(c, half, stride=2)
            out[at + a, rows] = pre[2 * b + a, rows] + values


def send_kernel(count, flags, pre, block_agg, coarse, *outs):
    nb, half = pre.shape[0] // 2, pre.shape[1] // 2
    table = jnp.broadcast_to(coarse[:1], (half, LANES))
    for s, out in enumerate(outs):
        for h in range(HALO // 2):
            if count == 2:
                b = jnp.where(flags[IX] == 0, nb - HALO // 2 + h, h)
            else:
                b = (nb - HALO // 2 + h, h)[s]
            lifted(pre, block_agg, table, out, b, 2 * h)


def correct_kernel(flags, pre, block_agg, coarse, out):
    table = jnp.broadcast_to(coarse[:1], (pre.shape[1] // 2, LANES))

    @pl.loop(0, pre.shape[0] // 2)
    def _(b):
        lifted(pre, block_agg, table, out, b, 2 * b)


def post_kernel(flags, wide_ref, forth, back, *refs):
    main, ends = refs[:6], refs[6:12]
    out, one, two, one_ends, two_ends = refs[12:]
    nx, ny = out.shape[0], out.shape[1]
    frame = Frame(nx, ny)
    wide, tall, span = frame.wide, frame.tall, frame.span
    wx, wy, wz_up, wz_low, inv_diag, start = main
    ex, ey, ez_up, ez_low, inv_ends, start_ends = ends
    for ref in (one, two, one_ends, two_ends):
        clear_spares(ref, frame)
    below, above = sides(flags, forth[...], back[...])
    two_ends[0, span], two_ends[1, span] = below, above
    kept = 1.0 - OMEGA_FINE
    buffers = ((wide_ref.at[0], two_ends), (one, one_ends), (two, two_ends), (one, one_ends))
    for s in range(POST):
        src, src_ends = buffers[s]
        join = joined(src_ends[0, span], src_ends[1, span])
        final = s == POST - 1
        dst, dst_ends = (None, None) if final else buffers[s + 1]

        def step(xs, edges, src=src, join=join, dst=dst, final=final):
            news = []
            for x in xs:
                here = src[x, span]
                total = main_sum(frame, src, x, join, wx, wy, wz_up, wz_low)
                news.append(kept * here + start[x, span] + inv_diag[x, span] * total)
                if not final:
                    edges = edge_step(here, x, edges)
            for x, new in zip(xs, news):
                if final:
                    out[x - HALO] = new[HALO : HALO + ny]
                else:
                    dst[x, span] = new
            return edges

        edges = batched(s + 1, wide - s - 1, step, jnp.zeros((tall, LANES), F32))
        if not final:
            near = ends_near(src_ends[0, span], src_ends[1, span], edges)
            news = []
            for e in range(2):
                total = ends_sum(frame, src_ends, e, near[2 * e], near[2 * e + 1], ex, ey, ez_up, ez_low)
                news.append(kept * src_ends[e, span] + start_ends[e, span] + inv_ends[e, span] * total)
            dst_ends[0, span], dst_ends[1, span] = news


def body(links, right_side, conductance, absorption, block_agg):
    nx, ny, nz = right_side.shape
    frame = Frame(nx, ny)
    nb = nx // 2
    ix, iy, iz = (lax.axis_index(a) for a in ("gx", "gy", "gz"))
    n_x, n_y, n_z = links.sizes
    flags = jnp.stack(
        [ix, iy % 2, ix > 0, ix < n_x - 1, iy > 0, iy < n_y - 1, iz > 0, iz < n_z - 1]
    ).astype(jnp.int32)
    arrays = (conductance, right_side, absorption, block_agg)
    n_send = 1 if n_x == 2 else 2
    x_sends = call(
        functools.partial(pack_x_kernel, n_x, WIDTHS),
        [shaped(sum(WIDTHS) + 1, ny, nz)] * n_send,
        [pltpu.VMEM((n_send, ny // 2, nz // 2), jnp.int32), pltpu.SemaphoreType.DMA((n_send * 4,))],
        in_specs=[pl.BlockSpec(memory_space=pltpu.HBM)] * 4,
    )(flags, *(pltpu.with_memory_space_constraint(a, pltpu.HBM) for a in arrays))
    pair = [pltpu.VMEM((AGG, SUB * LANES), BF16), pltpu.VMEM((2 * AGG, SUB * LANES), BF16)]
    scratch = [pltpu.VMEM((4, ny, LANES), F32), pltpu.VMEM((4, ny // 2, LANES), F32)] + pair
    bounds = [nb * p // 3 for p in range(4)]

    def own_part(p, *more):
        outs = [shaped(AGG, 2 * AGG), shaped(AGG, LANES)]
        if p == 2:
            outs = [jax.ShapeDtypeStruct((AGG, 2 * AGG), BF16), shaped(nb, SUB, LANES)]
            outs += [shaped(6, SUB, LANES), shaped(SUB, AGG)]
        kernel = functools.partial(own_kernel, bounds[p], bounds[p + 1] - bounds[p], p == 2)
        return call(kernel, outs, scratch)(flags, conductance, absorption, block_agg, *more)

    parts = [own_part(0, x_sends[0])]
    from_x = links.x(x_sends)
    from_x = lax.optimization_barrier((*from_x, *parts[0]))[:2]

    def beside(p):
        def run(sent):
            parts.append(own_part(p, *parts[-1], sent))
            return parts[-1]

        return run

    halo, from_y = widened(links, flags, WIDTHS, arrays, from_x, beside(1), beside(2))
    own_tile, block_label, face_label, inner_diag = parts[-1]
    outs = [shaped(*frame.main)] * 6 + [shaped(*frame.ends)] * 6 + [shaped(nx, ny, nz)]
    outs += [shaped(6, SUB, LANES)] * 2 + [shaped(SUB, AGG)] * 2
    scratch = [pltpu.VMEM(frame.main, F32), pltpu.VMEM(frame.ends, F32), pltpu.VMEM((nx, frame.rows, LANES), F32)]
    scratch += [pltpu.VMEM(frame.main, F32)]
    got = call(fine_kernel, outs, scratch, limit=28)(
        flags, *halo, *from_x, *from_y, block_label, face_label, inner_diag
    )
    fields, pre = got[:12], got[12]
    face_near, face_weight, scaled_rhs, scale = got[13:]
    tiles = call(faces_kernel, jax.ShapeDtypeStruct((7 * AGG, 2 * AGG), BF16), pair)(
        flags, own_tile, face_label, face_near, face_weight
    )
    coarse = scaled_rhs
    for _ in range(KC - 1):
        near = links.x([coarse] * n_send) + links.y(coarse, coarse) + links.z(coarse, coarse)
        coarse = call(turn_kernel, shaped(SUB, AGG))(flags, tiles, scaled_rhs, scale, coarse, *near)
    x_sends = call(functools.partial(send_kernel, n_x), [shaped(HALO, ny, nz)] * n_send)(
        flags, pre, block_agg, coarse
    )
    from_x = links.x(x_sends)
    corrected = call(correct_kernel, shaped(nx, ny, nz))(flags, pre, block_agg, coarse)
    halo, _ = widened(links, flags, (HALO,), (corrected,), from_x)
    scratch = [pltpu.VMEM(frame.main, F32)] * 2 + [pltpu.VMEM(frame.ends, F32)] * 2
    return call(post_kernel, shaped(nx, ny, nz), scratch, limit=24)(flags, *halo, *fields)


def solution(mesh):
    spec = P("gx", "gy", "gz")
    return jax.shard_map(
        functools.partial(body, Links(mesh)), mesh=mesh, in_specs=(spec,) * 4, out_specs=spec, check_vma=False
    )
```

```python
import functools

import jax
import jax.numpy as jnp
from jax import lax
from jax.experimental import pallas as pl
from jax.experimental.pallas import tpu as pltpu
from jax.sharding import PartitionSpec as P

AGG = 128
LANES = 128
SUB = 8
HALO = 4
WIDTHS = (4, 3, 3)
POST = 4
KC = 8
OMEGA_FINE = 0.8
OMEGA_COARSE = 0.7
F32 = jnp.float32
BF16 = jnp.bfloat16
SMEM = pl.BlockSpec(memory_space=pltpu.SMEM)
VMEM = pl.BlockSpec(memory_space=pltpu.VMEM)
IX, PARITY, X_LOW, X_HIGH, Y_LOW, Y_HIGH, Z_LOW, Z_HIGH = range(8)


def call(kernel, outs, scratch=(), limit=16, flops=10**6, in_specs=None):
    def run(flags, *arrays):
        return pl.pallas_call(
            kernel,
            out_shape=outs,
            in_specs=[SMEM] + (in_specs or [VMEM] * len(arrays)),
            out_specs=jax.tree.map(lambda _: VMEM, outs),
            scratch_shapes=list(scratch),
            compiler_params=pltpu.CompilerParams(vmem_limit_bytes=limit * 2**20),
            cost_estimate=pl.CostEstimate(flops=flops, bytes_accessed=10**5, transcendentals=0),
        )(flags, *arrays)

    return run


def shaped(*shape):
    return jax.ShapeDtypeStruct(shape, F32)


def lane_no(shape):
    return lax.broadcasted_iota(jnp.int32, shape, len(shape) - 1)


def row_no(shape):
    return lax.broadcasted_iota(jnp.int32, shape, len(shape) - 2)


def turned(values, shift, axis):
    if isinstance(shift, int):
        shift = shift % values.shape[axis]
        if shift == 0:
            return values
    return pltpu.roll(values, shift, axis)


def batched(low, high, step, carry, size=6):
    def some(i, carry):
        return step([low + i * size + k for k in range(size)], carry)

    carry = lax.fori_loop(0, (high - low) // size, some, carry)
    rest = (high - low) % size
    return step(list(range(high - rest, high)), carry) if rest else carry


def picked(values, index):
    return jnp.take_along_axis(values, index, axis=1, mode="promise_in_bounds")


class Frame:
    def __init__(self, nx, ny):
        self.nx, self.ny = nx, ny
        self.wide, self.tall = nx + 2 * HALO, ny + 2 * HALO
        self.rows = self.tall + 2 * SUB
        self.span = pl.ds(SUB, self.tall)
        self.own = SUB + HALO
        self.main = (self.wide, self.rows, LANES)
        self.ends = (2, self.rows, LANES)


def bases(widths):
    return [sum(widths[:f]) for f in range(len(widths) + 1)]


def pack_x_kernel(count, widths, flags, *refs):
    fields = len(widths)
    ins, refs = refs[: fields + 1], refs[fields + 1 :]
    kept, outs = refs[: fields + 1], refs[fields + 1 : -2]
    near, sems = refs[-2:]
    nx, ny = ins[0].shape[0], ins[0].shape[1]
    base = bases(widths)
    pairs = []
    for s, out in enumerate(outs):

        def place(size, width, s=s):
            if count == 2:
                return jnp.where(flags[IX] == 0, size - width, 0)
            return (size - width, 0)[s]

        for f, (ref, width) in enumerate(zip(ins, widths)):
            pairs.append((ref.at[pl.ds(place(nx, width), width)], out.at[pl.ds(base[f], width)]))
        pairs.append((ins[-1].at[place(nx // 2, 1)], near.at[s]))
    pairs += list(zip(ins, kept))
    copies = [pltpu.make_async_copy(src, dst, sems.at[n]) for n, (src, dst) in enumerate(pairs)]
    for copy in copies:
        copy.start()
    for out in outs:
        out[base[-1]] = jnp.zeros(out.shape[1:], F32)
    for copy in copies:
        copy.wait()
    for s, out in enumerate(outs):
        out[base[-1], : ny // 2, : near.shape[2]] = near[s].astype(F32)


def slab_of(own, low, high, base, width, x):
    nx = own.shape[0]
    if HALO <= x < HALO + nx:
        return own[x - HALO]
    if x < HALO:
        at = x - (HALO - width)
        return low[base + at] if at >= 0 else None
    at = x - HALO - nx
    return high[base + at] if at < width else None


def pack_y_kernel(widths, labels, flags, *refs):
    fields = len(widths)
    ins = refs[:fields]
    low, high = refs[fields + labels : fields + labels + 2]
    inner, outer = refs[fields + labels + 2 :]
    nx, ny = ins[0].shape[0], ins[0].shape[1]
    frame = Frame(nx, ny)
    base = bases(widths)
    even = flags[PARITY] == 0

    def send(at, count, to_high, to_low):
        inner[at : at + count] = jnp.where(even, to_high, to_low)
        outer[at : at + count] = jnp.where(even, to_low, to_high)

    for f in range(fields):
        for x in range(frame.wide):
            slab = slab_of(ins[f], low, high, base[f], widths[f], x)
            at = (f * frame.wide + x) * HALO
            if slab is None:
                slab = jnp.ones((ny, LANES), F32)
            send(at, HALO, slab[ny - HALO :], slab[:HALO])
    if labels:
        at = fields * frame.wide * HALO
        nb, rows, width = refs[fields].shape
        for out in (inner, outer):
            out[at:] = jnp.zeros((out.shape[0] - at, LANES), F32)
        for b in range(nb):
            high, low = (refs[fields][b, row : row + 1].astype(F32) for row in (rows - 1, 0))
            inner[at + b : at + b + 1, :width] = jnp.where(even, high, low)
            outer[at + b : at + b + 1, :width] = jnp.where(even, low, high)


def pack_z_kernel(widths, labels, flags, *refs):
    fields = len(widths)
    ins = refs[:fields]
    x_low, x_high, inner, outer = refs[fields + labels : fields + labels + 4]
    wide_ref, send_forth, send_back = refs[fields + labels + 4 :]
    nx, ny = ins[0].shape[0], ins[0].shape[1]
    frame = Frame(nx, ny)
    base = bases(widths)
    tall, own = frame.tall, frame.own
    even = flags[PARITY] == 0

    def send(at, count, to_high, to_low):
        send_forth[at : at + count] = jnp.where(even, to_high, to_low)
        send_back[at : at + count] = jnp.where(even, to_low, to_high)

    group = lane_no((tall, LANES)) // HALO
    spare = jnp.ones((SUB, LANES), F32)
    for f in range(fields):
        to_high = to_low = jnp.ones((tall, LANES), F32)
        for x in range(frame.wide):
            at = (f * frame.wide + x) * HALO
            slab = slab_of(ins[f], x_low, x_high, base[f], widths[f], x)
            wide_ref[f, x, own : own + ny] = jnp.ones((ny, LANES), F32) if slab is None else slab
            low, high = sides(flags, outer[at : at + HALO], inner[at : at + HALO])
            wide_ref[f, x, SUB:own] = low
            wide_ref[f, x, own + ny : own + ny + HALO] = high
            wide_ref[f, x, :SUB] = spare
            wide_ref[f, x, SUB + tall :] = spare
            moved = turned(wide_ref[f, x, SUB : SUB + tall], HALO * (x + 1), 1)
            to_high = jnp.where(group == x, moved, to_high)
            to_low = jnp.where(group == (x + 1) % frame.wide, moved, to_low)
        send(f * tall, tall, to_high, turned(to_low, -HALO, 1))
    if labels:
        nb, rows, width = refs[fields].shape
        lane = lane_no((rows, LANES))
        to_high = to_low = jnp.zeros((rows, LANES), F32)
        for b in range(nb):
            slab = refs[fields][b].astype(F32)
            to_high = jnp.where(lane == b, slab[:, width - 1 :], to_high)
            to_low = jnp.where(lane == b, slab[:, :1], to_low)
        send(fields * tall, rows, to_high, to_low)


class Links:
    def __init__(self, mesh):
        self.sizes = [mesh.shape[a] for a in ("gx", "gy", "gz")]
        n_x, n_y, n_z = self.sizes

        def at(i, j, k):
            return (i * n_y + j) * n_z + k

        self.ring_x = [(i, (i + 1) % n_x) for i in range(n_x)]
        self.inner, self.outer, self.snake = [], [], []
        for i in range(n_x):
            for j in range(n_y):
                for k in range(n_z):
                    self.inner.append((at(i, j, k), at(i, j ^ 1, k)))
                    over = (i, j + 1) if j % 2 else (i, j - 1)
                    over = over if 0 <= over[1] < n_y else (i ^ 1, j)
                    self.outer.append((at(i, j, k), at(*over, k)))
            for j in range(0, n_y, 2):
                nodes = [at(i, j, k) for k in range(n_z)] + [at(i, j + 1, k) for k in reversed(range(n_z))]
                self.snake += [(nodes[m], nodes[(m + 1) % len(nodes)]) for m in range(len(nodes))]

    @staticmethod
    def back(pairs):
        return [(b, a) for a, b in pairs]

    @staticmethod
    def send(values, pairs):
        return lax.ppermute(values, ("gx", "gy", "gz"), pairs)

    def x(self, sends):
        if self.sizes[0] == 2:
            return (lax.ppermute(sends[0], "gx", self.ring_x),)
        return lax.ppermute(sends[0], "gx", self.ring_x), lax.ppermute(sends[1], "gx", self.back(self.ring_x))

    def y(self, inner, outer):
        return self.send(inner, self.inner), self.send(outer, self.outer)

    def z(self, forth, back):
        return self.send(forth, self.snake), self.send(back, self.back(self.snake))


def widened(links, flags, widths, arrays, from_x, beside_y=None, beside_z=None):
    fields, labels = len(widths), len(arrays) - len(widths)
    nx, ny, nz = arrays[0].shape
    frame = Frame(nx, ny)
    rows = fields * frame.wide * HALO + labels * ny // 2
    sends = call(functools.partial(pack_y_kernel, widths, labels), [shaped(rows, nz)] * 2)(flags, *arrays, from_x[0], from_x[-1])
    work = beside_y(sends[0]) if beside_y else ()
    from_y = links.y(*sends)
    from_y = lax.optimization_barrier((*from_y, *work))[:2] if work else from_y
    rows = fields * frame.tall + labels * ny // 2
    wide, *sends = call(
        functools.partial(pack_z_kernel, widths, labels), [shaped(fields, *frame.main)] + [shaped(rows, nz)] * 2
    )(flags, *arrays, from_x[0], from_x[-1], *from_y)
    if beside_z:
        beside_z(sends[0])
    return (wide, *links.z(*sends)), from_y


def sides(flags, forth, back):
    even = flags[PARITY] == 0
    return jnp.where(even, forth, back), jnp.where(even, back, forth)


def weight(one, two):
    return 2.0 * (one * two) / (one + two)


def lane_mask(x):
    return ((lane_no((1, LANES)) - (HALO * x + HALO - 1)) & (LANES - 1)) < 2


def edge_step(here, x, edges):
    return jnp.where(lane_mask(x), turned(here, HALO * x + HALO, 1), edges)


def joined(below, above):
    lane = lane_no(below.shape)
    return jnp.where(lane % HALO == HALO - 1, turned(above, HALO - 1, 1), turned(below, 1, 1))


def next_and_last(here, join, x):
    lane = lane_no((1, LANES))
    edge = turned(join, (LANES - HALO) - HALO * x, 1)
    upper = jnp.where(lane == LANES - 1, edge, turned(here, -1, 1))
    lower = jnp.where(lane == 0, edge, turned(here, 1, 1))
    return upper, lower


def ends_near(below, above, edges):
    layer = lane_no((1, LANES)) % HALO
    return (
        jnp.where(layer == HALO - 1, turned(edges, -1, 1), turned(below, -1, 1)),
        turned(below, 1, 1),
        turned(above, -1, 1),
        jnp.where(layer == 0, turned(edges, 1 - HALO, 1), turned(above, 1, 1)),
    )


def main_sum(frame, field, x, join, wx, wy, wz_up, wz_low):
    span = frame.span
    upper, lower = next_and_last(field[x, span], join, x)
    total = wx[x, span] * field[x + 1, span] + wx[x - 1, span] * field[x - 1, span]
    total = total + wy[x, span] * field[x, pl.ds(SUB + 1, frame.tall)]
    down = pl.ds(SUB - 1, frame.tall)
    total = total + wy[x, down] * field[x, down]
    return total + wz_up[x, span] * upper + wz_low[x, span] * lower


def ends_sum(frame, ends, s, upper, lower, wx, wy, wz_up, wz_low):
    span, down = frame.span, pl.ds(SUB - 1, frame.tall)
    here = ends[s, span]
    total = wx[s, span] * turned(here, -HALO, 1) + turned(wx[s, span] * here, HALO, 1)
    total = total + wy[s, span] * ends[s, pl.ds(SUB + 1, frame.tall)] + wy[s, down] * ends[s, down]
    return total + wz_up[s, span] * upper + wz_low[s, span] * lower


def clear_spares(ref, frame):
    for x in range(ref.shape[0]):
        ref[x, :SUB] = jnp.zeros((SUB, LANES), F32)
        ref[x, SUB + frame.tall :] = jnp.zeros((SUB, LANES), F32)


def pack_rows(values):
    half = values.shape[0] // 2
    lane = lane_no((half, LANES))
    return jnp.where(lane < LANES // 2, values[:half], turned(values[half:], LANES // 2, 1))


def lane_total(values):
    return jnp.broadcast_to(jnp.sum(values.T, axis=0, keepdims=True), (SUB, LANES))


def paired(values):
    even = 2 * (lane_no(values.shape) % (LANES // 2))
    return picked(values + turned(values, -1, 1), even)


def fine_kernel(flags, wide_ref, forth, back, from_x_low, from_x_high, inner, outer, block_label,
                face_label, inner_diag, *refs):
    main, ends = refs[:6], refs[6:12]
    pre, face_near, face_weight, scaled_rhs, scale, once, once_ends, res, diag, block_res = refs[12:]
    wx, wy, wz_up, wz_low, inv_diag, start = main
    ex, ey, ez_up, ez_low, inv_ends, start_ends = ends
    nx, ny = pre.shape[0], pre.shape[1]
    frame = Frame(nx, ny)
    wide, tall, span = frame.wide, frame.tall, frame.span
    last = HALO + nx
    got = [sides(flags, forth[f * tall : (f + 1) * tall], back[f * tall : (f + 1) * tall]) for f in range(3)]
    (cond_below, cond_above), rhs_ends, absorb_ends = got
    for ref in (wy, start, once):
        clear_spares(ref, frame)
    for ref in (ey, start_ends, once_ends):
        clear_spares(ref, frame)

    row = row_no((tall, LANES))
    lane = lane_no((1, LANES))
    keep_y = jnp.where(
        row == HALO - 1, flags[Y_LOW], jnp.where(row == HALO + ny - 1, flags[Y_HIGH], 1)
    ).astype(F32)
    keep_low, keep_high = flags[Z_LOW].astype(F32), flags[Z_HIGH].astype(F32)

    def cond_edges(xs, edges):
        for x in xs:
            edges = edge_step(wide_ref[0, x, span], x, edges)
        return edges

    edges = batched(0, wide, cond_edges, jnp.ones((tall, LANES), F32), 8)
    near = ends_near(cond_below, cond_above, edges)
    slab = lane // HALO
    keep_x = jnp.where(
        slab == HALO - 1, flags[X_LOW], jnp.where(slab == last - 1, flags[X_HIGH], 1)
    ).astype(F32)
    layer = lane % HALO
    for s, here in enumerate((cond_below, cond_above)):
        up, low = weight(here, near[2 * s]), weight(here, near[2 * s + 1])
        if s == 0:
            up = up * jnp.where(layer == HALO - 1, keep_low, 1.0)
        else:
            low = low * jnp.where(layer == 0, keep_high, 1.0)
        face_x = keep_x * weight(here, turned(here, -HALO, 1))
        face_y = keep_y * weight(here, turned(here, -1, 0))
        ex[s, span], ey[s, span], ez_up[s, span], ez_low[s, span] = face_x, face_y, up, low
        total = absorb_ends[s] + face_x + turned(face_x, HALO, 1) + face_y + turned(face_y, 1, 0) + up + low
        inverse = OMEGA_FINE / total
        inv_ends[s, span] = inverse
        start_ends[s, span] = inverse * rhs_ends[s]

    join = joined(cond_below, cond_above)
    wz_under = ez_up[0, span]

    def fields(xs, carry):
        before, edges = carry
        stores = []
        for x in xs:
            here = wide_ref[0, x, span]
            keep = jnp.where(x == HALO - 1, flags[X_LOW], jnp.where(x == last - 1, flags[X_HIGH], 1)).astype(F32)
            upper = next_and_last(here, join, x)[0]
            face_x = keep * weight(here, wide_ref[0, jnp.minimum(x + 1, wide - 1), span])
            face_y = keep_y * weight(here, wide_ref[0, x, pl.ds(SUB + 1, tall)])
            up = weight(here, upper) * jnp.where(lane == LANES - 1, keep_high, 1.0)
            under = turned(wz_under, (LANES - HALO + 1) - HALO * x, 1)
            low = jnp.where(lane == 0, under, turned(up, 1, 1))
            total = wide_ref[2, x, span] + face_x + before + face_y + turned(face_y, 1, 0) + up + low
            inverse = OMEGA_FINE / total
            begin = inverse * wide_ref[1, x, span]
            stores.append((x, (face_x, face_y, up, low, inverse, begin, total)))
            edges = edge_step(begin, x, edges)
            before = face_x
        for x, values in stores:
            for ref, value in zip((*main, diag), values):
                ref[x, span] = value
        return before, edges

    nothing = jnp.zeros((tall, LANES), F32)
    _, edges = batched(0, wide, fields, (nothing, nothing), 4)

    join = joined(start_ends[0, span], start_ends[1, span])
    near = ends_near(start_ends[0, span], start_ends[1, span], edges)
    for s in range(2):
        total = ends_sum(frame, start_ends, s, near[2 * s], near[2 * s + 1], ex, ey, ez_up, ez_low)
        once_ends[s, span] = (2.0 - OMEGA_FINE) * start_ends[s, span] + inv_ends[s, span] * total

    def second(xs, carry):
        news = []
        for x in xs:
            total = main_sum(frame, start, x, join, wx, wy, wz_up, wz_low)
            news.append((2.0 - OMEGA_FINE) * start[x, span] + inv_diag[x, span] * total)
        for x, new in zip(xs, news):
            once[x, span] = new
        return carry

    batched(HALO - 1, last + 1, second, 0)
    join2 = joined(once_ends[0, span], once_ends[1, span])

    def remainder(xs, carry):
        news = []
        for x in xs:
            total = main_sum(frame, once, x, join2, wx, wy, wz_up, wz_low)
            news.append(wide_ref[1, x, span] - diag[x, span] * once[x, span] + total)
        for x, new in zip(xs, news):
            res[x - HALO, span] = new
        for x in xs:
            pre[x - HALO] = once[x, pl.ds(frame.own, ny)]
        return carry

    batched(HALO, last, remainder, 0)

    nb, half, width = nx // 2, ny // 2, LANES // 2
    iota = row_no((AGG, LANES)).astype(F32)

    def rows_at(ref, x, off):
        return ref[x, pl.ds(frame.own + off, half, stride=2)]

    def add_rows(total, labels, b, values, c):
        for r in range(SUB):
            total = total + jnp.where(labels[b, r : r + 1] == iota, values[c, r : r + 1], 0.0)
        return total

    def to_blocks(bs, carry):
        for b in bs:
            four = sum(rows_at(res, 2 * b + a, c) for a in range(2) for c in range(2))
            block_res[b] = pack_rows(paired(four))
        return carry

    batched(0, nb, to_blocks, 0)
    zeros = jnp.zeros((AGG, LANES), F32)

    def restrict(b, total):
        return add_rows(total, block_label, b, block_res, b)

    sums = lax.fori_loop(0, nb, restrict, zeros)

    blank = jnp.zeros((half - nb, LANES), F32)
    low_at, high_at = pl.ds(frame.own - 1, 1), pl.ds(frame.own + ny - 1, 1)
    face_weight[0] = pack_rows(paired(rows_at(wx, HALO - 1, 0) + rows_at(wx, HALO - 1, 1)))
    face_weight[1] = pack_rows(paired(rows_at(wx, last - 1, 0) + rows_at(wx, last - 1, 1)))
    for s, at in ((2, low_at), (3, high_at)):
        lines = [wy[HALO + 2 * b, at] + wy[HALO + 2 * b + 1, at] for b in range(nb)]
        face_weight[s] = pack_rows(paired(jnp.concatenate(lines + [blank], axis=0)))
    lane = lane_no((half, LANES))
    for s, (ref, side, layer_at) in ((4, (ez_up, 0, HALO - 1)), (5, (ez_low, 1, 0))):
        values = rows_at(ref, side, 0) + rows_at(ref, side, 1)
        values = values + turned(values, -HALO, 1)
        spot = jnp.minimum(2 * HALO * lane + HALO * HALO + layer_at, LANES - 1)
        face_weight[s] = pack_rows(jnp.where(lane < nb, picked(values, spot), 0.0))
    around = zeros
    for s in range(6):
        around = add_rows(around, face_label, s, face_weight, s)
    scale[...] = OMEGA_COARSE / (inner_diag[...] + lane_total(around))
    scaled_rhs[...] = scale[...] * lane_total(sums)

    at = sum(WIDTHS)
    face_near[0] = pack_rows(from_x_low[at, :half])
    face_near[1] = pack_rows(from_x_high[at, :half])
    at = 3 * wide * HALO
    for s, values in enumerate(sides(flags, outer[at : at + half], inner[at : at + half])):
        face_near[2 + s] = pack_rows(values)
    below, above = sides(flags, forth[3 * tall : 3 * tall + half], back[3 * tall : 3 * tall + half])
    face_near[4] = pack_rows(below)
    face_near[5] = pack_rows(above)


def fill(left, right, labels, b, pairs):
    iota = row_no((AGG, LANES)).astype(F32)
    for r in range(SUB):
        lanes = pl.ds(r * LANES, LANES)
        row = pl.ds(r, 1)
        left[:, lanes] = jnp.where(labels[b, row] == iota, 1.0, 0.0).astype(BF16)
        held = sum(jnp.where(near[row] == iota, w[row], 0.0) for near, w in pairs)
        high = held.astype(BF16)
        right[:AGG, lanes] = high
        right[AGG:, lanes] = (held - high.astype(F32)).astype(BF16)


def product(left, right):
    return lax.dot_general(left[...], right[...], (((1,), (1,)), ((), ())), preferred_element_type=F32)


def both_halves(tile):
    return tile[:, :AGG] + tile[:, AGG:]


def keep_tile(out, t, tile):
    high = tile.astype(BF16)
    rows = pl.ds(t * AGG, AGG)
    out[rows, :AGG] = high
    out[rows, AGG:] = (tile - high.astype(F32)).astype(BF16)


def blocks_kernel(flags, cond, absorb, block_agg, _, block_label, near, weights, inner, face_label, lift, part, line):
    nx, ny = cond.shape[0], cond.shape[1]
    nb, half, width = nx // 2, ny // 2, LANES // 2
    lane, row = lane_no((half, LANES)), row_no((half, LANES))

    def halves(values, slot):
        part[slot] = values
        return part[slot, pl.ds(0, half, stride=2)], part[slot, pl.ds(1, half, stride=2)]

    def label_at(b):
        values = block_agg[b].astype(F32)
        return jnp.concatenate([values, values], axis=1)

    def upper_x(b, slot):
        x = jnp.maximum(2 * b, 0)
        faces = weight(cond[x + 1], cond[jnp.minimum(x + 2, nx - 1)])
        return jnp.where((b == nb - 1) | (b < 0), 0.0, paired(sum(halves(faces, slot))))

    def step(bs, carry):
        low_x = upper_x(bs[0] - 1, 0)
        for k, b in enumerate(bs):
            x = 2 * b
            slot = 4 * k + 1
            one, two = cond[x], cond[x + 1]
            both_y = weight(one, turned(one, -1, 0)) + weight(two, turned(two, -1, 0))
            both_z = weight(one, turned(one, -1, 1)) + weight(two, turned(two, -1, 1))
            high_x = upper_x(b, slot)
            high_y = jnp.where(row == half - 1, 0.0, paired(halves(both_y, slot + 1)[1]))
            high_z = picked(sum(halves(both_z, slot + 2)), 2 * (lane % width) + 1)
            high_z = jnp.where(lane % width == width - 1, 0.0, high_z)
            low_y, low_z = turned(high_y, 1, 0), turned(high_z, 1, 1)
            own = label_at(b)
            near_x, past_x = label_at(jnp.minimum(b + 1, nb - 1)), label_at(jnp.maximum(b - 1, 0))
            near_y, past_y = turned(own, -1, 0), turned(own, 1, 0)
            near_z, past_z = turned(own, -1, 1), turned(own, 1, 1)
            total = paired(sum(halves(absorb[x] + absorb[x + 1], slot + 3)))
            for beside, values in (
                (near_x, high_x), (past_x, low_x), (near_y, high_y), (past_y, low_y), (near_z, high_z), (past_z, low_z)
            ):
                total = total + jnp.where(beside != own, values, 0.0)
            block_label[b] = pack_rows(own)
            inner[b] = pack_rows(total)
            for d, (beside, values) in enumerate(((near_x, high_x), (near_y, high_y), (near_z, high_z))):
                near[d, b], weights[d, b] = pack_rows(beside), pack_rows(values)
            lift[b] = picked(own, lane // 2).astype(jnp.int32)
            low_x = high_x
        return carry

    batched(0, nb, step, 0, 4)
    line[...] = jnp.zeros(line.shape, F32)
    low, high = jnp.zeros((half, LANES), F32), jnp.zeros((half, LANES), F32)
    for b in range(nb):
        own = label_at(b)
        line[0, b : b + 1], line[1, b : b + 1] = own[:1], own[half - 1 :]
        low = jnp.where(lane == b, own[:, :1], low)
        high = jnp.where(lane == b, own[:, width - 1 : width], high)
    face_label[0], face_label[1] = block_label[0], block_label[nb - 1]
    for s, values in enumerate((line[0], line[1], low, high)):
        face_label[2 + s] = pack_rows(values)


def own_kernel(first, last, total, flags, block_label, near, weights, inner, *refs):
    so_far, refs = (refs[0], refs[1:]) if first else (None, refs)
    refs = refs[1:]
    iota = row_no((AGG, LANES)).astype(F32)

    def step(bs, tile):
        for k, b in enumerate(bs):
            left, right = refs[-4 + 2 * (k % 2) :][:2]
            fill(left, right, block_label, b, [(near.at[d, b], weights.at[d, b]) for d in range(3)])
            tile = tile + product(left, right)
        return tile

    tile = so_far[...] if first else jnp.zeros((AGG, 2 * AGG), F32)
    tile = batched(first, last, step, tile, 2)
    if last < total:
        refs[0][...] = tile
        return
    out, inner_diag = refs[:2]
    tile = both_halves(tile)
    keep_tile(out, 0, jnp.where(row_no((AGG, AGG)) == lane_no((AGG, AGG)), 0.0, tile + tile.T))

    def gather(b, around):
        for r in range(SUB):
            around = around + jnp.where(block_label[b, r : r + 1] == iota, inner[b, r : r + 1], 0.0)
        return around

    inner_diag[...] = lane_total(lax.fori_loop(0, total, gather, jnp.zeros((AGG, LANES), F32)))


def faces_kernel(count, flags, own, face_label, face_near, face_weight, out, *factors):
    out[:AGG] = own[...]
    s = jnp.where(flags[IX] == 0, 1, 0)
    faces = ([s] if count == 2 else [0, 1]) + [2, 3, 4, 5]
    for t, s in enumerate(faces):
        left, right = factors[2 * (t % 2) :][:2]
        fill(left, right, face_near, s, [(face_label.at[s], face_weight.at[s])])
        keep_tile(out, t + 1, both_halves(product(left, right)))


def turn_kernel(flags, tiles, scaled_rhs, scale, own, *refs):
    *from_x, inner, outer, forth, back, out = refs
    vectors = [own[...]] + [ref[...] for ref in from_x]
    vectors += [*sides(flags, outer[...], inner[...]), *sides(flags, forth[...], back[...])]
    row = row_no((SUB, AGG))
    parts = []
    for v in vectors:
        high = v.astype(BF16).astype(F32)
        parts.append(jnp.where(row == 0, high, jnp.where(row == 1, v - high, 0.0)).astype(BF16))
    got = jnp.dot(jnp.concatenate(parts, axis=1), tiles[...], preferred_element_type=F32)
    applied = jnp.sum(got[:, :AGG] + got[:, AGG:], axis=0, keepdims=True)
    out[...] = (1.0 - OMEGA_COARSE) * own[...] + scaled_rhs[...] + scale[...] * applied


def lifted(pre, lift, table, out, bs, at):
    half = pre.shape[1] // 2
    for n, b in enumerate(bs):
        values = picked(table, lift[b])
        for a in range(2):
            for c in range(2):
                rows = pl.ds(c, half, stride=2)
                out[at + 2 * n + a, rows] = pre[2 * b + a, rows] + values


def send_kernel(count, flags, pre, lift, coarse, *outs):
    nb, half = pre.shape[0] // 2, pre.shape[1] // 2
    table = jnp.broadcast_to(coarse[:1], (half, LANES))
    for s, out in enumerate(outs):
        if count == 2:
            b = jnp.where(flags[IX] == 0, nb - HALO // 2, 0)
        else:
            b = (nb - HALO // 2, 0)[s]
        lifted(pre, lift, table, out, [b + h for h in range(HALO // 2)], 0)


def correct_kernel(flags, pre, lift, coarse, out):
    table = jnp.broadcast_to(coarse[:1], (pre.shape[1] // 2, LANES))

    def step(bs, carry):
        lifted(pre, lift, table, out, bs, 2 * bs[0])
        return carry

    batched(0, pre.shape[0] // 2, step, 0)


def post_kernel(flags, wide_ref, forth, back, *refs):
    main, ends = refs[:6], refs[6:12]
    out, one, two, one_ends, two_ends = refs[12:]
    nx, ny = out.shape[0], out.shape[1]
    frame = Frame(nx, ny)
    wide, tall, span = frame.wide, frame.tall, frame.span
    wx, wy, wz_up, wz_low, inv_diag, start = main
    ex, ey, ez_up, ez_low, inv_ends, start_ends = ends
    for ref in (one, two, one_ends, two_ends):
        clear_spares(ref, frame)
    below, above = sides(flags, forth[...], back[...])
    two_ends[0, span], two_ends[1, span] = below, above
    kept = 1.0 - OMEGA_FINE
    buffers = ((wide_ref.at[0], two_ends), (one, one_ends), (two, two_ends), (one, one_ends))
    for s in range(POST):
        src, src_ends = buffers[s]
        join = joined(src_ends[0, span], src_ends[1, span])
        final = s == POST - 1
        dst, dst_ends = (None, None) if final else buffers[s + 1]

        def step(xs, edges, src=src, join=join, dst=dst, final=final):
            news = []
            for x in xs:
                here = src[x, span]
                total = main_sum(frame, src, x, join, wx, wy, wz_up, wz_low)
                news.append(kept * here + start[x, span] + inv_diag[x, span] * total)
                if not final:
                    edges = edge_step(here, x, edges)
            for x, new in zip(xs, news):
                if final:
                    out[x - HALO] = new[HALO : HALO + ny]
                else:
                    dst[x, span] = new
            return edges

        edges = batched(s + 1, wide - s - 1, step, jnp.zeros((tall, LANES), F32))
        if not final:
            near = ends_near(src_ends[0, span], src_ends[1, span], edges)
            news = []
            for e in range(2):
                total = ends_sum(frame, src_ends, e, near[2 * e], near[2 * e + 1], ex, ey, ez_up, ez_low)
                news.append(kept * src_ends[e, span] + start_ends[e, span] + inv_ends[e, span] * total)
            dst_ends[0, span], dst_ends[1, span] = news


def body(links, right_side, conductance, absorption, block_agg):
    nx, ny, nz = right_side.shape
    frame = Frame(nx, ny)
    nb = nx // 2
    ix, iy, iz = (lax.axis_index(a) for a in ("gx", "gy", "gz"))
    n_x, n_y, n_z = links.sizes
    flags = jnp.stack(
        [ix, iy % 2, ix > 0, ix < n_x - 1, iy > 0, iy < n_y - 1, iz > 0, iz < n_z - 1]
    ).astype(jnp.int32)
    arrays = (conductance, right_side, absorption, block_agg)
    n_send = 1 if n_x == 2 else 2
    got = call(
        functools.partial(pack_x_kernel, n_x, WIDTHS),
        [jax.ShapeDtypeStruct(a.shape, a.dtype) for a in arrays] + [shaped(sum(WIDTHS) + 1, ny, nz)] * n_send,
        [pltpu.VMEM((n_send, ny // 2, nz // 2), jnp.int32), pltpu.SemaphoreType.DMA((n_send * 4 + 4,))],
        in_specs=[pl.BlockSpec(memory_space=pltpu.HBM)] * 4,
    )(flags, *(pltpu.with_memory_space_constraint(a, pltpu.HBM) for a in arrays))
    arrays, x_sends = got[:4], got[4:]
    blocks = (nb, SUB, LANES)
    outs = [shaped(*blocks), shaped(3, *blocks), shaped(3, *blocks), shaped(*blocks), shaped(6, SUB, LANES)]
    outs += [jax.ShapeDtypeStruct((nb, ny // 2, LANES), jnp.int32)]
    scratch = [pltpu.VMEM((17, ny, LANES), F32), pltpu.VMEM((2, ny // 2, LANES), F32)]
    pair = [pltpu.VMEM((AGG, SUB * LANES), BF16), pltpu.VMEM((2 * AGG, SUB * LANES), BF16)]
    *rows, face_label, lift = call(blocks_kernel, outs, scratch)(flags, arrays[0], arrays[2], arrays[3], x_sends[0])
    block_label = rows[0]
    first = call(functools.partial(own_kernel, 0, nb // 2, nb), [shaped(AGG, 2 * AGG)], pair * 2)(
        flags, *rows, x_sends[0]
    )[0]
    from_x = links.x(x_sends)
    from_x = lax.optimization_barrier((*from_x, first))[:-1]
    later = []

    def second_half(sent):
        outs = [jax.ShapeDtypeStruct((AGG, 2 * AGG), BF16), shaped(SUB, AGG)]
        later.extend(
            call(functools.partial(own_kernel, nb // 2, nb, nb), outs, pair * 2)(flags, *rows, first, sent)
        )
        return later

    halo, from_y = widened(links, flags, WIDTHS, arrays, from_x, second_half)
    own_tile, inner_diag = later
    outs = [shaped(*frame.main)] * 6 + [shaped(*frame.ends)] * 6 + [shaped(nx, ny, nz)]
    outs += [shaped(6, SUB, LANES)] * 2 + [shaped(SUB, AGG)] * 2
    scratch = [pltpu.VMEM(frame.main, F32), pltpu.VMEM(frame.ends, F32), pltpu.VMEM((nx, frame.rows, LANES), F32)]
    scratch += [pltpu.VMEM(frame.main, F32), pltpu.VMEM((nb, SUB, LANES), F32)]
    got = call(fine_kernel, outs, scratch, limit=28)(
        flags, *halo, from_x[0], from_x[-1], *from_y, block_label, face_label, inner_diag
    )
    fields, pre = got[:12], got[12]
    face_near, face_weight, scaled_rhs, scale = got[13:]
    tiles = call(
        functools.partial(faces_kernel, n_x),
        jax.ShapeDtypeStruct(((n_send + 5) * AGG, 2 * AGG), BF16),
        pair * 2,
    )(flags, own_tile, face_label, face_near, face_weight)
    coarse = scaled_rhs
    for _ in range(KC - 1):
        near = links.x([coarse] * n_send) + links.y(coarse, coarse) + links.z(coarse, coarse)
        coarse = call(turn_kernel, shaped(SUB, AGG))(flags, tiles, scaled_rhs, scale, coarse, *near)
    x_sends = call(functools.partial(send_kernel, n_x), [shaped(HALO, ny, nz)] * n_send)(flags, pre, lift, coarse)
    from_x = links.x(x_sends)
    corrected = call(correct_kernel, shaped(nx, ny, nz))(flags, pre, lift, coarse)
    halo, _ = widened(links, flags, (HALO,), (corrected,), from_x)
    scratch = [pltpu.VMEM(frame.main, F32)] * 2 + [pltpu.VMEM(frame.ends, F32)] * 2
    return call(post_kernel, shaped(nx, ny, nz), scratch, limit=24)(flags, *halo, *fields)


def solution(mesh):
    spec = P("gx", "gy", "gz")
    return jax.shard_map(
        functools.partial(body, Links(mesh)), mesh=mesh, in_specs=(spec,) * 4, out_specs=spec, check_vma=False
    )
```

```python
import functools

import jax
import jax.numpy as jnp
from jax import lax
from jax.experimental import pallas as pl
from jax.experimental.pallas import tpu as pltpu
from jax.sharding import PartitionSpec as P

AGG = 128
LANES = 128
SUB = 8
HALO = 4
WIDTHS = (4, 3, 3)
POST = 4
KC = 8
OMEGA_FINE = 0.8
OMEGA_COARSE = 0.7
F32 = jnp.float32
BF16 = jnp.bfloat16
SMEM = pl.BlockSpec(memory_space=pltpu.SMEM)
VMEM = pl.BlockSpec(memory_space=pltpu.VMEM)
IX, PARITY, X_LOW, X_HIGH, Y_LOW, Y_HIGH, Z_LOW, Z_HIGH = range(8)


def call(kernel, outs, scratch=(), limit=16, flops=10**6, in_specs=None, aliases=None):
    def run(flags, *arrays):
        return pl.pallas_call(
            kernel,
            out_shape=outs,
            in_specs=[SMEM] + (in_specs or [VMEM] * len(arrays)),
            out_specs=jax.tree.map(lambda _: VMEM, outs),
            scratch_shapes=list(scratch),
            input_output_aliases=aliases or {},
            compiler_params=pltpu.CompilerParams(vmem_limit_bytes=limit * 2**20),
            cost_estimate=pl.CostEstimate(flops=flops, bytes_accessed=10**5, transcendentals=0),
        )(flags, *arrays)

    return run


def shaped(*shape):
    return jax.ShapeDtypeStruct(shape, F32)


def lane_no(shape):
    return lax.broadcasted_iota(jnp.int32, shape, len(shape) - 1)


def row_no(shape):
    return lax.broadcasted_iota(jnp.int32, shape, len(shape) - 2)


def turned(values, shift, axis):
    if isinstance(shift, int):
        shift = shift % values.shape[axis]
        if shift == 0:
            return values
    return pltpu.roll(values, shift, axis)


def batched(low, high, step, carry, size=6):
    def some(i, carry):
        return step([low + i * size + k for k in range(size)], carry)

    carry = lax.fori_loop(0, (high - low) // size, some, carry)
    rest = (high - low) % size
    return step(list(range(high - rest, high)), carry) if rest else carry


def picked(values, index):
    return jnp.take_along_axis(values, index, axis=1, mode="promise_in_bounds")


class Frame:
    def __init__(self, nx, ny):
        self.nx, self.ny = nx, ny
        self.wide, self.tall = nx + 2 * HALO, ny + 2 * HALO
        self.rows = self.tall + 2 * SUB
        self.span = pl.ds(SUB, self.tall)
        self.own = SUB + HALO
        self.main = (self.wide, self.rows, LANES)
        self.ends = (2, self.rows, LANES)


def bases(widths):
    return [sum(widths[:f]) for f in range(len(widths) + 1)]


def copied(pairs, sems):
    copies = [pltpu.make_async_copy(src, dst, sems.at[n]) for n, (src, dst) in enumerate(pairs)]
    for copy in copies:
        copy.start()
    return copies


def pack_x_kernel(count, widths, flags, *refs):
    fields = len(widths)
    ins, outs = refs[: fields + 1], refs[fields + 1 : -2]
    near, sems = refs[-2:]
    nx, ny = ins[0].shape[0], ins[0].shape[1]
    base = bases(widths)
    pairs = []
    for s, out in enumerate(outs):

        def place(size, width, s=s):
            if count == 2:
                return jnp.where(flags[IX] == 0, size - width, 0)
            return (size - width, 0)[s]

        for f, (ref, width) in enumerate(zip(ins, widths)):
            pairs.append((ref.at[pl.ds(place(nx, width), width)], out.at[pl.ds(base[f], width)]))
        pairs.append((ins[-1].at[place(nx // 2, 1)], near.at[s]))
    copies = copied(pairs, sems)
    for out in outs:
        out[base[-1]] = jnp.zeros(out.shape[1:], F32)
    for copy in copies:
        copy.wait()
    for s, out in enumerate(outs):
        out[base[-1], : ny // 2, : near.shape[2]] = near[s].astype(F32)


def load_kernel(flags, *refs):
    count = (len(refs) - 2) // 2
    for copy in copied(list(zip(refs[:count], refs[count + 1 : -1])), refs[-1]):
        copy.wait()


def slab_of(own, low, high, base, width, x):
    nx = own.shape[0]
    if HALO <= x < HALO + nx:
        return own[x - HALO]
    if x < HALO:
        at = x - (HALO - width)
        return low[base + at] if at >= 0 else None
    at = x - HALO - nx
    return high[base + at] if at < width else None


def pack_y_kernel(widths, labels, flags, *refs):
    fields = len(widths)
    ins = refs[:fields]
    low, high = refs[fields + labels : fields + labels + 2]
    inner, outer = refs[fields + labels + 2 :]
    nx, ny = ins[0].shape[0], ins[0].shape[1]
    frame = Frame(nx, ny)
    base = bases(widths)
    even = flags[PARITY] == 0

    def send(at, count, to_high, to_low):
        inner[at : at + count] = jnp.where(even, to_high, to_low)
        outer[at : at + count] = jnp.where(even, to_low, to_high)

    for f in range(fields):
        for x in range(frame.wide):
            slab = slab_of(ins[f], low, high, base[f], widths[f], x)
            at = (f * frame.wide + x) * HALO
            if slab is None:
                slab = jnp.ones((ny, LANES), F32)
            send(at, HALO, slab[ny - HALO :], slab[:HALO])
    if labels:
        at = fields * frame.wide * HALO
        nb, rows, width = refs[fields].shape
        for out in (inner, outer):
            out[at:] = jnp.zeros((out.shape[0] - at, LANES), F32)
        for b in range(nb):
            high, low = (refs[fields][b, row : row + 1].astype(F32) for row in (rows - 1, 0))
            inner[at + b : at + b + 1, :width] = jnp.where(even, high, low)
            outer[at + b : at + b + 1, :width] = jnp.where(even, low, high)


def packed_lanes(wide_ref, f, frame, rows, to_high, to_low):
    group = lane_no((1, LANES)) // HALO
    nothing = jnp.ones((rows.size, LANES), F32)
    high, low = nothing, nothing
    for x in range(frame.wide):
        moved = turned(wide_ref[f, x, rows], HALO * (x + 1), 1)
        high = jnp.where(group == x, moved, high)
        low = jnp.where(group == (x + 1) % frame.wide, moved, low)
    at = pl.ds(f * frame.tall + rows.start - SUB, rows.size)
    to_high[at] = high
    to_low[at] = turned(low, -HALO, 1)


def frame_kernel(widths, labels, flags, *refs):
    fields = len(widths)
    ins = refs[:fields]
    x_low, x_high, _ = refs[fields : fields + 3]
    wide_ref, to_high, to_low = refs[fields + 3 :]
    nx, ny = ins[0].shape[0], ins[0].shape[1]
    frame = Frame(nx, ny)
    base = bases(widths)
    tall, own = frame.tall, frame.own
    spare = jnp.ones((SUB, LANES), F32)
    for f in range(fields):
        for x in range(frame.wide):
            slab = slab_of(ins[f], x_low, x_high, base[f], widths[f], x)
            wide_ref[f, x, own : own + ny] = jnp.ones((ny, LANES), F32) if slab is None else slab
            wide_ref[f, x, :SUB] = spare
            wide_ref[f, x, SUB + tall :] = spare
        packed_lanes(wide_ref, f, frame, pl.ds(2 * SUB, tall - 2 * SUB), to_high, to_low)


def pack_z_kernel(widths, labels, flags, wide_in, high_in, low_in, inner, outer, *refs):
    fields = len(widths)
    wide_ref, send_forth, send_back, to_high, to_low = refs[labels:]
    frame = Frame(wide_ref.shape[1] - 2 * HALO, wide_ref.shape[2] - 2 * (SUB + HALO))
    ny, tall, own = frame.ny, frame.tall, frame.own
    even = flags[PARITY] == 0
    for f in range(fields):
        for x in range(frame.wide):
            at = (f * frame.wide + x) * HALO
            low, high = sides(flags, outer[at : at + HALO], inner[at : at + HALO])
            wide_ref[f, x, SUB:own] = low
            wide_ref[f, x, own + ny : own + ny + HALO] = high
    size = fields * tall
    to_high[...], to_low[...] = high_in[...], low_in[...]
    for f in range(fields):
        for start in (SUB, tall):
            packed_lanes(wide_ref, f, frame, pl.ds(start, SUB), to_high, to_low)
    high, low = to_high[...], to_low[...]
    send_forth[:size], send_back[:size] = jnp.where(even, high, low), jnp.where(even, low, high)
    if labels:
        nb, rows, width = refs[0].shape
        lane = lane_no((rows, LANES))
        high = low = jnp.zeros((rows, LANES), F32)
        for b in range(nb):
            slab = refs[0][b].astype(F32)
            high = jnp.where(lane == b, slab[:, width - 1 :], high)
            low = jnp.where(lane == b, slab[:, :1], low)
        send_forth[size:], send_back[size:] = jnp.where(even, high, low), jnp.where(even, low, high)


class Links:
    def __init__(self, mesh):
        self.sizes = [mesh.shape[a] for a in ("gx", "gy", "gz")]
        n_x, n_y, n_z = self.sizes

        def at(i, j, k):
            return (i * n_y + j) * n_z + k

        self.ring_x = [(i, (i + 1) % n_x) for i in range(n_x)]
        self.inner, self.outer, self.snake = [], [], []
        for i in range(n_x):
            for j in range(n_y):
                for k in range(n_z):
                    self.inner.append((at(i, j, k), at(i, j ^ 1, k)))
                    over = (i, j + 1) if j % 2 else (i, j - 1)
                    over = over if 0 <= over[1] < n_y else (i ^ 1, j)
                    self.outer.append((at(i, j, k), at(*over, k)))
            for j in range(0, n_y, 2):
                nodes = [at(i, j, k) for k in range(n_z)] + [at(i, j + 1, k) for k in reversed(range(n_z))]
                self.snake += [(nodes[m], nodes[(m + 1) % len(nodes)]) for m in range(len(nodes))]

    @staticmethod
    def back(pairs):
        return [(b, a) for a, b in pairs]

    @staticmethod
    def send(values, pairs):
        return lax.ppermute(values, ("gx", "gy", "gz"), pairs)

    def x(self, sends):
        if self.sizes[0] == 2:
            return (lax.ppermute(sends[0], "gx", self.ring_x),)
        return lax.ppermute(sends[0], "gx", self.ring_x), lax.ppermute(sends[1], "gx", self.back(self.ring_x))

    def near(self, values):
        ring = [(j, (j + 1) % self.sizes[1]) for j in range(self.sizes[1])]
        forth, back = self.z(values, values)
        from_x = self.x([values, values])
        low, high = lax.ppermute(values, "gy", ring), lax.ppermute(values, "gy", self.back(ring))
        return (forth, back, *from_x, low, high)

    def y(self, inner, outer):
        return self.send(inner, self.inner), self.send(outer, self.outer)

    def z(self, forth, back):
        return self.send(forth, self.snake), self.send(back, self.back(self.snake))


def widened(links, flags, widths, arrays, from_x, beside_y=None, beside_z=None):
    fields, labels = len(widths), len(arrays) - len(widths)
    nx, ny, nz = arrays[0].shape
    frame = Frame(nx, ny)
    rows = fields * frame.wide * HALO + labels * ny // 2
    sends = call(functools.partial(pack_y_kernel, widths, labels), [shaped(rows, nz)] * 2)(
        flags, *arrays, from_x[0], from_x[-1]
    )
    size = fields * frame.tall
    framed = call(
        functools.partial(frame_kernel, widths, labels), [shaped(fields, *frame.main)] + [shaped(size, nz)] * 2
    )(flags, *arrays[:fields], from_x[0], from_x[-1], sends[0])
    work = beside_y(sends[0]) if beside_y else ()
    from_y = links.y(*sends)
    if work:
        from_y = lax.optimization_barrier((*from_y, *work))[:2]
    rows = size + labels * ny // 2
    wide, *sends = call(
        functools.partial(pack_z_kernel, widths, labels),
        [shaped(fields, *frame.main)] + [shaped(rows, nz)] * 2,
        [pltpu.VMEM((size, nz), F32)] * 2,
        aliases={1: 0},
    )(flags, *framed, *from_y, *arrays[fields:])
    if beside_z:
        beside_z(wide, sends[0])
    return (wide, *links.z(*sends)), from_y


def sides(flags, forth, back):
    even = flags[PARITY] == 0
    return jnp.where(even, forth, back), jnp.where(even, back, forth)


def weight(one, two):
    return 2.0 * (one * two) / (one + two)


def lane_mask(x):
    return ((lane_no((1, LANES)) - (HALO * x + HALO - 1)) & (LANES - 1)) < 2


def edge_step(here, x, edges):
    return jnp.where(lane_mask(x), turned(here, HALO * x + HALO, 1), edges)


def joined(below, above):
    lane = lane_no((1, LANES))
    return jnp.where(lane % HALO == HALO - 1, turned(above, HALO - 1, 1), turned(below, 1, 1))


def at_edges(join, x):
    lane = lane_no((1, LANES))
    return jnp.where((lane == 0) | (lane == LANES - 1), turned(join, (LANES - HALO) - HALO * x, 1), 0.0)


def ends_near(below, above, edges):
    layer = lane_no((1, LANES)) % HALO
    return (
        jnp.where(layer == HALO - 1, turned(edges, -1, 1), turned(below, -1, 1)),
        turned(below, 1, 1),
        turned(above, -1, 1),
        jnp.where(layer == 0, turned(edges, 1 - HALO, 1), turned(above, 1, 1)),
    )


def main_sum(frame, field, x, join, wx, wy, wz):
    span, down = frame.span, pl.ds(SUB - 1, frame.tall)
    here, face_z = field[x, span], wz[x, span]
    total = wx[x, span] * field[x + 1, span] + wx[x - 1, span] * field[x - 1, span]
    total = total + wy[x, span] * field[x, pl.ds(SUB + 1, frame.tall)] + wy[x, down] * field[x, down]
    total = total + face_z * turned(here, -1, 1) + turned(face_z * here, 1, 1)
    return total + at_edges(join, x)


def ends_sum(frame, ends, s, upper, lower, wx, wy, wz_up, wz_low):
    span, down = frame.span, pl.ds(SUB - 1, frame.tall)
    here = ends[s, span]
    total = wx[s, span] * turned(here, -HALO, 1) + turned(wx[s, span] * here, HALO, 1)
    total = total + wy[s, span] * ends[s, pl.ds(SUB + 1, frame.tall)] + wy[s, down] * ends[s, down]
    return total + wz_up[s, span] * upper + wz_low[s, span] * lower


def clear_spares(ref, frame):
    for x in range(ref.shape[0]):
        ref[x, :SUB] = jnp.zeros((SUB, LANES), F32)
        ref[x, SUB + frame.tall :] = jnp.zeros((SUB, LANES), F32)


def pack_rows(values):
    half = values.shape[0] // 2
    lane = lane_no((half, LANES))
    return jnp.where(lane < LANES // 2, values[:half], turned(values[half:], LANES // 2, 1))


def lane_total(values):
    return jnp.broadcast_to(jnp.sum(values.T, axis=0, keepdims=True), (SUB, LANES))


def paired(values):
    even = 2 * (lane_no(values.shape) % (LANES // 2))
    return picked(values + turned(values, -1, 1), even)


def faces_y_kept(flags, frame):
    row = row_no((frame.tall, LANES))
    at_low, at_high = row == HALO - 1, row == HALO + frame.ny - 1
    return jnp.where(at_low, flags[Y_LOW], jnp.where(at_high, flags[Y_HIGH], 1)).astype(F32)


def fields_kernel(flags, wide_ref, _, wx, wy, wz, partial, cond_edges):
    frame = Frame(wx.shape[0] - 2 * HALO, wx.shape[1] - 2 * (SUB + HALO))
    wide, tall, span = frame.wide, frame.tall, frame.span
    last = HALO + frame.nx
    keep_y = faces_y_kept(flags, frame)
    inside = jnp.where(lane_no((1, LANES)) == LANES - 1, 0.0, 1.0)
    clear_spares(wy, frame)

    def fields(xs, carry):
        before, edges = carry
        stores = []
        for x in xs:
            here = wide_ref[0, x, span]
            keep = jnp.where(x == HALO - 1, flags[X_LOW], jnp.where(x == last - 1, flags[X_HIGH], 1)).astype(F32)
            face_x = keep * weight(here, wide_ref[0, jnp.minimum(x + 1, wide - 1), span])
            face_y = keep_y * weight(here, wide_ref[0, x, pl.ds(SUB + 1, tall)])
            face_z = inside * weight(here, turned(here, -1, 1))
            total = wide_ref[2, x, span] + face_x + before + face_y + turned(face_y, 1, 0)
            total = total + face_z + turned(face_z, 1, 1)
            stores.append((x, (face_x, face_y, face_z, total)))
            edges = edge_step(here, x, edges)
            before = face_x
        for x, values in stores:
            for ref, value in zip((wx, wy, wz, partial), values):
                ref[x, span] = value
        return before, edges

    nothing = jnp.zeros((tall, LANES), F32)
    cond_edges[...] = batched(0, wide, fields, (nothing, nothing + 1.0), 4)[1]


def fine_kernel(flags, wide_ref, forth, back, from_x_low, from_x_high, inner, outer, wx, wy, wz, partial, cond_edges,
                block_label, face_label, inner_diag, *refs):
    inv_diag, start = refs[:2]
    ends = refs[2:8]
    pre, face_near, face_weight, scaled_rhs, scale, once, once_ends, res, diag, block_res = refs[8:]
    ex, ey, ez_up, ez_low, inv_ends, start_ends = ends
    nx, ny = pre.shape[0], pre.shape[1]
    frame = Frame(nx, ny)
    wide, tall, span = frame.wide, frame.tall, frame.span
    last = HALO + nx
    got = [sides(flags, forth[f * tall : (f + 1) * tall], back[f * tall : (f + 1) * tall]) for f in range(3)]
    (cond_below, cond_above), rhs_ends, absorb_ends = got
    for ref in (start, once, ey, start_ends, once_ends):
        clear_spares(ref, frame)

    lane = lane_no((1, LANES))
    keep_y = faces_y_kept(flags, frame)
    keep_low, keep_high = flags[Z_LOW].astype(F32), flags[Z_HIGH].astype(F32)
    near = ends_near(cond_below, cond_above, cond_edges[...])
    slab = lane // HALO
    keep_x = jnp.where(
        slab == HALO - 1, flags[X_LOW], jnp.where(slab == last - 1, flags[X_HIGH], 1)
    ).astype(F32)
    layer = lane % HALO
    for s, here in enumerate((cond_below, cond_above)):
        up, low = weight(here, near[2 * s]), weight(here, near[2 * s + 1])
        if s == 0:
            up = up * jnp.where(layer == HALO - 1, keep_low, 1.0)
        else:
            low = low * jnp.where(layer == 0, keep_high, 1.0)
        face_x = keep_x * weight(here, turned(here, -HALO, 1))
        face_y = keep_y * weight(here, turned(here, -1, 0))
        ex[s, span], ey[s, span], ez_up[s, span], ez_low[s, span] = face_x, face_y, up, low
        total = absorb_ends[s] + face_x + turned(face_x, HALO, 1) + face_y + turned(face_y, 1, 0) + up + low
        inverse = OMEGA_FINE / total
        inv_ends[s, span] = inverse
        start_ends[s, span] = inverse * rhs_ends[s]

    end_low, end_high = ez_up[0, span], ez_low[1, span]
    join_faces = joined(end_low, end_high)

    def first_sweep(xs, edges):
        stores = []
        for x in xs:
            total = partial[x, span] + at_edges(join_faces, x)
            inverse = OMEGA_FINE / total
            begin = inverse * wide_ref[1, x, span]
            stores.append((x, (total, inverse, begin)))
            edges = edge_step(begin, x, edges)
        for x, values in stores:
            for ref, value in zip((diag, inv_diag, start), values):
                ref[x, span] = value
        return edges

    edges = batched(0, wide, first_sweep, jnp.zeros((tall, LANES), F32), 4)

    join = joined(end_low * start_ends[0, span], end_high * start_ends[1, span])
    near = ends_near(start_ends[0, span], start_ends[1, span], edges)
    for s in range(2):
        total = ends_sum(frame, start_ends, s, near[2 * s], near[2 * s + 1], ex, ey, ez_up, ez_low)
        once_ends[s, span] = (2.0 - OMEGA_FINE) * start_ends[s, span] + inv_ends[s, span] * total

    def second(xs, carry):
        news = []
        for x in xs:
            total = main_sum(frame, start, x, join, wx, wy, wz)
            news.append((2.0 - OMEGA_FINE) * start[x, span] + inv_diag[x, span] * total)
        for x, new in zip(xs, news):
            once[x, span] = new
        return carry

    batched(HALO - 1, last + 1, second, 0)
    join2 = joined(end_low * once_ends[0, span], end_high * once_ends[1, span])

    def remainder(xs, carry):
        news = []
        for x in xs:
            total = main_sum(frame, once, x, join2, wx, wy, wz)
            news.append(wide_ref[1, x, span] - diag[x, span] * once[x, span] + total)
        for x, new in zip(xs, news):
            res[x - HALO, span] = new
        for x in xs:
            pre[x - HALO] = once[x, pl.ds(frame.own, ny)]
        return carry

    batched(HALO, last, remainder, 0)

    nb, half, width = nx // 2, ny // 2, LANES // 2
    iota = row_no((AGG, LANES)).astype(F32)

    def rows_at(ref, x, off):
        return ref[x, pl.ds(frame.own + off, half, stride=2)]

    def add_rows(total, labels, b, values, c):
        for r in range(SUB):
            total = total + jnp.where(labels[b, r : r + 1] == iota, values[c, r : r + 1], 0.0)
        return total

    def to_blocks(bs, carry):
        for b in bs:
            four = sum(rows_at(res, 2 * b + a, c) for a in range(2) for c in range(2))
            block_res[b] = pack_rows(paired(four))
        return carry

    batched(0, nb, to_blocks, 0)
    zeros = jnp.zeros((AGG, LANES), F32)

    def restrict(b, total):
        return add_rows(total, block_label, b, block_res, b)

    sums = lax.fori_loop(0, nb, restrict, zeros)

    blank = jnp.zeros((half - nb, LANES), F32)
    low_at, high_at = pl.ds(frame.own - 1, 1), pl.ds(frame.own + ny - 1, 1)
    face_weight[0] = pack_rows(paired(rows_at(wx, HALO - 1, 0) + rows_at(wx, HALO - 1, 1)))
    face_weight[1] = pack_rows(paired(rows_at(wx, last - 1, 0) + rows_at(wx, last - 1, 1)))
    for s, at in ((2, low_at), (3, high_at)):
        lines = [wy[HALO + 2 * b, at] + wy[HALO + 2 * b + 1, at] for b in range(nb)]
        face_weight[s] = pack_rows(paired(jnp.concatenate(lines + [blank], axis=0)))
    lane = lane_no((half, LANES))
    for s, (ref, side, layer_at) in ((4, (ez_up, 0, HALO - 1)), (5, (ez_low, 1, 0))):
        values = rows_at(ref, side, 0) + rows_at(ref, side, 1)
        values = values + turned(values, -HALO, 1)
        spot = jnp.minimum(2 * HALO * lane + HALO * HALO + layer_at, LANES - 1)
        face_weight[s] = pack_rows(jnp.where(lane < nb, picked(values, spot), 0.0))
    around = zeros
    for s in range(6):
        around = add_rows(around, face_label, s, face_weight, s)
    scale[...] = OMEGA_COARSE / (inner_diag[...] + lane_total(around))
    scaled_rhs[...] = scale[...] * lane_total(sums)

    at = sum(WIDTHS)
    face_near[0] = pack_rows(from_x_low[at, :half])
    face_near[1] = pack_rows(from_x_high[at, :half])
    at = 3 * wide * HALO
    for s, values in enumerate(sides(flags, outer[at : at + half], inner[at : at + half])):
        face_near[2 + s] = pack_rows(values)
    below, above = sides(flags, forth[3 * tall : 3 * tall + half], back[3 * tall : 3 * tall + half])
    face_near[4] = pack_rows(below)
    face_near[5] = pack_rows(above)


def fill(left, right, labels, b, pairs):
    iota = row_no((AGG, LANES)).astype(F32)
    for r in range(SUB):
        lanes = pl.ds(r * LANES, LANES)
        row = pl.ds(r, 1)
        left[:, lanes] = jnp.where(labels[b, row] == iota, 1.0, 0.0).astype(BF16)
        held = sum(jnp.where(near[row] == iota, w[row], 0.0) for near, w in pairs)
        high = held.astype(BF16)
        right[:AGG, lanes] = high
        right[AGG:, lanes] = (held - high.astype(F32)).astype(BF16)


def product(left, right):
    return lax.dot_general(left[...], right[...], (((1,), (1,)), ((), ())), preferred_element_type=F32)


def both_halves(tile):
    return tile[:, :AGG] + tile[:, AGG:]


def keep_tile(out, t, tile):
    high = tile.astype(BF16)
    rows = pl.ds(t * AGG, AGG)
    out[rows, :AGG] = high
    out[rows, AGG:] = (tile - high.astype(F32)).astype(BF16)


def blocks_kernel(flags, cond, absorb, block_agg, _, block_label, near, weights, inner, face_label, lift, part, line):
    nx, ny = cond.shape[0], cond.shape[1]
    nb, half, width = nx // 2, ny // 2, LANES // 2
    lane, row = lane_no((half, LANES)), row_no((half, LANES))

    def halves(values, slot):
        part[slot] = values
        return part[slot, pl.ds(0, half, stride=2)], part[slot, pl.ds(1, half, stride=2)]

    def label_at(b):
        values = block_agg[b].astype(F32)
        return jnp.concatenate([values, values], axis=1)

    def upper_x(b, slot):
        x = jnp.maximum(2 * b, 0)
        faces = weight(cond[x + 1], cond[jnp.minimum(x + 2, nx - 1)])
        return jnp.where((b == nb - 1) | (b < 0), 0.0, paired(sum(halves(faces, slot))))

    def step(bs, carry):
        low_x = upper_x(bs[0] - 1, 0)
        for k, b in enumerate(bs):
            x = 2 * b
            slot = 4 * k + 1
            one, two = cond[x], cond[x + 1]
            both_y = weight(one, turned(one, -1, 0)) + weight(two, turned(two, -1, 0))
            both_z = weight(one, turned(one, -1, 1)) + weight(two, turned(two, -1, 1))
            high_x = upper_x(b, slot)
            high_y = jnp.where(row == half - 1, 0.0, paired(halves(both_y, slot + 1)[1]))
            high_z = picked(sum(halves(both_z, slot + 2)), 2 * (lane % width) + 1)
            high_z = jnp.where(lane % width == width - 1, 0.0, high_z)
            low_y, low_z = turned(high_y, 1, 0), turned(high_z, 1, 1)
            own = label_at(b)
            near_x, past_x = label_at(jnp.minimum(b + 1, nb - 1)), label_at(jnp.maximum(b - 1, 0))
            near_y, past_y = turned(own, -1, 0), turned(own, 1, 0)
            near_z, past_z = turned(own, -1, 1), turned(own, 1, 1)
            total = paired(sum(halves(absorb[x] + absorb[x + 1], slot + 3)))
            for beside, values in (
                (near_x, high_x), (past_x, low_x), (near_y, high_y), (past_y, low_y), (near_z, high_z), (past_z, low_z)
            ):
                total = total + jnp.where(beside != own, values, 0.0)
            block_label[b] = pack_rows(own)
            inner[b] = pack_rows(total)
            for d, (beside, values) in enumerate(((near_x, high_x), (near_y, high_y), (near_z, high_z))):
                near[d, b], weights[d, b] = pack_rows(beside), pack_rows(values)
            lift[b] = picked(own, lane // 2).astype(jnp.int32)
            low_x = high_x
        return carry

    batched(0, nb, step, 0, 4)
    line[...] = jnp.zeros(line.shape, F32)
    low, high = jnp.zeros((half, LANES), F32), jnp.zeros((half, LANES), F32)
    for b in range(nb):
        own = label_at(b)
        line[0, b : b + 1], line[1, b : b + 1] = own[:1], own[half - 1 :]
        low = jnp.where(lane == b, own[:, :1], low)
        high = jnp.where(lane == b, own[:, width - 1 : width], high)
    face_label[0], face_label[1] = block_label[0], block_label[nb - 1]
    for s, values in enumerate((line[0], line[1], low, high)):
        face_label[2 + s] = pack_rows(values)


def own_kernel(first, last, total, flags, block_label, near, weights, inner, *refs):
    so_far, refs = (refs[0], refs[1:]) if first else (None, refs)
    refs = refs[1:]
    iota = row_no((AGG, LANES)).astype(F32)

    def step(bs, tile):
        for k, b in enumerate(bs):
            left, right = refs[-4 + 2 * (k % 2) :][:2]
            fill(left, right, block_label, b, [(near.at[d, b], weights.at[d, b]) for d in range(3)])
            tile = tile + product(left, right)
        return tile

    tile = so_far[...] if first else jnp.zeros((AGG, 2 * AGG), F32)
    tile = batched(first, last, step, tile, 2)
    if last < total:
        refs[0][...] = tile
        return
    out, inner_diag = refs[:2]
    tile = both_halves(tile)
    keep_tile(out, 0, jnp.where(row_no((AGG, AGG)) == lane_no((AGG, AGG)), 0.0, tile + tile.T))

    def gather(b, around):
        for r in range(SUB):
            around = around + jnp.where(block_label[b, r : r + 1] == iota, inner[b, r : r + 1], 0.0)
        return around

    inner_diag[...] = lane_total(lax.fori_loop(0, total, gather, jnp.zeros((AGG, LANES), F32)))


def faces_kernel(count, flags, own, face_label, face_near, face_weight, out, *factors):
    out[:AGG] = own[...]
    s = jnp.where(flags[IX] == 0, 1, 0)
    faces = ([s] if count == 2 else [0, 1]) + [2, 3, 4, 5]
    for t, s in enumerate(faces):
        left, right = factors[2 * (t % 2) :][:2]
        fill(left, right, face_near, s, [(face_label.at[s], face_weight.at[s])])
        keep_tile(out, t + 1, both_halves(product(left, right)))


def turn_kernel(flags, tiles, scaled_rhs, scale, own, *refs):
    forth, back, *others, out = refs
    vectors = [own[...]] + [ref[...] for ref in others] + [*sides(flags, forth[...], back[...])]
    row = row_no((SUB, AGG))
    parts = []
    for v in vectors:
        high = v.astype(BF16).astype(F32)
        parts.append(jnp.where(row == 0, high, jnp.where(row == 1, v - high, 0.0)).astype(BF16))
    got = jnp.dot(jnp.concatenate(parts, axis=1), tiles[...], preferred_element_type=F32)
    applied = jnp.sum(got[:, :AGG] + got[:, AGG:], axis=0, keepdims=True)
    out[...] = (1.0 - OMEGA_COARSE) * own[...] + scaled_rhs[...] + scale[...] * applied


def lifted(pre, lift, table, out, bs, at):
    half = pre.shape[1] // 2
    for n, b in enumerate(bs):
        values = picked(table, lift[b])
        for a in range(2):
            for c in range(2):
                rows = pl.ds(c, half, stride=2)
                out[at + 2 * n + a, rows] = pre[2 * b + a, rows] + values


def send_kernel(count, flags, pre, lift, coarse, *outs):
    nb, half = pre.shape[0] // 2, pre.shape[1] // 2
    table = jnp.broadcast_to(coarse[:1], (half, LANES))
    for s, out in enumerate(outs):
        if count == 2:
            b = jnp.where(flags[IX] == 0, nb - HALO // 2, 0)
        else:
            b = (nb - HALO // 2, 0)[s]
        lifted(pre, lift, table, out, [b + h for h in range(HALO // 2)], 0)


def correct_kernel(flags, pre, lift, coarse, out):
    table = jnp.broadcast_to(coarse[:1], (pre.shape[1] // 2, LANES))

    def step(bs, carry):
        lifted(pre, lift, table, out, bs, 2 * bs[0])
        return carry

    batched(0, pre.shape[0] // 2, step, 0)


def post_kernel(flags, wide_ref, forth, back, *refs):
    (wx, wy, wz, inv_diag, start), ends = refs[:5], refs[5:11]
    out, one, two, one_ends, two_ends = refs[11:]
    nx, ny = out.shape[0], out.shape[1]
    frame = Frame(nx, ny)
    wide, tall, span = frame.wide, frame.tall, frame.span
    ex, ey, ez_up, ez_low, inv_ends, start_ends = ends
    for ref in (one, two, one_ends, two_ends):
        clear_spares(ref, frame)
    below, above = sides(flags, forth[...], back[...])
    two_ends[0, span], two_ends[1, span] = below, above
    kept = 1.0 - OMEGA_FINE
    buffers = ((wide_ref.at[0], two_ends), (one, one_ends), (two, two_ends), (one, one_ends))
    for s in range(POST):
        src, src_ends = buffers[s]
        join = joined(ez_up[0, span] * src_ends[0, span], ez_low[1, span] * src_ends[1, span])
        final = s == POST - 1
        dst, dst_ends = (None, None) if final else buffers[s + 1]

        def step(xs, edges, src=src, join=join, dst=dst, final=final):
            news = []
            for x in xs:
                here = src[x, span]
                total = main_sum(frame, src, x, join, wx, wy, wz)
                news.append(kept * here + start[x, span] + inv_diag[x, span] * total)
                if not final:
                    edges = edge_step(here, x, edges)
            for x, new in zip(xs, news):
                if final:
                    out[x - HALO] = new[HALO : HALO + ny]
                else:
                    dst[x, span] = new
            return edges

        edges = batched(s + 1, wide - s - 1, step, jnp.zeros((tall, LANES), F32))
        if not final:
            near = ends_near(src_ends[0, span], src_ends[1, span], edges)
            news = []
            for e in range(2):
                total = ends_sum(frame, src_ends, e, near[2 * e], near[2 * e + 1], ex, ey, ez_up, ez_low)
                news.append(kept * src_ends[e, span] + start_ends[e, span] + inv_ends[e, span] * total)
            dst_ends[0, span], dst_ends[1, span] = news


def body(links, right_side, conductance, absorption, block_agg):
    nx, ny, nz = right_side.shape
    frame = Frame(nx, ny)
    nb = nx // 2
    ix, iy, iz = (lax.axis_index(a) for a in ("gx", "gy", "gz"))
    n_x, n_y, n_z = links.sizes
    flags = jnp.stack(
        [ix, iy % 2, ix > 0, ix < n_x - 1, iy > 0, iy < n_y - 1, iz > 0, iz < n_z - 1]
    ).astype(jnp.int32)
    arrays = (conductance, right_side, absorption, block_agg)
    n_send = 1 if n_x == 2 else 2
    pinned = [pltpu.with_memory_space_constraint(a, pltpu.HBM) for a in arrays]
    hbm = pl.BlockSpec(memory_space=pltpu.HBM)
    x_sends = call(
        functools.partial(pack_x_kernel, n_x, WIDTHS),
        [shaped(sum(WIDTHS) + 1, ny, nz)] * n_send,
        [pltpu.VMEM((n_send, ny // 2, nz // 2), jnp.int32), pltpu.SemaphoreType.DMA((n_send * 4,))],
        in_specs=[hbm] * 4,
    )(flags, *pinned)
    arrays = call(
        load_kernel,
        [jax.ShapeDtypeStruct(a.shape, a.dtype) for a in arrays],
        [pltpu.SemaphoreType.DMA((4,))],
        in_specs=[hbm] * 4 + [VMEM],
    )(flags, *pinned, x_sends[0])
    blocks = (nb, SUB, LANES)
    outs = [shaped(*blocks), shaped(3, *blocks), shaped(3, *blocks), shaped(*blocks), shaped(6, SUB, LANES)]
    outs += [jax.ShapeDtypeStruct((nb, ny // 2, LANES), jnp.int32)]
    scratch = [pltpu.VMEM((17, ny, LANES), F32), pltpu.VMEM((2, ny // 2, LANES), F32)]
    pair = [pltpu.VMEM((AGG, SUB * LANES), BF16), pltpu.VMEM((2 * AGG, SUB * LANES), BF16)]
    *rows, face_label, lift = call(blocks_kernel, outs, scratch)(flags, arrays[0], arrays[2], arrays[3], x_sends[0])
    block_label = rows[0]
    bounds = (0, nb // 6, nb * 7 // 12, nb)
    parts = []

    def own_part(p, sent):
        outs = [shaped(AGG, 2 * AGG)]
        if p == 2:
            outs = [jax.ShapeDtypeStruct((AGG, 2 * AGG), BF16), shaped(SUB, AGG)]
        kernel = functools.partial(own_kernel, bounds[p], bounds[p + 1], nb)
        parts.append(call(kernel, outs, pair * 2)(flags, *rows, *(parts[-1] if p else ()), sent))
        return parts[-1]

    first = own_part(0, x_sends[0])
    from_x = links.x(x_sends)
    from_x = lax.optimization_barrier((*from_x, *first))[:-1]
    fields = []

    def beside_z(wide, sent):
        fields.extend(
            call(fields_kernel, [shaped(*frame.main)] * 4 + [shaped(frame.tall, nz)], limit=24)(flags, wide, sent)
        )
        own_part(2, sent)

    halo, from_y = widened(links, flags, WIDTHS, arrays, from_x, lambda sent: own_part(1, sent), beside_z)
    own_tile, inner_diag = parts[-1]
    outs = [shaped(*frame.main)] * 2 + [shaped(*frame.ends)] * 6 + [shaped(nx, ny, nz)]
    outs += [shaped(6, SUB, LANES)] * 2 + [shaped(SUB, AGG)] * 2
    scratch = [pltpu.VMEM(frame.main, F32), pltpu.VMEM(frame.ends, F32), pltpu.VMEM((nx, frame.rows, LANES), F32)]
    scratch += [pltpu.VMEM(frame.main, F32), pltpu.VMEM(blocks, F32)]
    got = call(fine_kernel, outs, scratch, limit=28)(
        flags, *halo, from_x[0], from_x[-1], *from_y, *fields, block_label, face_label, inner_diag
    )
    fields, pre = (*fields[:3], *got[:8]), got[8]
    face_near, face_weight, scaled_rhs, scale = got[9:]
    tiles = call(
        functools.partial(faces_kernel, n_x),
        jax.ShapeDtypeStruct(((n_send + 5) * AGG, 2 * AGG), BF16),
        pair * 2,
    )(flags, own_tile, face_label, face_near, face_weight)
    coarse = scaled_rhs
    for _ in range(KC - 1):
        coarse = call(turn_kernel, shaped(SUB, AGG))(flags, tiles, scaled_rhs, scale, coarse, *links.near(coarse))
    x_sends = call(functools.partial(send_kernel, n_x), [shaped(HALO, ny, nz)] * n_send)(flags, pre, lift, coarse)
    from_x = links.x(x_sends)
    corrected = call(correct_kernel, shaped(nx, ny, nz))(flags, pre, lift, coarse)
    halo, _ = widened(links, flags, (HALO,), (corrected,), from_x)
    scratch = [pltpu.VMEM(frame.main, F32)] * 2 + [pltpu.VMEM(frame.ends, F32)] * 2
    return call(post_kernel, shaped(nx, ny, nz), scratch, limit=24)(flags, *halo, *fields)


def solution(mesh):
    spec = P("gx", "gy", "gz")
    return jax.shard_map(
        functools.partial(body, Links(mesh)), mesh=mesh, in_specs=(spec,) * 4, out_specs=spec, check_vma=False
    )
```

```python
import functools

import jax
import jax.numpy as jnp
from jax import lax
from jax.experimental import pallas as pl
from jax.experimental.pallas import tpu as pltpu
from jax.sharding import PartitionSpec as P

AGG = 128
LANES = 128
SUB = 8
HALO = 4
WIDTHS = (4, 3, 3)
POST = 4
KC = 8
OMEGA_FINE = 0.8
OMEGA_COARSE = 0.7
F32 = jnp.float32
BF16 = jnp.bfloat16
VMEM = pl.BlockSpec(memory_space=pltpu.VMEM)
IX, PARITY, X_LOW, X_HIGH, Y_LOW, Y_HIGH, Z_LOW, Z_HIGH = range(8)


def places():
    (ix, n_x), (iy, n_y), (iz, n_z) = ((lax.axis_index(a), lax.axis_size(a)) for a in ("gx", "gy", "gz"))
    flags = [ix, iy % 2, ix > 0, ix < n_x - 1, iy > 0, iy < n_y - 1, iz > 0, iz < n_z - 1]
    return [jnp.asarray(flag, jnp.int32) for flag in flags]


def call(kernel, outs, scratch=(), limit=16, flops=10**6, in_specs=None, aliases=None):
    def placed(*refs):
        kernel(places(), *refs)

    def run(*arrays):
        return pl.pallas_call(
            placed,
            out_shape=outs,
            in_specs=in_specs or [VMEM] * len(arrays),
            out_specs=jax.tree.map(lambda _: VMEM, outs),
            scratch_shapes=list(scratch),
            input_output_aliases=aliases or {},
            compiler_params=pltpu.CompilerParams(vmem_limit_bytes=limit * 2**20),
            cost_estimate=pl.CostEstimate(flops=flops, bytes_accessed=10**5, transcendentals=0),
        )(*arrays)

    return run


def shaped(*shape):
    return jax.ShapeDtypeStruct(shape, F32)


def lane_no(shape):
    return lax.broadcasted_iota(jnp.int32, shape, len(shape) - 1)


def row_no(shape):
    return lax.broadcasted_iota(jnp.int32, shape, len(shape) - 2)


def turned(values, shift, axis):
    if isinstance(shift, int):
        shift = shift % values.shape[axis]
        if shift == 0:
            return values
    return pltpu.roll(values, shift, axis)


def batched(low, high, step, carry, size=6):
    def some(i, carry):
        return step([low + i * size + k for k in range(size)], carry)

    carry = lax.fori_loop(0, (high - low) // size, some, carry)
    rest = (high - low) % size
    return step(list(range(high - rest, high)), carry) if rest else carry


def picked(values, index):
    return jnp.take_along_axis(values, index, axis=1, mode="promise_in_bounds")


class Frame:
    def __init__(self, nx, ny):
        self.nx, self.ny = nx, ny
        self.wide, self.tall = nx + 2 * HALO, ny + 2 * HALO
        self.rows = self.tall + 2 * SUB
        self.span = pl.ds(SUB, self.tall)
        self.own = SUB + HALO
        self.main = (self.wide, self.rows, LANES)
        self.ends = (2, self.rows, LANES)


def bases(widths):
    return [sum(widths[:f]) for f in range(len(widths) + 1)]


def copied(pairs, sems):
    copies = [pltpu.make_async_copy(src, dst, sems.at[n]) for n, (src, dst) in enumerate(pairs)]
    for copy in copies:
        copy.start()
    return copies


def pack_x_kernel(count, widths, flags, *refs):
    fields = len(widths)
    ins, outs = refs[: fields + 1], refs[fields + 1 : -2]
    near, sems = refs[-2:]
    nx, ny = ins[0].shape[0], ins[0].shape[1]
    base = bases(widths)
    pairs = []
    for s, out in enumerate(outs):

        def place(size, width, s=s):
            if count == 2:
                return jnp.where(flags[IX] == 0, size - width, 0)
            return (size - width, 0)[s]

        for f, (ref, width) in enumerate(zip(ins, widths)):
            pairs.append((ref.at[pl.ds(place(nx, width), width)], out.at[pl.ds(base[f], width)]))
        pairs.append((ins[-1].at[place(nx // 2, 1)], near.at[s]))
    copies = copied(pairs, sems)
    for out in outs:
        out[base[-1]] = jnp.zeros(out.shape[1:], F32)
    for copy in copies:
        copy.wait()
    for s, out in enumerate(outs):
        out[base[-1], : ny // 2, : near.shape[2]] = near[s].astype(F32)


def load_kernel(flags, *refs):
    count = (len(refs) - 2) // 2
    for copy in copied(list(zip(refs[:count], refs[count + 1 : -1])), refs[-1]):
        copy.wait()


def slab_of(own, low, high, base, width, x):
    nx = own.shape[0]
    if HALO <= x < HALO + nx:
        return own[x - HALO]
    if x < HALO:
        at = x - (HALO - width)
        return low[base + at] if at >= 0 else None
    at = x - HALO - nx
    return high[base + at] if at < width else None


def pack_y_kernel(widths, labels, flags, *refs):
    fields = len(widths)
    ins = refs[:fields]
    low, high = refs[fields + labels : fields + labels + 2]
    inner, outer = refs[fields + labels + 2 :]
    nx, ny = ins[0].shape[0], ins[0].shape[1]
    frame = Frame(nx, ny)
    base = bases(widths)
    even = flags[PARITY] == 0

    def send(at, count, to_high, to_low):
        inner[at : at + count] = jnp.where(even, to_high, to_low)
        outer[at : at + count] = jnp.where(even, to_low, to_high)

    for f in range(fields):
        for x in range(frame.wide):
            slab = slab_of(ins[f], low, high, base[f], widths[f], x)
            at = (f * frame.wide + x) * HALO
            if slab is None:
                slab = jnp.ones((ny, LANES), F32)
            send(at, HALO, slab[ny - HALO :], slab[:HALO])
    if labels:
        at = fields * frame.wide * HALO
        nb, rows, width = refs[fields].shape
        for out in (inner, outer):
            out[at:] = jnp.zeros((out.shape[0] - at, LANES), F32)
        for b in range(nb):
            high, low = (refs[fields][b, row : row + 1].astype(F32) for row in (rows - 1, 0))
            inner[at + b : at + b + 1, :width] = jnp.where(even, high, low)
            outer[at + b : at + b + 1, :width] = jnp.where(even, low, high)


def packed_lanes(wide_ref, f, frame, rows, to_high, to_low):
    group = lane_no((1, LANES)) // HALO
    nothing = jnp.ones((rows.size, LANES), F32)
    high, low = nothing, nothing
    for x in range(frame.wide):
        moved = turned(wide_ref[f, x, rows], HALO * (x + 1), 1)
        high = jnp.where(group == x, moved, high)
        low = jnp.where(group == (x + 1) % frame.wide, moved, low)
    at = pl.ds(f * frame.tall + rows.start - SUB, rows.size)
    to_high[at] = high
    to_low[at] = turned(low, -HALO, 1)


def frame_kernel(widths, labels, flags, *refs):
    fields = len(widths)
    ins = refs[:fields]
    x_low, x_high, _ = refs[fields : fields + 3]
    wide_ref, to_high, to_low = refs[fields + 3 :]
    nx, ny = ins[0].shape[0], ins[0].shape[1]
    frame = Frame(nx, ny)
    base = bases(widths)
    tall, own = frame.tall, frame.own
    spare = jnp.ones((SUB, LANES), F32)
    for f in range(fields):
        for x in range(frame.wide):
            slab = slab_of(ins[f], x_low, x_high, base[f], widths[f], x)
            wide_ref[f, x, own : own + ny] = jnp.ones((ny, LANES), F32) if slab is None else slab
            wide_ref[f, x, :SUB] = spare
            wide_ref[f, x, SUB + tall :] = spare
        packed_lanes(wide_ref, f, frame, pl.ds(2 * SUB, tall - 2 * SUB), to_high, to_low)


def pack_z_kernel(widths, labels, flags, wide_in, high_in, low_in, inner, outer, *refs):
    fields = len(widths)
    wide_ref, send_forth, send_back, to_high, to_low = refs[labels:]
    frame = Frame(wide_ref.shape[1] - 2 * HALO, wide_ref.shape[2] - 2 * (SUB + HALO))
    ny, tall, own = frame.ny, frame.tall, frame.own
    even = flags[PARITY] == 0
    for f in range(fields):
        for x in range(frame.wide):
            at = (f * frame.wide + x) * HALO
            low, high = sides(flags, outer[at : at + HALO], inner[at : at + HALO])
            wide_ref[f, x, SUB:own] = low
            wide_ref[f, x, own + ny : own + ny + HALO] = high
    size = fields * tall
    to_high[...], to_low[...] = high_in[...], low_in[...]
    for f in range(fields):
        for start in (SUB, tall):
            packed_lanes(wide_ref, f, frame, pl.ds(start, SUB), to_high, to_low)
    high, low = to_high[...], to_low[...]
    send_forth[:size], send_back[:size] = jnp.where(even, high, low), jnp.where(even, low, high)
    if labels:
        nb, rows, width = refs[0].shape
        lane = lane_no((rows, LANES))
        high = low = jnp.zeros((rows, LANES), F32)
        for b in range(nb):
            slab = refs[0][b].astype(F32)
            high = jnp.where(lane == b, slab[:, width - 1 :], high)
            low = jnp.where(lane == b, slab[:, :1], low)
        send_forth[size:], send_back[size:] = jnp.where(even, high, low), jnp.where(even, low, high)


class Links:
    def __init__(self, mesh):
        self.sizes = [mesh.shape[a] for a in ("gx", "gy", "gz")]
        n_x, n_y, n_z = self.sizes

        def at(i, j, k):
            return (i * n_y + j) * n_z + k

        self.ring_x = [(i, (i + 1) % n_x) for i in range(n_x)]
        self.inner, self.outer, self.snake = [], [], []
        for i in range(n_x):
            for j in range(n_y):
                for k in range(n_z):
                    self.inner.append((at(i, j, k), at(i, j ^ 1, k)))
                    over = (i, j + 1) if j % 2 else (i, j - 1)
                    over = over if 0 <= over[1] < n_y else (i ^ 1, j)
                    self.outer.append((at(i, j, k), at(*over, k)))
            for j in range(0, n_y, 2):
                nodes = [at(i, j, k) for k in range(n_z)] + [at(i, j + 1, k) for k in reversed(range(n_z))]
                self.snake += [(nodes[m], nodes[(m + 1) % len(nodes)]) for m in range(len(nodes))]

    @staticmethod
    def back(pairs):
        return [(b, a) for a, b in pairs]

    @staticmethod
    def send(values, pairs):
        return lax.ppermute(values, ("gx", "gy", "gz"), pairs)

    def x(self, sends):
        if self.sizes[0] == 2:
            return (lax.ppermute(sends[0], "gx", self.ring_x),)
        return lax.ppermute(sends[0], "gx", self.ring_x), lax.ppermute(sends[1], "gx", self.back(self.ring_x))

    def near(self, values):
        ring = [(j, (j + 1) % self.sizes[1]) for j in range(self.sizes[1])]
        forth, back = self.z(values, values)
        from_x = self.x([values, values])
        low, high = lax.ppermute(values, "gy", ring), lax.ppermute(values, "gy", self.back(ring))
        return (forth, back, *from_x, low, high)

    def y(self, inner, outer):
        return self.send(inner, self.inner), self.send(outer, self.outer)

    def z(self, forth, back):
        return self.send(forth, self.snake), self.send(back, self.back(self.snake))


def widened(links, widths, arrays, from_x, beside_y=None, beside_z=None):
    fields, labels = len(widths), len(arrays) - len(widths)
    nx, ny, nz = arrays[0].shape
    frame = Frame(nx, ny)
    rows = fields * frame.wide * HALO + labels * ny // 2
    sends = call(functools.partial(pack_y_kernel, widths, labels), [shaped(rows, nz)] * 2)(
        *arrays, from_x[0], from_x[-1]
    )
    size = fields * frame.tall
    framed = call(
        functools.partial(frame_kernel, widths, labels), [shaped(fields, *frame.main)] + [shaped(size, nz)] * 2
    )(*arrays[:fields], from_x[0], from_x[-1], sends[0])
    work = beside_y(sends[0]) if beside_y else ()
    from_y = links.y(*sends)
    if work:
        from_y = lax.optimization_barrier((*from_y, *work))[:2]
    rows = size + labels * ny // 2
    wide, *sends = call(
        functools.partial(pack_z_kernel, widths, labels),
        [shaped(fields, *frame.main)] + [shaped(rows, nz)] * 2,
        [pltpu.VMEM((size, nz), F32)] * 2,
        aliases={0: 0},
    )(*framed, *from_y, *arrays[fields:])
    if beside_z:
        beside_z(wide, sends[0])
    return (wide, *links.z(*sends)), from_y


def sides(flags, forth, back):
    even = flags[PARITY] == 0
    return jnp.where(even, forth, back), jnp.where(even, back, forth)


def weight(one, two):
    return 2.0 * (one * two) / (one + two)


def lane_mask(x):
    return ((lane_no((1, LANES)) - (HALO * x + HALO - 1)) & (LANES - 1)) < 2


def edge_step(here, x, edges):
    return jnp.where(lane_mask(x), turned(here, HALO * x + HALO, 1), edges)


def joined(below, above):
    lane = lane_no((1, LANES))
    return jnp.where(lane % HALO == HALO - 1, turned(above, HALO - 1, 1), turned(below, 1, 1))


def at_edges(join, x):
    lane = lane_no((1, LANES))
    return jnp.where((lane == 0) | (lane == LANES - 1), turned(join, (LANES - HALO) - HALO * x, 1), 0.0)


def ends_near(below, above, edges):
    layer = lane_no((1, LANES)) % HALO
    return (
        jnp.where(layer == HALO - 1, turned(edges, -1, 1), turned(below, -1, 1)),
        turned(below, 1, 1),
        turned(above, -1, 1),
        jnp.where(layer == 0, turned(edges, 1 - HALO, 1), turned(above, 1, 1)),
    )


def main_sum(frame, field, x, join, wx, wy, wz):
    span, down = frame.span, pl.ds(SUB - 1, frame.tall)
    here, face_z = field[x, span], wz[x, span]
    total = wx[x, span] * field[x + 1, span] + wx[x - 1, span] * field[x - 1, span]
    total = total + wy[x, span] * field[x, pl.ds(SUB + 1, frame.tall)] + wy[x, down] * field[x, down]
    total = total + face_z * turned(here, -1, 1) + turned(face_z * here, 1, 1)
    return total + at_edges(join, x)


def ends_sum(frame, ends, s, upper, lower, wx, wy, wz_up, wz_low):
    span, down = frame.span, pl.ds(SUB - 1, frame.tall)
    here = ends[s, span]
    total = wx[s, span] * turned(here, -HALO, 1) + turned(wx[s, span] * here, HALO, 1)
    total = total + wy[s, span] * ends[s, pl.ds(SUB + 1, frame.tall)] + wy[s, down] * ends[s, down]
    return total + wz_up[s, span] * upper + wz_low[s, span] * lower


def clear_spares(ref, frame):
    for x in range(ref.shape[0]):
        ref[x, :SUB] = jnp.zeros((SUB, LANES), F32)
        ref[x, SUB + frame.tall :] = jnp.zeros((SUB, LANES), F32)


def pack_rows(values):
    half = values.shape[0] // 2
    lane = lane_no((half, LANES))
    return jnp.where(lane < LANES // 2, values[:half], turned(values[half:], LANES // 2, 1))


def lane_total(values):
    return jnp.broadcast_to(jnp.sum(values.T, axis=0, keepdims=True), (SUB, LANES))


def paired(values):
    even = 2 * (lane_no(values.shape) % (LANES // 2))
    return picked(values + turned(values, -1, 1), even)


def faces_y_kept(flags, frame):
    row = row_no((frame.tall, LANES))
    at_low, at_high = row == HALO - 1, row == HALO + frame.ny - 1
    return jnp.where(at_low, flags[Y_LOW], jnp.where(at_high, flags[Y_HIGH], 1)).astype(F32)


def fields_kernel(flags, wide_ref, _, wx, wy, wz, partial, cond_edges):
    frame = Frame(wx.shape[0] - 2 * HALO, wx.shape[1] - 2 * (SUB + HALO))
    wide, tall, span = frame.wide, frame.tall, frame.span
    last = HALO + frame.nx
    keep_y = faces_y_kept(flags, frame)
    inside = jnp.where(lane_no((1, LANES)) == LANES - 1, 0.0, 1.0)
    clear_spares(wy, frame)

    def fields(xs, carry):
        before, edges = carry
        stores = []
        for x in xs:
            here = wide_ref[0, x, span]
            keep = jnp.where(x == HALO - 1, flags[X_LOW], jnp.where(x == last - 1, flags[X_HIGH], 1)).astype(F32)
            face_x = keep * weight(here, wide_ref[0, jnp.minimum(x + 1, wide - 1), span])
            face_y = keep_y * weight(here, wide_ref[0, x, pl.ds(SUB + 1, tall)])
            face_z = inside * weight(here, turned(here, -1, 1))
            total = wide_ref[2, x, span] + face_x + before + face_y + turned(face_y, 1, 0)
            total = total + face_z + turned(face_z, 1, 1)
            stores.append((x, (face_x, face_y, face_z, total)))
            edges = edge_step(here, x, edges)
            before = face_x
        for x, values in stores:
            for ref, value in zip((wx, wy, wz, partial), values):
                ref[x, span] = value
        return before, edges

    nothing = jnp.zeros((tall, LANES), F32)
    cond_edges[...] = batched(0, wide, fields, (nothing, nothing + 1.0), 4)[1]


def fine_kernel(flags, wide_ref, forth, back, from_x_low, from_x_high, inner, outer, wx, wy, wz, partial, cond_edges,
                block_label, face_label, inner_diag, *refs):
    inv_diag, start = refs[:2]
    ends = refs[2:8]
    pre, face_near, face_weight, scaled_rhs, scale, once, once_ends, res, diag, block_res = refs[8:]
    ex, ey, ez_up, ez_low, inv_ends, start_ends = ends
    nx, ny = pre.shape[0], pre.shape[1]
    frame = Frame(nx, ny)
    wide, tall, span = frame.wide, frame.tall, frame.span
    last = HALO + nx
    got = [sides(flags, forth[f * tall : (f + 1) * tall], back[f * tall : (f + 1) * tall]) for f in range(3)]
    (cond_below, cond_above), rhs_ends, absorb_ends = got
    for ref in (start, once, ey, start_ends, once_ends):
        clear_spares(ref, frame)

    lane = lane_no((1, LANES))
    keep_y = faces_y_kept(flags, frame)
    keep_low, keep_high = flags[Z_LOW].astype(F32), flags[Z_HIGH].astype(F32)
    near = ends_near(cond_below, cond_above, cond_edges[...])
    slab = lane // HALO
    keep_x = jnp.where(
        slab == HALO - 1, flags[X_LOW], jnp.where(slab == last - 1, flags[X_HIGH], 1)
    ).astype(F32)
    layer = lane % HALO
    for s, here in enumerate((cond_below, cond_above)):
        up, low = weight(here, near[2 * s]), weight(here, near[2 * s + 1])
        if s == 0:
            up = up * jnp.where(layer == HALO - 1, keep_low, 1.0)
        else:
            low = low * jnp.where(layer == 0, keep_high, 1.0)
        face_x = keep_x * weight(here, turned(here, -HALO, 1))
        face_y = keep_y * weight(here, turned(here, -1, 0))
        ex[s, span], ey[s, span], ez_up[s, span], ez_low[s, span] = face_x, face_y, up, low
        total = absorb_ends[s] + face_x + turned(face_x, HALO, 1) + face_y + turned(face_y, 1, 0) + up + low
        inverse = OMEGA_FINE / total
        inv_ends[s, span] = inverse
        start_ends[s, span] = inverse * rhs_ends[s]

    end_low, end_high = ez_up[0, span], ez_low[1, span]
    join_faces = joined(end_low, end_high)

    def first_sweep(xs, edges):
        stores = []
        for x in xs:
            total = partial[x, span] + at_edges(join_faces, x)
            inverse = OMEGA_FINE / total
            begin = inverse * wide_ref[1, x, span]
            stores.append((x, (total, inverse, begin)))
            edges = edge_step(begin, x, edges)
        for x, values in stores:
            for ref, value in zip((diag, inv_diag, start), values):
                ref[x, span] = value
        return edges

    edges = batched(0, wide, first_sweep, jnp.zeros((tall, LANES), F32), 4)

    join = joined(end_low * start_ends[0, span], end_high * start_ends[1, span])
    near = ends_near(start_ends[0, span], start_ends[1, span], edges)
    for s in range(2):
        total = ends_sum(frame, start_ends, s, near[2 * s], near[2 * s + 1], ex, ey, ez_up, ez_low)
        once_ends[s, span] = (2.0 - OMEGA_FINE) * start_ends[s, span] + inv_ends[s, span] * total

    def second(xs, carry):
        news = []
        for x in xs:
            total = main_sum(frame, start, x, join, wx, wy, wz)
            news.append((2.0 - OMEGA_FINE) * start[x, span] + inv_diag[x, span] * total)
        for x, new in zip(xs, news):
            once[x, span] = new
        return carry

    batched(HALO - 1, last + 1, second, 0)
    join2 = joined(end_low * once_ends[0, span], end_high * once_ends[1, span])

    def remainder(xs, carry):
        news = []
        for x in xs:
            total = main_sum(frame, once, x, join2, wx, wy, wz)
            news.append(wide_ref[1, x, span] - diag[x, span] * once[x, span] + total)
        for x, new in zip(xs, news):
            res[x - HALO, span] = new
        for x in xs:
            pre[x - HALO] = once[x, pl.ds(frame.own, ny)]
        return carry

    batched(HALO, last, remainder, 0)

    nb, half, width = nx // 2, ny // 2, LANES // 2
    iota = row_no((AGG, LANES)).astype(F32)

    def rows_at(ref, x, off):
        return ref[x, pl.ds(frame.own + off, half, stride=2)]

    def add_rows(total, labels, b, values, c):
        for r in range(SUB):
            total = total + jnp.where(labels[b, r : r + 1] == iota, values[c, r : r + 1], 0.0)
        return total

    def to_blocks(bs, carry):
        for b in bs:
            four = sum(rows_at(res, 2 * b + a, c) for a in range(2) for c in range(2))
            block_res[b] = pack_rows(paired(four))
        return carry

    batched(0, nb, to_blocks, 0)
    zeros = jnp.zeros((AGG, LANES), F32)

    def restrict(b, total):
        return add_rows(total, block_label, b, block_res, b)

    sums = lax.fori_loop(0, nb, restrict, zeros)

    blank = jnp.zeros((half - nb, LANES), F32)
    low_at, high_at = pl.ds(frame.own - 1, 1), pl.ds(frame.own + ny - 1, 1)
    face_weight[0] = pack_rows(paired(rows_at(wx, HALO - 1, 0) + rows_at(wx, HALO - 1, 1)))
    face_weight[1] = pack_rows(paired(rows_at(wx, last - 1, 0) + rows_at(wx, last - 1, 1)))
    for s, at in ((2, low_at), (3, high_at)):
        lines = [wy[HALO + 2 * b, at] + wy[HALO + 2 * b + 1, at] for b in range(nb)]
        face_weight[s] = pack_rows(paired(jnp.concatenate(lines + [blank], axis=0)))
    lane = lane_no((half, LANES))
    for s, (ref, side, layer_at) in ((4, (ez_up, 0, HALO - 1)), (5, (ez_low, 1, 0))):
        values = rows_at(ref, side, 0) + rows_at(ref, side, 1)
        values = values + turned(values, -HALO, 1)
        spot = jnp.minimum(2 * HALO * lane + HALO * HALO + layer_at, LANES - 1)
        face_weight[s] = pack_rows(jnp.where(lane < nb, picked(values, spot), 0.0))
    around = zeros
    for s in range(6):
        around = add_rows(around, face_label, s, face_weight, s)
    scale[...] = OMEGA_COARSE / (inner_diag[...] + lane_total(around))
    scaled_rhs[...] = scale[...] * lane_total(sums)

    at = sum(WIDTHS)
    face_near[0] = pack_rows(from_x_low[at, :half])
    face_near[1] = pack_rows(from_x_high[at, :half])
    at = 3 * wide * HALO
    for s, values in enumerate(sides(flags, outer[at : at + half], inner[at : at + half])):
        face_near[2 + s] = pack_rows(values)
    below, above = sides(flags, forth[3 * tall : 3 * tall + half], back[3 * tall : 3 * tall + half])
    face_near[4] = pack_rows(below)
    face_near[5] = pack_rows(above)


def fill(left, right, labels, b, pairs):
    iota = row_no((AGG, LANES)).astype(F32)
    for r in range(SUB):
        lanes = pl.ds(r * LANES, LANES)
        row = pl.ds(r, 1)
        left[:, lanes] = jnp.where(labels[b, row] == iota, 1.0, 0.0).astype(BF16)
        held = sum(jnp.where(near[row] == iota, w[row], 0.0) for near, w in pairs)
        high = held.astype(BF16)
        right[:AGG, lanes] = high
        right[AGG:, lanes] = (held - high.astype(F32)).astype(BF16)


def product(left, right):
    return lax.dot_general(left[...], right[...], (((1,), (1,)), ((), ())), preferred_element_type=F32)


def both_halves(tile):
    return tile[:, :AGG] + tile[:, AGG:]


def keep_tile(out, t, tile):
    high = tile.astype(BF16)
    rows = pl.ds(t * AGG, AGG)
    out[rows, :AGG] = high
    out[rows, AGG:] = (tile - high.astype(F32)).astype(BF16)


def blocks_kernel(flags, cond, absorb, block_agg, _, block_label, near, weights, inner, face_label, lift, part, line):
    nx, ny = cond.shape[0], cond.shape[1]
    nb, half, width = nx // 2, ny // 2, LANES // 2
    lane, row = lane_no((half, LANES)), row_no((half, LANES))

    def halves(values, slot):
        part[slot] = values
        return part[slot, pl.ds(0, half, stride=2)], part[slot, pl.ds(1, half, stride=2)]

    def label_at(b):
        values = block_agg[b].astype(F32)
        return jnp.concatenate([values, values], axis=1)

    def upper_x(b, slot):
        x = jnp.maximum(2 * b, 0)
        faces = weight(cond[x + 1], cond[jnp.minimum(x + 2, nx - 1)])
        return jnp.where((b == nb - 1) | (b < 0), 0.0, paired(sum(halves(faces, slot))))

    def step(bs, carry):
        low_x = upper_x(bs[0] - 1, 0)
        for k, b in enumerate(bs):
            x = 2 * b
            slot = 4 * k + 1
            one, two = cond[x], cond[x + 1]
            both_y = weight(one, turned(one, -1, 0)) + weight(two, turned(two, -1, 0))
            both_z = weight(one, turned(one, -1, 1)) + weight(two, turned(two, -1, 1))
            high_x = upper_x(b, slot)
            high_y = jnp.where(row == half - 1, 0.0, paired(halves(both_y, slot + 1)[1]))
            high_z = picked(sum(halves(both_z, slot + 2)), 2 * (lane % width) + 1)
            high_z = jnp.where(lane % width == width - 1, 0.0, high_z)
            low_y, low_z = turned(high_y, 1, 0), turned(high_z, 1, 1)
            own = label_at(b)
            near_x, past_x = label_at(jnp.minimum(b + 1, nb - 1)), label_at(jnp.maximum(b - 1, 0))
            near_y, past_y = turned(own, -1, 0), turned(own, 1, 0)
            near_z, past_z = turned(own, -1, 1), turned(own, 1, 1)
            total = paired(sum(halves(absorb[x] + absorb[x + 1], slot + 3)))
            for beside, values in (
                (near_x, high_x), (past_x, low_x), (near_y, high_y), (past_y, low_y), (near_z, high_z), (past_z, low_z)
            ):
                total = total + jnp.where(beside != own, values, 0.0)
            block_label[b] = pack_rows(own)
            inner[b] = pack_rows(total)
            for d, (beside, values) in enumerate(((near_x, high_x), (near_y, high_y), (near_z, high_z))):
                near[d, b], weights[d, b] = pack_rows(beside), pack_rows(values)
            lift[b] = picked(own, lane // 2).astype(jnp.int32)
            low_x = high_x
        return carry

    batched(0, nb, step, 0, 4)
    line[...] = jnp.zeros(line.shape, F32)
    low, high = jnp.zeros((half, LANES), F32), jnp.zeros((half, LANES), F32)
    for b in range(nb):
        own = label_at(b)
        line[0, b : b + 1], line[1, b : b + 1] = own[:1], own[half - 1 :]
        low = jnp.where(lane == b, own[:, :1], low)
        high = jnp.where(lane == b, own[:, width - 1 : width], high)
    face_label[0], face_label[1] = block_label[0], block_label[nb - 1]
    for s, values in enumerate((line[0], line[1], low, high)):
        face_label[2 + s] = pack_rows(values)


def own_kernel(first, last, total, flags, block_label, near, weights, inner, *refs):
    so_far, refs = (refs[0], refs[1:]) if first else (None, refs)
    refs = refs[1:]
    iota = row_no((AGG, LANES)).astype(F32)

    def step(bs, tile):
        for k, b in enumerate(bs):
            left, right = refs[-4 + 2 * (k % 2) :][:2]
            fill(left, right, block_label, b, [(near.at[d, b], weights.at[d, b]) for d in range(3)])
            tile = tile + product(left, right)
        return tile

    tile = so_far[...] if first else jnp.zeros((AGG, 2 * AGG), F32)
    tile = batched(first, last, step, tile, 2)
    if last < total:
        refs[0][...] = tile
        return
    out, inner_diag = refs[:2]
    tile = both_halves(tile)
    keep_tile(out, 0, jnp.where(row_no((AGG, AGG)) == lane_no((AGG, AGG)), 0.0, tile + tile.T))

    def gather(b, around):
        for r in range(SUB):
            around = around + jnp.where(block_label[b, r : r + 1] == iota, inner[b, r : r + 1], 0.0)
        return around

    inner_diag[...] = lane_total(lax.fori_loop(0, total, gather, jnp.zeros((AGG, LANES), F32)))


def faces_kernel(count, flags, own, face_label, face_near, face_weight, out, *factors):
    out[:AGG] = own[...]
    s = jnp.where(flags[IX] == 0, 1, 0)
    faces = ([s] if count == 2 else [0, 1]) + [2, 3, 4, 5]
    for t, s in enumerate(faces):
        left, right = factors[2 * (t % 2) :][:2]
        fill(left, right, face_near, s, [(face_label.at[s], face_weight.at[s])])
        keep_tile(out, t + 1, both_halves(product(left, right)))


def turn_kernel(flags, tiles, scaled_rhs, scale, own, *refs):
    forth, back, *others, out = refs
    vectors = [own[...]] + [ref[...] for ref in others] + [*sides(flags, forth[...], back[...])]
    row = row_no((SUB, AGG))
    parts = []
    for v in vectors:
        high = v.astype(BF16).astype(F32)
        parts.append(jnp.where(row == 0, high, jnp.where(row == 1, v - high, 0.0)).astype(BF16))
    got = jnp.dot(jnp.concatenate(parts, axis=1), tiles[...], preferred_element_type=F32)
    applied = jnp.sum(got[:, :AGG] + got[:, AGG:], axis=0, keepdims=True)
    out[...] = (1.0 - OMEGA_COARSE) * own[...] + scaled_rhs[...] + scale[...] * applied


def lifted(pre, lift, table, out, bs, at):
    half = pre.shape[1] // 2
    for n, b in enumerate(bs):
        values = picked(table, lift[b])
        for a in range(2):
            for c in range(2):
                rows = pl.ds(c, half, stride=2)
                out[at + 2 * n + a, rows] = pre[2 * b + a, rows] + values


def send_kernel(count, flags, pre, lift, coarse, *outs):
    nb, half = pre.shape[0] // 2, pre.shape[1] // 2
    table = jnp.broadcast_to(coarse[:1], (half, LANES))
    for s, out in enumerate(outs):
        if count == 2:
            b = jnp.where(flags[IX] == 0, nb - HALO // 2, 0)
        else:
            b = (nb - HALO // 2, 0)[s]
        lifted(pre, lift, table, out, [b + h for h in range(HALO // 2)], 0)


def correct_kernel(flags, pre, lift, coarse, out):
    table = jnp.broadcast_to(coarse[:1], (pre.shape[1] // 2, LANES))

    def step(bs, carry):
        lifted(pre, lift, table, out, bs, 2 * bs[0])
        return carry

    batched(0, pre.shape[0] // 2, step, 0)


def post_kernel(flags, wide_ref, forth, back, *refs):
    (wx, wy, wz, inv_diag, start), ends = refs[:5], refs[5:11]
    out, one, two, one_ends, two_ends = refs[11:]
    nx, ny = out.shape[0], out.shape[1]
    frame = Frame(nx, ny)
    wide, tall, span = frame.wide, frame.tall, frame.span
    ex, ey, ez_up, ez_low, inv_ends, start_ends = ends
    for ref in (one, two, one_ends, two_ends):
        clear_spares(ref, frame)
    below, above = sides(flags, forth[...], back[...])
    two_ends[0, span], two_ends[1, span] = below, above
    kept = 1.0 - OMEGA_FINE
    buffers = ((wide_ref.at[0], two_ends), (one, one_ends), (two, two_ends), (one, one_ends))
    for s in range(POST):
        src, src_ends = buffers[s]
        join = joined(ez_up[0, span] * src_ends[0, span], ez_low[1, span] * src_ends[1, span])
        final = s == POST - 1
        dst, dst_ends = (None, None) if final else buffers[s + 1]

        def step(xs, edges, src=src, join=join, dst=dst, final=final):
            news = []
            for x in xs:
                here = src[x, span]
                total = main_sum(frame, src, x, join, wx, wy, wz)
                news.append(kept * here + start[x, span] + inv_diag[x, span] * total)
                if not final:
                    edges = edge_step(here, x, edges)
            for x, new in zip(xs, news):
                if final:
                    out[x - HALO] = new[HALO : HALO + ny]
                else:
                    dst[x, span] = new
            return edges

        edges = batched(s + 1, wide - s - 1, step, jnp.zeros((tall, LANES), F32))
        if not final:
            near = ends_near(src_ends[0, span], src_ends[1, span], edges)
            news = []
            for e in range(2):
                total = ends_sum(frame, src_ends, e, near[2 * e], near[2 * e + 1], ex, ey, ez_up, ez_low)
                news.append(kept * src_ends[e, span] + start_ends[e, span] + inv_ends[e, span] * total)
            dst_ends[0, span], dst_ends[1, span] = news


def body(links, right_side, conductance, absorption, block_agg):
    nx, ny, nz = right_side.shape
    frame = Frame(nx, ny)
    nb = nx // 2
    n_x = links.sizes[0]
    arrays = (conductance, right_side, absorption, block_agg)
    n_send = 1 if n_x == 2 else 2
    pinned = [pltpu.with_memory_space_constraint(a, pltpu.HBM) for a in arrays]
    hbm = pl.BlockSpec(memory_space=pltpu.HBM)
    x_sends = call(
        functools.partial(pack_x_kernel, n_x, WIDTHS),
        [shaped(sum(WIDTHS) + 1, ny, nz)] * n_send,
        [pltpu.VMEM((n_send, ny // 2, nz // 2), jnp.int32), pltpu.SemaphoreType.DMA((n_send * 4,))],
        in_specs=[hbm] * 4,
    )(*pinned)
    arrays = call(
        load_kernel,
        [jax.ShapeDtypeStruct(a.shape, a.dtype) for a in arrays],
        [pltpu.SemaphoreType.DMA((4,))],
        in_specs=[hbm] * 4 + [VMEM],
    )(*pinned, x_sends[0])
    blocks = (nb, SUB, LANES)
    outs = [shaped(*blocks), shaped(3, *blocks), shaped(3, *blocks), shaped(*blocks), shaped(6, SUB, LANES)]
    outs += [jax.ShapeDtypeStruct((nb, ny // 2, LANES), jnp.int32)]
    scratch = [pltpu.VMEM((17, ny, LANES), F32), pltpu.VMEM((2, ny // 2, LANES), F32)]
    pair = [pltpu.VMEM((AGG, SUB * LANES), BF16), pltpu.VMEM((2 * AGG, SUB * LANES), BF16)]
    *rows, face_label, lift = call(blocks_kernel, outs, scratch)(arrays[0], arrays[2], arrays[3], x_sends[0])
    block_label = rows[0]
    bounds = (0, nb // 6, nb * 7 // 12, nb)
    parts = []

    def own_part(p, sent):
        outs = [shaped(AGG, 2 * AGG)]
        if p == 2:
            outs = [jax.ShapeDtypeStruct((AGG, 2 * AGG), BF16), shaped(SUB, AGG)]
        kernel = functools.partial(own_kernel, bounds[p], bounds[p + 1], nb)
        parts.append(call(kernel, outs, pair * 2)(*rows, *(parts[-1] if p else ()), sent))
        return parts[-1]

    first = own_part(0, x_sends[0])
    from_x = links.x(x_sends)
    from_x = lax.optimization_barrier((*from_x, *first))[:-1]
    fields = []

    def beside_z(wide, sent):
        fields.extend(
            call(fields_kernel, [shaped(*frame.main)] * 4 + [shaped(frame.tall, nz)], limit=24)(wide, sent)
        )
        own_part(2, sent)

    halo, from_y = widened(links, WIDTHS, arrays, from_x, lambda sent: own_part(1, sent), beside_z)
    own_tile, inner_diag = parts[-1]
    outs = [shaped(*frame.main)] * 2 + [shaped(*frame.ends)] * 6 + [shaped(nx, ny, nz)]
    outs += [shaped(6, SUB, LANES)] * 2 + [shaped(SUB, AGG)] * 2
    scratch = [pltpu.VMEM(frame.main, F32), pltpu.VMEM(frame.ends, F32), pltpu.VMEM((nx, frame.rows, LANES), F32)]
    scratch += [pltpu.VMEM(frame.main, F32), pltpu.VMEM(blocks, F32)]
    got = call(fine_kernel, outs, scratch, limit=28)(
        *halo, from_x[0], from_x[-1], *from_y, *fields, block_label, face_label, inner_diag
    )
    fields, pre = (*fields[:3], *got[:8]), got[8]
    face_near, face_weight, scaled_rhs, scale = got[9:]
    tiles = call(
        functools.partial(faces_kernel, n_x),
        jax.ShapeDtypeStruct(((n_send + 5) * AGG, 2 * AGG), BF16),
        pair * 2,
    )(own_tile, face_label, face_near, face_weight)
    coarse = scaled_rhs
    for _ in range(KC - 1):
        coarse = call(turn_kernel, shaped(SUB, AGG))(tiles, scaled_rhs, scale, coarse, *links.near(coarse))
    x_sends = call(functools.partial(send_kernel, n_x), [shaped(HALO, ny, nz)] * n_send)(pre, lift, coarse)
    from_x = links.x(x_sends)
    corrected = call(correct_kernel, shaped(nx, ny, nz))(pre, lift, coarse)
    halo, _ = widened(links, (HALO,), (corrected,), from_x)
    scratch = [pltpu.VMEM(frame.main, F32)] * 2 + [pltpu.VMEM(frame.ends, F32)] * 2
    return call(post_kernel, shaped(nx, ny, nz), scratch, limit=24)(*halo, *fields)


def solution(mesh):
    spec = P("gx", "gy", "gz")
    return jax.shard_map(
        functools.partial(body, Links(mesh)), mesh=mesh, in_specs=(spec,) * 4, out_specs=spec, check_vma=False
    )
```

```python
import functools
import math

import jax
import jax.numpy as jnp
from jax import lax
from jax.experimental import pallas as pl
from jax.experimental.pallas import tpu as pltpu
from jax.sharding import PartitionSpec as P

AGG = 128
LANES = 128
SUB = 8
HALO = 4
WIDTHS = (4, 3, 3)
POST = 4
KC = 8
OMEGA_FINE = 0.8
OMEGA_COARSE = 0.7
F32 = jnp.float32
BF16 = jnp.bfloat16
VMEM = pl.BlockSpec(memory_space=pltpu.VMEM)
IX, PARITY, X_LOW, X_HIGH, Y_LOW, Y_HIGH, Z_LOW, Z_HIGH = range(8)


def places():
    (ix, n_x), (iy, n_y), (iz, n_z) = ((lax.axis_index(a), lax.axis_size(a)) for a in ("gx", "gy", "gz"))
    flags = [ix, iy % 2, ix > 0, ix < n_x - 1, iy > 0, iy < n_y - 1, iz > 0, iz < n_z - 1]
    return [jnp.asarray(flag, jnp.int32) for flag in flags]


def call(kernel, outs, scratch=(), limit=16, flops=10**6, in_specs=None, aliases=None):
    def placed(*refs):
        kernel(places(), *refs)

    def run(*arrays):
        return pl.pallas_call(
            placed,
            out_shape=outs,
            in_specs=in_specs or [VMEM] * len(arrays),
            out_specs=jax.tree.map(lambda _: VMEM, outs),
            scratch_shapes=list(scratch),
            input_output_aliases=aliases or {},
            compiler_params=pltpu.CompilerParams(vmem_limit_bytes=limit * 2**20),
            cost_estimate=pl.CostEstimate(flops=flops, bytes_accessed=10**5, transcendentals=0),
        )(*arrays)

    return run


def shaped(*shape):
    return jax.ShapeDtypeStruct(shape, F32)


def lane_no(shape):
    return lax.broadcasted_iota(jnp.int32, shape, len(shape) - 1)


def row_no(shape):
    return lax.broadcasted_iota(jnp.int32, shape, len(shape) - 2)


def turned(values, shift, axis):
    if isinstance(shift, int):
        shift = shift % values.shape[axis]
        if shift == 0:
            return values
    return pltpu.roll(values, shift, axis)


def batched(low, high, step, carry, size=6):
    def some(i, carry):
        return step([low + i * size + k for k in range(size)], carry)

    carry = lax.fori_loop(0, (high - low) // size, some, carry)
    rest = (high - low) % size
    return step(list(range(high - rest, high)), carry) if rest else carry


def picked(values, index):
    return jnp.take_along_axis(values, index, axis=1, mode="promise_in_bounds")


class Frame:
    def __init__(self, nx, ny):
        self.nx, self.ny = nx, ny
        self.wide, self.tall = nx + 2 * HALO, ny + 2 * HALO
        self.rows = self.tall + 2 * SUB
        self.span = pl.ds(SUB, self.tall)
        self.own = SUB + HALO
        self.main = (self.wide, self.rows, LANES)
        self.ends = (2, self.rows, LANES)


def bases(widths):
    return [sum(widths[:f]) for f in range(len(widths) + 1)]


def copied(pairs, sems):
    copies = [pltpu.make_async_copy(src, dst, sems.at[n]) for n, (src, dst) in enumerate(pairs)]
    for copy in copies:
        copy.start()
    return copies


def pack_x_kernel(count, widths, flags, *refs):
    fields = len(widths)
    ins, outs = refs[: fields + 1], refs[fields + 1 : -2]
    near, sems = refs[-2:]
    nx, ny = ins[0].shape[0], ins[0].shape[1]
    base = bases(widths)
    pairs = []
    for s, out in enumerate(outs):

        def place(size, width, s=s):
            if count == 2:
                return jnp.where(flags[IX] == 0, size - width, 0)
            return (size - width, 0)[s]

        for f, (ref, width) in enumerate(zip(ins, widths)):
            pairs.append((ref.at[pl.ds(place(nx, width), width)], out.at[pl.ds(base[f], width)]))
        pairs.append((ins[-1].at[place(nx // 2, 1)], near.at[s]))
    copies = copied(pairs, sems)
    for out in outs:
        out[base[-1]] = jnp.zeros(out.shape[1:], F32)
    for copy in copies:
        copy.wait()
    for s, out in enumerate(outs):
        out[base[-1], : ny // 2, : near.shape[2]] = near[s].astype(F32)


def load_kernel(flags, *refs):
    count = (len(refs) - 2) // 2
    for copy in copied(list(zip(refs[:count], refs[count + 1 : -1])), refs[-1]):
        copy.wait()


def slab_of(own, low, high, base, width, x):
    nx = own.shape[0]
    if HALO <= x < HALO + nx:
        return own[x - HALO]
    if x < HALO:
        at = x - (HALO - width)
        return low[base + at] if at >= 0 else None
    at = x - HALO - nx
    return high[base + at] if at < width else None


def pack_y_kernel(widths, labels, ring, flags, *refs):
    fields = len(widths)
    ins = refs[:fields]
    low, high = refs[fields + 1 : fields + 3]
    one, two = refs[fields + 3 :]
    nx, ny = ins[0].shape[0], ins[0].shape[1]
    frame = Frame(nx, ny)
    base = bases(widths)
    even = flags[PARITY] == 0

    def send(at, count, to_high, to_low):
        one[at : at + count] = to_high if ring else jnp.where(even, to_high, to_low)
        two[at : at + count] = to_low if ring else jnp.where(even, to_low, to_high)

    for f in range(fields):
        for x in range(frame.wide):
            slab = slab_of(ins[f], low, high, base[f], widths[f], x)
            at = (f * frame.wide + x) * HALO
            if slab is None:
                slab = jnp.ones((ny, LANES), F32)
            send(at, HALO, slab[ny - HALO :], slab[:HALO])
    at = fields * frame.wide * HALO
    if ring:
        one[at:], two[at:] = refs[fields][...], refs[fields][...]
    if labels:
        nb, rows, width = refs[fields].shape
        for out in (one, two):
            out[at:] = jnp.zeros((out.shape[0] - at, LANES), F32)
        for b in range(nb):
            top, bottom = (refs[fields][b, row : row + 1].astype(F32) for row in (rows - 1, 0))
            one[at + b : at + b + 1, :width] = jnp.where(even, top, bottom)
            two[at + b : at + b + 1, :width] = jnp.where(even, bottom, top)


def packed_lanes(wide_ref, f, frame, rows, to_high, to_low):
    group = lane_no((1, LANES)) // HALO
    nothing = jnp.ones((rows.size, LANES), F32)
    high, low = nothing, nothing
    for x in range(frame.wide):
        moved = turned(wide_ref[f, x, rows], HALO * (x + 1), 1)
        high = jnp.where(group == x, moved, high)
        low = jnp.where(group == (x + 1) % frame.wide, moved, low)
    at = pl.ds(f * frame.tall + rows.start - SUB, rows.size)
    to_high[at] = high
    to_low[at] = turned(low, -HALO, 1)


def frame_kernel(widths, flags, *refs):
    fields = len(widths)
    ins = refs[:fields]
    x_low, x_high, _ = refs[fields : fields + 3]
    wide_ref, to_high, to_low = refs[fields + 3 :]
    nx, ny = ins[0].shape[0], ins[0].shape[1]
    frame = Frame(nx, ny)
    base = bases(widths)
    tall, own = frame.tall, frame.own
    spare = jnp.ones((SUB, LANES), F32)
    for f in range(fields):
        for x in range(frame.wide):
            slab = slab_of(ins[f], x_low, x_high, base[f], widths[f], x)
            wide_ref[f, x, own : own + ny] = jnp.ones((ny, LANES), F32) if slab is None else slab
            wide_ref[f, x, :SUB] = spare
            wide_ref[f, x, SUB + tall :] = spare
        packed_lanes(wide_ref, f, frame, pl.ds(2 * SUB, tall - 2 * SUB), to_high, to_low)


def pack_z_kernel(widths, labels, ring, flags, wide_in, high_in, low_in, from_low, from_high, rider, *refs):
    fields = len(widths)
    wide_ref, send_forth, send_back, to_high, to_low = refs
    frame = Frame(wide_ref.shape[1] - 2 * HALO, wide_ref.shape[2] - 2 * (SUB + HALO))
    ny, tall, own = frame.ny, frame.tall, frame.own
    even = flags[PARITY] == 0
    for f in range(fields):
        for x in range(frame.wide):
            at = (f * frame.wide + x) * HALO
            low, high = from_low[at : at + HALO], from_high[at : at + HALO]
            if not ring:
                low, high = jnp.where(even, high, low), jnp.where(even, low, high)
            wide_ref[f, x, SUB:own] = low
            wide_ref[f, x, own + ny : own + ny + HALO] = high
    size = fields * tall
    to_high[...], to_low[...] = high_in[...], low_in[...]
    for f in range(fields):
        for start in (SUB, tall):
            packed_lanes(wide_ref, f, frame, pl.ds(start, SUB), to_high, to_low)
    high, low = to_high[...], to_low[...]
    send_forth[:size], send_back[:size] = jnp.where(even, high, low), jnp.where(even, low, high)
    if ring:
        send_forth[size:], send_back[size:] = rider[...], rider[...]
    if labels:
        nb, rows, width = rider.shape
        lane = lane_no((rows, LANES))
        high = low = jnp.zeros((rows, LANES), F32)
        for b in range(nb):
            slab = rider[b].astype(F32)
            high = jnp.where(lane == b, slab[:, width - 1 :], high)
            low = jnp.where(lane == b, slab[:, :1], low)
        send_forth[size:], send_back[size:] = jnp.where(even, high, low), jnp.where(even, low, high)


class Links:
    def __init__(self, mesh):
        self.sizes = [mesh.shape[a] for a in ("gx", "gy", "gz")]
        n_x, n_y, n_z = self.sizes

        def at(i, j, k):
            return (i * n_y + j) * n_z + k

        self.ring_x = [(i, (i + 1) % n_x) for i in range(n_x)]
        self.inner, self.outer, self.snake = [], [], []
        for i in range(n_x):
            for j in range(n_y):
                for k in range(n_z):
                    self.inner.append((at(i, j, k), at(i, j ^ 1, k)))
                    over = (i, j + 1) if j % 2 else (i, j - 1)
                    over = over if 0 <= over[1] < n_y else (i ^ 1, j)
                    self.outer.append((at(i, j, k), at(*over, k)))
            for j in range(0, n_y, 2):
                nodes = [at(i, j, k) for k in range(n_z)] + [at(i, j + 1, k) for k in reversed(range(n_z))]
                self.snake += [(nodes[m], nodes[(m + 1) % len(nodes)]) for m in range(len(nodes))]

    @staticmethod
    def back(pairs):
        return [(b, a) for a, b in pairs]

    @staticmethod
    def send(values, pairs):
        return lax.ppermute(values, ("gx", "gy", "gz"), pairs)

    def x(self, sends):
        if self.sizes[0] == 2:
            return (lax.ppermute(sends[0], "gx", self.ring_x),)
        return lax.ppermute(sends[0], "gx", self.ring_x), lax.ppermute(sends[1], "gx", self.back(self.ring_x))

    def near(self, values, x=None, y=None, z=None):
        ring = [(j, (j + 1) % self.sizes[1]) for j in range(self.sizes[1])]
        forth, back = self.z(*(z or (values, values)))
        from_x = self.x(x or (values, values))
        to_high, to_low = y or (values, values)
        low, high = lax.ppermute(to_high, "gy", ring), lax.ppermute(to_low, "gy", self.back(ring))
        return (forth, back, *from_x, low, high)

    def all(self, values):
        total = math.prod(self.sizes)
        copies = jnp.broadcast_to(values, (total, *values.shape))
        return lax.all_to_all(copies, ("gx", "gy", "gz"), 0, 0, tiled=True)

    def y(self, inner, outer):
        return self.send(inner, self.inner), self.send(outer, self.outer)

    def z(self, forth, back):
        return self.send(forth, self.snake), self.send(back, self.back(self.snake))


def send_y(widths, arrays, rider, from_x, ring):
    nx, ny, nz = arrays[0].shape
    rows = len(widths) * Frame(nx, ny).wide * HALO + (SUB if ring else ny // 2)
    kernel = functools.partial(pack_y_kernel, widths, not ring, ring)
    return call(kernel, [shaped(rows, nz)] * 2)(*arrays, rider, from_x[0], from_x[-1])


def framed(widths, arrays, from_x, sent):
    nx, ny, nz = arrays[0].shape
    frame, fields = Frame(nx, ny), len(widths)
    outs = [shaped(fields, *frame.main)] + [shaped(fields * frame.tall, nz)] * 2
    return call(functools.partial(frame_kernel, widths), outs)(*arrays, from_x[0], from_x[-1], sent)


def send_z(widths, frames, from_y, rider, ring):
    wide, high, _ = frames
    rows = high.shape[0] + (SUB if ring else rider.shape[1])
    return call(
        functools.partial(pack_z_kernel, widths, not ring, ring),
        [shaped(*wide.shape)] + [shaped(rows, LANES)] * 2,
        [pltpu.VMEM(high.shape, F32)] * 2,
        aliases={0: 0},
    )(*frames, *from_y, rider)


def sides(flags, forth, back):
    even = flags[PARITY] == 0
    return jnp.where(even, forth, back), jnp.where(even, back, forth)


def weight(one, two):
    return 2.0 * (one * two) / (one + two)


def lane_mask(x):
    return ((lane_no((1, LANES)) - (HALO * x + HALO - 1)) & (LANES - 1)) < 2


def edge_step(here, x, edges):
    return jnp.where(lane_mask(x), turned(here, HALO * x + HALO, 1), edges)


def joined(below, above):
    lane = lane_no((1, LANES))
    return jnp.where(lane % HALO == HALO - 1, turned(above, HALO - 1, 1), turned(below, 1, 1))


def at_edges(join, x):
    lane = lane_no((1, LANES))
    return jnp.where((lane == 0) | (lane == LANES - 1), turned(join, (LANES - HALO) - HALO * x, 1), 0.0)


def ends_near(below, above, edges):
    layer = lane_no((1, LANES)) % HALO
    return (
        jnp.where(layer == HALO - 1, turned(edges, -1, 1), turned(below, -1, 1)),
        turned(below, 1, 1),
        turned(above, -1, 1),
        jnp.where(layer == 0, turned(edges, 1 - HALO, 1), turned(above, 1, 1)),
    )


def main_sum(frame, field, x, join, wx, wy, wz):
    span, down = frame.span, pl.ds(SUB - 1, frame.tall)
    here, face_z = field[x, span], wz[x, span]
    total = wx[x, span] * field[x + 1, span] + wx[x - 1, span] * field[x - 1, span]
    total = total + wy[x, span] * field[x, pl.ds(SUB + 1, frame.tall)] + wy[x, down] * field[x, down]
    total = total + face_z * turned(here, -1, 1) + turned(face_z * here, 1, 1)
    return total + at_edges(join, x)


def ends_sum(frame, ends, s, upper, lower, wx, wy, wz_up, wz_low):
    span, down = frame.span, pl.ds(SUB - 1, frame.tall)
    here = ends[s, span]
    total = wx[s, span] * turned(here, -HALO, 1) + turned(wx[s, span] * here, HALO, 1)
    total = total + wy[s, span] * ends[s, pl.ds(SUB + 1, frame.tall)] + wy[s, down] * ends[s, down]
    return total + wz_up[s, span] * upper + wz_low[s, span] * lower


def clear_spares(ref, frame):
    for x in range(ref.shape[0]):
        ref[x, :SUB] = jnp.zeros((SUB, LANES), F32)
        ref[x, SUB + frame.tall :] = jnp.zeros((SUB, LANES), F32)


def pack_rows(values):
    half = values.shape[0] // 2
    lane = lane_no((half, LANES))
    return jnp.where(lane < LANES // 2, values[:half], turned(values[half:], LANES // 2, 1))


def lane_total(values):
    return jnp.broadcast_to(jnp.sum(values.T, axis=0, keepdims=True), (SUB, LANES))


def paired(values):
    even = 2 * (lane_no(values.shape) % (LANES // 2))
    return picked(values + turned(values, -1, 1), even)


def faces_y_kept(flags, frame):
    row = row_no((frame.tall, LANES))
    at_low, at_high = row == HALO - 1, row == HALO + frame.ny - 1
    return jnp.where(at_low, flags[Y_LOW], jnp.where(at_high, flags[Y_HIGH], 1)).astype(F32)


def fields_kernel(flags, wide_ref, _, wx, wy, wz, partial, cond_edges):
    frame = Frame(wx.shape[0] - 2 * HALO, wx.shape[1] - 2 * (SUB + HALO))
    wide, tall, span = frame.wide, frame.tall, frame.span
    last = HALO + frame.nx
    keep_y = faces_y_kept(flags, frame)
    inside = jnp.where(lane_no((1, LANES)) == LANES - 1, 0.0, 1.0)
    clear_spares(wy, frame)

    def fields(xs, carry):
        before, edges = carry
        stores = []
        for x in xs:
            here = wide_ref[0, x, span]
            keep = jnp.where(x == HALO - 1, flags[X_LOW], jnp.where(x == last - 1, flags[X_HIGH], 1)).astype(F32)
            face_x = keep * weight(here, wide_ref[0, jnp.minimum(x + 1, wide - 1), span])
            face_y = keep_y * weight(here, wide_ref[0, x, pl.ds(SUB + 1, tall)])
            face_z = inside * weight(here, turned(here, -1, 1))
            total = wide_ref[2, x, span] + face_x + before + face_y + turned(face_y, 1, 0)
            total = total + face_z + turned(face_z, 1, 1)
            stores.append((x, (face_x, face_y, face_z, total)))
            edges = edge_step(here, x, edges)
            before = face_x
        for x, values in stores:
            for ref, value in zip((wx, wy, wz, partial), values):
                ref[x, span] = value
        return before, edges

    nothing = jnp.zeros((tall, LANES), F32)
    cond_edges[...] = batched(0, wide, fields, (nothing, nothing + 1.0), 4)[1]


def fine_kernel(flags, wide_ref, forth, back, from_x_low, from_x_high, inner, outer, wx, wy, wz, partial, cond_edges,
                block_label, face_label, inner_diag, *refs):
    inv_diag, start = refs[:2]
    ends = refs[2:8]
    pre, face_near, face_weight, scaled_rhs, scale, once, once_ends, res, diag, block_res = refs[8:]
    ex, ey, ez_up, ez_low, inv_ends, start_ends = ends
    nx, ny = pre.shape[0], pre.shape[1]
    frame = Frame(nx, ny)
    wide, tall, span = frame.wide, frame.tall, frame.span
    last = HALO + nx
    got = [sides(flags, forth[f * tall : (f + 1) * tall], back[f * tall : (f + 1) * tall]) for f in range(3)]
    (cond_below, cond_above), rhs_ends, absorb_ends = got
    for ref in (start, once, ey, start_ends, once_ends):
        clear_spares(ref, frame)

    lane = lane_no((1, LANES))
    keep_y = faces_y_kept(flags, frame)
    keep_low, keep_high = flags[Z_LOW].astype(F32), flags[Z_HIGH].astype(F32)
    near = ends_near(cond_below, cond_above, cond_edges[...])
    slab = lane // HALO
    keep_x = jnp.where(
        slab == HALO - 1, flags[X_LOW], jnp.where(slab == last - 1, flags[X_HIGH], 1)
    ).astype(F32)
    layer = lane % HALO
    for s, here in enumerate((cond_below, cond_above)):
        up, low = weight(here, near[2 * s]), weight(here, near[2 * s + 1])
        if s == 0:
            up = up * jnp.where(layer == HALO - 1, keep_low, 1.0)
        else:
            low = low * jnp.where(layer == 0, keep_high, 1.0)
        face_x = keep_x * weight(here, turned(here, -HALO, 1))
        face_y = keep_y * weight(here, turned(here, -1, 0))
        ex[s, span], ey[s, span], ez_up[s, span], ez_low[s, span] = face_x, face_y, up, low
        total = absorb_ends[s] + face_x + turned(face_x, HALO, 1) + face_y + turned(face_y, 1, 0) + up + low
        inverse = OMEGA_FINE / total
        inv_ends[s, span] = inverse
        start_ends[s, span] = inverse * rhs_ends[s]

    end_low, end_high = ez_up[0, span], ez_low[1, span]
    join_faces = joined(end_low, end_high)

    def first_sweep(xs, edges):
        stores = []
        for x in xs:
            total = partial[x, span] + at_edges(join_faces, x)
            inverse = OMEGA_FINE / total
            begin = inverse * wide_ref[1, x, span]
            stores.append((x, (total, inverse, begin)))
            edges = edge_step(begin, x, edges)
        for x, values in stores:
            for ref, value in zip((diag, inv_diag, start), values):
                ref[x, span] = value
        return edges

    edges = batched(0, wide, first_sweep, jnp.zeros((tall, LANES), F32), 4)

    join = joined(end_low * start_ends[0, span], end_high * start_ends[1, span])
    near = ends_near(start_ends[0, span], start_ends[1, span], edges)
    for s in range(2):
        total = ends_sum(frame, start_ends, s, near[2 * s], near[2 * s + 1], ex, ey, ez_up, ez_low)
        once_ends[s, span] = (2.0 - OMEGA_FINE) * start_ends[s, span] + inv_ends[s, span] * total

    def second(xs, carry):
        news = []
        for x in xs:
            total = main_sum(frame, start, x, join, wx, wy, wz)
            news.append((2.0 - OMEGA_FINE) * start[x, span] + inv_diag[x, span] * total)
        for x, new in zip(xs, news):
            once[x, span] = new
        return carry

    batched(HALO - 1, last + 1, second, 0)
    join2 = joined(end_low * once_ends[0, span], end_high * once_ends[1, span])

    def remainder(xs, carry):
        news = []
        for x in xs:
            total = main_sum(frame, once, x, join2, wx, wy, wz)
            news.append(wide_ref[1, x, span] - diag[x, span] * once[x, span] + total)
        for x, new in zip(xs, news):
            res[x - HALO, span] = new
        for x in xs:
            pre[x - HALO] = once[x, pl.ds(frame.own, ny)]
        return carry

    batched(HALO, last, remainder, 0)

    nb, half, width = nx // 2, ny // 2, LANES // 2
    iota = row_no((AGG, LANES)).astype(F32)

    def rows_at(ref, x, off):
        return ref[x, pl.ds(frame.own + off, half, stride=2)]

    def add_rows(total, labels, b, values, c):
        for r in range(SUB):
            total = total + jnp.where(labels[b, r : r + 1] == iota, values[c, r : r + 1], 0.0)
        return total

    def to_blocks(bs, carry):
        for b in bs:
            four = sum(rows_at(res, 2 * b + a, c) for a in range(2) for c in range(2))
            block_res[b] = pack_rows(paired(four))
        return carry

    batched(0, nb, to_blocks, 0)
    zeros = jnp.zeros((AGG, LANES), F32)

    def restrict(b, total):
        return add_rows(total, block_label, b, block_res, b)

    sums = lax.fori_loop(0, nb, restrict, zeros)

    blank = jnp.zeros((half - nb, LANES), F32)
    low_at, high_at = pl.ds(frame.own - 1, 1), pl.ds(frame.own + ny - 1, 1)
    face_weight[0] = pack_rows(paired(rows_at(wx, HALO - 1, 0) + rows_at(wx, HALO - 1, 1)))
    face_weight[1] = pack_rows(paired(rows_at(wx, last - 1, 0) + rows_at(wx, last - 1, 1)))
    for s, at in ((2, low_at), (3, high_at)):
        lines = [wy[HALO + 2 * b, at] + wy[HALO + 2 * b + 1, at] for b in range(nb)]
        face_weight[s] = pack_rows(paired(jnp.concatenate(lines + [blank], axis=0)))
    lane = lane_no((half, LANES))
    for s, (ref, side, layer_at) in ((4, (ez_up, 0, HALO - 1)), (5, (ez_low, 1, 0))):
        values = rows_at(ref, side, 0) + rows_at(ref, side, 1)
        values = values + turned(values, -HALO, 1)
        spot = jnp.minimum(2 * HALO * lane + HALO * HALO + layer_at, LANES - 1)
        face_weight[s] = pack_rows(jnp.where(lane < nb, picked(values, spot), 0.0))
    around = zeros
    for s in range(6):
        around = add_rows(around, face_label, s, face_weight, s)
    scale[...] = OMEGA_COARSE / (inner_diag[...] + lane_total(around))
    scaled_rhs[...] = scale[...] * lane_total(sums)

    at = sum(WIDTHS)
    face_near[0] = pack_rows(from_x_low[at, :half])
    face_near[1] = pack_rows(from_x_high[at, :half])
    at = 3 * wide * HALO
    for s, values in enumerate(sides(flags, outer[at : at + half], inner[at : at + half])):
        face_near[2 + s] = pack_rows(values)
    below, above = sides(flags, forth[3 * tall : 3 * tall + half], back[3 * tall : 3 * tall + half])
    face_near[4] = pack_rows(below)
    face_near[5] = pack_rows(above)


def fill(left, right, labels, b, pairs):
    iota = row_no((AGG, LANES)).astype(F32)
    for r in range(SUB):
        lanes = pl.ds(r * LANES, LANES)
        row = pl.ds(r, 1)
        left[:, lanes] = jnp.where(labels[b, row] == iota, 1.0, 0.0).astype(BF16)
        held = sum(jnp.where(near[row] == iota, w[row], 0.0) for near, w in pairs)
        high = held.astype(BF16)
        right[:AGG, lanes] = high
        right[AGG:, lanes] = (held - high.astype(F32)).astype(BF16)


def product(left, right):
    return lax.dot_general(left[...], right[...], (((1,), (1,)), ((), ())), preferred_element_type=F32)


def both_halves(tile):
    return tile[:, :AGG] + tile[:, AGG:]


def keep_tile(out, t, tile):
    high = tile.astype(BF16)
    rows = pl.ds(t * AGG, AGG)
    out[rows, :AGG] = high
    out[rows, AGG:] = (tile - high.astype(F32)).astype(BF16)


def blocks_kernel(flags, cond, absorb, block_agg, _, block_label, near, weights, inner, face_label, fine_label,
                  part, line):
    nx, ny = cond.shape[0], cond.shape[1]
    nb, half, width = nx // 2, ny // 2, LANES // 2
    lane, row = lane_no((half, LANES)), row_no((half, LANES))

    def halves(values, slot):
        part[slot] = values
        return part[slot, pl.ds(0, half, stride=2)], part[slot, pl.ds(1, half, stride=2)]

    def label_at(b):
        values = block_agg[b].astype(F32)
        return jnp.concatenate([values, values], axis=1)

    def upper_x(b, slot):
        x = jnp.maximum(2 * b, 0)
        faces = weight(cond[x + 1], cond[jnp.minimum(x + 2, nx - 1)])
        return jnp.where((b == nb - 1) | (b < 0), 0.0, paired(sum(halves(faces, slot))))

    def step(bs, carry):
        low_x = upper_x(bs[0] - 1, 0)
        for k, b in enumerate(bs):
            x = 2 * b
            slot = 4 * k + 1
            one, two = cond[x], cond[x + 1]
            both_y = weight(one, turned(one, -1, 0)) + weight(two, turned(two, -1, 0))
            both_z = weight(one, turned(one, -1, 1)) + weight(two, turned(two, -1, 1))
            high_x = upper_x(b, slot)
            high_y = jnp.where(row == half - 1, 0.0, paired(halves(both_y, slot + 1)[1]))
            high_z = picked(sum(halves(both_z, slot + 2)), 2 * (lane % width) + 1)
            high_z = jnp.where(lane % width == width - 1, 0.0, high_z)
            low_y, low_z = turned(high_y, 1, 0), turned(high_z, 1, 1)
            own = label_at(b)
            near_x, past_x = label_at(jnp.minimum(b + 1, nb - 1)), label_at(jnp.maximum(b - 1, 0))
            near_y, past_y = turned(own, -1, 0), turned(own, 1, 0)
            near_z, past_z = turned(own, -1, 1), turned(own, 1, 1)
            total = paired(sum(halves(absorb[x] + absorb[x + 1], slot + 3)))
            for beside, values in (
                (near_x, high_x), (past_x, low_x), (near_y, high_y), (past_y, low_y), (near_z, high_z), (past_z, low_z)
            ):
                total = total + jnp.where(beside != own, values, 0.0)
            block_label[b] = pack_rows(own)
            inner[b] = pack_rows(total)
            for d, (beside, values) in enumerate(((near_x, high_x), (near_y, high_y), (near_z, high_z))):
                near[d, b], weights[d, b] = pack_rows(beside), pack_rows(values)
            spread = picked(own, lane // 2)
            for a in range(2):
                for c in range(2):
                    fine_label[x + a, pl.ds(c, half, stride=2)] = spread
            low_x = high_x
        return carry

    batched(0, nb, step, 0, 4)
    line[...] = jnp.zeros(line.shape, F32)
    low, high = jnp.zeros((half, LANES), F32), jnp.zeros((half, LANES), F32)
    for b in range(nb):
        own = label_at(b)
        line[0, b : b + 1], line[1, b : b + 1] = own[:1], own[half - 1 :]
        low = jnp.where(lane == b, own[:, :1], low)
        high = jnp.where(lane == b, own[:, width - 1 : width], high)
    face_label[0], face_label[1] = block_label[0], block_label[nb - 1]
    for s, values in enumerate((line[0], line[1], low, high)):
        face_label[2 + s] = pack_rows(values)


def own_kernel(first, last, total, flags, block_label, near, weights, inner, *refs):
    so_far, refs = (refs[0], refs[1:]) if first else (None, refs)
    refs = refs[1:]
    iota = row_no((AGG, LANES)).astype(F32)

    def step(bs, tile):
        for k, b in enumerate(bs):
            left, right = refs[-4 + 2 * (k % 2) :][:2]
            fill(left, right, block_label, b, [(near.at[d, b], weights.at[d, b]) for d in range(3)])
            tile = tile + product(left, right)
        return tile

    tile = so_far[...] if first else jnp.zeros((AGG, 2 * AGG), F32)
    tile = batched(first, last, step, tile, 2)
    if last < total:
        refs[0][...] = tile
        return
    out, inner_diag = refs[:2]
    tile = both_halves(tile)
    keep_tile(out, 0, jnp.where(row_no((AGG, AGG)) == lane_no((AGG, AGG)), 0.0, tile + tile.T))

    def gather(b, around):
        for r in range(SUB):
            around = around + jnp.where(block_label[b, r : r + 1] == iota, inner[b, r : r + 1], 0.0)
        return around

    inner_diag[...] = lane_total(lax.fori_loop(0, total, gather, jnp.zeros((AGG, LANES), F32)))


def faces_kernel(count, flags, own, face_label, face_near, face_weight, out, *factors):
    out[:AGG] = own[...]
    s = jnp.where(flags[IX] == 0, 1, 0)
    faces = ([s] if count == 2 else [0, 1]) + [2, 3, 4, 5]
    for t, s in enumerate(faces):
        left, right = factors[2 * (t % 2) :][:2]
        fill(left, right, face_near, s, [(face_label.at[s], face_weight.at[s])])
        keep_tile(out, t + 1, both_halves(product(left, right)))


def turn_kernel(flags, tiles, scaled_rhs, scale, own, *refs):
    forth, back, *others, out = refs
    got = [ref[ref.shape[0] - 1, :SUB] if len(ref.shape) == 3 else ref[ref.shape[0] - SUB :] for ref in (*others, forth, back)]
    vectors = [own[...], *got[:-2], *sides(flags, *got[-2:])]
    row = row_no((SUB, AGG))
    parts = []
    for v in vectors:
        high = v.astype(BF16).astype(F32)
        parts.append(jnp.where(row == 0, high, jnp.where(row == 1, v - high, 0.0)).astype(BF16))
    got = jnp.dot(jnp.concatenate(parts, axis=1), tiles[...], preferred_element_type=F32)
    applied = jnp.sum(got[:, :AGG] + got[:, AGG:], axis=0, keepdims=True)
    out[...] = (1.0 - OMEGA_COARSE) * own[...] + scaled_rhs[...] + scale[...] * applied


def ride_kernel(count, flags, pre, fine_label, coarse, *outs):
    nx = pre.shape[0]
    for s, out in enumerate(outs):
        at = jnp.where(flags[IX] == 0, nx - HALO, 0) if count == 2 else (nx - HALO, 0)[s]
        for f, field in enumerate((pre, fine_label)):
            for x in range(HALO):
                out[HALO * f + x] = field[at + x]
        out[2 * HALO] = jnp.zeros(out.shape[1:], F32)
        out[2 * HALO, :SUB] = coarse[...]


def lift_kernel(flags, wide_ref, forth, back, main, ends):
    frame = Frame(wide_ref.shape[1] - 2 * HALO, wide_ref.shape[2] - 2 * (SUB + HALO))
    tall = frame.tall
    for b in range(frame.wide // 2):
        main[b] = wide_ref[1, 2 * b, frame.span].astype(jnp.int32)
    rows = pl.ds(tall, tall)
    for s, values in enumerate(sides(flags, forth[rows], back[rows])):
        ends[s] = values.astype(jnp.int32)


def post_kernel(sizes, flags, table, labels, end_labels, wide_ref, forth, back, *refs):
    (wx, wy, wz, inv_diag, start), ends = refs[:5], refs[5:11]
    out, one, two, one_ends, two_ends = refs[11:]
    nx, ny = out.shape[0], out.shape[1]
    frame = Frame(nx, ny)
    wide, tall, span = frame.wide, frame.tall, frame.span
    ex, ey, ez_up, ez_low, inv_ends, start_ends = ends
    for ref in (one, two, one_ends, two_ends):
        clear_spares(ref, frame)
    place = [lax.axis_index(a) for a in ("gx", "gy", "gz")]
    row, lane = row_no((tall, LANES)), lane_no((tall, LANES))

    def table_at(dx, dz):
        tables = []
        for dy in (-1, 0, 1):
            at = [jnp.clip(p + d, 0, n - 1) for p, d, n in zip(place, (dx, dy, dz), sizes)]
            tables.append(table[(at[0] * sizes[1] + at[1]) * sizes[2] + at[2]])
        return jnp.where(row < HALO, tables[0], jnp.where(row < HALO + ny, tables[1], tables[2]))

    for x_from, x_to, dx in ((0, HALO, -1), (HALO, HALO + nx, 0), (HALO + nx, wide, 1)):
        values = table_at(dx, 0)

        def lift(bs, carry, values=values):
            news = [picked(values, labels[b]) for b in bs]
            for b, new in zip(bs, news):
                for a in range(2):
                    two[2 * b + a, span] = wide_ref[0, 2 * b + a, span] + new
            return carry

        batched(x_from // 2, x_to // 2, lift, 0, 4)
    for s, (dz, base) in enumerate(zip((-1, 1), sides(flags, forth[:tall], back[:tall]))):
        below, inside, above = (picked(table_at(dx, dz), end_labels[s]) for dx in (-1, 0, 1))
        spot = lane // HALO
        lifted = jnp.where(spot < HALO, below, jnp.where(spot < HALO + nx, inside, above))
        two_ends[s, span] = base + lifted
    kept = 1.0 - OMEGA_FINE
    buffers = ((two, two_ends), (one, one_ends), (two, two_ends), (one, one_ends))
    for s in range(POST):
        src, src_ends = buffers[s]
        join = joined(ez_up[0, span] * src_ends[0, span], ez_low[1, span] * src_ends[1, span])
        final = s == POST - 1
        dst, dst_ends = (None, None) if final else buffers[s + 1]

        def step(xs, edges, src=src, join=join, dst=dst, final=final):
            news = []
            for x in xs:
                here = src[x, span]
                total = main_sum(frame, src, x, join, wx, wy, wz)
                news.append(kept * here + start[x, span] + inv_diag[x, span] * total)
                if not final:
                    edges = edge_step(here, x, edges)
            for x, new in zip(xs, news):
                if final:
                    out[x - HALO] = new[HALO : HALO + ny]
                else:
                    dst[x, span] = new
            return edges

        edges = batched(s + 1, wide - s - 1, step, jnp.zeros((tall, LANES), F32))
        if not final:
            near = ends_near(src_ends[0, span], src_ends[1, span], edges)
            news = []
            for e in range(2):
                total = ends_sum(frame, src_ends, e, near[2 * e], near[2 * e + 1], ex, ey, ez_up, ez_low)
                news.append(kept * src_ends[e, span] + start_ends[e, span] + inv_ends[e, span] * total)
            dst_ends[0, span], dst_ends[1, span] = news


def body(links, right_side, conductance, absorption, block_agg):
    nx, ny, nz = right_side.shape
    frame = Frame(nx, ny)
    nb = nx // 2
    n_x = links.sizes[0]
    arrays = (conductance, right_side, absorption, block_agg)
    n_send = 1 if n_x == 2 else 2
    pinned = [pltpu.with_memory_space_constraint(a, pltpu.HBM) for a in arrays]
    hbm = pl.BlockSpec(memory_space=pltpu.HBM)
    x_sends = call(
        functools.partial(pack_x_kernel, n_x, WIDTHS),
        [shaped(sum(WIDTHS) + 1, ny, nz)] * n_send,
        [pltpu.VMEM((n_send, ny // 2, nz // 2), jnp.int32), pltpu.SemaphoreType.DMA((n_send * 4,))],
        in_specs=[hbm] * 4,
    )(*pinned)
    arrays = call(
        load_kernel,
        [jax.ShapeDtypeStruct(a.shape, a.dtype) for a in arrays],
        [pltpu.SemaphoreType.DMA((4,))],
        in_specs=[hbm] * 4 + [VMEM],
    )(*pinned, x_sends[0])
    blocks = (nb, SUB, LANES)
    outs = [shaped(*blocks), shaped(3, *blocks), shaped(3, *blocks), shaped(*blocks), shaped(6, SUB, LANES)]
    outs += [shaped(nx, ny, nz)]
    scratch = [pltpu.VMEM((17, ny, LANES), F32), pltpu.VMEM((2, ny // 2, LANES), F32)]
    pair = [pltpu.VMEM((AGG, SUB * LANES), BF16), pltpu.VMEM((2 * AGG, SUB * LANES), BF16)]
    *rows, face_label, fine_label = call(blocks_kernel, outs, scratch)(arrays[0], arrays[2], arrays[3], x_sends[0])
    block_label = rows[0]
    bounds = (0, nb // 4, nb * 5 // 6, nb)
    parts = []

    def own_part(p, sent):
        outs = [shaped(AGG, 2 * AGG)]
        if p == 2:
            outs = [jax.ShapeDtypeStruct((AGG, 2 * AGG), BF16), shaped(SUB, AGG)]
        kernel = functools.partial(own_kernel, bounds[p], bounds[p + 1], nb)
        parts.append(call(kernel, outs, pair * 2)(*rows, *(parts[-1] if p else ()), sent))
        return parts[-1]

    first = own_part(0, x_sends[0])
    from_x = links.x(x_sends)
    from_x = lax.optimization_barrier((*from_x, *first))[:-1]

    sends = send_y(WIDTHS, arrays[:3], arrays[3], from_x, False)
    frames = framed(WIDTHS, arrays[:3], from_x, sends[0])
    second = own_part(1, sends[0])
    from_y = links.y(*sends)
    from_y = lax.optimization_barrier((*from_y, *second))[:2]
    wide, *sends = send_z(WIDTHS, frames, from_y, arrays[3], False)
    fields = call(fields_kernel, [shaped(*frame.main)] * 4 + [shaped(frame.tall, nz)], limit=24)(wide, sends[0])
    own_tile, inner_diag = own_part(2, sends[0])
    halo = (wide, *links.z(*sends))
    outs = [shaped(*frame.main)] * 2 + [shaped(*frame.ends)] * 6 + [shaped(nx, ny, nz)]
    outs += [shaped(6, SUB, LANES)] * 2 + [shaped(SUB, AGG)] * 2
    scratch = [pltpu.VMEM(frame.main, F32), pltpu.VMEM(frame.ends, F32), pltpu.VMEM((nx, frame.rows, LANES), F32)]
    scratch += [pltpu.VMEM(frame.main, F32), pltpu.VMEM(blocks, F32)]
    got = call(fine_kernel, outs, scratch, limit=28)(
        *halo, from_x[0], from_x[-1], *from_y, *fields, block_label, face_label, inner_diag
    )
    fields, pre = (*fields[:3], *got[:8]), got[8]
    face_near, face_weight, scaled_rhs, scale = got[9:]
    tiles = call(
        functools.partial(faces_kernel, n_x),
        jax.ShapeDtypeStruct(((n_send + 5) * AGG, 2 * AGG), BF16),
        pair * 2,
    )(own_tile, face_label, face_near, face_weight)
    coarse = scaled_rhs

    def turn(**more):
        near = links.near(coarse, **more)
        return call(turn_kernel, shaped(SUB, AGG))(tiles, scaled_rhs, scale, coarse, *near), near

    widths, both = (HALO, HALO), (pre, fine_label)
    rides = call(functools.partial(ride_kernel, n_x), [shaped(2 * HALO + 1, ny, nz)] * n_send)(*both, coarse)
    coarse, near = turn(x=rides)
    from_x = near[2:-2]
    rides = send_y(widths, both, coarse, from_x, True)
    frames = framed(widths, both, from_x, rides[0])
    coarse, near = turn(y=rides)
    wide, *rides = send_z(widths, frames, near[-2:], coarse, True)
    coarse, near = turn(z=rides)
    halo = (wide, *near[:2])
    outs = [jax.ShapeDtypeStruct((frame.wide // 2, frame.tall, nz), jnp.int32)]
    outs += [jax.ShapeDtypeStruct((2, frame.tall, nz), jnp.int32)]
    lifts = call(lift_kernel, outs)(*halo)
    for _ in range(KC - 4):
        coarse, _ = turn()
    table = links.all(coarse[:1])
    scratch = [pltpu.VMEM(frame.main, F32)] * 2 + [pltpu.VMEM(frame.ends, F32)] * 2
    kernel = functools.partial(post_kernel, links.sizes)
    return call(kernel, shaped(nx, ny, nz), scratch, limit=24)(table, *lifts, *halo, *fields)


def solution(mesh):
    spec = P("gx", "gy", "gz")
    return jax.shard_map(
        functools.partial(body, Links(mesh)), mesh=mesh, in_specs=(spec,) * 4, out_specs=spec, check_vma=False
    )
```

```python
import functools

import jax
import jax.numpy as jnp
from jax import lax
from jax.experimental import pallas as pl
from jax.experimental.pallas import tpu as pltpu
from jax.sharding import PartitionSpec as P

AGG = 128
LANES = 128
SUB = 8
HALO = 4
WIDTHS = (4, 3, 3)
POST = 4
KC = 8
OMEGA_FINE = 0.8
OMEGA_COARSE = 0.7
F32 = jnp.float32
BF16 = jnp.bfloat16
VMEM = pl.BlockSpec(memory_space=pltpu.VMEM)
IX, PARITY, X_LOW, X_HIGH, Y_LOW, Y_HIGH, Z_LOW, Z_HIGH = range(8)


def places():
    (ix, n_x), (iy, n_y), (iz, n_z) = ((lax.axis_index(a), lax.axis_size(a)) for a in ("gx", "gy", "gz"))
    flags = [ix, iy % 2, ix > 0, ix < n_x - 1, iy > 0, iy < n_y - 1, iz > 0, iz < n_z - 1]
    return [jnp.asarray(flag, jnp.int32) for flag in flags]


def call(kernel, outs, scratch=(), limit=16, flops=10**6, in_specs=None, aliases=None):
    def placed(*refs):
        kernel(places(), *refs)

    def run(*arrays):
        return pl.pallas_call(
            placed,
            out_shape=outs,
            in_specs=in_specs or [VMEM] * len(arrays),
            out_specs=jax.tree.map(lambda _: VMEM, outs),
            scratch_shapes=list(scratch),
            input_output_aliases=aliases or {},
            compiler_params=pltpu.CompilerParams(vmem_limit_bytes=limit * 2**20),
            cost_estimate=pl.CostEstimate(flops=flops, bytes_accessed=10**5, transcendentals=0),
        )(*arrays)

    return run


def shaped(*shape):
    return jax.ShapeDtypeStruct(shape, F32)


def lane_no(shape):
    return lax.broadcasted_iota(jnp.int32, shape, len(shape) - 1)


def row_no(shape):
    return lax.broadcasted_iota(jnp.int32, shape, len(shape) - 2)


def turned(values, shift, axis):
    if isinstance(shift, int):
        shift = shift % values.shape[axis]
        if shift == 0:
            return values
    return pltpu.roll(values, shift, axis)


def batched(low, high, step, carry, size=6):
    def some(i, carry):
        return step([low + i * size + k for k in range(size)], carry)

    carry = lax.fori_loop(0, (high - low) // size, some, carry)
    rest = (high - low) % size
    return step(list(range(high - rest, high)), carry) if rest else carry


def picked(values, index):
    return jnp.take_along_axis(values, index, axis=1, mode="promise_in_bounds")


class Frame:
    def __init__(self, nx, ny):
        self.nx, self.ny = nx, ny
        self.wide, self.tall = nx + 2 * HALO, ny + 2 * HALO
        self.rows = self.tall + 2 * SUB
        self.span = pl.ds(SUB, self.tall)
        self.own = SUB + HALO
        self.main = (self.wide, self.rows, LANES)
        self.ends = (2, self.rows, LANES)


def bases(widths):
    return [sum(widths[:f]) for f in range(len(widths) + 1)]


def copied(pairs, sems):
    copies = [pltpu.make_async_copy(src, dst, sems.at[n]) for n, (src, dst) in enumerate(pairs)]
    for copy in copies:
        copy.start()
    return copies


def pack_x_kernel(count, widths, flags, *refs):
    fields = len(widths)
    ins, outs = refs[: fields + 1], refs[fields + 1 : -2]
    near, sems = refs[-2:]
    nx, ny = ins[0].shape[0], ins[0].shape[1]
    base = bases(widths)
    pairs = []
    for s, out in enumerate(outs):

        def place(size, width, s=s):
            if count == 2:
                return jnp.where(flags[IX] == 0, size - width, 0)
            return (size - width, 0)[s]

        for f, (ref, width) in enumerate(zip(ins, widths)):
            pairs.append((ref.at[pl.ds(place(nx, width), width)], out.at[pl.ds(base[f], width)]))
        pairs.append((ins[-1].at[place(nx // 2, 1)], near.at[s]))
    copies = copied(pairs, sems)
    for out in outs:
        out[base[-1]] = jnp.zeros(out.shape[1:], F32)
    for copy in copies:
        copy.wait()
    for s, out in enumerate(outs):
        out[base[-1], : ny // 2, : near.shape[2]] = near[s].astype(F32)


def load_kernel(flags, *refs):
    count = (len(refs) - 2) // 2
    for copy in copied(list(zip(refs[:count], refs[count + 1 : -1])), refs[-1]):
        copy.wait()


def slab_of(own, low, high, base, width, x):
    nx = own.shape[0]
    if HALO <= x < HALO + nx:
        return own[x - HALO]
    if x < HALO:
        at = x - (HALO - width)
        return low[base + at] if at >= 0 else None
    at = x - HALO - nx
    return high[base + at] if at < width else None


def pack_y_kernel(widths, labels, ring, flags, *refs):
    fields = len(widths)
    ins = refs[:fields]
    low, high = refs[fields + 1 : fields + 3]
    one, two = refs[fields + 3 :]
    nx, ny = ins[0].shape[0], ins[0].shape[1]
    frame = Frame(nx, ny)
    base = bases(widths)
    even = flags[PARITY] == 0

    def send(at, count, to_high, to_low):
        one[at : at + count] = to_high if ring else jnp.where(even, to_high, to_low)
        two[at : at + count] = to_low if ring else jnp.where(even, to_low, to_high)

    for f in range(fields):
        for x in range(frame.wide):
            slab = slab_of(ins[f], low, high, base[f], widths[f], x)
            at = (f * frame.wide + x) * HALO
            if slab is None:
                slab = jnp.ones((ny, LANES), F32)
            send(at, HALO, slab[ny - HALO :], slab[:HALO])
    at = fields * frame.wide * HALO
    if ring:
        one[at:], two[at:] = refs[fields][...], refs[fields][...]
    if labels:
        nb, rows, width = refs[fields].shape
        for out in (one, two):
            out[at:] = jnp.zeros((out.shape[0] - at, LANES), F32)
        for b in range(nb):
            top, bottom = (refs[fields][b, row : row + 1].astype(F32) for row in (rows - 1, 0))
            one[at + b : at + b + 1, :width] = jnp.where(even, top, bottom)
            two[at + b : at + b + 1, :width] = jnp.where(even, bottom, top)


def packed_lanes(wide_ref, f, frame, rows, to_high, to_low):
    group = lane_no((1, LANES)) // HALO
    nothing = jnp.ones((rows.size, LANES), F32)
    high, low = nothing, nothing
    for x in range(frame.wide):
        moved = turned(wide_ref[f, x, rows], HALO * (x + 1), 1)
        high = jnp.where(group == x, moved, high)
        low = jnp.where(group == (x + 1) % frame.wide, moved, low)
    at = pl.ds(f * frame.tall + rows.start - SUB, rows.size)
    to_high[at] = high
    to_low[at] = turned(low, -HALO, 1)


def frame_kernel(widths, flags, *refs):
    fields = len(widths)
    ins = refs[:fields]
    x_low, x_high, _ = refs[fields : fields + 3]
    wide_ref, to_high, to_low = refs[fields + 3 :]
    nx, ny = ins[0].shape[0], ins[0].shape[1]
    frame = Frame(nx, ny)
    base = bases(widths)
    tall, own = frame.tall, frame.own
    spare = jnp.ones((SUB, LANES), F32)
    for f in range(fields):
        for x in range(frame.wide):
            slab = slab_of(ins[f], x_low, x_high, base[f], widths[f], x)
            wide_ref[f, x, own : own + ny] = jnp.ones((ny, LANES), F32) if slab is None else slab
            wide_ref[f, x, :SUB] = spare
            wide_ref[f, x, SUB + tall :] = spare
        packed_lanes(wide_ref, f, frame, pl.ds(2 * SUB, tall - 2 * SUB), to_high, to_low)


def pack_z_kernel(widths, labels, ring, flags, wide_in, high_in, low_in, from_low, from_high, rider, *refs):
    fields = len(widths)
    wide_ref, send_forth, send_back, to_high, to_low = refs
    frame = Frame(wide_ref.shape[1] - 2 * HALO, wide_ref.shape[2] - 2 * (SUB + HALO))
    ny, tall, own = frame.ny, frame.tall, frame.own
    even = flags[PARITY] == 0
    for f in range(fields):
        for x in range(frame.wide):
            at = (f * frame.wide + x) * HALO
            low, high = from_low[at : at + HALO], from_high[at : at + HALO]
            if not ring:
                low, high = jnp.where(even, high, low), jnp.where(even, low, high)
            wide_ref[f, x, SUB:own] = low
            wide_ref[f, x, own + ny : own + ny + HALO] = high
    size = fields * tall
    to_high[...], to_low[...] = high_in[...], low_in[...]
    for f in range(fields):
        for start in (SUB, tall):
            packed_lanes(wide_ref, f, frame, pl.ds(start, SUB), to_high, to_low)
    high, low = to_high[...], to_low[...]
    send_forth[:size], send_back[:size] = jnp.where(even, high, low), jnp.where(even, low, high)
    if ring:
        send_forth[size:], send_back[size:] = rider[...], rider[...]
    if labels:
        nb, rows, width = rider.shape
        lane = lane_no((rows, LANES))
        high = low = jnp.zeros((rows, LANES), F32)
        for b in range(nb):
            slab = rider[b].astype(F32)
            high = jnp.where(lane == b, slab[:, width - 1 :], high)
            low = jnp.where(lane == b, slab[:, :1], low)
        send_forth[size:], send_back[size:] = jnp.where(even, high, low), jnp.where(even, low, high)


class Links:
    def __init__(self, mesh):
        self.sizes = [mesh.shape[a] for a in ("gx", "gy", "gz")]
        n_x, n_y, n_z = self.sizes

        def at(i, j, k):
            return (i * n_y + j) * n_z + k

        self.ring_x = [(i, (i + 1) % n_x) for i in range(n_x)]
        self.inner, self.outer, self.snake = [], [], []
        for i in range(n_x):
            for j in range(n_y):
                for k in range(n_z):
                    self.inner.append((at(i, j, k), at(i, j ^ 1, k)))
                    over = (i, j + 1) if j % 2 else (i, j - 1)
                    over = over if 0 <= over[1] < n_y else (i ^ 1, j)
                    self.outer.append((at(i, j, k), at(*over, k)))
            for j in range(0, n_y, 2):
                nodes = [at(i, j, k) for k in range(n_z)] + [at(i, j + 1, k) for k in reversed(range(n_z))]
                self.snake += [(nodes[m], nodes[(m + 1) % len(nodes)]) for m in range(len(nodes))]

    @staticmethod
    def back(pairs):
        return [(b, a) for a, b in pairs]

    @staticmethod
    def send(values, pairs):
        return lax.ppermute(values, ("gx", "gy", "gz"), pairs)

    def x(self, sends):
        if self.sizes[0] == 2:
            return (lax.ppermute(sends[0], "gx", self.ring_x),)
        return lax.ppermute(sends[0], "gx", self.ring_x), lax.ppermute(sends[1], "gx", self.back(self.ring_x))

    def near(self, values, x=None, y=None, z=None):
        forth, back = self.z(*(z or (values, values)))
        from_x = self.x(x or (values, values))
        return (forth, back, *from_x, *self.ring_y(*(y or (values, values))))

    def ring_y(self, to_high, to_low):
        ring = [(j, (j + 1) % self.sizes[1]) for j in range(self.sizes[1])]
        return lax.ppermute(to_high, "gy", ring), lax.ppermute(to_low, "gy", self.back(ring))

    def y(self, inner, outer):
        return self.send(inner, self.inner), self.send(outer, self.outer)

    def z(self, forth, back):
        return self.send(forth, self.snake), self.send(back, self.back(self.snake))


def send_y(widths, arrays, rider, from_x, ring):
    nx, ny, nz = arrays[0].shape
    rows = len(widths) * Frame(nx, ny).wide * HALO + (SUB if ring else ny // 2)
    kernel = functools.partial(pack_y_kernel, widths, not ring, ring)
    return call(kernel, [shaped(rows, nz)] * 2)(*arrays, rider, from_x[0], from_x[-1])


def framed(widths, arrays, from_x, sent):
    nx, ny, nz = arrays[0].shape
    frame, fields = Frame(nx, ny), len(widths)
    outs = [shaped(fields, *frame.main)] + [shaped(fields * frame.tall, nz)] * 2
    return call(functools.partial(frame_kernel, widths), outs)(*arrays, from_x[0], from_x[-1], sent)


def send_z(widths, frames, from_y, rider, ring):
    wide, high, _ = frames
    rows = high.shape[0] + (SUB if ring else rider.shape[1])
    return call(
        functools.partial(pack_z_kernel, widths, not ring, ring),
        [shaped(*wide.shape)] + [shaped(rows, LANES)] * 2,
        [pltpu.VMEM(high.shape, F32)] * 2,
        aliases={0: 0},
    )(*frames, *from_y, rider)


def sides(flags, forth, back):
    even = flags[PARITY] == 0
    return jnp.where(even, forth, back), jnp.where(even, back, forth)


def weight(one, two):
    return 2.0 * (one * two) / (one + two)


def lane_mask(x):
    return ((lane_no((1, LANES)) - (HALO * x + HALO - 1)) & (LANES - 1)) < 2


def edge_step(here, x, edges):
    return jnp.where(lane_mask(x), turned(here, HALO * x + HALO, 1), edges)


def joined(below, above):
    lane = lane_no((1, LANES))
    return jnp.where(lane % HALO == HALO - 1, turned(above, HALO - 1, 1), turned(below, 1, 1))


def at_edges(join, x):
    lane = lane_no((1, LANES))
    return jnp.where((lane == 0) | (lane == LANES - 1), turned(join, (LANES - HALO) - HALO * x, 1), 0.0)


def ends_near(below, above, edges):
    layer = lane_no((1, LANES)) % HALO
    return (
        jnp.where(layer == HALO - 1, turned(edges, -1, 1), turned(below, -1, 1)),
        turned(below, 1, 1),
        turned(above, -1, 1),
        jnp.where(layer == 0, turned(edges, 1 - HALO, 1), turned(above, 1, 1)),
    )


def main_sum(frame, field, x, join, wx, wy, wz):
    span, down = frame.span, pl.ds(SUB - 1, frame.tall)
    here, face_z = field[x, span], wz[x, span]
    total = wx[x, span] * field[x + 1, span] + wx[x - 1, span] * field[x - 1, span]
    total = total + wy[x, span] * field[x, pl.ds(SUB + 1, frame.tall)] + wy[x, down] * field[x, down]
    total = total + face_z * turned(here, -1, 1) + turned(face_z * here, 1, 1)
    return total + at_edges(join, x)


def ends_sum(frame, ends, s, upper, lower, wx, wy, wz_up, wz_low):
    span, down = frame.span, pl.ds(SUB - 1, frame.tall)
    here = ends[s, span]
    total = wx[s, span] * turned(here, -HALO, 1) + turned(wx[s, span] * here, HALO, 1)
    total = total + wy[s, span] * ends[s, pl.ds(SUB + 1, frame.tall)] + wy[s, down] * ends[s, down]
    return total + wz_up[s, span] * upper + wz_low[s, span] * lower


def clear_spares(ref, frame):
    for x in range(ref.shape[0]):
        ref[x, :SUB] = jnp.zeros((SUB, LANES), F32)
        ref[x, SUB + frame.tall :] = jnp.zeros((SUB, LANES), F32)


def pack_rows(values):
    half = values.shape[0] // 2
    lane = lane_no((half, LANES))
    return jnp.where(lane < LANES // 2, values[:half], turned(values[half:], LANES // 2, 1))


def lane_total(values):
    return jnp.broadcast_to(jnp.sum(values.T, axis=0, keepdims=True), (SUB, LANES))


def paired(values):
    even = 2 * (lane_no(values.shape) % (LANES // 2))
    return picked(values + turned(values, -1, 1), even)


def faces_y_kept(flags, frame):
    row = row_no((frame.tall, LANES))
    at_low, at_high = row == HALO - 1, row == HALO + frame.ny - 1
    return jnp.where(at_low, flags[Y_LOW], jnp.where(at_high, flags[Y_HIGH], 1)).astype(F32)


def fields_kernel(flags, wide_ref, _, wx, wy, wz, partial, cond_edges):
    frame = Frame(wx.shape[0] - 2 * HALO, wx.shape[1] - 2 * (SUB + HALO))
    wide, tall, span = frame.wide, frame.tall, frame.span
    last = HALO + frame.nx
    keep_y = faces_y_kept(flags, frame)
    inside = jnp.where(lane_no((1, LANES)) == LANES - 1, 0.0, 1.0)
    clear_spares(wy, frame)

    def fields(xs, carry):
        before, edges = carry
        stores = []
        for x in xs:
            here = wide_ref[0, x, span]
            keep = jnp.where(x == HALO - 1, flags[X_LOW], jnp.where(x == last - 1, flags[X_HIGH], 1)).astype(F32)
            face_x = keep * weight(here, wide_ref[0, jnp.minimum(x + 1, wide - 1), span])
            face_y = keep_y * weight(here, wide_ref[0, x, pl.ds(SUB + 1, tall)])
            face_z = inside * weight(here, turned(here, -1, 1))
            total = wide_ref[2, x, span] + face_x + before + face_y + turned(face_y, 1, 0)
            total = total + face_z + turned(face_z, 1, 1)
            stores.append((x, (face_x, face_y, face_z, total)))
            edges = edge_step(here, x, edges)
            before = face_x
        for x, values in stores:
            for ref, value in zip((wx, wy, wz, partial), values):
                ref[x, span] = value
        return before, edges

    nothing = jnp.zeros((tall, LANES), F32)
    cond_edges[...] = batched(0, wide, fields, (nothing, nothing + 1.0), 4)[1]


def fine_kernel(flags, wide_ref, forth, back, from_x_low, from_x_high, inner, outer, wx, wy, wz, partial, cond_edges,
                block_label, face_label, inner_diag, *refs):
    inv_diag, start = refs[:2]
    ends = refs[2:8]
    pre, face_near, face_weight, scaled_rhs, scale, once, once_ends, res, diag, block_res = refs[8:]
    ex, ey, ez_up, ez_low, inv_ends, start_ends = ends
    nx, ny = pre.shape[0], pre.shape[1]
    frame = Frame(nx, ny)
    wide, tall, span = frame.wide, frame.tall, frame.span
    last = HALO + nx
    got = [sides(flags, forth[f * tall : (f + 1) * tall], back[f * tall : (f + 1) * tall]) for f in range(3)]
    (cond_below, cond_above), rhs_ends, absorb_ends = got
    for ref in (start, once, ey, start_ends, once_ends):
        clear_spares(ref, frame)

    lane = lane_no((1, LANES))
    keep_y = faces_y_kept(flags, frame)
    keep_low, keep_high = flags[Z_LOW].astype(F32), flags[Z_HIGH].astype(F32)
    near = ends_near(cond_below, cond_above, cond_edges[...])
    slab = lane // HALO
    keep_x = jnp.where(
        slab == HALO - 1, flags[X_LOW], jnp.where(slab == last - 1, flags[X_HIGH], 1)
    ).astype(F32)
    layer = lane % HALO
    for s, here in enumerate((cond_below, cond_above)):
        up, low = weight(here, near[2 * s]), weight(here, near[2 * s + 1])
        if s == 0:
            up = up * jnp.where(layer == HALO - 1, keep_low, 1.0)
        else:
            low = low * jnp.where(layer == 0, keep_high, 1.0)
        face_x = keep_x * weight(here, turned(here, -HALO, 1))
        face_y = keep_y * weight(here, turned(here, -1, 0))
        ex[s, span], ey[s, span], ez_up[s, span], ez_low[s, span] = face_x, face_y, up, low
        total = absorb_ends[s] + face_x + turned(face_x, HALO, 1) + face_y + turned(face_y, 1, 0) + up + low
        inverse = OMEGA_FINE / total
        inv_ends[s, span] = inverse
        start_ends[s, span] = inverse * rhs_ends[s]

    end_low, end_high = ez_up[0, span], ez_low[1, span]
    join_faces = joined(end_low, end_high)

    def first_sweep(xs, edges):
        stores = []
        for x in xs:
            total = partial[x, span] + at_edges(join_faces, x)
            inverse = OMEGA_FINE / total
            begin = inverse * wide_ref[1, x, span]
            stores.append((x, (total, inverse, begin)))
            edges = edge_step(begin, x, edges)
        for x, values in stores:
            for ref, value in zip((diag, inv_diag, start), values):
                ref[x, span] = value
        return edges

    edges = batched(0, wide, first_sweep, jnp.zeros((tall, LANES), F32), 4)

    join = joined(end_low * start_ends[0, span], end_high * start_ends[1, span])
    near = ends_near(start_ends[0, span], start_ends[1, span], edges)
    for s in range(2):
        total = ends_sum(frame, start_ends, s, near[2 * s], near[2 * s + 1], ex, ey, ez_up, ez_low)
        once_ends[s, span] = (2.0 - OMEGA_FINE) * start_ends[s, span] + inv_ends[s, span] * total

    def second(xs, carry):
        news = []
        for x in xs:
            total = main_sum(frame, start, x, join, wx, wy, wz)
            news.append((2.0 - OMEGA_FINE) * start[x, span] + inv_diag[x, span] * total)
        for x, new in zip(xs, news):
            once[x, span] = new
        return carry

    batched(HALO - 1, last + 1, second, 0)
    join2 = joined(end_low * once_ends[0, span], end_high * once_ends[1, span])

    def remainder(xs, carry):
        news = []
        for x in xs:
            total = main_sum(frame, once, x, join2, wx, wy, wz)
            news.append(wide_ref[1, x, span] - diag[x, span] * once[x, span] + total)
        for x, new in zip(xs, news):
            res[x - HALO, span] = new
        for x in xs:
            pre[x - HALO] = once[x, pl.ds(frame.own, ny)]
        return carry

    batched(HALO, last, remainder, 0)

    nb, half, width = nx // 2, ny // 2, LANES // 2
    iota = row_no((AGG, LANES)).astype(F32)

    def rows_at(ref, x, off):
        return ref[x, pl.ds(frame.own + off, half, stride=2)]

    def add_rows(total, labels, b, values, c):
        for r in range(SUB):
            total = total + jnp.where(labels[b, r : r + 1] == iota, values[c, r : r + 1], 0.0)
        return total

    def to_blocks(bs, carry):
        for b in bs:
            four = sum(rows_at(res, 2 * b + a, c) for a in range(2) for c in range(2))
            block_res[b] = pack_rows(paired(four))
        return carry

    batched(0, nb, to_blocks, 0)
    zeros = jnp.zeros((AGG, LANES), F32)

    def restrict(b, total):
        return add_rows(total, block_label, b, block_res, b)

    sums = lax.fori_loop(0, nb, restrict, zeros)

    blank = jnp.zeros((half - nb, LANES), F32)
    low_at, high_at = pl.ds(frame.own - 1, 1), pl.ds(frame.own + ny - 1, 1)
    face_weight[0] = pack_rows(paired(rows_at(wx, HALO - 1, 0) + rows_at(wx, HALO - 1, 1)))
    face_weight[1] = pack_rows(paired(rows_at(wx, last - 1, 0) + rows_at(wx, last - 1, 1)))
    for s, at in ((2, low_at), (3, high_at)):
        lines = [wy[HALO + 2 * b, at] + wy[HALO + 2 * b + 1, at] for b in range(nb)]
        face_weight[s] = pack_rows(paired(jnp.concatenate(lines + [blank], axis=0)))
    lane = lane_no((half, LANES))
    for s, (ref, side, layer_at) in ((4, (ez_up, 0, HALO - 1)), (5, (ez_low, 1, 0))):
        values = rows_at(ref, side, 0) + rows_at(ref, side, 1)
        values = values + turned(values, -HALO, 1)
        spot = jnp.minimum(2 * HALO * lane + HALO * HALO + layer_at, LANES - 1)
        face_weight[s] = pack_rows(jnp.where(lane < nb, picked(values, spot), 0.0))
    around = zeros
    for s in range(6):
        around = add_rows(around, face_label, s, face_weight, s)
    scale[...] = OMEGA_COARSE / (inner_diag[...] + lane_total(around))
    scaled_rhs[...] = scale[...] * lane_total(sums)

    at = sum(WIDTHS)
    face_near[0] = pack_rows(from_x_low[at, :half])
    face_near[1] = pack_rows(from_x_high[at, :half])
    at = 3 * wide * HALO
    for s, values in enumerate(sides(flags, outer[at : at + half], inner[at : at + half])):
        face_near[2 + s] = pack_rows(values)
    below, above = sides(flags, forth[3 * tall : 3 * tall + half], back[3 * tall : 3 * tall + half])
    face_near[4] = pack_rows(below)
    face_near[5] = pack_rows(above)


def fill(left, right, labels, b, pairs):
    iota = row_no((AGG, LANES)).astype(F32)
    for r in range(SUB):
        lanes = pl.ds(r * LANES, LANES)
        row = pl.ds(r, 1)
        left[:, lanes] = jnp.where(labels[b, row] == iota, 1.0, 0.0).astype(BF16)
        held = sum(jnp.where(near[row] == iota, w[row], 0.0) for near, w in pairs)
        high = held.astype(BF16)
        right[:AGG, lanes] = high
        right[AGG:, lanes] = (held - high.astype(F32)).astype(BF16)


def product(left, right):
    return lax.dot_general(left[...], right[...], (((1,), (1,)), ((), ())), preferred_element_type=F32)


def both_halves(tile):
    return tile[:, :AGG] + tile[:, AGG:]


def keep_tile(out, t, tile):
    high = tile.astype(BF16)
    rows = pl.ds(t * AGG, AGG)
    out[rows, :AGG] = high
    out[rows, AGG:] = (tile - high.astype(F32)).astype(BF16)


def blocks_kernel(flags, cond, absorb, block_agg, _, block_label, near, weights, inner, face_label, fine_label,
                  part, line):
    nx, ny = cond.shape[0], cond.shape[1]
    nb, half, width = nx // 2, ny // 2, LANES // 2
    lane, row = lane_no((half, LANES)), row_no((half, LANES))

    def halves(values, slot):
        part[slot] = values
        return part[slot, pl.ds(0, half, stride=2)], part[slot, pl.ds(1, half, stride=2)]

    def label_at(b):
        values = block_agg[b].astype(F32)
        return jnp.concatenate([values, values], axis=1)

    def upper_x(b, slot):
        x = jnp.maximum(2 * b, 0)
        faces = weight(cond[x + 1], cond[jnp.minimum(x + 2, nx - 1)])
        return jnp.where((b == nb - 1) | (b < 0), 0.0, paired(sum(halves(faces, slot))))

    def step(bs, carry):
        low_x = upper_x(bs[0] - 1, 0)
        for k, b in enumerate(bs):
            x = 2 * b
            slot = 4 * k + 1
            one, two = cond[x], cond[x + 1]
            both_y = weight(one, turned(one, -1, 0)) + weight(two, turned(two, -1, 0))
            both_z = weight(one, turned(one, -1, 1)) + weight(two, turned(two, -1, 1))
            high_x = upper_x(b, slot)
            high_y = jnp.where(row == half - 1, 0.0, paired(halves(both_y, slot + 1)[1]))
            high_z = picked(sum(halves(both_z, slot + 2)), 2 * (lane % width) + 1)
            high_z = jnp.where(lane % width == width - 1, 0.0, high_z)
            low_y, low_z = turned(high_y, 1, 0), turned(high_z, 1, 1)
            own = label_at(b)
            near_x, past_x = label_at(jnp.minimum(b + 1, nb - 1)), label_at(jnp.maximum(b - 1, 0))
            near_y, past_y = turned(own, -1, 0), turned(own, 1, 0)
            near_z, past_z = turned(own, -1, 1), turned(own, 1, 1)
            total = paired(sum(halves(absorb[x] + absorb[x + 1], slot + 3)))
            for beside, values in (
                (near_x, high_x), (past_x, low_x), (near_y, high_y), (past_y, low_y), (near_z, high_z), (past_z, low_z)
            ):
                total = total + jnp.where(beside != own, values, 0.0)
            block_label[b] = pack_rows(own)
            inner[b] = pack_rows(total)
            for d, (beside, values) in enumerate(((near_x, high_x), (near_y, high_y), (near_z, high_z))):
                near[d, b], weights[d, b] = pack_rows(beside), pack_rows(values)
            spread = picked(own, lane // 2)
            for a in range(2):
                for c in range(2):
                    fine_label[x + a, pl.ds(c, half, stride=2)] = spread
            low_x = high_x
        return carry

    batched(0, nb, step, 0, 4)
    line[...] = jnp.zeros(line.shape, F32)
    low, high = jnp.zeros((half, LANES), F32), jnp.zeros((half, LANES), F32)
    for b in range(nb):
        own = label_at(b)
        line[0, b : b + 1], line[1, b : b + 1] = own[:1], own[half - 1 :]
        low = jnp.where(lane == b, own[:, :1], low)
        high = jnp.where(lane == b, own[:, width - 1 : width], high)
    face_label[0], face_label[1] = block_label[0], block_label[nb - 1]
    for s, values in enumerate((line[0], line[1], low, high)):
        face_label[2 + s] = pack_rows(values)


def own_kernel(first, last, total, flags, block_label, near, weights, inner, *refs):
    so_far, refs = (refs[0], refs[1:]) if first else (None, refs)
    refs = refs[1:]
    iota = row_no((AGG, LANES)).astype(F32)

    def step(bs, tile):
        for k, b in enumerate(bs):
            left, right = refs[-4 + 2 * (k % 2) :][:2]
            fill(left, right, block_label, b, [(near.at[d, b], weights.at[d, b]) for d in range(3)])
            tile = tile + product(left, right)
        return tile

    tile = so_far[...] if first else jnp.zeros((AGG, 2 * AGG), F32)
    tile = batched(first, last, step, tile, 2)
    if last < total:
        refs[0][...] = tile
        return
    out, inner_diag = refs[:2]
    tile = both_halves(tile)
    keep_tile(out, 0, jnp.where(row_no((AGG, AGG)) == lane_no((AGG, AGG)), 0.0, tile + tile.T))

    def gather(b, around):
        for r in range(SUB):
            around = around + jnp.where(block_label[b, r : r + 1] == iota, inner[b, r : r + 1], 0.0)
        return around

    inner_diag[...] = lane_total(lax.fori_loop(0, total, gather, jnp.zeros((AGG, LANES), F32)))


def faces_kernel(count, flags, own, face_label, face_near, face_weight, out, *factors):
    out[:AGG] = own[...]
    s = jnp.where(flags[IX] == 0, 1, 0)
    faces = ([s] if count == 2 else [0, 1]) + [2, 3, 4, 5]
    for t, s in enumerate(faces):
        left, right = factors[2 * (t % 2) :][:2]
        fill(left, right, face_near, s, [(face_label.at[s], face_weight.at[s])])
        keep_tile(out, t + 1, both_halves(product(left, right)))


def turn_kernel(flags, tiles, scaled_rhs, scale, own, *refs):
    forth, back, *others, out = refs
    got = [ref[ref.shape[0] - 1, :SUB] if len(ref.shape) == 3 else ref[ref.shape[0] - SUB :] for ref in (*others, forth, back)]
    vectors = [own[...], *got[:-2], *sides(flags, *got[-2:])]
    row = row_no((SUB, AGG))
    parts = []
    for v in vectors:
        high = v.astype(BF16).astype(F32)
        parts.append(jnp.where(row == 0, high, jnp.where(row == 1, v - high, 0.0)).astype(BF16))
    got = jnp.dot(jnp.concatenate(parts, axis=1), tiles[...], preferred_element_type=F32)
    applied = jnp.sum(got[:, :AGG] + got[:, AGG:], axis=0, keepdims=True)
    out[...] = (1.0 - OMEGA_COARSE) * own[...] + scaled_rhs[...] + scale[...] * applied


def ride_kernel(count, flags, pre, fine_label, coarse, *outs):
    nx = pre.shape[0]
    for s, out in enumerate(outs):
        at = jnp.where(flags[IX] == 0, nx - HALO, 0) if count == 2 else (nx - HALO, 0)[s]
        for f, field in enumerate((pre, fine_label)):
            for x in range(HALO):
                out[HALO * f + x] = field[at + x]
        out[2 * HALO] = jnp.zeros(out.shape[1:], F32)
        out[2 * HALO, :SUB] = coarse[...]


def three_kernel(flags, low, mid, high, out):
    row = row_no(out.shape)
    out[...] = jnp.where(row == 0, low[...], jnp.where(row == 1, mid[...], high[...]))


def nine_kernel(flags, low, mid, high, out):
    out[...] = jnp.zeros(out.shape, F32)
    for n, ref in enumerate((low, mid, high)):
        out[3 * n : 3 * n + 3] = ref[:3]


def lift_kernel(flags, wide_ref, forth, back, main, ends):
    frame = Frame(wide_ref.shape[1] - 2 * HALO, wide_ref.shape[2] - 2 * (SUB + HALO))
    tall = frame.tall
    for b in range(frame.wide // 2):
        main[b] = wide_ref[1, 2 * b, frame.span].astype(jnp.int32)
    rows = pl.ds(tall, tall)
    for s, values in enumerate(sides(flags, forth[rows], back[rows])):
        ends[s] = values.astype(jnp.int32)


def post_kernel(flags, table, table_forth, table_back, labels, end_labels, wide_ref, forth, back, *refs):
    (wx, wy, wz, inv_diag, start), ends = refs[:5], refs[5:11]
    out, one, two, one_ends, two_ends = refs[11:]
    nx, ny = out.shape[0], out.shape[1]
    frame = Frame(nx, ny)
    wide, tall, span = frame.wide, frame.tall, frame.span
    ex, ey, ez_up, ez_low, inv_ends, start_ends = ends
    for ref in (one, two, one_ends, two_ends):
        clear_spares(ref, frame)
    row, lane = row_no((tall, LANES)), lane_no((tall, LANES))
    under, over = sides(flags, table_forth[...], table_back[...])
    tables = {-1: under, 0: table[...], 1: over}

    def table_at(dx, dz):
        low, mid, high = (tables[dz][3 * n + dx + 1 : 3 * n + dx + 2] for n in range(3))
        return jnp.where(row < HALO, low, jnp.where(row < HALO + ny, mid, high))

    for x_from, x_to, dx in ((0, HALO, -1), (HALO, HALO + nx, 0), (HALO + nx, wide, 1)):
        values = table_at(dx, 0)

        def lift(bs, carry, values=values):
            news = [picked(values, labels[b]) for b in bs]
            for b, new in zip(bs, news):
                for a in range(2):
                    two[2 * b + a, span] = wide_ref[0, 2 * b + a, span] + new
            return carry

        batched(x_from // 2, x_to // 2, lift, 0, 4)
    for s, (dz, base) in enumerate(zip((-1, 1), sides(flags, forth[:tall], back[:tall]))):
        below, inside, above = (picked(table_at(dx, dz), end_labels[s]) for dx in (-1, 0, 1))
        spot = lane // HALO
        lifted = jnp.where(spot < HALO, below, jnp.where(spot < HALO + nx, inside, above))
        two_ends[s, span] = base + lifted
    kept = 1.0 - OMEGA_FINE
    buffers = ((two, two_ends), (one, one_ends), (two, two_ends), (one, one_ends))
    for s in range(POST):
        src, src_ends = buffers[s]
        join = joined(ez_up[0, span] * src_ends[0, span], ez_low[1, span] * src_ends[1, span])
        final = s == POST - 1
        dst, dst_ends = (None, None) if final else buffers[s + 1]

        def step(xs, edges, src=src, join=join, dst=dst, final=final):
            news = []
            for x in xs:
                here = src[x, span]
                total = main_sum(frame, src, x, join, wx, wy, wz)
                news.append(kept * here + start[x, span] + inv_diag[x, span] * total)
                if not final:
                    edges = edge_step(here, x, edges)
            for x, new in zip(xs, news):
                if final:
                    out[x - HALO] = new[HALO : HALO + ny]
                else:
                    dst[x, span] = new
            return edges

        edges = batched(s + 1, wide - s - 1, step, jnp.zeros((tall, LANES), F32))
        if not final:
            near = ends_near(src_ends[0, span], src_ends[1, span], edges)
            news = []
            for e in range(2):
                total = ends_sum(frame, src_ends, e, near[2 * e], near[2 * e + 1], ex, ey, ez_up, ez_low)
                news.append(kept * src_ends[e, span] + start_ends[e, span] + inv_ends[e, span] * total)
            dst_ends[0, span], dst_ends[1, span] = news


def body(links, right_side, conductance, absorption, block_agg):
    nx, ny, nz = right_side.shape
    frame = Frame(nx, ny)
    nb = nx // 2
    n_x = links.sizes[0]
    arrays = (conductance, right_side, absorption, block_agg)
    n_send = 1 if n_x == 2 else 2
    pinned = [pltpu.with_memory_space_constraint(a, pltpu.HBM) for a in arrays]
    hbm = pl.BlockSpec(memory_space=pltpu.HBM)
    x_sends = call(
        functools.partial(pack_x_kernel, n_x, WIDTHS),
        [shaped(sum(WIDTHS) + 1, ny, nz)] * n_send,
        [pltpu.VMEM((n_send, ny // 2, nz // 2), jnp.int32), pltpu.SemaphoreType.DMA((n_send * 4,))],
        in_specs=[hbm] * 4,
    )(*pinned)
    arrays = call(
        load_kernel,
        [jax.ShapeDtypeStruct(a.shape, a.dtype) for a in arrays],
        [pltpu.SemaphoreType.DMA((4,))],
        in_specs=[hbm] * 4 + [VMEM],
    )(*pinned, x_sends[0])
    blocks = (nb, SUB, LANES)
    outs = [shaped(*blocks), shaped(3, *blocks), shaped(3, *blocks), shaped(*blocks), shaped(6, SUB, LANES)]
    outs += [shaped(nx, ny, nz)]
    scratch = [pltpu.VMEM((17, ny, LANES), F32), pltpu.VMEM((2, ny // 2, LANES), F32)]
    pair = [pltpu.VMEM((AGG, SUB * LANES), BF16), pltpu.VMEM((2 * AGG, SUB * LANES), BF16)]
    *rows, face_label, fine_label = call(blocks_kernel, outs, scratch)(arrays[0], arrays[2], arrays[3], x_sends[0])
    block_label = rows[0]
    bounds = (0, nb // 4, nb * 5 // 6, nb)
    parts = []

    def own_part(p, sent):
        outs = [shaped(AGG, 2 * AGG)]
        if p == 2:
            outs = [jax.ShapeDtypeStruct((AGG, 2 * AGG), BF16), shaped(SUB, AGG)]
        kernel = functools.partial(own_kernel, bounds[p], bounds[p + 1], nb)
        parts.append(call(kernel, outs, pair * 2)(*rows, *(parts[-1] if p else ()), sent))
        return parts[-1]

    first = own_part(0, x_sends[0])
    from_x = links.x(x_sends)
    from_x = lax.optimization_barrier((*from_x, *first))[:-1]

    sends = send_y(WIDTHS, arrays[:3], arrays[3], from_x, False)
    frames = framed(WIDTHS, arrays[:3], from_x, sends[0])
    second = own_part(1, sends[0])
    from_y = links.y(*sends)
    from_y = lax.optimization_barrier((*from_y, *second))[:2]
    wide, *sends = send_z(WIDTHS, frames, from_y, arrays[3], False)
    fields = call(fields_kernel, [shaped(*frame.main)] * 4 + [shaped(frame.tall, nz)], limit=24)(wide, sends[0])
    own_tile, inner_diag = own_part(2, sends[0])
    halo = (wide, *links.z(*sends))
    outs = [shaped(*frame.main)] * 2 + [shaped(*frame.ends)] * 6 + [shaped(nx, ny, nz)]
    outs += [shaped(6, SUB, LANES)] * 2 + [shaped(SUB, AGG)] * 2
    scratch = [pltpu.VMEM(frame.main, F32), pltpu.VMEM(frame.ends, F32), pltpu.VMEM((nx, frame.rows, LANES), F32)]
    scratch += [pltpu.VMEM(frame.main, F32), pltpu.VMEM(blocks, F32)]
    got = call(fine_kernel, outs, scratch, limit=28)(
        *halo, from_x[0], from_x[-1], *from_y, *fields, block_label, face_label, inner_diag
    )
    fields, pre = (*fields[:3], *got[:8]), got[8]
    face_near, face_weight, scaled_rhs, scale = got[9:]
    tiles = call(
        functools.partial(faces_kernel, n_x),
        jax.ShapeDtypeStruct(((n_send + 5) * AGG, 2 * AGG), BF16),
        pair * 2,
    )(own_tile, face_label, face_near, face_weight)
    coarse = scaled_rhs

    def turn(**more):
        near = links.near(coarse, **more)
        return call(turn_kernel, shaped(SUB, AGG))(tiles, scaled_rhs, scale, coarse, *near), near

    widths, both = (HALO, HALO), (pre, fine_label)
    rides = call(functools.partial(ride_kernel, n_x), [shaped(2 * HALO + 1, ny, nz)] * n_send)(*both, coarse)
    coarse, near = turn(x=rides)
    from_x = near[2:-2]
    rides = send_y(widths, both, coarse, from_x, True)
    frames = framed(widths, both, from_x, rides[0])
    coarse, near = turn(y=rides)
    wide, *rides = send_z(widths, frames, near[-2:], coarse, True)
    coarse, near = turn(z=rides)
    halo = (wide, *near[:2])
    outs = [jax.ShapeDtypeStruct((frame.wide // 2, frame.tall, nz), jnp.int32)]
    outs += [jax.ShapeDtypeStruct((2, frame.tall, nz), jnp.int32)]
    lifts = call(lift_kernel, outs)(*halo)
    for _ in range(KC - 4):
        coarse, _ = turn()
    from_x = links.x([coarse] * n_send)
    three = call(three_kernel, shaped(SUB, AGG))(from_x[0], coarse, from_x[-1])
    low, high = links.ring_y(three, three)
    nine = call(nine_kernel, shaped(2 * SUB, AGG))(low, three, high)
    tables = (nine, *links.z(nine, nine))
    scratch = [pltpu.VMEM(frame.main, F32)] * 2 + [pltpu.VMEM(frame.ends, F32)] * 2
    return call(post_kernel, shaped(nx, ny, nz), scratch, limit=24)(*tables, *lifts, *halo, *fields)


def solution(mesh):
    spec = P("gx", "gy", "gz")
    return jax.shard_map(
        functools.partial(body, Links(mesh)), mesh=mesh, in_specs=(spec,) * 4, out_specs=spec, check_vma=False
    )
```

```python
import functools

import jax
import jax.numpy as jnp
from jax import lax
from jax.experimental import pallas as pl
from jax.experimental.pallas import tpu as pltpu
from jax.sharding import PartitionSpec as P

AGG = 128
LANES = 128
SUB = 8
HALO = 4
WIDTHS = (4, 3, 3)
POST = 4
KC = 8
OMEGA_FINE = 0.8
OMEGA_COARSE = 0.7
F32 = jnp.float32
BF16 = jnp.bfloat16
VMEM = pl.BlockSpec(memory_space=pltpu.VMEM)
IX, PARITY, X_LOW, X_HIGH, Y_LOW, Y_HIGH, Z_LOW, Z_HIGH = range(8)


def places():
    (ix, n_x), (iy, n_y), (iz, n_z) = ((lax.axis_index(a), lax.axis_size(a)) for a in ("gx", "gy", "gz"))
    flags = [ix, iy % 2, ix > 0, ix < n_x - 1, iy > 0, iy < n_y - 1, iz > 0, iz < n_z - 1]
    return [jnp.asarray(flag, jnp.int32) for flag in flags]


def call(kernel, outs, scratch=(), limit=16, flops=10**6, in_specs=None, aliases=None, out_specs=None):
    def placed(*refs):
        kernel(places(), *refs)

    def run(*arrays):
        return pl.pallas_call(
            placed,
            out_shape=outs,
            in_specs=in_specs or [VMEM] * len(arrays),
            out_specs=out_specs or jax.tree.map(lambda _: VMEM, outs),
            scratch_shapes=list(scratch),
            input_output_aliases=aliases or {},
            compiler_params=pltpu.CompilerParams(vmem_limit_bytes=limit * 2**20),
            cost_estimate=pl.CostEstimate(flops=flops, bytes_accessed=10**5, transcendentals=0),
        )(*arrays)

    return run


def shaped(*shape):
    return jax.ShapeDtypeStruct(shape, F32)


def lane_no(shape):
    return lax.broadcasted_iota(jnp.int32, shape, len(shape) - 1)


def row_no(shape):
    return lax.broadcasted_iota(jnp.int32, shape, len(shape) - 2)


def turned(values, shift, axis):
    if isinstance(shift, int):
        shift = shift % values.shape[axis]
        if shift == 0:
            return values
    return pltpu.roll(values, shift, axis)


def batched(low, high, step, carry, size=6):
    def some(i, carry):
        return step([low + i * size + k for k in range(size)], carry)

    carry = lax.fori_loop(0, (high - low) // size, some, carry)
    rest = (high - low) % size
    return step(list(range(high - rest, high)), carry) if rest else carry


def picked(values, index):
    return jnp.take_along_axis(values, index, axis=1, mode="promise_in_bounds")


class Frame:
    def __init__(self, nx, ny):
        self.nx, self.ny = nx, ny
        self.wide, self.tall = nx + 2 * HALO, ny + 2 * HALO
        self.rows = self.tall + 2 * SUB
        self.span = pl.ds(SUB, self.tall)
        self.own = SUB + HALO
        self.main = (self.wide, self.rows, LANES)
        self.ends = (2, self.rows, LANES)


def bases(widths):
    return [sum(widths[:f]) for f in range(len(widths) + 1)]


def copied(pairs, sems):
    copies = [pltpu.make_async_copy(src, dst, sems.at[n]) for n, (src, dst) in enumerate(pairs)]
    for copy in copies:
        copy.start()
    return copies


def pack_x_kernel(count, widths, flags, *refs):
    fields = len(widths)
    ins, outs = refs[: fields + 1], refs[fields + 1 : -2]
    near, sems = refs[-2:]
    nx, ny = ins[0].shape[0], ins[0].shape[1]
    base = bases(widths)
    pairs = []
    for s, out in enumerate(outs):

        def place(size, width, s=s):
            if count == 2:
                return jnp.where(flags[IX] == 0, size - width, 0)
            return (size - width, 0)[s]

        for f, (ref, width) in enumerate(zip(ins, widths)):
            pairs.append((ref.at[pl.ds(place(nx, width), width)], out.at[pl.ds(base[f], width)]))
        pairs.append((ins[-1].at[place(nx // 2, 1)], near.at[s]))
    copies = copied(pairs, sems)
    for out in outs:
        out[base[-1]] = jnp.zeros(out.shape[1:], F32)
    for copy in copies:
        copy.wait()
    for s, out in enumerate(outs):
        out[base[-1], : ny // 2, : near.shape[2]] = near[s].astype(F32)


def load_kernel(flags, *refs):
    count = (len(refs) - 2) // 2
    for copy in copied(list(zip(refs[:count], refs[count + 1 : -1])), refs[-1]):
        copy.wait()


def slab_of(own, low, high, base, width, x):
    nx = own.shape[0]
    if HALO <= x < HALO + nx:
        return own[x - HALO]
    if x < HALO:
        at = x - (HALO - width)
        return low[base + at] if at >= 0 else None
    at = x - HALO - nx
    return high[base + at] if at < width else None


def pack_y_kernel(widths, labels, ring, flags, *refs):
    fields = len(widths)
    ins = refs[:fields]
    low, high = refs[fields + 1 : fields + 3]
    one, two = refs[fields + 3 :]
    nx, ny = ins[0].shape[0], ins[0].shape[1]
    frame = Frame(nx, ny)
    base = bases(widths)
    even = flags[PARITY] == 0

    def send(at, count, to_high, to_low):
        one[at : at + count] = to_high if ring else jnp.where(even, to_high, to_low)
        two[at : at + count] = to_low if ring else jnp.where(even, to_low, to_high)

    for f in range(fields):
        for x in range(frame.wide):
            slab = slab_of(ins[f], low, high, base[f], widths[f], x)
            at = (f * frame.wide + x) * HALO
            if slab is None:
                slab = jnp.ones((ny, LANES), F32)
            send(at, HALO, slab[ny - HALO :], slab[:HALO])
    at = fields * frame.wide * HALO
    if ring:
        one[at:], two[at:] = refs[fields][...], refs[fields][...]
    if labels:
        nb, rows, width = refs[fields].shape
        for out in (one, two):
            out[at:] = jnp.zeros((out.shape[0] - at, LANES), F32)
        for b in range(nb):
            top, bottom = (refs[fields][b, row : row + 1].astype(F32) for row in (rows - 1, 0))
            one[at + b : at + b + 1, :width] = jnp.where(even, top, bottom)
            two[at + b : at + b + 1, :width] = jnp.where(even, bottom, top)


def packed_lanes(wide_ref, f, frame, rows, to_high, to_low):
    group = lane_no((1, LANES)) // HALO
    nothing = jnp.ones((rows.size, LANES), F32)
    high, low = nothing, nothing
    for x in range(frame.wide):
        moved = turned(wide_ref[f, x, rows], HALO * (x + 1), 1)
        high = jnp.where(group == x, moved, high)
        low = jnp.where(group == (x + 1) % frame.wide, moved, low)
    at = pl.ds(f * frame.tall + rows.start - SUB, rows.size)
    to_high[at] = high
    to_low[at] = turned(low, -HALO, 1)


def frame_kernel(widths, flags, *refs):
    fields = len(widths)
    ins = refs[:fields]
    x_low, x_high, _ = refs[fields : fields + 3]
    wide_ref, to_high, to_low = refs[fields + 3 :]
    nx, ny = ins[0].shape[0], ins[0].shape[1]
    frame = Frame(nx, ny)
    base = bases(widths)
    tall, own = frame.tall, frame.own
    spare = jnp.ones((SUB, LANES), F32)
    for f in range(fields):
        for x in range(frame.wide):
            slab = slab_of(ins[f], x_low, x_high, base[f], widths[f], x)
            wide_ref[f, x, own : own + ny] = jnp.ones((ny, LANES), F32) if slab is None else slab
            wide_ref[f, x, :SUB] = spare
            wide_ref[f, x, SUB + tall :] = spare
        packed_lanes(wide_ref, f, frame, pl.ds(2 * SUB, tall - 2 * SUB), to_high, to_low)


def pack_z_kernel(widths, labels, ring, flags, wide_in, high_in, low_in, from_low, from_high, rider, *refs):
    fields = len(widths)
    wide_ref, send_forth, send_back, to_high, to_low = refs
    frame = Frame(wide_ref.shape[1] - 2 * HALO, wide_ref.shape[2] - 2 * (SUB + HALO))
    ny, tall, own = frame.ny, frame.tall, frame.own
    even = flags[PARITY] == 0
    for f in range(fields):
        for x in range(frame.wide):
            at = (f * frame.wide + x) * HALO
            low, high = from_low[at : at + HALO], from_high[at : at + HALO]
            if not ring:
                low, high = jnp.where(even, high, low), jnp.where(even, low, high)
            wide_ref[f, x, SUB:own] = low
            wide_ref[f, x, own + ny : own + ny + HALO] = high
    size = fields * tall
    to_high[...], to_low[...] = high_in[...], low_in[...]
    for f in range(fields):
        for start in (SUB, tall):
            packed_lanes(wide_ref, f, frame, pl.ds(start, SUB), to_high, to_low)
    high, low = to_high[...], to_low[...]
    send_forth[:size], send_back[:size] = jnp.where(even, high, low), jnp.where(even, low, high)
    if ring:
        send_forth[size:], send_back[size:] = rider[...], rider[...]
    if labels:
        nb, rows, width = rider.shape
        lane = lane_no((rows, LANES))
        high = low = jnp.zeros((rows, LANES), F32)
        for b in range(nb):
            slab = rider[b].astype(F32)
            high = jnp.where(lane == b, slab[:, width - 1 :], high)
            low = jnp.where(lane == b, slab[:, :1], low)
        send_forth[size:], send_back[size:] = jnp.where(even, high, low), jnp.where(even, low, high)


class Links:
    def __init__(self, mesh):
        self.sizes = [mesh.shape[a] for a in ("gx", "gy", "gz")]
        n_x, n_y, n_z = self.sizes

        def at(i, j, k):
            return (i * n_y + j) * n_z + k

        self.ring_x = [(i, (i + 1) % n_x) for i in range(n_x)]
        self.inner, self.outer, self.snake = [], [], []
        for i in range(n_x):
            for j in range(n_y):
                for k in range(n_z):
                    self.inner.append((at(i, j, k), at(i, j ^ 1, k)))
                    over = (i, j + 1) if j % 2 else (i, j - 1)
                    over = over if 0 <= over[1] < n_y else (i ^ 1, j)
                    self.outer.append((at(i, j, k), at(*over, k)))
            for j in range(0, n_y, 2):
                nodes = [at(i, j, k) for k in range(n_z)] + [at(i, j + 1, k) for k in reversed(range(n_z))]
                self.snake += [(nodes[m], nodes[(m + 1) % len(nodes)]) for m in range(len(nodes))]

    @staticmethod
    def back(pairs):
        return [(b, a) for a, b in pairs]

    @staticmethod
    def send(values, pairs):
        return lax.ppermute(values, ("gx", "gy", "gz"), pairs)

    def x(self, sends):
        if self.sizes[0] == 2:
            return (lax.ppermute(sends[0], "gx", self.ring_x),)
        return lax.ppermute(sends[0], "gx", self.ring_x), lax.ppermute(sends[1], "gx", self.back(self.ring_x))

    def near(self, values, x=None, y=None, z=None):
        forth, back = self.z(*(z or (values, values)))
        from_x = self.x(x or (values, values))
        return (forth, back, *from_x, *self.ring_y(*(y or (values, values))))

    def ring_y(self, to_high, to_low):
        ring = [(j, (j + 1) % self.sizes[1]) for j in range(self.sizes[1])]
        return lax.ppermute(to_high, "gy", ring), lax.ppermute(to_low, "gy", self.back(ring))

    def y(self, inner, outer):
        return self.send(inner, self.inner), self.send(outer, self.outer)

    def z(self, forth, back):
        return self.send(forth, self.snake), self.send(back, self.back(self.snake))


def send_y(widths, arrays, rider, from_x, ring):
    nx, ny, nz = arrays[0].shape
    rows = len(widths) * Frame(nx, ny).wide * HALO + (SUB if ring else ny // 2)
    kernel = functools.partial(pack_y_kernel, widths, not ring, ring)
    return call(kernel, [shaped(rows, nz)] * 2)(*arrays, rider, from_x[0], from_x[-1])


def framed(widths, arrays, from_x, sent):
    nx, ny, nz = arrays[0].shape
    frame, fields = Frame(nx, ny), len(widths)
    outs = [shaped(fields, *frame.main)] + [shaped(fields * frame.tall, nz)] * 2
    return call(functools.partial(frame_kernel, widths), outs)(*arrays, from_x[0], from_x[-1], sent)


def send_z(widths, frames, from_y, rider, ring):
    wide, high, _ = frames
    rows = high.shape[0] + (SUB if ring else rider.shape[1])
    return call(
        functools.partial(pack_z_kernel, widths, not ring, ring),
        [shaped(*wide.shape)] + [shaped(rows, LANES)] * 2,
        [pltpu.VMEM(high.shape, F32)] * 2,
        aliases={0: 0},
    )(*frames, *from_y, rider)


def sides(flags, forth, back):
    even = flags[PARITY] == 0
    return jnp.where(even, forth, back), jnp.where(even, back, forth)


def weight(one, two):
    return 2.0 * (one * two) / (one + two)


def lane_mask(x):
    return ((lane_no((1, LANES)) - (HALO * x + HALO - 1)) & (LANES - 1)) < 2


def edge_step(here, x, edges):
    return jnp.where(lane_mask(x), turned(here, HALO * x + HALO, 1), edges)


def joined(below, above):
    lane = lane_no((1, LANES))
    return jnp.where(lane % HALO == HALO - 1, turned(above, HALO - 1, 1), turned(below, 1, 1))


def at_edges(join, x):
    lane = lane_no((1, LANES))
    return jnp.where((lane == 0) | (lane == LANES - 1), turned(join, (LANES - HALO) - HALO * x, 1), 0.0)


def ends_near(below, above, edges):
    layer = lane_no((1, LANES)) % HALO
    return (
        jnp.where(layer == HALO - 1, turned(edges, -1, 1), turned(below, -1, 1)),
        turned(below, 1, 1),
        turned(above, -1, 1),
        jnp.where(layer == 0, turned(edges, 1 - HALO, 1), turned(above, 1, 1)),
    )


def main_sums(frame, field, xs, join, wx, wy, wz):
    span = frame.span
    slabs = [field[xs[0] - 1 + k, span] for k in range(len(xs) + 2)]
    faces = [wx[xs[0] - 1 + k, span] for k in range(len(xs) + 1)]
    totals = []
    for k, x in enumerate(xs):
        here, face_y, face_z = slabs[k + 1], wy[x, span], wz[x, span]
        total = faces[k + 1] * slabs[k + 2] + faces[k] * slabs[k]
        total = total + face_y * turned(here, -1, 0) + turned(face_y * here, 1, 0)
        total = total + face_z * turned(here, -1, 1) + turned(face_z * here, 1, 1)
        totals.append(total + at_edges(join, x))
    return slabs[1:-1], totals


def ends_sum(frame, ends, s, upper, lower, wx, wy, wz_up, wz_low):
    span, down = frame.span, pl.ds(SUB - 1, frame.tall)
    here = ends[s, span]
    total = wx[s, span] * turned(here, -HALO, 1) + turned(wx[s, span] * here, HALO, 1)
    total = total + wy[s, span] * ends[s, pl.ds(SUB + 1, frame.tall)] + wy[s, down] * ends[s, down]
    return total + wz_up[s, span] * upper + wz_low[s, span] * lower


def clear_spares(ref, frame):
    for x in range(ref.shape[0]):
        ref[x, :SUB] = jnp.zeros((SUB, LANES), F32)
        ref[x, SUB + frame.tall :] = jnp.zeros((SUB, LANES), F32)


def pack_rows(values):
    half = values.shape[0] // 2
    lane = lane_no((half, LANES))
    return jnp.where(lane < LANES // 2, values[:half], turned(values[half:], LANES // 2, 1))


def lane_total(values):
    return jnp.broadcast_to(jnp.sum(values.T, axis=0, keepdims=True), (SUB, LANES))


def paired(values):
    even = 2 * (lane_no(values.shape) % (LANES // 2))
    return picked(values + turned(values, -1, 1), even)


def faces_y_kept(flags, frame):
    row = row_no((frame.tall, LANES))
    at_low, at_high = row == HALO - 1, row == HALO + frame.ny - 1
    return jnp.where(at_low, flags[Y_LOW], jnp.where(at_high, flags[Y_HIGH], 1)).astype(F32)


def face_rows(count, flags, nb):
    x = [(jnp.where(flags[IX] == 0, 1, 0), SUB)] if count == 2 else [(0, SUB), (1, SUB)]
    return x + [(2, nb // 2), (3, nb // 2), (4, 2), (5, 2)]


def add_rows(total, labels, b, values, c, rows=SUB):
    iota = row_no((AGG, LANES)).astype(F32)
    for r in range(rows):
        row = pl.ds(r, 1)
        total = total + jnp.where(labels[b, row] == iota, values[c, row], 0.0)
    return total


def pack_lanes(values):
    lane = lane_no((2, LANES))
    packed = values[:2]
    for g in range(1, SUB):
        packed = jnp.where(lane // 16 == g, turned(values[2 * g : 2 * g + 2], 16 * g, 1), packed)
    return packed


def fields_kernel(count, flags, wide_ref, face_label, inner_diag, wx, wy, wz, partial, cond_edges, face_weight, diag):
    frame = Frame(wx.shape[0] - 2 * HALO, wx.shape[1] - 2 * (SUB + HALO))
    wide, tall, span = frame.wide, frame.tall, frame.span
    last = HALO + frame.nx
    keep_y = faces_y_kept(flags, frame)
    inside = jnp.where(lane_no((1, LANES)) == LANES - 1, 0.0, 1.0)

    def fields(xs, carry):
        before, edges = carry
        stores = []
        for x in xs:
            here = wide_ref[0, x, span]
            keep = jnp.where(x == HALO - 1, flags[X_LOW], jnp.where(x == last - 1, flags[X_HIGH], 1)).astype(F32)
            face_x = keep * weight(here, wide_ref[0, jnp.minimum(x + 1, wide - 1), span])
            face_y = keep_y * weight(here, wide_ref[0, x, pl.ds(SUB + 1, tall)])
            face_z = inside * weight(here, turned(here, -1, 1))
            total = wide_ref[2, x, span] + face_x + before + face_y + turned(face_y, 1, 0)
            total = total + face_z + turned(face_z, 1, 1)
            stores.append((x, (face_x, face_y, face_z, total)))
            edges = edge_step(here, x, edges)
            before = face_x
        for x, values in stores:
            for ref, value in zip((wx, wy, wz, partial), values):
                ref[x, span] = value
        return before, edges

    nothing = jnp.zeros((tall, LANES), F32)
    cond_edges[...] = batched(0, wide, fields, (nothing, nothing + 1.0), 4)[1]
    nb, ny = frame.nx // 2, frame.ny
    for s, x in enumerate((HALO - 1, last - 1)):
        rows = [wx[x, pl.ds(frame.own + c, ny // 2, stride=2)] for c in range(2)]
        face_weight[s] = pack_rows(paired(rows[0] + rows[1]))
    for s, at in ((2, frame.own - 1), (3, frame.own + ny - 1)):
        lines = [wy[HALO + 2 * b, at : at + 1] + wy[HALO + 2 * b + 1, at : at + 1] for b in range(nb)]
        face_weight[s, : nb // 2] = pack_rows(paired(jnp.concatenate(lines, axis=0)))
    around = jnp.zeros((AGG, LANES), F32)
    for s, rows in face_rows(count, flags, nb)[:-2]:
        around = add_rows(around, face_label, s, face_weight, s, rows)
    diag[...] = inner_diag[...] + lane_total(around)


def fine_kernel(flags, wide_ref, forth, back, wx, wy, wz, partial, cond_edges, block_label, face_label, some_diag,
                *refs):
    inv_diag, start = refs[:2]
    ends = refs[2:8]
    pre, face_weight, scaled_rhs, scale, once, once_ends, res, diag, block_res = refs[8:]
    ex, ey, ez_up, ez_low, inv_ends, start_ends = ends
    nx, ny = pre.shape[0], pre.shape[1]
    frame = Frame(nx, ny)
    wide, tall, span = frame.wide, frame.tall, frame.span
    last = HALO + nx
    got = [sides(flags, forth[f * tall : (f + 1) * tall], back[f * tall : (f + 1) * tall]) for f in range(3)]
    (cond_below, cond_above), rhs_ends, absorb_ends = got
    for ref in (ey, start_ends, once_ends):
        clear_spares(ref, frame)

    lane = lane_no((1, LANES))
    keep_y = faces_y_kept(flags, frame)
    keep_low, keep_high = flags[Z_LOW].astype(F32), flags[Z_HIGH].astype(F32)
    near = ends_near(cond_below, cond_above, cond_edges[...])
    slab = lane // HALO
    keep_x = jnp.where(
        slab == HALO - 1, flags[X_LOW], jnp.where(slab == last - 1, flags[X_HIGH], 1)
    ).astype(F32)
    layer = lane % HALO
    for s, here in enumerate((cond_below, cond_above)):
        up, low = weight(here, near[2 * s]), weight(here, near[2 * s + 1])
        if s == 0:
            up = up * jnp.where(layer == HALO - 1, keep_low, 1.0)
        else:
            low = low * jnp.where(layer == 0, keep_high, 1.0)
        face_x = keep_x * weight(here, turned(here, -HALO, 1))
        face_y = keep_y * weight(here, turned(here, -1, 0))
        ex[s, span], ey[s, span], ez_up[s, span], ez_low[s, span] = face_x, face_y, up, low
        total = absorb_ends[s] + face_x + turned(face_x, HALO, 1) + face_y + turned(face_y, 1, 0) + up + low
        inverse = OMEGA_FINE / total
        inv_ends[s, span] = inverse
        start_ends[s, span] = inverse * rhs_ends[s]

    end_low, end_high = ez_up[0, span], ez_low[1, span]
    join_faces = joined(end_low, end_high)

    def first_sweep(xs, edges):
        stores = []
        for x in xs:
            total = partial[x, span] + at_edges(join_faces, x)
            inverse = OMEGA_FINE / total
            begin = inverse * wide_ref[1, x, span]
            stores.append((x, (total, inverse, begin)))
            edges = edge_step(begin, x, edges)
        for x, values in stores:
            for ref, value in zip((diag, inv_diag, start), values):
                ref[x, span] = value
        return edges

    edges = batched(0, wide, first_sweep, jnp.zeros((tall, LANES), F32), 4)

    join = joined(end_low * start_ends[0, span], end_high * start_ends[1, span])
    near = ends_near(start_ends[0, span], start_ends[1, span], edges)
    for s in range(2):
        total = ends_sum(frame, start_ends, s, near[2 * s], near[2 * s + 1], ex, ey, ez_up, ez_low)
        once_ends[s, span] = (2.0 - OMEGA_FINE) * start_ends[s, span] + inv_ends[s, span] * total

    def second(xs, carry):
        news = []
        for x, here, total in zip(xs, *main_sums(frame, start, xs, join, wx, wy, wz)):
            news.append((2.0 - OMEGA_FINE) * here + inv_diag[x, span] * total)
        for x, new in zip(xs, news):
            once[x, span] = new
        return carry

    batched(HALO - 1, last + 1, second, 0, 13 if (nx + 2) % 13 == 0 else 6)
    join2 = joined(end_low * once_ends[0, span], end_high * once_ends[1, span])

    def remainder(xs, carry):
        news = []
        for x, here, total in zip(xs, *main_sums(frame, once, xs, join2, wx, wy, wz)):
            news.append(wide_ref[1, x, span] - diag[x, span] * here + total)
        for x, new in zip(xs, news):
            res[x - HALO, span] = new
        for x in xs:
            pre[x - HALO] = once[x, pl.ds(frame.own, ny)]
        return carry

    batched(HALO, last, remainder, 0, 8)

    nb, half = nx // 2, ny // 2

    def rows_at(ref, x, off):
        return ref[x, pl.ds(frame.own + off, half, stride=2)]

    def to_blocks(bs, carry):
        for b in bs:
            four = sum(rows_at(res, 2 * b + a, c) for a in range(2) for c in range(2))
            block_res[b] = pack_rows(paired(four))
        return carry

    batched(0, nb, to_blocks, 0)
    zeros = jnp.zeros((AGG, LANES), F32)
    sums = lax.fori_loop(0, nb, lambda b, total: add_rows(total, block_label, b, block_res, b), zeros)

    lane = lane_no((half, LANES))
    around = zeros
    for s, (ref, side, layer_at) in enumerate(((ez_up, 0, HALO - 1), (ez_low, 1, 0))):
        values = rows_at(ref, side, 0) + rows_at(ref, side, 1)
        values = values + turned(values, -HALO, 1)
        spot = jnp.minimum(2 * HALO * lane + HALO * HALO + layer_at, LANES - 1)
        face_weight[s, :2] = pack_lanes(jnp.where(lane < nb, picked(values, spot), 0.0))
        around = add_rows(around, face_label, 4 + s, face_weight, s, 2)
    scale[...] = OMEGA_COARSE / (some_diag[...] + lane_total(around))
    scaled_rhs[...] = scale[...] * lane_total(sums)


def tile_sum(tile, rows, label_at, pairs_at, group=4):
    iota = row_no((AGG, LANES)).astype(F32)
    for first in range(0, rows, group):
        places, highs, lows = [], [], []
        for r in range(first, min(first + group, rows)):
            places.append(jnp.where(label_at(r) == iota, 1.0, 0.0).astype(BF16))
            held = sum(jnp.where(near == iota, w, 0.0) for near, w in pairs_at(r))
            highs.append(held.astype(BF16))
            lows.append((held - highs[-1].astype(F32)).astype(BF16))
        left = jnp.concatenate(places, axis=1)
        right = jnp.concatenate([jnp.concatenate(highs, axis=1), jnp.concatenate(lows, axis=1)], axis=0)
        tile = tile + lax.dot_general(left, right, (((1,), (1,)), ((), ())), preferred_element_type=F32)
    return tile


def both_halves(tile):
    return tile[:, :AGG] + tile[:, AGG:]


def keep_tile(out, t, tile):
    high = tile.astype(BF16)
    rows = pl.ds(t * AGG, AGG)
    out[rows, :AGG] = high
    out[rows, AGG:] = (tile - high.astype(F32)).astype(BF16)


def blocks_kernel(flags, cond, absorb, block_agg, _, block_label, near, weights, inner, face_label, fine_label,
                  part, line):
    nx, ny = cond.shape[0], cond.shape[1]
    nb, half, width = nx // 2, ny // 2, LANES // 2
    lane, row = lane_no((half, LANES)), row_no((half, LANES))

    def halves(values, slot):
        part[slot] = values
        return part[slot, pl.ds(0, half, stride=2)], part[slot, pl.ds(1, half, stride=2)]

    def label_at(b):
        values = block_agg[b].astype(F32)
        return jnp.concatenate([values, values], axis=1)

    def upper_x(b, slot):
        x = jnp.maximum(2 * b, 0)
        faces = weight(cond[x + 1], cond[jnp.minimum(x + 2, nx - 1)])
        return jnp.where((b == nb - 1) | (b < 0), 0.0, paired(sum(halves(faces, slot))))

    def step(bs, carry):
        low_x = upper_x(bs[0] - 1, 0)
        for k, b in enumerate(bs):
            x = 2 * b
            slot = 4 * k + 1
            one, two = cond[x], cond[x + 1]
            both_y = weight(one, turned(one, -1, 0)) + weight(two, turned(two, -1, 0))
            both_z = weight(one, turned(one, -1, 1)) + weight(two, turned(two, -1, 1))
            high_x = upper_x(b, slot)
            high_y = jnp.where(row == half - 1, 0.0, paired(halves(both_y, slot + 1)[1]))
            high_z = picked(sum(halves(both_z, slot + 2)), 2 * (lane % width) + 1)
            high_z = jnp.where(lane % width == width - 1, 0.0, high_z)
            low_y, low_z = turned(high_y, 1, 0), turned(high_z, 1, 1)
            own = label_at(b)
            near_x, past_x = label_at(jnp.minimum(b + 1, nb - 1)), label_at(jnp.maximum(b - 1, 0))
            near_y, past_y = turned(own, -1, 0), turned(own, 1, 0)
            near_z, past_z = turned(own, -1, 1), turned(own, 1, 1)
            total = paired(sum(halves(absorb[x] + absorb[x + 1], slot + 3)))
            for beside, values in (
                (near_x, high_x), (past_x, low_x), (near_y, high_y), (past_y, low_y), (near_z, high_z), (past_z, low_z)
            ):
                total = total + jnp.where(beside != own, values, 0.0)
            block_label[b] = pack_rows(own)
            inner[b] = pack_rows(total)
            for d, (beside, values) in enumerate(((near_x, high_x), (near_y, high_y), (near_z, high_z))):
                near[d, b], weights[d, b] = pack_rows(beside), pack_rows(values)
            spread = picked(own, lane // 2)
            for a in range(2):
                for c in range(2):
                    fine_label[x + a, pl.ds(c, half, stride=2)] = spread
            low_x = high_x
        return carry

    batched(0, nb, step, 0, 4)
    line[...] = jnp.zeros(line.shape, F32)
    low, high = jnp.zeros((half, LANES), F32), jnp.zeros((half, LANES), F32)
    for b in range(nb):
        own = label_at(b)
        line[0, b : b + 1], line[1, b : b + 1] = own[:1], own[half - 1 :]
        low = jnp.where(lane == b, own[:, :1], low)
        high = jnp.where(lane == b, own[:, width - 1 : width], high)
    face_label[0], face_label[1] = block_label[0], block_label[nb - 1]
    for s in range(2):
        face_label[2 + s, : nb // 2] = pack_rows(line[s, :nb])
        face_label[4 + s, :2] = pack_lanes((low, high)[s])


def own_kernel(first, last, total, flags, block_label, near, weights, inner, *refs):
    so_far, refs = (refs[0], refs[1:]) if first else (None, refs)
    refs = refs[1:]

    def step(b, tile):
        def pairs_at(r):
            return [(near[d, b, pl.ds(r, 1)], weights[d, b, pl.ds(r, 1)]) for d in range(3)]

        return tile_sum(tile, SUB, lambda r: block_label[b, pl.ds(r, 1)], pairs_at)

    tile = so_far[...] if first else jnp.zeros((AGG, 2 * AGG), F32)
    tile = lax.fori_loop(first, last, step, tile)
    if last < total:
        refs[0][...] = tile
        return
    out, inner_diag = refs
    tile = both_halves(tile)
    keep_tile(out, 0, jnp.where(row_no((AGG, AGG)) == lane_no((AGG, AGG)), 0.0, tile + tile.T))
    around = jnp.zeros((AGG, LANES), F32)
    around = lax.fori_loop(0, total, lambda b, around: add_rows(around, block_label, b, inner, b), around)
    inner_diag[...] = lane_total(around)


def faces_kernel(count, nb, flags, own, face_label, weight_xy, weight_z, x_low, x_high, inner, outer, forth, back, out,
                 near, weights):
    out[:AGG] = own[...]
    at, half = x_low.shape[0] - 1, x_low.shape[1] // 2
    near[0], near[1] = pack_rows(x_low[at, :half]), pack_rows(x_high[at, :half])
    at = inner.shape[0] - half
    for s, values in enumerate(sides(flags, outer[at:], inner[at:])):
        near[2 + s, : nb // 2] = pack_rows(values[:nb])
    at = forth.shape[0] - half
    for s, values in enumerate(sides(flags, forth[at:], back[at:])):
        near[4 + s, :2] = pack_lanes(values)
    weights[:4], weights[4:] = weight_xy[...], weight_z[...]
    for t, (s, rows) in enumerate(face_rows(count, flags, nb)):
        tile = tile_sum(
            jnp.zeros((AGG, 2 * AGG), F32),
            rows,
            lambda r, s=s: near[s, pl.ds(r, 1)],
            lambda r, s=s: [(face_label[s, pl.ds(r, 1)], weights[s, pl.ds(r, 1)])],
        )
        keep_tile(out, t + 1, both_halves(tile))


def turn_kernel(flags, tiles, scaled_rhs, scale, own, *refs):
    forth, back, *others, out = refs
    got = [ref[ref.shape[0] - 1, :SUB] if len(ref.shape) == 3 else ref[ref.shape[0] - SUB :] for ref in (*others, forth, back)]
    vectors = [own[...], *got[:-2], *sides(flags, *got[-2:])]
    row = row_no((SUB, AGG))
    parts = []
    for v in vectors:
        high = v.astype(BF16).astype(F32)
        parts.append(jnp.where(row == 0, high, jnp.where(row == 1, v - high, 0.0)).astype(BF16))
    got = jnp.dot(jnp.concatenate(parts, axis=1), tiles[...], preferred_element_type=F32)
    applied = jnp.sum(got[:, :AGG] + got[:, AGG:], axis=0, keepdims=True)
    out[...] = (1.0 - OMEGA_COARSE) * own[...] + scaled_rhs[...] + scale[...] * applied


def ride_kernel(count, flags, pre, fine_label, coarse, *outs):
    nx = pre.shape[0]
    for s, out in enumerate(outs):
        at = jnp.where(flags[IX] == 0, nx - HALO, 0) if count == 2 else (nx - HALO, 0)[s]
        for f, field in enumerate((pre, fine_label)):
            for x in range(HALO):
                out[HALO * f + x] = field[at + x]
        out[2 * HALO] = jnp.zeros(out.shape[1:], F32)
        out[2 * HALO, :SUB] = coarse[...]


def three_kernel(flags, low, mid, high, out):
    row = row_no(out.shape)
    out[...] = jnp.where(row == 0, low[...], jnp.where(row == 1, mid[...], high[...]))


def nine_kernel(flags, low, mid, high, out):
    out[...] = jnp.zeros(out.shape, F32)
    for n, ref in enumerate((low, mid, high)):
        out[3 * n : 3 * n + 3] = ref[:3]


def lift_kernel(flags, wide_ref, forth, back, main, ends):
    frame = Frame(wide_ref.shape[1] - 2 * HALO, wide_ref.shape[2] - 2 * (SUB + HALO))
    tall = frame.tall
    for b in range(frame.wide // 2):
        main[b] = wide_ref[1, 2 * b, frame.span].astype(jnp.int32)
    rows = pl.ds(tall, tall)
    for s, values in enumerate(sides(flags, forth[rows], back[rows])):
        ends[s] = values.astype(jnp.int32)


def post_kernel(flags, table, table_forth, table_back, labels, end_labels, wide_ref, forth, back, *refs):
    (wx, wy, wz, inv_diag, start), ends = refs[:5], refs[5:11]
    out, one, two, one_ends, two_ends, kept_out, sems = refs[11:]
    nx, ny = out.shape[0], out.shape[1]
    frame = Frame(nx, ny)
    wide, tall, span = frame.wide, frame.tall, frame.span
    ex, ey, ez_up, ez_low, inv_ends, start_ends = ends
    for ref in (one_ends, two_ends):
        clear_spares(ref, frame)
    row, lane = row_no((tall, LANES)), lane_no((tall, LANES))
    under, over = sides(flags, table_forth[...], table_back[...])
    tables = {-1: under, 0: table[...], 1: over}

    def table_at(dx, dz):
        low, mid, high = (tables[dz][3 * n + dx + 1 : 3 * n + dx + 2] for n in range(3))
        return jnp.where(row < HALO, low, jnp.where(row < HALO + ny, mid, high))

    for x_from, x_to, dx in ((0, HALO, -1), (HALO, HALO + nx, 0), (HALO + nx, wide, 1)):
        values = table_at(dx, 0)

        def lift(bs, carry, values=values):
            news = [picked(values, labels[b]) for b in bs]
            for b, new in zip(bs, news):
                for a in range(2):
                    two[2 * b + a, span] = wide_ref[0, 2 * b + a, span] + new
            return carry

        batched(x_from // 2, x_to // 2, lift, 0, 4)
    for s, (dz, base) in enumerate(zip((-1, 1), sides(flags, forth[:tall], back[:tall]))):
        below, inside, above = (picked(table_at(dx, dz), end_labels[s]) for dx in (-1, 0, 1))
        spot = lane // HALO
        lifted = jnp.where(spot < HALO, below, jnp.where(spot < HALO + nx, inside, above))
        two_ends[s, span] = base + lifted
    kept = 1.0 - OMEGA_FINE

    def result(at, count):
        rows = pl.ds(at, count)
        return pltpu.make_async_copy(kept_out.at[rows], out.at[rows], sems.at[at // count])

    buffers = ((two, two_ends), (one, one_ends), (two, two_ends), (one, one_ends))
    for s in range(POST):
        src, src_ends = buffers[s]
        join = joined(ez_up[0, span] * src_ends[0, span], ez_low[1, span] * src_ends[1, span])
        final = s == POST - 1
        dst, dst_ends = (None, None) if final else buffers[s + 1]

        def step(xs, edges, src=src, join=join, dst=dst, final=final):
            news = []
            for x, here, total in zip(xs, *main_sums(frame, src, xs, join, wx, wy, wz)):
                news.append(kept * here + start[x, span] + inv_diag[x, span] * total)
                if not final:
                    edges = edge_step(here, x, edges)
            for x, new in zip(xs, news):
                if final:
                    kept_out[x - HALO] = new[HALO : HALO + ny]
                else:
                    dst[x, span] = new
            if final:
                result(xs[0] - HALO, len(xs)).start()
            return edges

        size = 8 if final else 10
        edges = batched(s + 1, wide - s - 1, step, jnp.zeros((tall, LANES), F32), size)
        if not final:
            near = ends_near(src_ends[0, span], src_ends[1, span], edges)
            news = []
            for e in range(2):
                total = ends_sum(frame, src_ends, e, near[2 * e], near[2 * e + 1], ex, ey, ez_up, ez_low)
                news.append(kept * src_ends[e, span] + start_ends[e, span] + inv_ends[e, span] * total)
            dst_ends[0, span], dst_ends[1, span] = news
    for n in range(nx // 8):
        result(8 * n, 8).wait()


def body(links, right_side, conductance, absorption, block_agg):
    nx, ny, nz = right_side.shape
    frame = Frame(nx, ny)
    nb = nx // 2
    n_x = links.sizes[0]
    arrays = (conductance, right_side, absorption, block_agg)
    n_send = 1 if n_x == 2 else 2
    pinned = [pltpu.with_memory_space_constraint(a, pltpu.HBM) for a in arrays]
    hbm = pl.BlockSpec(memory_space=pltpu.HBM)
    x_sends = call(
        functools.partial(pack_x_kernel, n_x, WIDTHS),
        [shaped(sum(WIDTHS) + 1, ny, nz)] * n_send,
        [pltpu.VMEM((n_send, ny // 2, nz // 2), jnp.int32), pltpu.SemaphoreType.DMA((n_send * 4,))],
        in_specs=[hbm] * 4,
    )(*pinned)
    arrays = call(
        load_kernel,
        [jax.ShapeDtypeStruct(a.shape, a.dtype) for a in arrays],
        [pltpu.SemaphoreType.DMA((4,))],
        in_specs=[hbm] * 4 + [VMEM],
    )(*pinned, x_sends[0])
    blocks = (nb, SUB, LANES)
    outs = [shaped(*blocks), shaped(3, *blocks), shaped(3, *blocks), shaped(*blocks), shaped(6, SUB, LANES)]
    outs += [shaped(nx, ny, nz)]
    scratch = [pltpu.VMEM((17, ny, LANES), F32), pltpu.VMEM((2, ny // 2, LANES), F32)]
    *rows, face_label, fine_label = call(blocks_kernel, outs, scratch)(arrays[0], arrays[2], arrays[3], x_sends[0])
    block_label = rows[0]
    bounds = (0, nb * 5 // 12, nb)
    parts = []

    def own_part(p, sent):
        outs = [shaped(AGG, 2 * AGG)]
        if p == 1:
            outs = [jax.ShapeDtypeStruct((AGG, 2 * AGG), BF16), shaped(SUB, AGG)]
        kernel = functools.partial(own_kernel, bounds[p], bounds[p + 1], nb)
        parts.append(call(kernel, outs)(*rows, *(parts[-1] if p else ()), sent))
        return parts[-1]

    first = own_part(0, x_sends[0])
    from_x = links.x(x_sends)
    from_x = lax.optimization_barrier((*from_x, *first))[:-1]

    sends = send_y(WIDTHS, arrays[:3], arrays[3], from_x, False)
    frames = framed(WIDTHS, arrays[:3], from_x, sends[0])
    own_tile, inner_diag = own_part(1, sends[0])
    from_y = links.y(*sends)
    *from_y, own_tile, inner_diag = lax.optimization_barrier((*from_y, own_tile, inner_diag))
    wide, *sends = send_z(WIDTHS, frames, from_y, arrays[3], False)
    outs = [shaped(*frame.main)] * 4 + [shaped(frame.tall, nz), shaped(4, SUB, LANES), shaped(SUB, AGG)]
    *fields, weight_xy, some_diag = call(functools.partial(fields_kernel, n_x), outs, limit=24)(
        wide, face_label, inner_diag
    )
    halo = (wide, *links.z(*sends))
    outs = [shaped(*frame.main)] * 2 + [shaped(*frame.ends)] * 6 + [shaped(nx, ny, nz)]
    outs += [shaped(2, SUB, LANES)] + [shaped(SUB, AGG)] * 2
    scratch = [pltpu.VMEM(frame.main, F32), pltpu.VMEM(frame.ends, F32), pltpu.VMEM((nx, frame.rows, LANES), F32)]
    scratch += [pltpu.VMEM(frame.main, F32), pltpu.VMEM(blocks, F32)]
    got = call(fine_kernel, outs, scratch, limit=28)(
        *halo, *fields, block_label, face_label, some_diag
    )
    fields, pre = (*fields[:3], *got[:8]), got[8]
    weight_z, scaled_rhs, scale = got[9:]
    tiles = call(
        functools.partial(faces_kernel, n_x, nb),
        jax.ShapeDtypeStruct(((n_send + 5) * AGG, 2 * AGG), BF16),
        [pltpu.VMEM((6, SUB, LANES), F32)] * 2,
    )(own_tile, face_label, weight_xy, weight_z, from_x[0], from_x[-1], *from_y, *halo[1:])
    coarse = scaled_rhs

    def turn(**more):
        near = links.near(coarse, **more)
        return call(turn_kernel, shaped(SUB, AGG))(tiles, scaled_rhs, scale, coarse, *near), near

    widths, both = (HALO, HALO), (pre, fine_label)
    rides = call(functools.partial(ride_kernel, n_x), [shaped(2 * HALO + 1, ny, nz)] * n_send)(*both, coarse)
    coarse, near = turn(x=rides)
    from_x = near[2:-2]
    rides = send_y(widths, both, coarse, from_x, True)
    frames = framed(widths, both, from_x, rides[0])
    coarse, near = turn(y=rides)
    wide, *rides = send_z(widths, frames, near[-2:], coarse, True)
    coarse, near = turn(z=rides)
    halo = (wide, *near[:2])
    outs = [jax.ShapeDtypeStruct((frame.wide // 2, frame.tall, nz), jnp.int32)]
    outs += [jax.ShapeDtypeStruct((2, frame.tall, nz), jnp.int32)]
    lifts = call(lift_kernel, outs)(*halo)
    for _ in range(KC - 4):
        coarse, _ = turn()
    from_x = links.x([coarse] * n_send)
    three = call(three_kernel, shaped(SUB, AGG))(from_x[0], coarse, from_x[-1])
    low, high = links.ring_y(three, three)
    nine = call(nine_kernel, shaped(2 * SUB, AGG))(low, three, high)
    tables = (nine, *links.z(nine, nine))
    scratch = [pltpu.VMEM(frame.main, F32)] * 2 + [pltpu.VMEM(frame.ends, F32)] * 2
    scratch += [pltpu.VMEM((nx, ny, nz), F32), pltpu.SemaphoreType.DMA((nx // 8,))]
    return call(post_kernel, shaped(nx, ny, nz), scratch, limit=24, out_specs=pl.BlockSpec(memory_space=pl.ANY))(
        *tables, *lifts, *halo, *fields
    )


def solution(mesh):
    spec = P("gx", "gy", "gz")
    return jax.shard_map(
        functools.partial(body, Links(mesh)), mesh=mesh, in_specs=(spec,) * 4, out_specs=spec, check_vma=False
    )
```

```python
import functools

import jax
import jax.numpy as jnp
from jax import lax
from jax.experimental import pallas as pl
from jax.experimental.pallas import tpu as pltpu
from jax.sharding import PartitionSpec as P

AGG = 128
LANES = 128
SUB = 8
HALO = 4
WIDTHS = (4, 3, 3)
POST = 4
KC = 8
OMEGA_FINE = 0.8
OMEGA_COARSE = 0.7
F32 = jnp.float32
BF16 = jnp.bfloat16
VMEM = pl.BlockSpec(memory_space=pltpu.VMEM)
IX, PARITY, X_LOW, X_HIGH, Y_LOW, Y_HIGH, Z_LOW, Z_HIGH = range(8)


def places():
    (ix, n_x), (iy, n_y), (iz, n_z) = ((lax.axis_index(a), lax.axis_size(a)) for a in ("gx", "gy", "gz"))
    flags = [ix, iy % 2, ix > 0, ix < n_x - 1, iy > 0, iy < n_y - 1, iz > 0, iz < n_z - 1]
    return [jnp.asarray(flag, jnp.int32) for flag in flags]


def call(kernel, outs, scratch=(), limit=16, flops=10**6, in_specs=None, aliases=None, out_specs=None):
    def placed(*refs):
        kernel(places(), *refs)

    def run(*arrays):
        return pl.pallas_call(
            placed,
            out_shape=outs,
            in_specs=in_specs or [VMEM] * len(arrays),
            out_specs=out_specs or jax.tree.map(lambda _: VMEM, outs),
            scratch_shapes=list(scratch),
            input_output_aliases=aliases or {},
            compiler_params=pltpu.CompilerParams(vmem_limit_bytes=limit * 2**20),
            cost_estimate=pl.CostEstimate(flops=flops, bytes_accessed=10**5, transcendentals=0),
        )(*arrays)

    return run


def shaped(*shape):
    return jax.ShapeDtypeStruct(shape, F32)


def lane_no(shape):
    return lax.broadcasted_iota(jnp.int32, shape, len(shape) - 1)


def row_no(shape):
    return lax.broadcasted_iota(jnp.int32, shape, len(shape) - 2)


def turned(values, shift, axis):
    if isinstance(shift, int):
        shift = shift % values.shape[axis]
        if shift == 0:
            return values
    return pltpu.roll(values, shift, axis)


def batched(low, high, step, carry, size=6):
    def some(i, carry):
        return step([low + i * size + k for k in range(size)], carry)

    carry = lax.fori_loop(0, (high - low) // size, some, carry)
    rest = (high - low) % size
    return step(list(range(high - rest, high)), carry) if rest else carry


def picked(values, index):
    return jnp.take_along_axis(values, index, axis=1, mode="promise_in_bounds")


class Frame:
    def __init__(self, nx, ny):
        self.nx, self.ny = nx, ny
        self.wide, self.tall = nx + 2 * HALO, ny + 2 * HALO
        self.rows = self.tall + 2 * SUB
        self.span = pl.ds(SUB, self.tall)
        self.own = SUB + HALO
        self.main = (self.wide, self.rows, LANES)
        self.ends = (2, self.rows, LANES)


def bases(widths):
    return [sum(widths[:f]) for f in range(len(widths) + 1)]


def copied(pairs, sems):
    copies = [pltpu.make_async_copy(src, dst, sems.at[n]) for n, (src, dst) in enumerate(pairs)]
    for copy in copies:
        copy.start()
    return copies


def pack_kernel(count, widths, flags, *refs):
    fields = len(widths)
    n_x = 1 if count == 2 else 2
    ins, kept = refs[: fields + 1], refs[fields + 1 : 2 * fields + 2]
    outs, sems = refs[2 * fields + 2 : -1], refs[-1]
    x_outs, y_outs, corner_outs = outs[:n_x], outs[n_x : n_x + 2], outs[n_x + 2 :]
    nx, ny = ins[0].shape[0], ins[0].shape[1]
    nb, half, width = ins[-1].shape
    thirds = 3
    copies = []
    for ref, out in zip(ins, kept):
        for t in range(thirds):
            size = ref.shape[0] // thirds
            rows = pl.ds(t * size, size)
            copies.append(pltpu.make_async_copy(ref.at[rows], out.at[rows], sems.at[len(copies)]))
    for copy in copies:
        copy.start()
    for out in (*x_outs, *y_outs):
        out[...] = jnp.zeros(out.shape, F32)
    for copy in copies:
        copy.wait()
    base = bases(widths)
    labels = kept[-1]
    for s, out in enumerate(x_outs):

        def place(size, thick, s=s):
            if count == 2:
                return jnp.where(flags[IX] == 0, size - thick, 0)
            return (size - thick, 0)[s]

        for f, thick in enumerate(widths):
            at = place(nx, thick)
            for k in range(thick):
                slab = kept[f][at + k]
                out[base[f] + k] = slab
                row = (sum(w * w for w in widths[:f])) + k * thick
                corner_outs[2 * s][row : row + thick] = slab[ny - thick :]
                corner_outs[2 * s + 1][row : row + thick] = slab[:thick]
        out[base[-1], :half, :width] = labels[place(nb, 1)].astype(F32)
    for out, high in zip(y_outs, (True, False)):
        for f, thick in enumerate(widths):
            for x in range(nx):
                row = base[f] * nx + x * thick
                out[row : row + thick] = kept[f][x, ny - thick :] if high else kept[f][x, :thick]
        row = base[-1] * nx
        for b in range(nb):
            line = labels[b, half - 1 :] if high else labels[b, :1]
            out[row + b : row + b + 1, :width] = line.astype(F32)


def slab_of(own, low, high, base, width, x):
    nx = own.shape[0]
    if HALO <= x < HALO + nx:
        return own[x - HALO]
    if x < HALO:
        at = x - (HALO - width)
        return low[base + at] if at >= 0 else None
    at = x - HALO - nx
    return high[base + at] if at < width else None


def pack_y_kernel(fields, flags, *refs):
    ins, rider = refs[:fields], refs[fields]
    low, high, to_high, to_low = refs[fields + 1 :]
    nx, ny = ins[0].shape[0], ins[0].shape[1]
    wide = nx + 2 * HALO
    for f in range(fields):
        for x in range(wide):
            slab = slab_of(ins[f], low, high, HALO * f, HALO, x)
            at = (f * wide + x) * HALO
            to_high[at : at + HALO] = slab[ny - HALO :]
            to_low[at : at + HALO] = slab[:HALO]
    at = fields * wide * HALO
    to_high[at:], to_low[at:] = rider[...], rider[...]


def packed_lanes(wide_ref, f, frame, rows, to_high, to_low):
    group = lane_no((1, LANES)) // HALO
    nothing = jnp.ones((rows.size, LANES), F32)
    high, low = nothing, nothing
    for x in range(frame.wide):
        moved = turned(wide_ref[f, x, rows], HALO * (x + 1), 1)
        high = jnp.where(group == x, moved, high)
        low = jnp.where(group == (x + 1) % frame.wide, moved, low)
    at = pl.ds(f * frame.tall + rows.start - SUB, rows.size)
    to_high[at] = high
    to_low[at] = turned(low, -HALO, 1)


def first_frame_kernel(count, widths, flags, *refs):
    fields = len(widths)
    ins, labels, refs = refs[:fields], refs[fields], refs[fields + 1 :]
    x_low, x_high, y_low, y_high = refs[:4]
    corners = refs[4:6] * 2 if count == 2 else refs[4:8]
    wide_ref, send_forth, send_back, to_high, to_low = refs[-5:]
    nx, ny = ins[0].shape[0], ins[0].shape[1]
    frame = Frame(nx, ny)
    base = bases(widths)
    tall, own = frame.tall, frame.own
    even = flags[PARITY] == 0
    ones = jnp.ones((frame.rows, LANES), F32)
    for f, thick in enumerate(widths):
        for x in range(frame.wide):
            slab = slab_of(ins[f], x_low, x_high, base[f], thick, x)
            if slab is None:
                wide_ref[f, x] = ones
                continue
            edge = ones[: SUB + HALO]
            wide_ref[f, x, :own] = edge
            wide_ref[f, x, own + ny :] = edge
            wide_ref[f, x, own : own + ny] = slab
            if HALO <= x < HALO + nx:
                low, high, row = y_low, y_high, base[f] * nx + (x - HALO) * thick
            else:
                above = x >= HALO
                low, high = corners[2 * above : 2 * above + 2]
                at = x - HALO - nx if above else x - (HALO - thick)
                row = sum(w * w for w in widths[:f]) + at * thick
            wide_ref[f, x, own - thick : own] = low[row : row + thick]
            wide_ref[f, x, own + ny : own + ny + thick] = high[row : row + thick]
        packed_lanes(wide_ref, f, frame, pl.ds(SUB, tall), to_high, to_low)
    high, low = to_high[...], to_low[...]
    size = fields * tall
    send_forth[:size], send_back[:size] = jnp.where(even, high, low), jnp.where(even, low, high)
    nb, rows, width = labels.shape
    lane = lane_no((rows, LANES))
    high = low = jnp.zeros((rows, LANES), F32)
    for b in range(nb):
        slab = labels[b].astype(F32)
        high = jnp.where(lane == b, slab[:, width - 1 :], high)
        low = jnp.where(lane == b, slab[:, :1], low)
    send_forth[size:], send_back[size:] = jnp.where(even, high, low), jnp.where(even, low, high)


def frame_kernel(fields, flags, *refs):
    ins = refs[:fields]
    x_low, x_high, _ = refs[fields : fields + 3]
    wide_ref, to_high, to_low = refs[fields + 3 :]
    nx, ny = ins[0].shape[0], ins[0].shape[1]
    frame = Frame(nx, ny)
    spare = jnp.ones((SUB, LANES), F32)
    for f in range(fields):
        for x in range(frame.wide):
            wide_ref[f, x, frame.own : frame.own + ny] = slab_of(ins[f], x_low, x_high, HALO * f, HALO, x)
            wide_ref[f, x, :SUB] = spare
            wide_ref[f, x, SUB + frame.tall :] = spare
        packed_lanes(wide_ref, f, frame, pl.ds(2 * SUB, frame.tall - 2 * SUB), to_high, to_low)


def pack_z_kernel(fields, flags, wide_in, high_in, low_in, from_low, from_high, rider, *refs):
    wide_ref, send_forth, send_back, to_high, to_low = refs
    frame = Frame(wide_ref.shape[1] - 2 * HALO, wide_ref.shape[2] - 2 * (SUB + HALO))
    ny, tall, own = frame.ny, frame.tall, frame.own
    even = flags[PARITY] == 0
    for f in range(fields):
        for x in range(frame.wide):
            at = (f * frame.wide + x) * HALO
            wide_ref[f, x, SUB:own] = from_low[at : at + HALO]
            wide_ref[f, x, own + ny : own + ny + HALO] = from_high[at : at + HALO]
    size = fields * tall
    to_high[...], to_low[...] = high_in[...], low_in[...]
    for f in range(fields):
        for start in (SUB, tall):
            packed_lanes(wide_ref, f, frame, pl.ds(start, SUB), to_high, to_low)
    high, low = to_high[...], to_low[...]
    send_forth[:size], send_back[:size] = jnp.where(even, high, low), jnp.where(even, low, high)
    send_forth[size:], send_back[size:] = rider[...], rider[...]


class Links:
    def __init__(self, mesh):
        self.sizes = [mesh.shape[a] for a in ("gx", "gy", "gz")]
        n_x, n_y, n_z = self.sizes

        def at(i, j, k):
            return (i % n_x * n_y + j % n_y) * n_z + k

        every = [(i, j, k) for i in range(n_x) for j in range(n_y) for k in range(n_z)]
        self.ring_x = [(i, (i + 1) % n_x) for i in range(n_x)]
        self.corner = {d: [(at(i, j, k), at(i + d, j + 1, k)) for i, j, k in every] for d in (1, -1)}
        self.snake = []
        for i in range(n_x):
            for j in range(0, n_y, 2):
                nodes = [at(i, j, k) for k in range(n_z)] + [at(i, j + 1, k) for k in reversed(range(n_z))]
                self.snake += [(nodes[m], nodes[(m + 1) % len(nodes)]) for m in range(len(nodes))]

    @staticmethod
    def back(pairs):
        return [(b, a) for a, b in pairs]

    @staticmethod
    def send(values, pairs):
        return lax.ppermute(values, ("gx", "gy", "gz"), pairs)

    def x(self, sends):
        if self.sizes[0] == 2:
            return (lax.ppermute(sends[0], "gx", self.ring_x),)
        return lax.ppermute(sends[0], "gx", self.ring_x), lax.ppermute(sends[1], "gx", self.back(self.ring_x))

    def near(self, values, x=None, y=None, z=None):
        forth, back = self.z(*(z or (values, values)))
        from_x = self.x(x or (values, values))
        return (forth, back, *from_x, *self.ring_y(*(y or (values, values))))

    def ring_y(self, to_high, to_low):
        ring = [(j, (j + 1) % self.sizes[1]) for j in range(self.sizes[1])]
        return lax.ppermute(to_high, "gy", ring), lax.ppermute(to_low, "gy", self.back(ring))

    def corners(self, sends):
        if self.sizes[0] == 2:
            return self.send(sends[0], self.corner[1]), self.send(sends[1], self.back(self.corner[1]))
        return (
            self.send(sends[0], self.corner[1]),
            self.send(sends[1], self.back(self.corner[-1])),
            self.send(sends[2], self.corner[-1]),
            self.send(sends[3], self.back(self.corner[1])),
        )

    def z(self, forth, back):
        return self.send(forth, self.snake), self.send(back, self.back(self.snake))


def send_y(arrays, rider, from_x):
    nx, ny, nz = arrays[0].shape
    rows = len(arrays) * Frame(nx, ny).wide * HALO + SUB
    kernel = functools.partial(pack_y_kernel, len(arrays))
    return call(kernel, [shaped(rows, nz)] * 2)(*arrays, rider, from_x[0], from_x[-1])


def framed(arrays, from_x, sent):
    nx, ny, nz = arrays[0].shape
    frame, fields = Frame(nx, ny), len(arrays)
    outs = [shaped(fields, *frame.main)] + [shaped(fields * frame.tall, nz)] * 2
    return call(functools.partial(frame_kernel, fields), outs)(*arrays, from_x[0], from_x[-1], sent)


def send_z(frames, from_y, rider):
    wide, high, _ = frames
    return call(
        functools.partial(pack_z_kernel, wide.shape[0]),
        [shaped(*wide.shape)] + [shaped(high.shape[0] + SUB, LANES)] * 2,
        [pltpu.VMEM(high.shape, F32)] * 2,
        aliases={0: 0},
    )(*frames, *from_y, rider)


def sides(flags, forth, back):
    even = flags[PARITY] == 0
    return jnp.where(even, forth, back), jnp.where(even, back, forth)


def weight(one, two):
    return 2.0 * (one * two) / (one + two)


def lane_mask(x):
    return ((lane_no((1, LANES)) - (HALO * x + HALO - 1)) & (LANES - 1)) < 2


def edge_step(here, x, edges):
    return jnp.where(lane_mask(x), turned(here, HALO * x + HALO, 1), edges)


def joined(below, above):
    lane = lane_no((1, LANES))
    return jnp.where(lane % HALO == HALO - 1, turned(above, HALO - 1, 1), turned(below, 1, 1))


def at_edges(join, x):
    lane = lane_no((1, LANES))
    return jnp.where((lane == 0) | (lane == LANES - 1), turned(join, (LANES - HALO) - HALO * x, 1), 0.0)


def ends_near(below, above, edges):
    layer = lane_no((1, LANES)) % HALO
    return (
        jnp.where(layer == HALO - 1, turned(edges, -1, 1), turned(below, -1, 1)),
        turned(below, 1, 1),
        turned(above, -1, 1),
        jnp.where(layer == 0, turned(edges, 1 - HALO, 1), turned(above, 1, 1)),
    )


def main_sums(frame, field, xs, join, wx, wy, wz):
    span = frame.span
    slabs = [field[xs[0] - 1 + k, span] for k in range(len(xs) + 2)]
    faces = [wx[xs[0] - 1 + k, span] for k in range(len(xs) + 1)]
    totals = []
    for k, x in enumerate(xs):
        here, face_y, face_z = slabs[k + 1], wy[x, span], wz[x, span]
        total = faces[k + 1] * slabs[k + 2] + faces[k] * slabs[k]
        total = total + face_y * turned(here, -1, 0) + turned(face_y * here, 1, 0)
        total = total + face_z * turned(here, -1, 1) + turned(face_z * here, 1, 1)
        totals.append(total + at_edges(join, x))
    return slabs[1:-1], totals


def ends_sum(frame, ends, s, upper, lower, wx, wy, wz_up, wz_low):
    span, down = frame.span, pl.ds(SUB - 1, frame.tall)
    here = ends[s, span]
    total = wx[s, span] * turned(here, -HALO, 1) + turned(wx[s, span] * here, HALO, 1)
    total = total + wy[s, span] * ends[s, pl.ds(SUB + 1, frame.tall)] + wy[s, down] * ends[s, down]
    return total + wz_up[s, span] * upper + wz_low[s, span] * lower


def clear_spares(ref, frame):
    for x in range(ref.shape[0]):
        ref[x, :SUB] = jnp.zeros((SUB, LANES), F32)
        ref[x, SUB + frame.tall :] = jnp.zeros((SUB, LANES), F32)


def pack_rows(values):
    half = values.shape[0] // 2
    lane = lane_no((half, LANES))
    return jnp.where(lane < LANES // 2, values[:half], turned(values[half:], LANES // 2, 1))


def lane_total(values):
    return jnp.broadcast_to(jnp.sum(values.T, axis=0, keepdims=True), (SUB, LANES))


def paired(values):
    even = 2 * (lane_no(values.shape) % (LANES // 2))
    return picked(values + turned(values, -1, 1), even)


def faces_y_kept(flags, frame):
    row = row_no((frame.tall, LANES))
    at_low, at_high = row == HALO - 1, row == HALO + frame.ny - 1
    return jnp.where(at_low, flags[Y_LOW], jnp.where(at_high, flags[Y_HIGH], 1)).astype(F32)


def face_rows(count, flags, nb):
    x = [(jnp.where(flags[IX] == 0, 1, 0), SUB)] if count == 2 else [(0, SUB), (1, SUB)]
    return x + [(2, nb // 2), (3, nb // 2), (4, 2), (5, 2)]


def add_rows(total, labels, b, values, c, rows=SUB):
    iota = row_no((AGG, LANES)).astype(F32)
    for r in range(rows):
        row = pl.ds(r, 1)
        total = total + jnp.where(labels[b, row] == iota, values[c, row], 0.0)
    return total


def pack_lanes(values):
    lane = lane_no((2, LANES))
    packed = values[:2]
    for g in range(1, SUB):
        packed = jnp.where(lane // 16 == g, turned(values[2 * g : 2 * g + 2], 16 * g, 1), packed)
    return packed


def fields_kernel(count, flags, wide_ref, block_label, inner, face_label, wx, wy, wz, partial, cond_edges, face_weight, diag):
    frame = Frame(wx.shape[0] - 2 * HALO, wx.shape[1] - 2 * (SUB + HALO))
    wide, tall, span = frame.wide, frame.tall, frame.span
    last = HALO + frame.nx
    keep_y = faces_y_kept(flags, frame)
    inside = jnp.where(lane_no((1, LANES)) == LANES - 1, 0.0, 1.0)

    def fields(xs, carry):
        before, edges = carry
        stores = []
        for x in xs:
            here = wide_ref[0, x, span]
            keep = jnp.where(x == HALO - 1, flags[X_LOW], jnp.where(x == last - 1, flags[X_HIGH], 1)).astype(F32)
            face_x = keep * weight(here, wide_ref[0, jnp.minimum(x + 1, wide - 1), span])
            face_y = keep_y * weight(here, wide_ref[0, x, pl.ds(SUB + 1, tall)])
            face_z = inside * weight(here, turned(here, -1, 1))
            total = wide_ref[2, x, span] + face_x + before + face_y + turned(face_y, 1, 0)
            total = total + face_z + turned(face_z, 1, 1)
            stores.append((x, (face_x, face_y, face_z, total)))
            edges = edge_step(here, x, edges)
            before = face_x
        for x, values in stores:
            for ref, value in zip((wx, wy, wz, partial), values):
                ref[x, span] = value
        return before, edges

    nothing = jnp.zeros((tall, LANES), F32)
    cond_edges[...] = batched(0, wide, fields, (nothing, nothing + 1.0), 4)[1]
    nb, ny = frame.nx // 2, frame.ny
    for s, x in enumerate((HALO - 1, last - 1)):
        rows = [wx[x, pl.ds(frame.own + c, ny // 2, stride=2)] for c in range(2)]
        face_weight[s] = pack_rows(paired(rows[0] + rows[1]))
    for s, at in ((2, frame.own - 1), (3, frame.own + ny - 1)):
        lines = [wy[HALO + 2 * b, at : at + 1] + wy[HALO + 2 * b + 1, at : at + 1] for b in range(nb)]
        face_weight[s, : nb // 2] = pack_rows(paired(jnp.concatenate(lines, axis=0)))
    around = jnp.zeros((AGG, LANES), F32)
    around = lax.fori_loop(0, nb, lambda b, around: add_rows(around, block_label, b, inner, b), around)
    for s, rows in face_rows(count, flags, nb)[:-2]:
        around = add_rows(around, face_label, s, face_weight, s, rows)
    diag[...] = lane_total(around)


def fine_kernel(flags, wide_ref, forth, back, wx, wy, wz, partial, cond_edges, block_label, face_label, some_diag,
                *refs):
    inv_diag, start = refs[:2]
    ends = refs[2:8]
    pre, face_weight, scaled_rhs, scale, once, once_ends, res, diag, block_res = refs[8:]
    ex, ey, ez_up, ez_low, inv_ends, start_ends = ends
    nx, ny = pre.shape[0], pre.shape[1]
    frame = Frame(nx, ny)
    wide, tall, span = frame.wide, frame.tall, frame.span
    last = HALO + nx
    got = [sides(flags, forth[f * tall : (f + 1) * tall], back[f * tall : (f + 1) * tall]) for f in range(3)]
    (cond_below, cond_above), rhs_ends, absorb_ends = got
    for ref in (ey, start_ends, once_ends):
        clear_spares(ref, frame)

    lane = lane_no((1, LANES))
    keep_y = faces_y_kept(flags, frame)
    keep_low, keep_high = flags[Z_LOW].astype(F32), flags[Z_HIGH].astype(F32)
    near = ends_near(cond_below, cond_above, cond_edges[...])
    slab = lane // HALO
    keep_x = jnp.where(
        slab == HALO - 1, flags[X_LOW], jnp.where(slab == last - 1, flags[X_HIGH], 1)
    ).astype(F32)
    layer = lane % HALO
    for s, here in enumerate((cond_below, cond_above)):
        up, low = weight(here, near[2 * s]), weight(here, near[2 * s + 1])
        if s == 0:
            up = up * jnp.where(layer == HALO - 1, keep_low, 1.0)
        else:
            low = low * jnp.where(layer == 0, keep_high, 1.0)
        face_x = keep_x * weight(here, turned(here, -HALO, 1))
        face_y = keep_y * weight(here, turned(here, -1, 0))
        ex[s, span], ey[s, span], ez_up[s, span], ez_low[s, span] = face_x, face_y, up, low
        total = absorb_ends[s] + face_x + turned(face_x, HALO, 1) + face_y + turned(face_y, 1, 0) + up + low
        inverse = OMEGA_FINE / total
        inv_ends[s, span] = inverse
        start_ends[s, span] = inverse * rhs_ends[s]

    end_low, end_high = ez_up[0, span], ez_low[1, span]
    join_faces = joined(end_low, end_high)

    def first_sweep(xs, edges):
        stores = []
        for x in xs:
            total = partial[x, span] + at_edges(join_faces, x)
            inverse = OMEGA_FINE / total
            begin = inverse * wide_ref[1, x, span]
            stores.append((x, (total, inverse, begin)))
            edges = edge_step(begin, x, edges)
        for x, values in stores:
            for ref, value in zip((diag, inv_diag, start), values):
                ref[x, span] = value
        return edges

    edges = batched(0, wide, first_sweep, jnp.zeros((tall, LANES), F32), 4)

    join = joined(end_low * start_ends[0, span], end_high * start_ends[1, span])
    near = ends_near(start_ends[0, span], start_ends[1, span], edges)
    for s in range(2):
        total = ends_sum(frame, start_ends, s, near[2 * s], near[2 * s + 1], ex, ey, ez_up, ez_low)
        once_ends[s, span] = (2.0 - OMEGA_FINE) * start_ends[s, span] + inv_ends[s, span] * total

    def second(xs, carry):
        news = []
        for x, here, total in zip(xs, *main_sums(frame, start, xs, join, wx, wy, wz)):
            news.append((2.0 - OMEGA_FINE) * here + inv_diag[x, span] * total)
        for x, new in zip(xs, news):
            once[x, span] = new
        return carry

    batched(HALO - 1, last + 1, second, 0, 13 if (nx + 2) % 13 == 0 else 6)
    join2 = joined(end_low * once_ends[0, span], end_high * once_ends[1, span])

    def remainder(xs, carry):
        news = []
        for x, here, total in zip(xs, *main_sums(frame, once, xs, join2, wx, wy, wz)):
            news.append(wide_ref[1, x, span] - diag[x, span] * here + total)
        for x, new in zip(xs, news):
            res[x - HALO, span] = new
        for x in xs:
            pre[x - HALO] = once[x, pl.ds(frame.own, ny)]
        return carry

    batched(HALO, last, remainder, 0, 8)

    nb, half = nx // 2, ny // 2

    def rows_at(ref, x, off):
        return ref[x, pl.ds(frame.own + off, half, stride=2)]

    def to_blocks(bs, carry):
        for b in bs:
            four = sum(rows_at(res, 2 * b + a, c) for a in range(2) for c in range(2))
            block_res[b] = pack_rows(paired(four))
        return carry

    batched(0, nb, to_blocks, 0)
    zeros = jnp.zeros((AGG, LANES), F32)
    sums = lax.fori_loop(0, nb, lambda b, total: add_rows(total, block_label, b, block_res, b), zeros)

    lane = lane_no((half, LANES))
    around = zeros
    for s, (ref, side, layer_at) in enumerate(((ez_up, 0, HALO - 1), (ez_low, 1, 0))):
        values = rows_at(ref, side, 0) + rows_at(ref, side, 1)
        values = values + turned(values, -HALO, 1)
        spot = jnp.minimum(2 * HALO * lane + HALO * HALO + layer_at, LANES - 1)
        face_weight[s, :2] = pack_lanes(jnp.where(lane < nb, picked(values, spot), 0.0))
        around = add_rows(around, face_label, 4 + s, face_weight, s, 2)
    scale[...] = OMEGA_COARSE / (some_diag[...] + lane_total(around))
    scaled_rhs[...] = scale[...] * lane_total(sums)


def tile_sum(tile, rows, label_at, pairs_at, group=4):
    iota = row_no((AGG, LANES)).astype(F32)
    for first in range(0, rows, group):
        places, highs, lows = [], [], []
        for r in range(first, min(first + group, rows)):
            places.append(jnp.where(label_at(r) == iota, 1.0, 0.0).astype(BF16))
            held = sum(jnp.where(near == iota, w, 0.0) for near, w in pairs_at(r))
            highs.append(held.astype(BF16))
            lows.append((held - highs[-1].astype(F32)).astype(BF16))
        left = jnp.concatenate(places, axis=1)
        right = jnp.concatenate([jnp.concatenate(highs, axis=1), jnp.concatenate(lows, axis=1)], axis=0)
        tile = tile + lax.dot_general(left, right, (((1,), (1,)), ((), ())), preferred_element_type=F32)
    return tile


def both_halves(tile):
    return tile[:, :AGG] + tile[:, AGG:]


def keep_tile(out, t, tile):
    high = tile.astype(BF16)
    rows = pl.ds(t * AGG, AGG)
    out[rows, :AGG] = high
    out[rows, AGG:] = (tile - high.astype(F32)).astype(BF16)


def blocks_kernel(flags, cond, absorb, block_agg, block_label, near, weights, inner, face_label, fine_label,
                  part, line):
    nx, ny = cond.shape[0], cond.shape[1]
    nb, half, width = nx // 2, ny // 2, LANES // 2
    lane, row = lane_no((half, LANES)), row_no((half, LANES))

    def halves(values, slot):
        part[slot] = values
        return part[slot, pl.ds(0, half, stride=2)], part[slot, pl.ds(1, half, stride=2)]

    def label_at(b):
        values = block_agg[b].astype(F32)
        return jnp.concatenate([values, values], axis=1)

    def upper_x(b, slot):
        x = jnp.maximum(2 * b, 0)
        faces = weight(cond[x + 1], cond[jnp.minimum(x + 2, nx - 1)])
        return jnp.where((b == nb - 1) | (b < 0), 0.0, paired(sum(halves(faces, slot))))

    def step(bs, carry):
        low_x = upper_x(bs[0] - 1, 0)
        for k, b in enumerate(bs):
            x = 2 * b
            slot = 4 * k + 1
            one, two = cond[x], cond[x + 1]
            both_y = weight(one, turned(one, -1, 0)) + weight(two, turned(two, -1, 0))
            both_z = weight(one, turned(one, -1, 1)) + weight(two, turned(two, -1, 1))
            high_x = upper_x(b, slot)
            high_y = jnp.where(row == half - 1, 0.0, paired(halves(both_y, slot + 1)[1]))
            high_z = picked(sum(halves(both_z, slot + 2)), 2 * (lane % width) + 1)
            high_z = jnp.where(lane % width == width - 1, 0.0, high_z)
            low_y, low_z = turned(high_y, 1, 0), turned(high_z, 1, 1)
            own = label_at(b)
            near_x, past_x = label_at(jnp.minimum(b + 1, nb - 1)), label_at(jnp.maximum(b - 1, 0))
            near_y, past_y = turned(own, -1, 0), turned(own, 1, 0)
            near_z, past_z = turned(own, -1, 1), turned(own, 1, 1)
            total = paired(sum(halves(absorb[x] + absorb[x + 1], slot + 3)))
            for beside, values in (
                (near_x, high_x), (past_x, low_x), (near_y, high_y), (past_y, low_y), (near_z, high_z), (past_z, low_z)
            ):
                total = total + jnp.where(beside != own, values, 0.0)
            block_label[b] = pack_rows(own)
            inner[b] = pack_rows(total)
            for d, (beside, values) in enumerate(((near_x, high_x), (near_y, high_y), (near_z, high_z))):
                near[d, b], weights[d, b] = pack_rows(beside), pack_rows(values)
            spread = picked(own, lane // 2)
            for a in range(2):
                for c in range(2):
                    fine_label[x + a, pl.ds(c, half, stride=2)] = spread
            low_x = high_x
        return carry

    batched(0, nb, step, 0, 4)
    line[...] = jnp.zeros(line.shape, F32)
    low, high = jnp.zeros((half, LANES), F32), jnp.zeros((half, LANES), F32)
    for b in range(nb):
        own = label_at(b)
        line[0, b : b + 1], line[1, b : b + 1] = own[:1], own[half - 1 :]
        low = jnp.where(lane == b, own[:, :1], low)
        high = jnp.where(lane == b, own[:, width - 1 : width], high)
    face_label[0], face_label[1] = block_label[0], block_label[nb - 1]
    for s in range(2):
        face_label[2 + s, : nb // 2] = pack_rows(line[s, :nb])
        face_label[4 + s, :2] = pack_lanes((low, high)[s])


def own_kernel(first, last, total, flags, block_label, near, weights, *refs):
    so_far, refs = (refs[0], refs[1:]) if first else (None, refs)
    refs = refs[1:]

    def step(b, tile):
        def pairs_at(r):
            return [(near[d, b, pl.ds(r, 1)], weights[d, b, pl.ds(r, 1)]) for d in range(3)]

        return tile_sum(tile, SUB, lambda r: block_label[b, pl.ds(r, 1)], pairs_at)

    tile = so_far[...] if first else jnp.zeros((AGG, 2 * AGG), F32)
    tile = lax.fori_loop(first, last, step, tile)
    if last < total:
        refs[0][...] = tile
        return
    tile = both_halves(tile)
    keep_tile(refs[0], 0, jnp.where(row_no((AGG, AGG)) == lane_no((AGG, AGG)), 0.0, tile + tile.T))


def faces_kernel(count, nb, flags, own, face_label, weight_xy, weight_z, x_low, x_high, y_low, y_high, forth, back, out,
                 near, weights):
    out[:AGG] = own[...]
    at, half = x_low.shape[0] - 1, x_low.shape[1] // 2
    near[0], near[1] = pack_rows(x_low[at, :half]), pack_rows(x_high[at, :half])
    at = sum(WIDTHS) * 2 * nb
    for s, ref in enumerate((y_low, y_high)):
        near[2 + s, : nb // 2] = pack_rows(ref[at : at + nb])
    at = forth.shape[0] - half
    for s, values in enumerate(sides(flags, forth[at:], back[at:])):
        near[4 + s, :2] = pack_lanes(values)
    weights[:4], weights[4:] = weight_xy[...], weight_z[...]
    for t, (s, rows) in enumerate(face_rows(count, flags, nb)):
        tile = tile_sum(
            jnp.zeros((AGG, 2 * AGG), F32),
            rows,
            lambda r, s=s: near[s, pl.ds(r, 1)],
            lambda r, s=s: [(face_label[s, pl.ds(r, 1)], weights[s, pl.ds(r, 1)])],
        )
        keep_tile(out, t + 1, both_halves(tile))


def turn_kernel(flags, tiles, scaled_rhs, scale, own, *refs):
    forth, back, *others, out = refs
    got = [ref[ref.shape[0] - 1, :SUB] if len(ref.shape) == 3 else ref[ref.shape[0] - SUB :] for ref in (*others, forth, back)]
    vectors = [own[...], *got[:-2], *sides(flags, *got[-2:])]
    row = row_no((SUB, AGG))
    parts = []
    for v in vectors:
        high = v.astype(BF16).astype(F32)
        parts.append(jnp.where(row == 0, high, jnp.where(row == 1, v - high, 0.0)).astype(BF16))
    got = jnp.dot(jnp.concatenate(parts, axis=1), tiles[...], preferred_element_type=F32)
    applied = jnp.sum(got[:, :AGG] + got[:, AGG:], axis=0, keepdims=True)
    out[...] = (1.0 - OMEGA_COARSE) * own[...] + scaled_rhs[...] + scale[...] * applied


def ride_kernel(count, flags, pre, fine_label, coarse, *outs):
    nx = pre.shape[0]
    for s, out in enumerate(outs):
        at = jnp.where(flags[IX] == 0, nx - HALO, 0) if count == 2 else (nx - HALO, 0)[s]
        for f, field in enumerate((pre, fine_label)):
            for x in range(HALO):
                out[HALO * f + x] = field[at + x]
        out[2 * HALO] = jnp.zeros(out.shape[1:], F32)
        out[2 * HALO, :SUB] = coarse[...]


def three_kernel(flags, low, mid, high, out):
    row = row_no(out.shape)
    out[...] = jnp.where(row == 0, low[...], jnp.where(row == 1, mid[...], high[...]))


def nine_kernel(flags, low, mid, high, out):
    out[...] = jnp.zeros(out.shape, F32)
    for n, ref in enumerate((low, mid, high)):
        out[3 * n : 3 * n + 3] = ref[:3]


def lift_kernel(flags, wide_ref, forth, back, main, ends):
    frame = Frame(wide_ref.shape[1] - 2 * HALO, wide_ref.shape[2] - 2 * (SUB + HALO))
    tall = frame.tall
    for b in range(frame.wide // 2):
        main[b] = wide_ref[1, 2 * b, frame.span].astype(jnp.int32)
    rows = pl.ds(tall, tall)
    for s, values in enumerate(sides(flags, forth[rows], back[rows])):
        ends[s] = values.astype(jnp.int32)


def post_kernel(flags, table, table_forth, table_back, labels, end_labels, wide_ref, forth, back, *refs):
    (wx, wy, wz, inv_diag, start), ends = refs[:5], refs[5:11]
    out, one, two, one_ends, two_ends, kept_out, sems = refs[11:]
    nx, ny = out.shape[0], out.shape[1]
    frame = Frame(nx, ny)
    wide, tall, span = frame.wide, frame.tall, frame.span
    ex, ey, ez_up, ez_low, inv_ends, start_ends = ends
    for ref in (one_ends, two_ends):
        clear_spares(ref, frame)
    row, lane = row_no((tall, LANES)), lane_no((tall, LANES))
    under, over = sides(flags, table_forth[...], table_back[...])
    tables = {-1: under, 0: table[...], 1: over}

    def table_at(dx, dz):
        low, mid, high = (tables[dz][3 * n + dx + 1 : 3 * n + dx + 2] for n in range(3))
        return jnp.where(row < HALO, low, jnp.where(row < HALO + ny, mid, high))

    for x_from, x_to, dx in ((0, HALO, -1), (HALO, HALO + nx, 0), (HALO + nx, wide, 1)):
        values = table_at(dx, 0)

        def lift(bs, carry, values=values):
            news = [picked(values, labels[b]) for b in bs]
            for b, new in zip(bs, news):
                for a in range(2):
                    two[2 * b + a, span] = wide_ref[0, 2 * b + a, span] + new
            return carry

        batched(x_from // 2, x_to // 2, lift, 0, 4)
    for s, (dz, base) in enumerate(zip((-1, 1), sides(flags, forth[:tall], back[:tall]))):
        below, inside, above = (picked(table_at(dx, dz), end_labels[s]) for dx in (-1, 0, 1))
        spot = lane // HALO
        lifted = jnp.where(spot < HALO, below, jnp.where(spot < HALO + nx, inside, above))
        two_ends[s, span] = base + lifted
    kept = 1.0 - OMEGA_FINE

    def result(at, count):
        rows = pl.ds(at, count)
        return pltpu.make_async_copy(kept_out.at[rows], out.at[rows], sems.at[at // count])

    buffers = ((two, two_ends), (one, one_ends), (two, two_ends), (one, one_ends))
    for s in range(POST):
        src, src_ends = buffers[s]
        join = joined(ez_up[0, span] * src_ends[0, span], ez_low[1, span] * src_ends[1, span])
        final = s == POST - 1
        dst, dst_ends = (None, None) if final else buffers[s + 1]

        def step(xs, edges, src=src, join=join, dst=dst, final=final):
            news = []
            for x, here, total in zip(xs, *main_sums(frame, src, xs, join, wx, wy, wz)):
                news.append(kept * here + start[x, span] + inv_diag[x, span] * total)
                if not final:
                    edges = edge_step(here, x, edges)
            for x, new in zip(xs, news):
                if final:
                    kept_out[x - HALO] = new[HALO : HALO + ny]
                else:
                    dst[x, span] = new
            if final:
                result(xs[0] - HALO, len(xs)).start()
            return edges

        size = 8 if final else 10
        edges = batched(s + 1, wide - s - 1, step, jnp.zeros((tall, LANES), F32), size)
        if not final:
            near = ends_near(src_ends[0, span], src_ends[1, span], edges)
            news = []
            for e in range(2):
                total = ends_sum(frame, src_ends, e, near[2 * e], near[2 * e + 1], ex, ey, ez_up, ez_low)
                news.append(kept * src_ends[e, span] + start_ends[e, span] + inv_ends[e, span] * total)
            dst_ends[0, span], dst_ends[1, span] = news
    for n in range(nx // 8):
        result(8 * n, 8).wait()


def body(links, right_side, conductance, absorption, block_agg):
    nx, ny, nz = right_side.shape
    frame = Frame(nx, ny)
    nb = nx // 2
    n_x = links.sizes[0]
    arrays = (conductance, right_side, absorption, block_agg)
    n_send = 1 if n_x == 2 else 2
    pinned = [pltpu.with_memory_space_constraint(a, pltpu.HBM) for a in arrays]
    outs = [jax.ShapeDtypeStruct(a.shape, a.dtype) for a in arrays]
    outs += [shaped(sum(WIDTHS) + 1, ny, nz)] * n_send + [shaped(sum(WIDTHS) * nx + 16, nz)] * 2
    outs += [shaped(-(-sum(w * w for w in WIDTHS) // SUB) * SUB, nz)] * (2 * n_send)
    got = call(
        functools.partial(pack_kernel, n_x, WIDTHS),
        outs,
        [pltpu.SemaphoreType.DMA((3 * 4,))],
        in_specs=[pl.BlockSpec(memory_space=pltpu.HBM)] * 4,
    )(*pinned)
    arrays, sends = got[:4], got[4:]
    from_x = links.x(sends[:n_send])
    from_y = links.ring_y(*sends[n_send : n_send + 2])
    from_corners = links.corners(sends[n_send + 2 :])
    blocks = (nb, SUB, LANES)
    outs = [shaped(*blocks), shaped(3, *blocks), shaped(3, *blocks), shaped(*blocks), shaped(6, SUB, LANES)]
    outs += [shaped(nx, ny, nz)]
    scratch = [pltpu.VMEM((17, ny, LANES), F32), pltpu.VMEM((2, ny // 2, LANES), F32)]
    *rows, inner, face_label, fine_label = call(blocks_kernel, outs, scratch)(arrays[0], arrays[2], arrays[3])
    block_label = rows[0]
    bounds = (0, nb * 5 // 12, nb * 10 // 12, nb)

    def own_part(p, *more):
        out = jax.ShapeDtypeStruct((AGG, 2 * AGG), BF16) if p == 2 else shaped(AGG, 2 * AGG)
        return call(functools.partial(own_kernel, bounds[p], bounds[p + 1], nb), [out])(*rows, *more)[0]

    own_tile = own_part(0, sends[0])
    got = lax.optimization_barrier((*from_x, *from_y, *from_corners, own_tile))
    from_x, from_y, from_corners = got[:n_send], got[n_send : n_send + 2], got[n_send + 2 : -1]
    size = len(WIDTHS) * frame.tall
    wide, *sends = call(
        functools.partial(first_frame_kernel, n_x, WIDTHS),
        [shaped(len(WIDTHS), *frame.main)] + [shaped(size + ny // 2, nz)] * 2,
        [pltpu.VMEM((size, nz), F32)] * 2,
    )(*arrays, from_x[0], from_x[-1], *from_y, *from_corners)
    outs = [shaped(*frame.main)] * 4 + [shaped(frame.tall, nz), shaped(4, SUB, LANES), shaped(SUB, AGG)]
    *fields, weight_xy, some_diag = call(functools.partial(fields_kernel, n_x), outs, limit=24)(
        wide, block_label, inner, face_label
    )
    own_tile = own_part(1, own_tile, sends[0])
    halo = (wide, *links.z(*sends))
    *halo, own_tile = lax.optimization_barrier((*halo, own_tile))
    outs = [shaped(*frame.main)] * 2 + [shaped(*frame.ends)] * 6 + [shaped(nx, ny, nz)]
    outs += [shaped(2, SUB, LANES)] + [shaped(SUB, AGG)] * 2
    scratch = [pltpu.VMEM(frame.main, F32), pltpu.VMEM(frame.ends, F32), pltpu.VMEM((nx, frame.rows, LANES), F32)]
    scratch += [pltpu.VMEM(frame.main, F32), pltpu.VMEM(blocks, F32)]
    got = call(fine_kernel, outs, scratch, limit=28)(
        *halo, *fields, block_label, face_label, some_diag
    )
    fields, pre = (*fields[:3], *got[:8]), got[8]
    weight_z, scaled_rhs, scale = got[9:]
    own_tile = own_part(2, own_tile, scaled_rhs)
    tiles = call(
        functools.partial(faces_kernel, n_x, nb),
        jax.ShapeDtypeStruct(((n_send + 5) * AGG, 2 * AGG), BF16),
        [pltpu.VMEM((6, SUB, LANES), F32)] * 2,
    )(own_tile, face_label, weight_xy, weight_z, from_x[0], from_x[-1], *from_y, *halo[1:])
    coarse = scaled_rhs

    def turn(**more):
        near = links.near(coarse, **more)
        return call(turn_kernel, shaped(SUB, AGG))(tiles, scaled_rhs, scale, coarse, *near), near

    both = (pre, fine_label)
    rides = call(functools.partial(ride_kernel, n_x), [shaped(2 * HALO + 1, ny, nz)] * n_send)(*both, coarse)
    coarse, near = turn(x=rides)
    from_x = near[2:-2]
    rides = send_y(both, coarse, from_x)
    frames = framed(both, from_x, rides[0])
    coarse, near = turn(y=rides)
    wide, *rides = send_z(frames, near[-2:], coarse)
    coarse, near = turn(z=rides)
    halo = (wide, *near[:2])
    outs = [jax.ShapeDtypeStruct((frame.wide // 2, frame.tall, nz), jnp.int32)]
    outs += [jax.ShapeDtypeStruct((2, frame.tall, nz), jnp.int32)]
    lifts = call(lift_kernel, outs)(*halo)
    for _ in range(KC - 4):
        coarse, _ = turn()
    from_x = links.x([coarse] * n_send)
    three = call(three_kernel, shaped(SUB, AGG))(from_x[0], coarse, from_x[-1])
    low, high = links.ring_y(three, three)
    nine = call(nine_kernel, shaped(2 * SUB, AGG))(low, three, high)
    tables = (nine, *links.z(nine, nine))
    scratch = [pltpu.VMEM(frame.main, F32)] * 2 + [pltpu.VMEM(frame.ends, F32)] * 2
    scratch += [pltpu.VMEM((nx, ny, nz), F32), pltpu.SemaphoreType.DMA((nx // 8,))]
    return call(post_kernel, shaped(nx, ny, nz), scratch, limit=24, out_specs=pl.BlockSpec(memory_space=pl.ANY))(
        *tables, *lifts, *halo, *fields
    )


def solution(mesh):
    spec = P("gx", "gy", "gz")
    return jax.shard_map(
        functools.partial(body, Links(mesh)), mesh=mesh, in_specs=(spec,) * 4, out_specs=spec, check_vma=False
    )
```

```python
import functools

import jax
import jax.numpy as jnp
from jax import lax
from jax.experimental import pallas as pl
from jax.experimental.pallas import tpu as pltpu
from jax.sharding import PartitionSpec as P

AGG = 128
LANES = 128
SUB = 8
HALO = 4
WIDTHS = (4, 3, 3)
POST = 4
KC = 8
OMEGA_FINE = 0.8
OMEGA_COARSE = 0.7
F32 = jnp.float32
BF16 = jnp.bfloat16
VMEM = pl.BlockSpec(memory_space=pltpu.VMEM)
IX, PARITY, X_LOW, X_HIGH, Y_LOW, Y_HIGH, Z_LOW, Z_HIGH = range(8)


def places():
    (ix, n_x), (iy, n_y), (iz, n_z) = ((lax.axis_index(a), lax.axis_size(a)) for a in ("gx", "gy", "gz"))
    flags = [ix, iy % 2, ix > 0, ix < n_x - 1, iy > 0, iy < n_y - 1, iz > 0, iz < n_z - 1]
    return [jnp.asarray(flag, jnp.int32) for flag in flags]


def call(kernel, outs, scratch=(), limit=16, flops=10**6, in_specs=None, aliases=None, out_specs=None):
    def placed(*refs):
        kernel(places(), *refs)

    def run(*arrays):
        return pl.pallas_call(
            placed,
            out_shape=outs,
            in_specs=in_specs or [VMEM] * len(arrays),
            out_specs=out_specs or jax.tree.map(lambda _: VMEM, outs),
            scratch_shapes=list(scratch),
            input_output_aliases=aliases or {},
            compiler_params=pltpu.CompilerParams(vmem_limit_bytes=limit * 2**20),
            cost_estimate=pl.CostEstimate(flops=flops, bytes_accessed=10**5, transcendentals=0),
        )(*arrays)

    return run


def shaped(*shape):
    return jax.ShapeDtypeStruct(shape, F32)


def lane_no(shape):
    return lax.broadcasted_iota(jnp.int32, shape, len(shape) - 1)


def row_no(shape):
    return lax.broadcasted_iota(jnp.int32, shape, len(shape) - 2)


def turned(values, shift, axis):
    if isinstance(shift, int):
        shift = shift % values.shape[axis]
        if shift == 0:
            return values
    return pltpu.roll(values, shift, axis)


def batched(low, high, step, carry, size=6):
    def some(i, carry):
        return step([low + i * size + k for k in range(size)], carry)

    carry = lax.fori_loop(0, (high - low) // size, some, carry)
    rest = (high - low) % size
    return step(list(range(high - rest, high)), carry) if rest else carry


def picked(values, index):
    return jnp.take_along_axis(values, index, axis=1, mode="promise_in_bounds")


class Frame:
    def __init__(self, nx, ny):
        self.nx, self.ny = nx, ny
        self.wide, self.tall = nx + 2 * HALO, ny + 2 * HALO
        self.rows = self.tall + 2 * SUB
        self.span = pl.ds(SUB, self.tall)
        self.own = SUB + HALO
        self.main = (self.wide, self.rows, LANES)
        self.ends = (2, self.rows, LANES)


def bases(widths):
    return [sum(widths[:f]) for f in range(len(widths) + 1)]


def copied(pairs, sems):
    copies = [pltpu.make_async_copy(src, dst, sems.at[n]) for n, (src, dst) in enumerate(pairs)]
    for copy in copies:
        copy.start()
    return copies


def pack_kernel(count, widths, flags, *refs):
    fields = len(widths)
    n_x = 1 if count == 2 else 2
    ins, kept = refs[: fields + 1], refs[fields + 1 : 2 * fields + 2]
    outs, sems = refs[2 * fields + 2 : -1], refs[-1]
    x_outs, y_outs, corner_outs = outs[:n_x], outs[n_x : n_x + 2], outs[n_x + 2 :]
    nx, ny = ins[0].shape[0], ins[0].shape[1]
    nb, half, width = ins[-1].shape
    thirds = 3
    copies = []
    for ref, out in zip(ins, kept):
        for t in range(thirds):
            size = ref.shape[0] // thirds
            rows = pl.ds(t * size, size)
            copies.append(pltpu.make_async_copy(ref.at[rows], out.at[rows], sems.at[len(copies)]))
    for copy in copies:
        copy.start()
    for out in (*x_outs, *y_outs):
        out[...] = jnp.zeros(out.shape, F32)
    for copy in copies:
        copy.wait()
    base = bases(widths)
    labels = kept[-1]
    for s, out in enumerate(x_outs):

        def place(size, thick, s=s):
            if count == 2:
                return jnp.where(flags[IX] == 0, size - thick, 0)
            return (size - thick, 0)[s]

        for f, thick in enumerate(widths):
            at = place(nx, thick)
            for k in range(thick):
                slab = kept[f][at + k]
                out[base[f] + k] = slab
                row = (sum(w * w for w in widths[:f])) + k * thick
                corner_outs[2 * s][row : row + thick] = slab[ny - thick :]
                corner_outs[2 * s + 1][row : row + thick] = slab[:thick]
        out[base[-1], :half, :width] = labels[place(nb, 1)].astype(F32)
    for out, high in zip(y_outs, (True, False)):
        for f, thick in enumerate(widths):
            for x in range(nx):
                row = base[f] * nx + x * thick
                out[row : row + thick] = kept[f][x, ny - thick :] if high else kept[f][x, :thick]
        row = base[-1] * nx
        for b in range(nb):
            line = labels[b, half - 1 :] if high else labels[b, :1]
            out[row + b : row + b + 1, :width] = line.astype(F32)


def slab_of(own, low, high, base, width, x):
    nx = own.shape[0]
    if HALO <= x < HALO + nx:
        return own[x - HALO]
    if x < HALO:
        at = x - (HALO - width)
        return low[base + at] if at >= 0 else None
    at = x - HALO - nx
    return high[base + at] if at < width else None


def pack_y_kernel(fields, flags, *refs):
    ins, rider = refs[:fields], refs[fields]
    low, high, to_high, to_low = refs[fields + 1 :]
    nx, ny = ins[0].shape[0], ins[0].shape[1]
    wide = nx + 2 * HALO
    for f in range(fields):
        for x in range(wide):
            slab = slab_of(ins[f], low, high, HALO * f, HALO, x)
            at = (f * wide + x) * HALO
            to_high[at : at + HALO] = slab[ny - HALO :]
            to_low[at : at + HALO] = slab[:HALO]
    at = fields * wide * HALO
    to_high[at:], to_low[at:] = rider[...], rider[...]


def packed_lanes(wide_ref, f, frame, rows, to_high, to_low):
    group = lane_no((1, LANES)) // HALO
    nothing = jnp.ones((rows.size, LANES), F32)
    high, low = nothing, nothing
    for x in range(frame.wide):
        moved = turned(wide_ref[f, x, rows], HALO * (x + 1), 1)
        high = jnp.where(group == x, moved, high)
        low = jnp.where(group == (x + 1) % frame.wide, moved, low)
    at = pl.ds(f * frame.tall + rows.start - SUB, rows.size)
    to_high[at] = high
    to_low[at] = turned(low, -HALO, 1)


def first_frame_kernel(count, widths, flags, *refs):
    fields = len(widths)
    ins, labels, refs = refs[:fields], refs[fields], refs[fields + 1 :]
    x_low, x_high, y_low, y_high = refs[:4]
    corners = refs[4:6] * 2 if count == 2 else refs[4:8]
    wide_ref, send_forth, send_back, to_high, to_low = refs[-5:]
    nx, ny = ins[0].shape[0], ins[0].shape[1]
    frame = Frame(nx, ny)
    base = bases(widths)
    tall, own = frame.tall, frame.own
    even = flags[PARITY] == 0
    ones = jnp.ones((frame.rows, LANES), F32)
    for f, thick in enumerate(widths):
        for x in range(frame.wide):
            slab = slab_of(ins[f], x_low, x_high, base[f], thick, x)
            if slab is None:
                wide_ref[f, x] = ones
                continue
            edge = ones[: SUB + HALO]
            wide_ref[f, x, :own] = edge
            wide_ref[f, x, own + ny :] = edge
            wide_ref[f, x, own : own + ny] = slab
            if HALO <= x < HALO + nx:
                low, high, row = y_low, y_high, base[f] * nx + (x - HALO) * thick
            else:
                above = x >= HALO
                low, high = corners[2 * above : 2 * above + 2]
                at = x - HALO - nx if above else x - (HALO - thick)
                row = sum(w * w for w in widths[:f]) + at * thick
            wide_ref[f, x, own - thick : own] = low[row : row + thick]
            wide_ref[f, x, own + ny : own + ny + thick] = high[row : row + thick]
        packed_lanes(wide_ref, f, frame, pl.ds(SUB, tall), to_high, to_low)
    high, low = to_high[...], to_low[...]
    size = fields * tall
    send_forth[:size], send_back[:size] = jnp.where(even, high, low), jnp.where(even, low, high)
    nb, rows, width = labels.shape
    lane = lane_no((rows, LANES))
    high = low = jnp.zeros((rows, LANES), F32)
    for b in range(nb):
        slab = labels[b].astype(F32)
        high = jnp.where(lane == b, slab[:, width - 1 :], high)
        low = jnp.where(lane == b, slab[:, :1], low)
    send_forth[size:], send_back[size:] = jnp.where(even, high, low), jnp.where(even, low, high)


def frame_kernel(fields, flags, *refs):
    ins = refs[:fields]
    x_low, x_high, _ = refs[fields : fields + 3]
    wide_ref, to_high, to_low = refs[fields + 3 :]
    nx, ny = ins[0].shape[0], ins[0].shape[1]
    frame = Frame(nx, ny)
    spare = jnp.ones((SUB, LANES), F32)
    for f in range(fields):
        for x in range(frame.wide):
            wide_ref[f, x, frame.own : frame.own + ny] = slab_of(ins[f], x_low, x_high, HALO * f, HALO, x)
            wide_ref[f, x, :SUB] = spare
            wide_ref[f, x, SUB + frame.tall :] = spare
        packed_lanes(wide_ref, f, frame, pl.ds(2 * SUB, frame.tall - 2 * SUB), to_high, to_low)


def pack_z_kernel(fields, flags, wide_in, high_in, low_in, from_low, from_high, rider, *refs):
    wide_ref, send_forth, send_back, to_high, to_low = refs
    frame = Frame(wide_ref.shape[1] - 2 * HALO, wide_ref.shape[2] - 2 * (SUB + HALO))
    ny, tall, own = frame.ny, frame.tall, frame.own
    even = flags[PARITY] == 0
    for f in range(fields):
        for x in range(frame.wide):
            at = (f * frame.wide + x) * HALO
            wide_ref[f, x, SUB:own] = from_low[at : at + HALO]
            wide_ref[f, x, own + ny : own + ny + HALO] = from_high[at : at + HALO]
    size = fields * tall
    to_high[...], to_low[...] = high_in[...], low_in[...]
    for f in range(fields):
        for start in (SUB, tall):
            packed_lanes(wide_ref, f, frame, pl.ds(start, SUB), to_high, to_low)
    high, low = to_high[...], to_low[...]
    send_forth[:size], send_back[:size] = jnp.where(even, high, low), jnp.where(even, low, high)
    send_forth[size:], send_back[size:] = rider[...], rider[...]


class Links:
    def __init__(self, mesh):
        self.sizes = [mesh.shape[a] for a in ("gx", "gy", "gz")]
        n_x, n_y, n_z = self.sizes

        def at(i, j, k):
            return (i % n_x * n_y + j % n_y) * n_z + k

        every = [(i, j, k) for i in range(n_x) for j in range(n_y) for k in range(n_z)]
        self.ring_x = [(i, (i + 1) % n_x) for i in range(n_x)]
        self.corner = {d: [(at(i, j, k), at(i + d, j + 1, k)) for i, j, k in every] for d in (1, -1)}
        self.snake = []
        for i in range(n_x):
            for j in range(0, n_y, 2):
                nodes = [at(i, j, k) for k in range(n_z)] + [at(i, j + 1, k) for k in reversed(range(n_z))]
                self.snake += [(nodes[m], nodes[(m + 1) % len(nodes)]) for m in range(len(nodes))]

    @staticmethod
    def back(pairs):
        return [(b, a) for a, b in pairs]

    @staticmethod
    def send(values, pairs):
        return lax.ppermute(values, ("gx", "gy", "gz"), pairs)

    def x(self, sends):
        if self.sizes[0] == 2:
            return (lax.ppermute(sends[0], "gx", self.ring_x),)
        return lax.ppermute(sends[0], "gx", self.ring_x), lax.ppermute(sends[1], "gx", self.back(self.ring_x))

    def near(self, values, x=None, y=None, z=None):
        forth, back = self.z(*(z or (values, values)))
        from_x = self.x(x or (values, values))
        return (forth, back, *from_x, *self.ring_y(*(y or (values, values))))

    def ring_y(self, to_high, to_low):
        ring = [(j, (j + 1) % self.sizes[1]) for j in range(self.sizes[1])]
        return lax.ppermute(to_high, "gy", ring), lax.ppermute(to_low, "gy", self.back(ring))

    def corners(self, sends):
        if self.sizes[0] == 2:
            return self.send(sends[0], self.corner[1]), self.send(sends[1], self.back(self.corner[1]))
        return (
            self.send(sends[0], self.corner[1]),
            self.send(sends[1], self.back(self.corner[-1])),
            self.send(sends[2], self.corner[-1]),
            self.send(sends[3], self.back(self.corner[1])),
        )

    def z(self, forth, back):
        return self.send(forth, self.snake), self.send(back, self.back(self.snake))


def send_y(arrays, rider, from_x):
    nx, ny, nz = arrays[0].shape
    rows = len(arrays) * Frame(nx, ny).wide * HALO + SUB
    kernel = functools.partial(pack_y_kernel, len(arrays))
    return call(kernel, [shaped(rows, nz)] * 2)(*arrays, rider, from_x[0], from_x[-1])


def framed(arrays, from_x, sent):
    nx, ny, nz = arrays[0].shape
    frame, fields = Frame(nx, ny), len(arrays)
    outs = [shaped(fields, *frame.main)] + [shaped(fields * frame.tall, nz)] * 2
    return call(functools.partial(frame_kernel, fields), outs)(*arrays, from_x[0], from_x[-1], sent)


def send_z(frames, from_y, rider):
    wide, high, _ = frames
    return call(
        functools.partial(pack_z_kernel, wide.shape[0]),
        [shaped(*wide.shape)] + [shaped(high.shape[0] + SUB, LANES)] * 2,
        [pltpu.VMEM(high.shape, F32)] * 2,
        aliases={0: 0},
    )(*frames, *from_y, rider)


def sides(flags, forth, back):
    even = flags[PARITY] == 0
    return jnp.where(even, forth, back), jnp.where(even, back, forth)


def weight(one, two):
    return 2.0 * (one * two) / (one + two)


def lane_mask(x):
    return ((lane_no((1, LANES)) - (HALO * x + HALO - 1)) & (LANES - 1)) < 2


def edge_step(here, x, edges):
    return jnp.where(lane_mask(x), turned(here, HALO * x + HALO, 1), edges)


def joined(below, above):
    lane = lane_no((1, LANES))
    return jnp.where(lane % HALO == HALO - 1, turned(above, HALO - 1, 1), turned(below, 1, 1))


def at_edges(join, x):
    lane = lane_no((1, LANES))
    return jnp.where((lane == 0) | (lane == LANES - 1), turned(join, (LANES - HALO) - HALO * x, 1), 0.0)


def ends_near(below, above, edges):
    layer = lane_no((1, LANES)) % HALO
    return (
        jnp.where(layer == HALO - 1, turned(edges, -1, 1), turned(below, -1, 1)),
        turned(below, 1, 1),
        turned(above, -1, 1),
        jnp.where(layer == 0, turned(edges, 1 - HALO, 1), turned(above, 1, 1)),
    )


def main_sums(frame, field, xs, join, wx, wy, wz):
    span = frame.span
    slabs = [field[xs[0] - 1 + k, span] for k in range(len(xs) + 2)]
    faces = [wx[xs[0] - 1 + k, span] for k in range(len(xs) + 1)]
    totals = []
    for k, x in enumerate(xs):
        here, face_y, face_z = slabs[k + 1], wy[x, span], wz[x, span]
        total = faces[k + 1] * slabs[k + 2] + faces[k] * slabs[k]
        total = total + face_y * turned(here, -1, 0) + turned(face_y * here, 1, 0)
        total = total + face_z * turned(here, -1, 1) + turned(face_z * here, 1, 1)
        totals.append(total + at_edges(join, x))
    return slabs[1:-1], totals


def ends_sum(frame, ends, s, upper, lower, wx, wy, wz_up, wz_low):
    span, down = frame.span, pl.ds(SUB - 1, frame.tall)
    here = ends[s, span]
    total = wx[s, span] * turned(here, -HALO, 1) + turned(wx[s, span] * here, HALO, 1)
    total = total + wy[s, span] * ends[s, pl.ds(SUB + 1, frame.tall)] + wy[s, down] * ends[s, down]
    return total + wz_up[s, span] * upper + wz_low[s, span] * lower


def clear_spares(ref, frame):
    for x in range(ref.shape[0]):
        ref[x, :SUB] = jnp.zeros((SUB, LANES), F32)
        ref[x, SUB + frame.tall :] = jnp.zeros((SUB, LANES), F32)


def pack_rows(values):
    half = values.shape[0] // 2
    lane = lane_no((half, LANES))
    return jnp.where(lane < LANES // 2, values[:half], turned(values[half:], LANES // 2, 1))


def lane_total(values):
    return jnp.broadcast_to(jnp.sum(values.T, axis=0, keepdims=True), (SUB, LANES))


def paired(values):
    even = 2 * (lane_no(values.shape) % (LANES // 2))
    return picked(values + turned(values, -1, 1), even)


def faces_y_kept(flags, frame):
    row = row_no((frame.tall, LANES))
    at_low, at_high = row == HALO - 1, row == HALO + frame.ny - 1
    return jnp.where(at_low, flags[Y_LOW], jnp.where(at_high, flags[Y_HIGH], 1)).astype(F32)


def face_rows(count, flags, nb):
    x = [(jnp.where(flags[IX] == 0, 1, 0), SUB)] if count == 2 else [(0, SUB), (1, SUB)]
    return x + [(2, nb // 2), (3, nb // 2), (4, 2), (5, 2)]


def add_rows(total, labels, b, values, c, rows=SUB):
    iota = row_no((AGG, LANES)).astype(F32)
    for r in range(rows):
        row = pl.ds(r, 1)
        total = total + jnp.where(labels[b, row] == iota, values[c, row], 0.0)
    return total


def pack_lanes(values):
    lane = lane_no((2, LANES))
    packed = values[:2]
    for g in range(1, SUB):
        packed = jnp.where(lane // 16 == g, turned(values[2 * g : 2 * g + 2], 16 * g, 1), packed)
    return packed


def fields_kernel(count, flags, wide_ref, block_label, inner, face_label, wx, wy, wz, partial, cond_edges, face_weight, diag):
    frame = Frame(wx.shape[0] - 2 * HALO, wx.shape[1] - 2 * (SUB + HALO))
    wide, tall, span = frame.wide, frame.tall, frame.span
    last = HALO + frame.nx
    keep_y = faces_y_kept(flags, frame)
    inside = jnp.where(lane_no((1, LANES)) == LANES - 1, 0.0, 1.0)

    def fields(xs, carry):
        before, edges = carry
        stores = []
        for x in xs:
            here = wide_ref[0, x, span]
            keep = jnp.where(x == HALO - 1, flags[X_LOW], jnp.where(x == last - 1, flags[X_HIGH], 1)).astype(F32)
            face_x = keep * weight(here, wide_ref[0, jnp.minimum(x + 1, wide - 1), span])
            face_y = keep_y * weight(here, wide_ref[0, x, pl.ds(SUB + 1, tall)])
            face_z = inside * weight(here, turned(here, -1, 1))
            total = wide_ref[2, x, span] + face_x + before + face_y + turned(face_y, 1, 0)
            total = total + face_z + turned(face_z, 1, 1)
            stores.append((x, (face_x, face_y, face_z, total)))
            edges = edge_step(here, x, edges)
            before = face_x
        for x, values in stores:
            for ref, value in zip((wx, wy, wz, partial), values):
                ref[x, span] = value
        return before, edges

    nothing = jnp.zeros((tall, LANES), F32)
    cond_edges[...] = batched(0, wide, fields, (nothing, nothing + 1.0), 4)[1]
    nb, ny = frame.nx // 2, frame.ny
    for s, x in enumerate((HALO - 1, last - 1)):
        rows = [wx[x, pl.ds(frame.own + c, ny // 2, stride=2)] for c in range(2)]
        face_weight[s] = pack_rows(paired(rows[0] + rows[1]))
    for s, at in ((2, frame.own - 1), (3, frame.own + ny - 1)):
        lines = [wy[HALO + 2 * b, at : at + 1] + wy[HALO + 2 * b + 1, at : at + 1] for b in range(nb)]
        face_weight[s, : nb // 2] = pack_rows(paired(jnp.concatenate(lines, axis=0)))
    around = jnp.zeros((AGG, LANES), F32)
    around = lax.fori_loop(0, nb, lambda b, around: add_rows(around, block_label, b, inner, b), around)
    for s, rows in face_rows(count, flags, nb)[:-2]:
        around = add_rows(around, face_label, s, face_weight, s, rows)
    diag[...] = lane_total(around)


def fine_kernel(flags, wide_ref, forth, back, wx, wy, wz, partial, cond_edges, block_label, face_label, some_diag,
                *refs):
    inv_diag, start = refs[:2]
    ends = refs[2:8]
    pre, face_weight, scaled_rhs, scale, once, once_ends, res, diag, block_res = refs[8:]
    ex, ey, ez_up, ez_low, inv_ends, start_ends = ends
    nx, ny = pre.shape[0], pre.shape[1]
    frame = Frame(nx, ny)
    wide, tall, span = frame.wide, frame.tall, frame.span
    last = HALO + nx
    got = [sides(flags, forth[f * tall : (f + 1) * tall], back[f * tall : (f + 1) * tall]) for f in range(3)]
    (cond_below, cond_above), rhs_ends, absorb_ends = got
    for ref in (ey, start_ends, once_ends):
        clear_spares(ref, frame)

    lane = lane_no((1, LANES))
    keep_y = faces_y_kept(flags, frame)
    keep_low, keep_high = flags[Z_LOW].astype(F32), flags[Z_HIGH].astype(F32)
    near = ends_near(cond_below, cond_above, cond_edges[...])
    slab = lane // HALO
    keep_x = jnp.where(
        slab == HALO - 1, flags[X_LOW], jnp.where(slab == last - 1, flags[X_HIGH], 1)
    ).astype(F32)
    layer = lane % HALO
    for s, here in enumerate((cond_below, cond_above)):
        up, low = weight(here, near[2 * s]), weight(here, near[2 * s + 1])
        if s == 0:
            up = up * jnp.where(layer == HALO - 1, keep_low, 1.0)
        else:
            low = low * jnp.where(layer == 0, keep_high, 1.0)
        face_x = keep_x * weight(here, turned(here, -HALO, 1))
        face_y = keep_y * weight(here, turned(here, -1, 0))
        ex[s, span], ey[s, span], ez_up[s, span], ez_low[s, span] = face_x, face_y, up, low
        total = absorb_ends[s] + face_x + turned(face_x, HALO, 1) + face_y + turned(face_y, 1, 0) + up + low
        inverse = OMEGA_FINE / total
        inv_ends[s, span] = inverse
        start_ends[s, span] = inverse * rhs_ends[s]

    end_low, end_high = ez_up[0, span], ez_low[1, span]
    join_faces = joined(end_low, end_high)

    def first_sweep(xs, edges):
        stores = []
        for x in xs:
            total = partial[x, span] + at_edges(join_faces, x)
            inverse = OMEGA_FINE / total
            begin = inverse * wide_ref[1, x, span]
            stores.append((x, (total, inverse, begin)))
            edges = edge_step(begin, x, edges)
        for x, values in stores:
            for ref, value in zip((diag, inv_diag, start), values):
                ref[x, span] = value
        return edges

    edges = batched(0, wide, first_sweep, jnp.zeros((tall, LANES), F32), 4)

    join = joined(end_low * start_ends[0, span], end_high * start_ends[1, span])
    near = ends_near(start_ends[0, span], start_ends[1, span], edges)
    for s in range(2):
        total = ends_sum(frame, start_ends, s, near[2 * s], near[2 * s + 1], ex, ey, ez_up, ez_low)
        once_ends[s, span] = (2.0 - OMEGA_FINE) * start_ends[s, span] + inv_ends[s, span] * total

    def second(xs, carry):
        news = []
        for x, here, total in zip(xs, *main_sums(frame, start, xs, join, wx, wy, wz)):
            news.append((2.0 - OMEGA_FINE) * here + inv_diag[x, span] * total)
        for x, new in zip(xs, news):
            once[x, span] = new
        return carry

    batched(HALO - 1, last + 1, second, 0, 13 if (nx + 2) % 13 == 0 else 6)
    join2 = joined(end_low * once_ends[0, span], end_high * once_ends[1, span])

    def remainder(xs, carry):
        news = []
        for x, here, total in zip(xs, *main_sums(frame, once, xs, join2, wx, wy, wz)):
            news.append(wide_ref[1, x, span] - diag[x, span] * here + total)
        for x, new in zip(xs, news):
            res[x - HALO, span] = new
        for x in xs:
            pre[x - HALO] = once[x, pl.ds(frame.own, ny)]
        return carry

    batched(HALO, last, remainder, 0, 8)

    nb, half = nx // 2, ny // 2

    def rows_at(ref, x, off):
        return ref[x, pl.ds(frame.own + off, half, stride=2)]

    def to_blocks(bs, carry):
        for b in bs:
            four = sum(rows_at(res, 2 * b + a, c) for a in range(2) for c in range(2))
            block_res[b] = pack_rows(paired(four))
        return carry

    batched(0, nb, to_blocks, 0)
    zeros = jnp.zeros((AGG, LANES), F32)
    sums = lax.fori_loop(0, nb, lambda b, total: add_rows(total, block_label, b, block_res, b), zeros)

    lane = lane_no((half, LANES))
    around = zeros
    for s, (ref, side, layer_at) in enumerate(((ez_up, 0, HALO - 1), (ez_low, 1, 0))):
        values = rows_at(ref, side, 0) + rows_at(ref, side, 1)
        values = values + turned(values, -HALO, 1)
        spot = jnp.minimum(2 * HALO * lane + HALO * HALO + layer_at, LANES - 1)
        face_weight[s, :2] = pack_lanes(jnp.where(lane < nb, picked(values, spot), 0.0))
        around = add_rows(around, face_label, 4 + s, face_weight, s, 2)
    scale[...] = OMEGA_COARSE / (some_diag[...] + lane_total(around))
    scaled_rhs[...] = scale[...] * lane_total(sums)


def tile_sum(tile, rows, label_at, pairs_at, group=4):
    iota = row_no((AGG, LANES)).astype(F32)
    for first in range(0, rows, group):
        places, highs, lows = [], [], []
        for r in range(first, min(first + group, rows)):
            places.append(jnp.where(label_at(r) == iota, 1.0, 0.0).astype(BF16))
            held = sum(jnp.where(near == iota, w, 0.0) for near, w in pairs_at(r))
            highs.append(held.astype(BF16))
            lows.append((held - highs[-1].astype(F32)).astype(BF16))
        left = jnp.concatenate(places, axis=1)
        right = jnp.concatenate([jnp.concatenate(highs, axis=1), jnp.concatenate(lows, axis=1)], axis=0)
        tile = tile + lax.dot_general(left, right, (((1,), (1,)), ((), ())), preferred_element_type=F32)
    return tile


def both_halves(tile):
    return tile[:, :AGG] + tile[:, AGG:]


def keep_tile(out, t, tile):
    high = tile.astype(BF16)
    rows = pl.ds(t * AGG, AGG)
    out[rows, :AGG] = high
    out[rows, AGG:] = (tile - high.astype(F32)).astype(BF16)


def blocks_kernel(flags, cond, absorb, block_agg, block_label, near, weights, inner, face_label, fine_label,
                  part, line):
    nx, ny = cond.shape[0], cond.shape[1]
    nb, half, width = nx // 2, ny // 2, LANES // 2
    lane, row = lane_no((half, LANES)), row_no((half, LANES))

    def halves(values, slot):
        part[slot] = values
        return part[slot, pl.ds(0, half, stride=2)], part[slot, pl.ds(1, half, stride=2)]

    def label_at(b):
        values = block_agg[b].astype(F32)
        return jnp.concatenate([values, values], axis=1)

    def upper_x(b, slot):
        x = jnp.maximum(2 * b, 0)
        faces = weight(cond[x + 1], cond[jnp.minimum(x + 2, nx - 1)])
        return jnp.where((b == nb - 1) | (b < 0), 0.0, paired(sum(halves(faces, slot))))

    def step(bs, carry):
        low_x = upper_x(bs[0] - 1, 0)
        for k, b in enumerate(bs):
            x = 2 * b
            slot = 4 * k + 1
            one, two = cond[x], cond[x + 1]
            both_y = weight(one, turned(one, -1, 0)) + weight(two, turned(two, -1, 0))
            both_z = weight(one, turned(one, -1, 1)) + weight(two, turned(two, -1, 1))
            high_x = upper_x(b, slot)
            high_y = jnp.where(row == half - 1, 0.0, paired(halves(both_y, slot + 1)[1]))
            high_z = picked(sum(halves(both_z, slot + 2)), 2 * (lane % width) + 1)
            high_z = jnp.where(lane % width == width - 1, 0.0, high_z)
            low_y, low_z = turned(high_y, 1, 0), turned(high_z, 1, 1)
            own = label_at(b)
            near_x, past_x = label_at(jnp.minimum(b + 1, nb - 1)), label_at(jnp.maximum(b - 1, 0))
            near_y, past_y = turned(own, -1, 0), turned(own, 1, 0)
            near_z, past_z = turned(own, -1, 1), turned(own, 1, 1)
            total = paired(sum(halves(absorb[x] + absorb[x + 1], slot + 3)))
            for beside, values in (
                (near_x, high_x), (past_x, low_x), (near_y, high_y), (past_y, low_y), (near_z, high_z), (past_z, low_z)
            ):
                total = total + jnp.where(beside != own, values, 0.0)
            block_label[b] = pack_rows(own)
            inner[b] = pack_rows(total)
            for d, (beside, values) in enumerate(((near_x, high_x), (near_y, high_y), (near_z, high_z))):
                near[d, b], weights[d, b] = pack_rows(beside), pack_rows(values)
            spread = picked(own, lane // 2)
            for a in range(2):
                for c in range(2):
                    fine_label[x + a, pl.ds(c, half, stride=2)] = spread
            low_x = high_x
        return carry

    batched(0, nb, step, 0, 4)
    line[...] = jnp.zeros(line.shape, F32)
    low, high = jnp.zeros((half, LANES), F32), jnp.zeros((half, LANES), F32)
    for b in range(nb):
        own = label_at(b)
        line[0, b : b + 1], line[1, b : b + 1] = own[:1], own[half - 1 :]
        low = jnp.where(lane == b, own[:, :1], low)
        high = jnp.where(lane == b, own[:, width - 1 : width], high)
    face_label[0], face_label[1] = block_label[0], block_label[nb - 1]
    for s in range(2):
        face_label[2 + s, : nb // 2] = pack_rows(line[s, :nb])
        face_label[4 + s, :2] = pack_lanes((low, high)[s])


def own_kernel(first, last, total, flags, block_label, near, weights, *refs):
    so_far, refs = (refs[0], refs[1:]) if first else (None, refs)
    refs = refs[1:]

    def step(b, tile):
        def pairs_at(r):
            return [(near[d, b, pl.ds(r, 1)], weights[d, b, pl.ds(r, 1)]) for d in range(3)]

        return tile_sum(tile, SUB, lambda r: block_label[b, pl.ds(r, 1)], pairs_at)

    tile = so_far[...] if first else jnp.zeros((AGG, 2 * AGG), F32)
    tile = lax.fori_loop(first, last, step, tile)
    if last < total:
        refs[0][...] = tile
        return
    tile = both_halves(tile)
    keep_tile(refs[0], 0, jnp.where(row_no((AGG, AGG)) == lane_no((AGG, AGG)), 0.0, tile + tile.T))


def faces_kernel(count, nb, flags, own, face_label, weight_xy, weight_z, x_low, x_high, y_low, y_high, forth, back, out,
                 near, weights):
    out[:AGG] = own[...]
    at, half = x_low.shape[0] - 1, x_low.shape[1] // 2
    near[0], near[1] = pack_rows(x_low[at, :half]), pack_rows(x_high[at, :half])
    at = sum(WIDTHS) * 2 * nb
    for s, ref in enumerate((y_low, y_high)):
        near[2 + s, : nb // 2] = pack_rows(ref[at : at + nb])
    at = forth.shape[0] - half
    for s, values in enumerate(sides(flags, forth[at:], back[at:])):
        near[4 + s, :2] = pack_lanes(values)
    weights[:4], weights[4:] = weight_xy[...], weight_z[...]
    for t, (s, rows) in enumerate(face_rows(count, flags, nb)):
        tile = tile_sum(
            jnp.zeros((AGG, 2 * AGG), F32),
            rows,
            lambda r, s=s: near[s, pl.ds(r, 1)],
            lambda r, s=s: [(face_label[s, pl.ds(r, 1)], weights[s, pl.ds(r, 1)])],
        )
        keep_tile(out, t + 1, both_halves(tile))


def turn_kernel(flags, tiles, scaled_rhs, scale, own, *refs):
    forth, back, *others, out = refs
    got = [ref[ref.shape[0] - 1, :SUB] if len(ref.shape) == 3 else ref[ref.shape[0] - SUB :] for ref in (*others, forth, back)]
    vectors = [own[...], *got[:-2], *sides(flags, *got[-2:])]
    row = row_no((SUB, AGG))
    parts = []
    for v in vectors:
        high = v.astype(BF16).astype(F32)
        parts.append(jnp.where(row == 0, high, jnp.where(row == 1, v - high, 0.0)).astype(BF16))
    got = jnp.dot(jnp.concatenate(parts, axis=1), tiles[...], preferred_element_type=F32)
    applied = jnp.sum(got[:, :AGG] + got[:, AGG:], axis=0, keepdims=True)
    out[...] = (1.0 - OMEGA_COARSE) * own[...] + scaled_rhs[...] + scale[...] * applied


def ride_kernel(count, flags, pre, fine_label, coarse, *outs):
    nx = pre.shape[0]
    for s, out in enumerate(outs):
        at = jnp.where(flags[IX] == 0, nx - HALO, 0) if count == 2 else (nx - HALO, 0)[s]
        for f, field in enumerate((pre, fine_label)):
            for x in range(HALO):
                out[HALO * f + x] = field[at + x]
        out[2 * HALO] = jnp.zeros(out.shape[1:], F32)
        out[2 * HALO, :SUB] = coarse[...]


def three_kernel(flags, low, mid, high, out):
    row = row_no(out.shape)
    out[...] = jnp.where(row == 0, low[...], jnp.where(row == 1, mid[...], high[...]))


def nine_kernel(flags, low, mid, high, out):
    out[...] = jnp.zeros(out.shape, F32)
    for n, ref in enumerate((low, mid, high)):
        out[3 * n : 3 * n + 3] = ref[:3]


def lift_kernel(flags, wide_ref, forth, back, main, ends):
    frame = Frame(wide_ref.shape[1] - 2 * HALO, wide_ref.shape[2] - 2 * (SUB + HALO))
    tall = frame.tall
    for b in range(frame.wide // 2):
        main[b] = wide_ref[1, 2 * b, frame.span].astype(jnp.int32)
    rows = pl.ds(tall, tall)
    for s, values in enumerate(sides(flags, forth[rows], back[rows])):
        ends[s] = values.astype(jnp.int32)


def post_kernel(flags, table, table_forth, table_back, labels, end_labels, wide_ref, forth, back, *refs):
    (wx, wy, wz, inv_diag, start), ends = refs[:5], refs[5:11]
    out, one, two, one_ends, two_ends, kept_out, sems = refs[11:]
    nx, ny = out.shape[0], out.shape[1]
    frame = Frame(nx, ny)
    wide, tall, span = frame.wide, frame.tall, frame.span
    ex, ey, ez_up, ez_low, inv_ends, start_ends = ends
    for ref in (one_ends, two_ends):
        clear_spares(ref, frame)
    row, lane = row_no((tall, LANES)), lane_no((tall, LANES))
    under, over = sides(flags, table_forth[...], table_back[...])
    tables = {-1: under, 0: table[...], 1: over}

    def table_at(dx, dz):
        low, mid, high = (tables[dz][3 * n + dx + 1 : 3 * n + dx + 2] for n in range(3))
        return jnp.where(row < HALO, low, jnp.where(row < HALO + ny, mid, high))

    for x_from, x_to, dx in ((0, HALO, -1), (HALO, HALO + nx, 0), (HALO + nx, wide, 1)):
        values = table_at(dx, 0)

        def lift(bs, carry, values=values):
            news = [picked(values, labels[b]) for b in bs]
            for b, new in zip(bs, news):
                for a in range(2):
                    two[2 * b + a, span] = wide_ref[0, 2 * b + a, span] + new
            return carry

        batched(x_from // 2, x_to // 2, lift, 0, 4)
    for s, (dz, base) in enumerate(zip((-1, 1), sides(flags, forth[:tall], back[:tall]))):
        below, inside, above = (picked(table_at(dx, dz), end_labels[s]) for dx in (-1, 0, 1))
        spot = lane // HALO
        lifted = jnp.where(spot < HALO, below, jnp.where(spot < HALO + nx, inside, above))
        two_ends[s, span] = base + lifted
    kept = 1.0 - OMEGA_FINE

    def result(at, count):
        rows = pl.ds(at, count)
        return pltpu.make_async_copy(kept_out.at[rows], out.at[rows], sems.at[at // count])

    buffers = ((two, two_ends), (one, one_ends), (two, two_ends), (one, one_ends))
    for s in range(POST):
        src, src_ends = buffers[s]
        join = joined(ez_up[0, span] * src_ends[0, span], ez_low[1, span] * src_ends[1, span])
        final = s == POST - 1
        dst, dst_ends = (None, None) if final else buffers[s + 1]

        def step(xs, edges, src=src, join=join, dst=dst, final=final):
            news = []
            for x, here, total in zip(xs, *main_sums(frame, src, xs, join, wx, wy, wz)):
                news.append(kept * here + start[x, span] + inv_diag[x, span] * total)
                if not final:
                    edges = edge_step(here, x, edges)
            for x, new in zip(xs, news):
                if final:
                    kept_out[x - HALO] = new[HALO : HALO + ny]
                else:
                    dst[x, span] = new
            if final:
                result(xs[0] - HALO, len(xs)).start()
            return edges

        size = 8 if final else 10
        edges = batched(s + 1, wide - s - 1, step, jnp.zeros((tall, LANES), F32), size)
        if not final:
            near = ends_near(src_ends[0, span], src_ends[1, span], edges)
            news = []
            for e in range(2):
                total = ends_sum(frame, src_ends, e, near[2 * e], near[2 * e + 1], ex, ey, ez_up, ez_low)
                news.append(kept * src_ends[e, span] + start_ends[e, span] + inv_ends[e, span] * total)
            dst_ends[0, span], dst_ends[1, span] = news
    for n in range(nx // 8):
        result(8 * n, 8).wait()


def body(links, right_side, conductance, absorption, block_agg):
    nx, ny, nz = right_side.shape
    frame = Frame(nx, ny)
    nb = nx // 2
    n_x = links.sizes[0]
    arrays = (conductance, right_side, absorption, block_agg)
    n_send = 1 if n_x == 2 else 2
    pinned = [pltpu.with_memory_space_constraint(a, pltpu.HBM) for a in arrays]
    outs = [jax.ShapeDtypeStruct(a.shape, a.dtype) for a in arrays]
    outs += [shaped(sum(WIDTHS) + 1, ny, nz)] * n_send + [shaped(sum(WIDTHS) * nx + 16, nz)] * 2
    outs += [shaped(-(-sum(w * w for w in WIDTHS) // SUB) * SUB, nz)] * (2 * n_send)
    got = call(
        functools.partial(pack_kernel, n_x, WIDTHS),
        outs,
        [pltpu.SemaphoreType.DMA((3 * 4,))],
        in_specs=[pl.BlockSpec(memory_space=pltpu.HBM)] * 4,
    )(*pinned)
    arrays, sends = got[:4], got[4:]
    from_x = links.x(sends[:n_send])
    from_y = links.ring_y(*sends[n_send : n_send + 2])
    blocks = (nb, SUB, LANES)
    outs = [shaped(*blocks), shaped(3, *blocks), shaped(3, *blocks), shaped(*blocks), shaped(6, SUB, LANES)]
    outs += [shaped(nx, ny, nz)]
    scratch = [pltpu.VMEM((17, ny, LANES), F32), pltpu.VMEM((2, ny // 2, LANES), F32)]
    *rows, inner, face_label, fine_label = call(blocks_kernel, outs, scratch)(arrays[0], arrays[2], arrays[3])
    block_label = rows[0]
    *corner_sends, inner = lax.optimization_barrier((*sends[n_send + 2 :], inner))
    from_corners = links.corners(corner_sends)
    bounds = (0, nb * 5 // 12, nb * 8 // 12, nb)

    def own_part(p, *more):
        out = jax.ShapeDtypeStruct((AGG, 2 * AGG), BF16) if p == 2 else shaped(AGG, 2 * AGG)
        return call(functools.partial(own_kernel, bounds[p], bounds[p + 1], nb), [out])(*rows, *more)[0]

    own_tile = own_part(0, sends[0])
    got = lax.optimization_barrier((*from_x, *from_y, *from_corners, own_tile))
    from_x, from_y, from_corners = got[:n_send], got[n_send : n_send + 2], got[n_send + 2 : -1]
    size = len(WIDTHS) * frame.tall
    wide, *sends = call(
        functools.partial(first_frame_kernel, n_x, WIDTHS),
        [shaped(len(WIDTHS), *frame.main)] + [shaped(size + ny // 2, nz)] * 2,
        [pltpu.VMEM((size, nz), F32)] * 2,
    )(*arrays, from_x[0], from_x[-1], *from_y, *from_corners)
    outs = [shaped(*frame.main)] * 4 + [shaped(frame.tall, nz), shaped(4, SUB, LANES), shaped(SUB, AGG)]
    *fields, weight_xy, some_diag = call(functools.partial(fields_kernel, n_x), outs, limit=24)(
        wide, block_label, inner, face_label
    )
    own_tile = own_part(1, own_tile, sends[0])
    halo = (wide, *links.z(*sends))
    *halo, own_tile = lax.optimization_barrier((*halo, own_tile))
    outs = [shaped(*frame.main)] * 2 + [shaped(*frame.ends)] * 6 + [shaped(nx, ny, nz)]
    outs += [shaped(2, SUB, LANES)] + [shaped(SUB, AGG)] * 2
    scratch = [pltpu.VMEM(frame.main, F32), pltpu.VMEM(frame.ends, F32), pltpu.VMEM((nx, frame.rows, LANES), F32)]
    scratch += [pltpu.VMEM(frame.main, F32), pltpu.VMEM(blocks, F32)]
    got = call(fine_kernel, outs, scratch, limit=28)(
        *halo, *fields, block_label, face_label, some_diag
    )
    fields, pre = (*fields[:3], *got[:8]), got[8]
    weight_z, scaled_rhs, scale = got[9:]
    own_tile = own_part(2, own_tile, scaled_rhs)
    tiles = call(
        functools.partial(faces_kernel, n_x, nb),
        jax.ShapeDtypeStruct(((n_send + 5) * AGG, 2 * AGG), BF16),
        [pltpu.VMEM((6, SUB, LANES), F32)] * 2,
    )(own_tile, face_label, weight_xy, weight_z, from_x[0], from_x[-1], *from_y, *halo[1:])
    coarse = scaled_rhs

    def turn(**more):
        near = links.near(coarse, **more)
        return call(turn_kernel, shaped(SUB, AGG))(tiles, scaled_rhs, scale, coarse, *near), near

    both = (pre, fine_label)
    rides = call(functools.partial(ride_kernel, n_x), [shaped(2 * HALO + 1, ny, nz)] * n_send)(*both, coarse)
    coarse, near = turn(x=rides)
    from_x = near[2:-2]
    rides = send_y(both, coarse, from_x)
    frames = framed(both, from_x, rides[0])
    coarse, near = turn(y=rides)
    wide, *rides = send_z(frames, near[-2:], coarse)
    coarse, near = turn(z=rides)
    halo = (wide, *near[:2])
    outs = [jax.ShapeDtypeStruct((frame.wide // 2, frame.tall, nz), jnp.int32)]
    outs += [jax.ShapeDtypeStruct((2, frame.tall, nz), jnp.int32)]
    lifts = call(lift_kernel, outs)(*halo)
    for _ in range(KC - 4):
        coarse, _ = turn()
    from_x = links.x([coarse] * n_send)
    three = call(three_kernel, shaped(SUB, AGG))(from_x[0], coarse, from_x[-1])
    low, high = links.ring_y(three, three)
    nine = call(nine_kernel, shaped(2 * SUB, AGG))(low, three, high)
    tables = (nine, *links.z(nine, nine))
    scratch = [pltpu.VMEM(frame.main, F32)] * 2 + [pltpu.VMEM(frame.ends, F32)] * 2
    scratch += [pltpu.VMEM((nx, ny, nz), F32), pltpu.SemaphoreType.DMA((nx // 8,))]
    return call(post_kernel, shaped(nx, ny, nz), scratch, limit=24, out_specs=pl.BlockSpec(memory_space=pl.ANY))(
        *tables, *lifts, *halo, *fields
    )


def solution(mesh):
    spec = P("gx", "gy", "gz")
    return jax.shard_map(
        functools.partial(body, Links(mesh)), mesh=mesh, in_specs=(spec,) * 4, out_specs=spec, check_vma=False
    )
```

```python
import functools

import jax
import jax.numpy as jnp
from jax import lax
from jax.experimental import pallas as pl
from jax.experimental.pallas import tpu as pltpu
from jax.sharding import PartitionSpec as P

AGG = 128
LANES = 128
SUB = 8
HALO = 4
WIDTHS = (4, 3, 3)
POST = 4
KC = 8
OMEGA_FINE = 0.8
OMEGA_COARSE = 0.7
F32 = jnp.float32
BF16 = jnp.bfloat16
VMEM = pl.BlockSpec(memory_space=pltpu.VMEM)
IX, PARITY, X_LOW, X_HIGH, Y_LOW, Y_HIGH, Z_LOW, Z_HIGH = range(8)


def places():
    (ix, n_x), (iy, n_y), (iz, n_z) = ((lax.axis_index(a), lax.axis_size(a)) for a in ("gx", "gy", "gz"))
    flags = [ix, iy % 2, ix > 0, ix < n_x - 1, iy > 0, iy < n_y - 1, iz > 0, iz < n_z - 1]
    return [jnp.asarray(flag, jnp.int32) for flag in flags]


def call(kernel, outs, scratch=(), limit=16, flops=10**6, in_specs=None, aliases=None, out_specs=None):
    def placed(*refs):
        kernel(places(), *refs)

    def run(*arrays):
        return pl.pallas_call(
            placed,
            out_shape=outs,
            in_specs=in_specs or [VMEM] * len(arrays),
            out_specs=out_specs or jax.tree.map(lambda _: VMEM, outs),
            scratch_shapes=list(scratch),
            input_output_aliases=aliases or {},
            compiler_params=pltpu.CompilerParams(vmem_limit_bytes=limit * 2**20),
            cost_estimate=pl.CostEstimate(flops=flops, bytes_accessed=10**5, transcendentals=0),
        )(*arrays)

    return run


def shaped(*shape):
    return jax.ShapeDtypeStruct(shape, F32)


def lane_no(shape):
    return lax.broadcasted_iota(jnp.int32, shape, len(shape) - 1)


def row_no(shape):
    return lax.broadcasted_iota(jnp.int32, shape, len(shape) - 2)


def turned(values, shift, axis):
    if isinstance(shift, int):
        shift = shift % values.shape[axis]
        if shift == 0:
            return values
    return pltpu.roll(values, shift, axis)


def batched(low, high, step, carry, size=6):
    def some(i, carry):
        return step([low + i * size + k for k in range(size)], carry)

    carry = lax.fori_loop(0, (high - low) // size, some, carry)
    rest = (high - low) % size
    return step(list(range(high - rest, high)), carry) if rest else carry


def picked(values, index):
    return jnp.take_along_axis(values, index, axis=1, mode="promise_in_bounds")


class Frame:
    def __init__(self, nx, ny):
        self.nx, self.ny = nx, ny
        self.wide, self.tall = nx + 2 * HALO, ny + 2 * HALO
        self.rows = self.tall + 2 * SUB
        self.span = pl.ds(SUB, self.tall)
        self.own = SUB + HALO
        self.main = (self.wide, self.rows, LANES)
        self.ends = (2, self.rows, LANES)


def bases(widths):
    return [sum(widths[:f]) for f in range(len(widths) + 1)]


def copied(pairs, sems):
    copies = [pltpu.make_async_copy(src, dst, sems.at[n]) for n, (src, dst) in enumerate(pairs)]
    for copy in copies:
        copy.start()
    return copies


def pack_kernel(count, widths, flags, *refs):
    fields = len(widths)
    n_x = 1 if count == 2 else 2
    ins, kept = refs[: fields + 1], refs[fields + 1 : 2 * fields + 2]
    outs, sems = refs[2 * fields + 2 : -1], refs[-1]
    x_outs, y_outs, corner_outs = outs[:n_x], outs[n_x : n_x + 2], outs[n_x + 2 :]
    nx, ny = ins[0].shape[0], ins[0].shape[1]
    nb, half, width = ins[-1].shape
    thirds = 3
    copies = []
    for ref, out in zip(ins, kept):
        for t in range(thirds):
            size = ref.shape[0] // thirds
            rows = pl.ds(t * size, size)
            copies.append(pltpu.make_async_copy(ref.at[rows], out.at[rows], sems.at[len(copies)]))
    for copy in copies:
        copy.start()
    for out in (*x_outs, *y_outs):
        out[...] = jnp.zeros(out.shape, F32)
    for copy in copies:
        copy.wait()
    base = bases(widths)
    labels = kept[-1]
    for s, out in enumerate(x_outs):

        def place(size, thick, s=s):
            if count == 2:
                return jnp.where(flags[IX] == 0, size - thick, 0)
            return (size - thick, 0)[s]

        for f, thick in enumerate(widths):
            at = place(nx, thick)
            for k in range(thick):
                slab = kept[f][at + k]
                out[base[f] + k] = slab
                row = (sum(w * w for w in widths[:f])) + k * thick
                corner_outs[2 * s][row : row + thick] = slab[ny - thick :]
                corner_outs[2 * s + 1][row : row + thick] = slab[:thick]
        out[base[-1], :half, :width] = labels[place(nb, 1)].astype(F32)
    for out, high in zip(y_outs, (True, False)):
        for f, thick in enumerate(widths):
            for x in range(nx):
                row = base[f] * nx + x * thick
                out[row : row + thick] = kept[f][x, ny - thick :] if high else kept[f][x, :thick]
        row = base[-1] * nx
        for b in range(nb):
            line = labels[b, half - 1 :] if high else labels[b, :1]
            out[row + b : row + b + 1, :width] = line.astype(F32)


def slab_of(own, low, high, base, width, x):
    nx = own.shape[0]
    if HALO <= x < HALO + nx:
        return own[x - HALO]
    if x < HALO:
        at = x - (HALO - width)
        return low[base + at] if at >= 0 else None
    at = x - HALO - nx
    return high[base + at] if at < width else None


def pack_y_kernel(fields, flags, *refs):
    ins, rider = refs[:fields], refs[fields]
    low, high, to_high, to_low = refs[fields + 1 :]
    nx, ny = ins[0].shape[0], ins[0].shape[1]
    wide = nx + 2 * HALO
    for f in range(fields):
        for x in range(wide):
            slab = slab_of(ins[f], low, high, HALO * f, HALO, x)
            at = (f * wide + x) * HALO
            to_high[at : at + HALO] = slab[ny - HALO :]
            to_low[at : at + HALO] = slab[:HALO]
    at = fields * wide * HALO
    to_high[at:], to_low[at:] = rider[...], rider[...]


def packed_lanes(wide_ref, f, frame, rows, to_high, to_low):
    group = lane_no((1, LANES)) // HALO
    nothing = jnp.ones((rows.size, LANES), F32)
    high, low = nothing, nothing
    for x in range(frame.wide):
        moved = turned(wide_ref[f, x, rows], HALO * (x + 1), 1)
        high = jnp.where(group == x, moved, high)
        low = jnp.where(group == (x + 1) % frame.wide, moved, low)
    at = pl.ds(f * frame.tall + rows.start - SUB, rows.size)
    to_high[at] = high
    to_low[at] = turned(low, -HALO, 1)


def first_frame_kernel(count, widths, flags, *refs):
    fields = len(widths)
    ins, labels, refs = refs[:fields], refs[fields], refs[fields + 1 :]
    x_low, x_high, y_low, y_high = refs[:4]
    corners = refs[4:6] * 2 if count == 2 else refs[4:8]
    wide_ref, send_forth, send_back, to_high, to_low = refs[-5:]
    nx, ny = ins[0].shape[0], ins[0].shape[1]
    frame = Frame(nx, ny)
    base = bases(widths)
    tall, own = frame.tall, frame.own
    even = flags[PARITY] == 0
    ones = jnp.ones((frame.rows, LANES), F32)
    for f, thick in enumerate(widths):
        for x in range(frame.wide):
            slab = slab_of(ins[f], x_low, x_high, base[f], thick, x)
            if slab is None:
                wide_ref[f, x] = ones
                continue
            edge = ones[: SUB + HALO]
            wide_ref[f, x, :own] = edge
            wide_ref[f, x, own + ny :] = edge
            wide_ref[f, x, own : own + ny] = slab
            if HALO <= x < HALO + nx:
                low, high, row = y_low, y_high, base[f] * nx + (x - HALO) * thick
            else:
                above = x >= HALO
                low, high = corners[2 * above : 2 * above + 2]
                at = x - HALO - nx if above else x - (HALO - thick)
                row = sum(w * w for w in widths[:f]) + at * thick
            wide_ref[f, x, own - thick : own] = low[row : row + thick]
            wide_ref[f, x, own + ny : own + ny + thick] = high[row : row + thick]
        packed_lanes(wide_ref, f, frame, pl.ds(SUB, tall), to_high, to_low)
    high, low = to_high[...], to_low[...]
    size = fields * tall
    send_forth[:size], send_back[:size] = jnp.where(even, high, low), jnp.where(even, low, high)
    nb, rows, width = labels.shape
    lane = lane_no((rows, LANES))
    high = low = jnp.zeros((rows, LANES), F32)
    for b in range(nb):
        slab = labels[b].astype(F32)
        high = jnp.where(lane == b, slab[:, width - 1 :], high)
        low = jnp.where(lane == b, slab[:, :1], low)
    send_forth[size:], send_back[size:] = jnp.where(even, high, low), jnp.where(even, low, high)


def frame_kernel(fields, flags, *refs):
    ins = refs[:fields]
    x_low, x_high, _ = refs[fields : fields + 3]
    wide_ref, to_high, to_low = refs[fields + 3 :]
    nx, ny = ins[0].shape[0], ins[0].shape[1]
    frame = Frame(nx, ny)
    spare = jnp.ones((SUB, LANES), F32)
    for f in range(fields):
        for x in range(frame.wide):
            wide_ref[f, x, frame.own : frame.own + ny] = slab_of(ins[f], x_low, x_high, HALO * f, HALO, x)
            wide_ref[f, x, :SUB] = spare
            wide_ref[f, x, SUB + frame.tall :] = spare
        packed_lanes(wide_ref, f, frame, pl.ds(2 * SUB, frame.tall - 2 * SUB), to_high, to_low)


def pack_z_kernel(fields, flags, wide_in, high_in, low_in, from_low, from_high, rider, *refs):
    wide_ref, send_forth, send_back, to_high, to_low = refs
    frame = Frame(wide_ref.shape[1] - 2 * HALO, wide_ref.shape[2] - 2 * (SUB + HALO))
    ny, tall, own = frame.ny, frame.tall, frame.own
    even = flags[PARITY] == 0
    for f in range(fields):
        for x in range(frame.wide):
            at = (f * frame.wide + x) * HALO
            wide_ref[f, x, SUB:own] = from_low[at : at + HALO]
            wide_ref[f, x, own + ny : own + ny + HALO] = from_high[at : at + HALO]
    size = fields * tall
    to_high[...], to_low[...] = high_in[...], low_in[...]
    for f in range(fields):
        for start in (SUB, tall):
            packed_lanes(wide_ref, f, frame, pl.ds(start, SUB), to_high, to_low)
    high, low = to_high[...], to_low[...]
    send_forth[:size], send_back[:size] = jnp.where(even, high, low), jnp.where(even, low, high)
    send_forth[size:], send_back[size:] = rider[...], rider[...]


class Links:
    def __init__(self, mesh):
        self.sizes = [mesh.shape[a] for a in ("gx", "gy", "gz")]
        n_x, n_y, n_z = self.sizes

        def at(i, j, k):
            return (i % n_x * n_y + j % n_y) * n_z + k

        every = [(i, j, k) for i in range(n_x) for j in range(n_y) for k in range(n_z)]
        self.ring_x = [(i, (i + 1) % n_x) for i in range(n_x)]
        self.corner = {d: [(at(i, j, k), at(i + d, j + 1, k)) for i, j, k in every] for d in (1, -1)}
        self.snake = []
        for i in range(n_x):
            for j in range(0, n_y, 2):
                nodes = [at(i, j, k) for k in range(n_z)] + [at(i, j + 1, k) for k in reversed(range(n_z))]
                self.snake += [(nodes[m], nodes[(m + 1) % len(nodes)]) for m in range(len(nodes))]

    @staticmethod
    def back(pairs):
        return [(b, a) for a, b in pairs]

    @staticmethod
    def send(values, pairs):
        return lax.ppermute(values, ("gx", "gy", "gz"), pairs)

    def x(self, sends):
        if self.sizes[0] == 2:
            return (lax.ppermute(sends[0], "gx", self.ring_x),)
        return lax.ppermute(sends[0], "gx", self.ring_x), lax.ppermute(sends[1], "gx", self.back(self.ring_x))

    def near(self, values, x=None, y=None, z=None):
        forth, back = self.z(*(z or (values, values)))
        from_x = self.x(x or (values, values))
        return (forth, back, *from_x, *self.ring_y(*(y or (values, values))))

    def ring_y(self, to_high, to_low):
        ring = [(j, (j + 1) % self.sizes[1]) for j in range(self.sizes[1])]
        return lax.ppermute(to_high, "gy", ring), lax.ppermute(to_low, "gy", self.back(ring))

    def corners(self, sends):
        if self.sizes[0] == 2:
            return self.send(sends[0], self.corner[1]), self.send(sends[1], self.back(self.corner[1]))
        return (
            self.send(sends[0], self.corner[1]),
            self.send(sends[1], self.back(self.corner[-1])),
            self.send(sends[2], self.corner[-1]),
            self.send(sends[3], self.back(self.corner[1])),
        )

    def z(self, forth, back):
        return self.send(forth, self.snake), self.send(back, self.back(self.snake))


def send_y(arrays, rider, from_x):
    nx, ny, nz = arrays[0].shape
    rows = len(arrays) * Frame(nx, ny).wide * HALO + SUB
    kernel = functools.partial(pack_y_kernel, len(arrays))
    return call(kernel, [shaped(rows, nz)] * 2)(*arrays, rider, from_x[0], from_x[-1])


def framed(arrays, from_x, sent):
    nx, ny, nz = arrays[0].shape
    frame, fields = Frame(nx, ny), len(arrays)
    outs = [shaped(fields, *frame.main)] + [shaped(fields * frame.tall, nz)] * 2
    return call(functools.partial(frame_kernel, fields), outs)(*arrays, from_x[0], from_x[-1], sent)


def send_z(frames, from_y, rider):
    wide, high, _ = frames
    return call(
        functools.partial(pack_z_kernel, wide.shape[0]),
        [shaped(*wide.shape)] + [shaped(high.shape[0] + SUB, LANES)] * 2,
        [pltpu.VMEM(high.shape, F32)] * 2,
        aliases={0: 0},
    )(*frames, *from_y, rider)


def sides(flags, forth, back):
    even = flags[PARITY] == 0
    return jnp.where(even, forth, back), jnp.where(even, back, forth)


def weight(one, two):
    return 2.0 * (one * two) / (one + two)


def lane_mask(x):
    return ((lane_no((1, LANES)) - (HALO * x + HALO - 1)) & (LANES - 1)) < 2


def edge_step(here, x, edges):
    return jnp.where(lane_mask(x), turned(here, HALO * x + HALO, 1), edges)


def joined(below, above):
    lane = lane_no((1, LANES))
    return jnp.where(lane % HALO == HALO - 1, turned(above, HALO - 1, 1), turned(below, 1, 1))


def at_edges(join, x):
    lane = lane_no((1, LANES))
    return jnp.where((lane == 0) | (lane == LANES - 1), turned(join, (LANES - HALO) - HALO * x, 1), 0.0)


def ends_near(below, above, edges):
    layer = lane_no((1, LANES)) % HALO
    return (
        jnp.where(layer == HALO - 1, turned(edges, -1, 1), turned(below, -1, 1)),
        turned(below, 1, 1),
        turned(above, -1, 1),
        jnp.where(layer == 0, turned(edges, 1 - HALO, 1), turned(above, 1, 1)),
    )


def main_sums(frame, field, xs, join, wx, wy, wz):
    span = frame.span
    slabs = [field[xs[0] - 1 + k, span] for k in range(len(xs) + 2)]
    faces = [wx[xs[0] - 1 + k, span] for k in range(len(xs) + 1)]
    totals = []
    for k, x in enumerate(xs):
        here, face_y, face_z = slabs[k + 1], wy[x, span], wz[x, span]
        total = faces[k + 1] * slabs[k + 2] + faces[k] * slabs[k]
        total = total + face_y * turned(here, -1, 0) + turned(face_y * here, 1, 0)
        total = total + face_z * turned(here, -1, 1) + turned(face_z * here, 1, 1)
        totals.append(total + at_edges(join, x))
    return slabs[1:-1], totals


def ends_sum(frame, ends, s, upper, lower, wx, wy, wz_up, wz_low):
    span, down = frame.span, pl.ds(SUB - 1, frame.tall)
    here = ends[s, span]
    total = wx[s, span] * turned(here, -HALO, 1) + turned(wx[s, span] * here, HALO, 1)
    total = total + wy[s, span] * ends[s, pl.ds(SUB + 1, frame.tall)] + wy[s, down] * ends[s, down]
    return total + wz_up[s, span] * upper + wz_low[s, span] * lower


def clear_spares(ref, frame):
    for x in range(ref.shape[0]):
        ref[x, :SUB] = jnp.zeros((SUB, LANES), F32)
        ref[x, SUB + frame.tall :] = jnp.zeros((SUB, LANES), F32)


def pack_rows(values):
    half = values.shape[0] // 2
    lane = lane_no((half, LANES))
    return jnp.where(lane < LANES // 2, values[:half], turned(values[half:], LANES // 2, 1))


def lane_total(values):
    return jnp.broadcast_to(jnp.sum(values.T, axis=0, keepdims=True), (SUB, LANES))


def paired(values):
    even = 2 * (lane_no(values.shape) % (LANES // 2))
    return picked(values + turned(values, -1, 1), even)


def faces_y_kept(flags, frame):
    row = row_no((frame.tall, LANES))
    at_low, at_high = row == HALO - 1, row == HALO + frame.ny - 1
    return jnp.where(at_low, flags[Y_LOW], jnp.where(at_high, flags[Y_HIGH], 1)).astype(F32)


def face_rows(count, flags, nb):
    x = [(jnp.where(flags[IX] == 0, 1, 0), SUB)] if count == 2 else [(0, SUB), (1, SUB)]
    return x + [(2, nb // 2), (3, nb // 2), (4, 2), (5, 2)]


def add_rows(total, labels, b, values, c, rows=SUB):
    iota = row_no((AGG, LANES)).astype(F32)
    for r in range(rows):
        row = pl.ds(r, 1)
        total = total + jnp.where(labels[b, row] == iota, values[c, row], 0.0)
    return total


def pack_lanes(values):
    lane = lane_no((2, LANES))
    packed = values[:2]
    for g in range(1, SUB):
        packed = jnp.where(lane // 16 == g, turned(values[2 * g : 2 * g + 2], 16 * g, 1), packed)
    return packed


def fields_kernel(count, flags, wide_ref, block_label, inner, face_label, wx, wy, wz, partial, cond_edges, face_weight, diag):
    frame = Frame(wx.shape[0] - 2 * HALO, wx.shape[1] - 2 * (SUB + HALO))
    wide, tall, span = frame.wide, frame.tall, frame.span
    last = HALO + frame.nx
    keep_y = faces_y_kept(flags, frame)
    inside = jnp.where(lane_no((1, LANES)) == LANES - 1, 0.0, 1.0)

    def fields(xs, carry):
        before, edges = carry
        stores = []
        for x in xs:
            here = wide_ref[0, x, span]
            keep = jnp.where(x == HALO - 1, flags[X_LOW], jnp.where(x == last - 1, flags[X_HIGH], 1)).astype(F32)
            face_x = keep * weight(here, wide_ref[0, jnp.minimum(x + 1, wide - 1), span])
            face_y = keep_y * weight(here, wide_ref[0, x, pl.ds(SUB + 1, tall)])
            face_z = inside * weight(here, turned(here, -1, 1))
            total = wide_ref[2, x, span] + face_x + before + face_y + turned(face_y, 1, 0)
            total = total + face_z + turned(face_z, 1, 1)
            stores.append((x, (face_x, face_y, face_z, total)))
            edges = edge_step(here, x, edges)
            before = face_x
        for x, values in stores:
            for ref, value in zip((wx, wy, wz, partial), values):
                ref[x, span] = value
        return before, edges

    nothing = jnp.zeros((tall, LANES), F32)
    cond_edges[...] = batched(0, wide, fields, (nothing, nothing + 1.0), 4)[1]
    nb, ny = frame.nx // 2, frame.ny
    for s, x in enumerate((HALO - 1, last - 1)):
        rows = [wx[x, pl.ds(frame.own + c, ny // 2, stride=2)] for c in range(2)]
        face_weight[s] = pack_rows(paired(rows[0] + rows[1]))
    for s, at in ((2, frame.own - 1), (3, frame.own + ny - 1)):
        lines = [wy[HALO + 2 * b, at : at + 1] + wy[HALO + 2 * b + 1, at : at + 1] for b in range(nb)]
        face_weight[s, : nb // 2] = pack_rows(paired(jnp.concatenate(lines, axis=0)))
    around = jnp.zeros((AGG, LANES), F32)
    around = lax.fori_loop(0, nb, lambda b, around: add_rows(around, block_label, b, inner, b), around)
    for s, rows in face_rows(count, flags, nb)[:-2]:
        around = add_rows(around, face_label, s, face_weight, s, rows)
    diag[...] = lane_total(around)


def fine_kernel(flags, wide_ref, forth, back, wx, wy, wz, partial, cond_edges, block_label, face_label, some_diag,
                *refs):
    inv_diag, start = refs[:2]
    ends = refs[2:8]
    pre, face_weight, scaled_rhs, scale, once, once_ends, res, diag, block_res = refs[8:]
    ex, ey, ez_up, ez_low, inv_ends, start_ends = ends
    nx, ny = pre.shape[0], pre.shape[1]
    frame = Frame(nx, ny)
    wide, tall, span = frame.wide, frame.tall, frame.span
    last = HALO + nx
    got = [sides(flags, forth[f * tall : (f + 1) * tall], back[f * tall : (f + 1) * tall]) for f in range(3)]
    (cond_below, cond_above), rhs_ends, absorb_ends = got
    for ref in (ey, start_ends, once_ends):
        clear_spares(ref, frame)

    lane = lane_no((1, LANES))
    keep_y = faces_y_kept(flags, frame)
    keep_low, keep_high = flags[Z_LOW].astype(F32), flags[Z_HIGH].astype(F32)
    near = ends_near(cond_below, cond_above, cond_edges[...])
    slab = lane // HALO
    keep_x = jnp.where(
        slab == HALO - 1, flags[X_LOW], jnp.where(slab == last - 1, flags[X_HIGH], 1)
    ).astype(F32)
    layer = lane % HALO
    for s, here in enumerate((cond_below, cond_above)):
        up, low = weight(here, near[2 * s]), weight(here, near[2 * s + 1])
        if s == 0:
            up = up * jnp.where(layer == HALO - 1, keep_low, 1.0)
        else:
            low = low * jnp.where(layer == 0, keep_high, 1.0)
        face_x = keep_x * weight(here, turned(here, -HALO, 1))
        face_y = keep_y * weight(here, turned(here, -1, 0))
        ex[s, span], ey[s, span], ez_up[s, span], ez_low[s, span] = face_x, face_y, up, low
        total = absorb_ends[s] + face_x + turned(face_x, HALO, 1) + face_y + turned(face_y, 1, 0) + up + low
        inverse = OMEGA_FINE / total
        inv_ends[s, span] = inverse
        start_ends[s, span] = inverse * rhs_ends[s]

    end_low, end_high = ez_up[0, span], ez_low[1, span]
    join_faces = joined(end_low, end_high)

    def first_sweep(xs, edges):
        stores = []
        for x in xs:
            total = partial[x, span] + at_edges(join_faces, x)
            inverse = OMEGA_FINE / total
            begin = inverse * wide_ref[1, x, span]
            stores.append((x, (total, inverse, begin)))
            edges = edge_step(begin, x, edges)
        for x, values in stores:
            for ref, value in zip((diag, inv_diag, start), values):
                ref[x, span] = value
        return edges

    edges = batched(0, wide, first_sweep, jnp.zeros((tall, LANES), F32), 4)

    join = joined(end_low * start_ends[0, span], end_high * start_ends[1, span])
    near = ends_near(start_ends[0, span], start_ends[1, span], edges)
    for s in range(2):
        total = ends_sum(frame, start_ends, s, near[2 * s], near[2 * s + 1], ex, ey, ez_up, ez_low)
        once_ends[s, span] = (2.0 - OMEGA_FINE) * start_ends[s, span] + inv_ends[s, span] * total

    def second(xs, carry):
        news = []
        for x, here, total in zip(xs, *main_sums(frame, start, xs, join, wx, wy, wz)):
            news.append((2.0 - OMEGA_FINE) * here + inv_diag[x, span] * total)
        for x, new in zip(xs, news):
            once[x, span] = new
        return carry

    batched(HALO - 1, last + 1, second, 0, 13 if (nx + 2) % 13 == 0 else 6)
    join2 = joined(end_low * once_ends[0, span], end_high * once_ends[1, span])

    def remainder(xs, carry):
        news = []
        for x, here, total in zip(xs, *main_sums(frame, once, xs, join2, wx, wy, wz)):
            news.append(wide_ref[1, x, span] - diag[x, span] * here + total)
        for x, new in zip(xs, news):
            res[x - HALO, span] = new
        for x in xs:
            pre[x - HALO] = once[x, pl.ds(frame.own, ny)]
        return carry

    batched(HALO, last, remainder, 0, 8)

    nb, half = nx // 2, ny // 2

    def rows_at(ref, x, off):
        return ref[x, pl.ds(frame.own + off, half, stride=2)]

    def to_blocks(bs, carry):
        for b in bs:
            four = sum(rows_at(res, 2 * b + a, c) for a in range(2) for c in range(2))
            block_res[b] = pack_rows(paired(four))
        return carry

    batched(0, nb, to_blocks, 0)
    zeros = jnp.zeros((AGG, LANES), F32)
    sums = lax.fori_loop(0, nb, lambda b, total: add_rows(total, block_label, b, block_res, b), zeros)

    lane = lane_no((half, LANES))
    around = zeros
    for s, (ref, side, layer_at) in enumerate(((ez_up, 0, HALO - 1), (ez_low, 1, 0))):
        values = rows_at(ref, side, 0) + rows_at(ref, side, 1)
        values = values + turned(values, -HALO, 1)
        spot = jnp.minimum(2 * HALO * lane + HALO * HALO + layer_at, LANES - 1)
        face_weight[s, :2] = pack_lanes(jnp.where(lane < nb, picked(values, spot), 0.0))
        around = add_rows(around, face_label, 4 + s, face_weight, s, 2)
    scale[...] = OMEGA_COARSE / (some_diag[...] + lane_total(around))
    scaled_rhs[...] = scale[...] * lane_total(sums)


def tile_sum(tile, rows, label_at, pairs_at, group=4):
    iota = row_no((AGG, LANES)).astype(F32)
    for first in range(0, rows, group):
        places, highs, lows = [], [], []
        for r in range(first, min(first + group, rows)):
            places.append(jnp.where(label_at(r) == iota, 1.0, 0.0).astype(BF16))
            held = sum(jnp.where(near == iota, w, 0.0) for near, w in pairs_at(r))
            highs.append(held.astype(BF16))
            lows.append((held - highs[-1].astype(F32)).astype(BF16))
        left = jnp.concatenate(places, axis=1)
        right = jnp.concatenate([jnp.concatenate(highs, axis=1), jnp.concatenate(lows, axis=1)], axis=0)
        tile = tile + lax.dot_general(left, right, (((1,), (1,)), ((), ())), preferred_element_type=F32)
    return tile


def both_halves(tile):
    return tile[:, :AGG] + tile[:, AGG:]


def keep_tile(out, t, tile):
    high = tile.astype(BF16)
    rows = pl.ds(t * AGG, AGG)
    out[rows, :AGG] = high
    out[rows, AGG:] = (tile - high.astype(F32)).astype(BF16)


def blocks_kernel(flags, cond, absorb, block_agg, block_label, near, weights, inner, face_label, fine_label,
                  part, line):
    nx, ny = cond.shape[0], cond.shape[1]
    nb, half, width = nx // 2, ny // 2, LANES // 2
    lane, row = lane_no((half, LANES)), row_no((half, LANES))

    def halves(values, slot):
        part[slot] = values
        return part[slot, pl.ds(0, half, stride=2)], part[slot, pl.ds(1, half, stride=2)]

    def label_at(b):
        values = block_agg[b].astype(F32)
        return jnp.concatenate([values, values], axis=1)

    def upper_x(b, slot):
        x = jnp.maximum(2 * b, 0)
        faces = weight(cond[x + 1], cond[jnp.minimum(x + 2, nx - 1)])
        return jnp.where((b == nb - 1) | (b < 0), 0.0, paired(sum(halves(faces, slot))))

    def step(bs, carry):
        low_x = upper_x(bs[0] - 1, 0)
        for k, b in enumerate(bs):
            x = 2 * b
            slot = 4 * k + 1
            one, two = cond[x], cond[x + 1]
            both_y = weight(one, turned(one, -1, 0)) + weight(two, turned(two, -1, 0))
            both_z = weight(one, turned(one, -1, 1)) + weight(two, turned(two, -1, 1))
            high_x = upper_x(b, slot)
            high_y = jnp.where(row == half - 1, 0.0, paired(halves(both_y, slot + 1)[1]))
            high_z = picked(sum(halves(both_z, slot + 2)), 2 * (lane % width) + 1)
            high_z = jnp.where(lane % width == width - 1, 0.0, high_z)
            low_y, low_z = turned(high_y, 1, 0), turned(high_z, 1, 1)
            own = label_at(b)
            near_x, past_x = label_at(jnp.minimum(b + 1, nb - 1)), label_at(jnp.maximum(b - 1, 0))
            near_y, past_y = turned(own, -1, 0), turned(own, 1, 0)
            near_z, past_z = turned(own, -1, 1), turned(own, 1, 1)
            total = paired(sum(halves(absorb[x] + absorb[x + 1], slot + 3)))
            for beside, values in (
                (near_x, high_x), (past_x, low_x), (near_y, high_y), (past_y, low_y), (near_z, high_z), (past_z, low_z)
            ):
                total = total + jnp.where(beside != own, values, 0.0)
            block_label[b] = pack_rows(own)
            inner[b] = pack_rows(total)
            for d, (beside, values) in enumerate(((near_x, high_x), (near_y, high_y), (near_z, high_z))):
                near[d, b], weights[d, b] = pack_rows(beside), pack_rows(values)
            spread = picked(own, lane // 2)
            for a in range(2):
                for c in range(2):
                    fine_label[x + a, pl.ds(c, half, stride=2)] = spread
            low_x = high_x
        return carry

    batched(0, nb, step, 0, 4)
    line[...] = jnp.zeros(line.shape, F32)
    low, high = jnp.zeros((half, LANES), F32), jnp.zeros((half, LANES), F32)
    for b in range(nb):
        own = label_at(b)
        line[0, b : b + 1], line[1, b : b + 1] = own[:1], own[half - 1 :]
        low = jnp.where(lane == b, own[:, :1], low)
        high = jnp.where(lane == b, own[:, width - 1 : width], high)
    face_label[0], face_label[1] = block_label[0], block_label[nb - 1]
    for s in range(2):
        face_label[2 + s, : nb // 2] = pack_rows(line[s, :nb])
        face_label[4 + s, :2] = pack_lanes((low, high)[s])


def own_kernel(first, last, total, flags, block_label, near, weights, *refs):
    so_far, refs = (refs[0], refs[1:]) if first else (None, refs)
    refs = refs[1:]

    def step(b, tile):
        def pairs_at(r):
            return [(near[d, b, pl.ds(r, 1)], weights[d, b, pl.ds(r, 1)]) for d in range(3)]

        return tile_sum(tile, SUB, lambda r: block_label[b, pl.ds(r, 1)], pairs_at)

    tile = so_far[...] if first else jnp.zeros((AGG, 2 * AGG), F32)
    tile = lax.fori_loop(first, last, step, tile)
    if last < total:
        refs[0][...] = tile
        return
    tile = both_halves(tile)
    keep_tile(refs[0], 0, jnp.where(row_no((AGG, AGG)) == lane_no((AGG, AGG)), 0.0, tile + tile.T))


def faces_kernel(count, nb, flags, own, face_label, weight_xy, weight_z, x_low, x_high, y_low, y_high, forth, back, out,
                 near, weights):
    out[:AGG] = own[...]
    at, half = x_low.shape[0] - 1, x_low.shape[1] // 2
    near[0], near[1] = pack_rows(x_low[at, :half]), pack_rows(x_high[at, :half])
    at = sum(WIDTHS) * 2 * nb
    for s, ref in enumerate((y_low, y_high)):
        near[2 + s, : nb // 2] = pack_rows(ref[at : at + nb])
    at = forth.shape[0] - half
    for s, values in enumerate(sides(flags, forth[at:], back[at:])):
        near[4 + s, :2] = pack_lanes(values)
    weights[:4], weights[4:] = weight_xy[...], weight_z[...]
    for t, (s, rows) in enumerate(face_rows(count, flags, nb)):
        tile = tile_sum(
            jnp.zeros((AGG, 2 * AGG), F32),
            rows,
            lambda r, s=s: near[s, pl.ds(r, 1)],
            lambda r, s=s: [(face_label[s, pl.ds(r, 1)], weights[s, pl.ds(r, 1)])],
        )
        keep_tile(out, t + 1, both_halves(tile))


def turn_kernel(flags, tiles, scaled_rhs, scale, own, *refs):
    forth, back, *others, out = refs
    got = [ref[ref.shape[0] - 1, :SUB] if len(ref.shape) == 3 else ref[ref.shape[0] - SUB :] for ref in (*others, forth, back)]
    vectors = [own[...], *got[:-2], *sides(flags, *got[-2:])]
    row = row_no((SUB, AGG))
    parts = []
    for v in vectors:
        high = v.astype(BF16).astype(F32)
        parts.append(jnp.where(row == 0, high, jnp.where(row == 1, v - high, 0.0)).astype(BF16))
    got = jnp.dot(jnp.concatenate(parts, axis=1), tiles[...], preferred_element_type=F32)
    applied = jnp.sum(got[:, :AGG] + got[:, AGG:], axis=0, keepdims=True)
    out[...] = (1.0 - OMEGA_COARSE) * own[...] + scaled_rhs[...] + scale[...] * applied


def ride_kernel(count, flags, field, coarse, *outs):
    nx = field.shape[0]
    for s, out in enumerate(outs):
        at = jnp.where(flags[IX] == 0, nx - HALO, 0) if count == 2 else (nx - HALO, 0)[s]
        for x in range(HALO):
            out[x] = field[at + x]
        out[HALO] = jnp.zeros(out.shape[1:], F32)
        out[HALO, :SUB] = coarse[...]


def three_kernel(flags, low, mid, high, out):
    row = row_no(out.shape)
    out[...] = jnp.where(row == 0, low[...], jnp.where(row == 1, mid[...], high[...]))


def nine_kernel(flags, low, mid, high, out):
    out[...] = jnp.zeros(out.shape, F32)
    for n, ref in enumerate((low, mid, high)):
        out[3 * n : 3 * n + 3] = ref[:3]


def lift_kernel(flags, wide_ref, forth, back, main, ends):
    frame = Frame(wide_ref.shape[1] - 2 * HALO, wide_ref.shape[2] - 2 * (SUB + HALO))
    tall = frame.tall
    for b in range(frame.wide // 2):
        main[b] = wide_ref[0, 2 * b, frame.span].astype(jnp.int32)
    rows = pl.ds(0, tall)
    for s, values in enumerate(sides(flags, forth[rows], back[rows])):
        ends[s] = values.astype(jnp.int32)


def post_kernel(flags, table, table_forth, table_back, labels, end_labels, wide_ref, forth, back, *refs):
    (wx, wy, wz, inv_diag, start), ends = refs[:5], refs[5:11]
    out, one, two, one_ends, two_ends, kept_out, sems = refs[11:]
    nx, ny = out.shape[0], out.shape[1]
    frame = Frame(nx, ny)
    wide, tall, span = frame.wide, frame.tall, frame.span
    ex, ey, ez_up, ez_low, inv_ends, start_ends = ends
    for ref in (one_ends, two_ends):
        clear_spares(ref, frame)
    row, lane = row_no((tall, LANES)), lane_no((tall, LANES))
    under, over = sides(flags, table_forth[...], table_back[...])
    tables = {-1: under, 0: table[...], 1: over}

    def table_at(dx, dz):
        low, mid, high = (tables[dz][3 * n + dx + 1 : 3 * n + dx + 2] for n in range(3))
        return jnp.where(row < HALO, low, jnp.where(row < HALO + ny, mid, high))

    for x_from, x_to, dx in ((0, HALO, -1), (HALO, HALO + nx, 0), (HALO + nx, wide, 1)):
        values = table_at(dx, 0)

        def lift(bs, carry, values=values):
            news = [picked(values, labels[b]) for b in bs]
            for b, new in zip(bs, news):
                for a in range(2):
                    two[2 * b + a, span] = wide_ref[0, 2 * b + a, span] + new
            return carry

        batched(x_from // 2, x_to // 2, lift, 0, 4)
    for s, (dz, base) in enumerate(zip((-1, 1), sides(flags, forth[:tall], back[:tall]))):
        below, inside, above = (picked(table_at(dx, dz), end_labels[s]) for dx in (-1, 0, 1))
        spot = lane // HALO
        lifted = jnp.where(spot < HALO, below, jnp.where(spot < HALO + nx, inside, above))
        two_ends[s, span] = base + lifted
    kept = 1.0 - OMEGA_FINE

    def result(at, count):
        rows = pl.ds(at, count)
        return pltpu.make_async_copy(kept_out.at[rows], out.at[rows], sems.at[at // count])

    buffers = ((two, two_ends), (one, one_ends), (two, two_ends), (one, one_ends))
    for s in range(POST):
        src, src_ends = buffers[s]
        join = joined(ez_up[0, span] * src_ends[0, span], ez_low[1, span] * src_ends[1, span])
        final = s == POST - 1
        dst, dst_ends = (None, None) if final else buffers[s + 1]

        def step(xs, edges, src=src, join=join, dst=dst, final=final):
            news = []
            for x, here, total in zip(xs, *main_sums(frame, src, xs, join, wx, wy, wz)):
                news.append(kept * here + start[x, span] + inv_diag[x, span] * total)
                if not final:
                    edges = edge_step(here, x, edges)
            for x, new in zip(xs, news):
                if final:
                    kept_out[x - HALO] = new[HALO : HALO + ny]
                else:
                    dst[x, span] = new
            if final:
                result(xs[0] - HALO, len(xs)).start()
            return edges

        size = 8 if final else 10
        edges = batched(s + 1, wide - s - 1, step, jnp.zeros((tall, LANES), F32), size)
        if not final:
            near = ends_near(src_ends[0, span], src_ends[1, span], edges)
            news = []
            for e in range(2):
                total = ends_sum(frame, src_ends, e, near[2 * e], near[2 * e + 1], ex, ey, ez_up, ez_low)
                news.append(kept * src_ends[e, span] + start_ends[e, span] + inv_ends[e, span] * total)
            dst_ends[0, span], dst_ends[1, span] = news
    for n in range(nx // 8):
        result(8 * n, 8).wait()


def body(links, right_side, conductance, absorption, block_agg):
    nx, ny, nz = right_side.shape
    frame = Frame(nx, ny)
    nb = nx // 2
    n_x = links.sizes[0]
    arrays = (conductance, right_side, absorption, block_agg)
    n_send = 1 if n_x == 2 else 2
    pinned = [pltpu.with_memory_space_constraint(a, pltpu.HBM) for a in arrays]
    outs = [jax.ShapeDtypeStruct(a.shape, a.dtype) for a in arrays]
    outs += [shaped(sum(WIDTHS) + 1, ny, nz)] * n_send + [shaped(sum(WIDTHS) * nx + 16, nz)] * 2
    outs += [shaped(-(-sum(w * w for w in WIDTHS) // SUB) * SUB, nz)] * (2 * n_send)
    got = call(
        functools.partial(pack_kernel, n_x, WIDTHS),
        outs,
        [pltpu.SemaphoreType.DMA((3 * 4,))],
        in_specs=[pl.BlockSpec(memory_space=pltpu.HBM)] * 4,
    )(*pinned)
    arrays, sends = got[:4], got[4:]
    from_x = links.x(sends[:n_send])
    from_y = links.ring_y(*sends[n_send : n_send + 2])
    blocks = (nb, SUB, LANES)
    outs = [shaped(*blocks), shaped(3, *blocks), shaped(3, *blocks), shaped(*blocks), shaped(6, SUB, LANES)]
    outs += [shaped(nx, ny, nz)]
    scratch = [pltpu.VMEM((17, ny, LANES), F32), pltpu.VMEM((2, ny // 2, LANES), F32)]
    *rows, inner, face_label, fine_label = call(blocks_kernel, outs, scratch)(arrays[0], arrays[2], arrays[3])
    block_label = rows[0]
    bounds = [nb * n // 12 for n in (0, 5, 8, 11, 12)]

    def own_part(p, *more):
        out = jax.ShapeDtypeStruct((AGG, 2 * AGG), BF16) if p == 3 else shaped(AGG, 2 * AGG)
        return call(functools.partial(own_kernel, bounds[p], bounds[p + 1], nb), [out])(*rows, *more)[0]

    own_tile = own_part(0, sends[0])
    *corner_sends, own_tile = lax.optimization_barrier((*sends[n_send + 2 :], own_tile))
    from_corners = links.corners(corner_sends)
    own_tile = own_part(1, own_tile, sends[0])
    got = lax.optimization_barrier((*from_x, *from_y, *from_corners, own_tile))
    from_x, from_y, from_corners, own_tile = got[:n_send], got[n_send : n_send + 2], got[n_send + 2 : -1], got[-1]
    size = len(WIDTHS) * frame.tall
    wide, *sends = call(
        functools.partial(first_frame_kernel, n_x, WIDTHS),
        [shaped(len(WIDTHS), *frame.main)] + [shaped(size + ny // 2, nz)] * 2,
        [pltpu.VMEM((size, nz), F32)] * 2,
    )(*arrays, from_x[0], from_x[-1], *from_y, *from_corners)
    outs = [shaped(*frame.main)] * 4 + [shaped(frame.tall, nz), shaped(4, SUB, LANES), shaped(SUB, AGG)]
    *fields, weight_xy, some_diag = call(functools.partial(fields_kernel, n_x), outs, limit=24)(
        wide, block_label, inner, face_label
    )
    own_tile = own_part(2, own_tile, sends[0])
    halo = (wide, *links.z(*sends))
    *halo, own_tile = lax.optimization_barrier((*halo, own_tile))
    outs = [shaped(*frame.main)] * 2 + [shaped(*frame.ends)] * 6 + [shaped(nx, ny, nz)]
    outs += [shaped(2, SUB, LANES)] + [shaped(SUB, AGG)] * 2
    scratch = [pltpu.VMEM(frame.main, F32), pltpu.VMEM(frame.ends, F32), pltpu.VMEM((nx, frame.rows, LANES), F32)]
    scratch += [pltpu.VMEM(frame.main, F32), pltpu.VMEM(blocks, F32)]
    got = call(fine_kernel, outs, scratch, limit=28)(
        *halo, *fields, block_label, face_label, some_diag
    )
    fields, pre = (*fields[:3], *got[:8]), got[8]
    weight_z, scaled_rhs, scale = got[9:]
    own_tile = own_part(3, own_tile, scaled_rhs)
    tiles = call(
        functools.partial(faces_kernel, n_x, nb),
        jax.ShapeDtypeStruct(((n_send + 5) * AGG, 2 * AGG), BF16),
        [pltpu.VMEM((6, SUB, LANES), F32)] * 2,
    )(own_tile, face_label, weight_xy, weight_z, from_x[0], from_x[-1], *from_y, *halo[1:])
    coarse = scaled_rhs

    def turn(coarse, **more):
        near = links.near(coarse, **more)
        return call(turn_kernel, shaped(SUB, AGG))(tiles, scaled_rhs, scale, coarse, *near), near

    def ridden(field, coarse):
        kernel = functools.partial(ride_kernel, n_x)
        rides = call(kernel, [shaped(HALO + 1, ny, nz)] * n_send)(field, coarse)
        coarse, near = turn(coarse, x=rides)
        from_x = near[2:-2]
        rides = send_y((field,), coarse, from_x)
        frames = framed((field,), from_x, rides[0])
        coarse, near = turn(coarse, y=rides)
        wide, *rides = send_z(frames, near[-2:], coarse)
        coarse, near = turn(coarse, z=rides)
        return coarse, (wide, *near[:2])

    coarse, halo = ridden(pre, coarse)
    coarse, label_halo = ridden(fine_label, coarse)
    outs = [jax.ShapeDtypeStruct((frame.wide // 2, frame.tall, nz), jnp.int32)]
    outs += [jax.ShapeDtypeStruct((2, frame.tall, nz), jnp.int32)]
    lifts = call(lift_kernel, outs)(*label_halo)
    for _ in range(KC - 7):
        coarse, _ = turn(coarse)
    from_x = links.x([coarse] * n_send)
    three = call(three_kernel, shaped(SUB, AGG))(from_x[0], coarse, from_x[-1])
    low, high = links.ring_y(three, three)
    nine = call(nine_kernel, shaped(2 * SUB, AGG))(low, three, high)
    tables = (nine, *links.z(nine, nine))
    scratch = [pltpu.VMEM(frame.main, F32)] * 2 + [pltpu.VMEM(frame.ends, F32)] * 2
    scratch += [pltpu.VMEM((nx, ny, nz), F32), pltpu.SemaphoreType.DMA((nx // 8,))]
    return call(post_kernel, shaped(nx, ny, nz), scratch, limit=24, out_specs=pl.BlockSpec(memory_space=pl.ANY))(
        *tables, *lifts, *halo, *fields
    )


def solution(mesh):
    spec = P("gx", "gy", "gz")
    return jax.shard_map(
        functools.partial(body, Links(mesh)), mesh=mesh, in_specs=(spec,) * 4, out_specs=spec, check_vma=False
    )
```

```python
import functools

import jax
import jax.numpy as jnp
from jax import lax
from jax.experimental import pallas as pl
from jax.experimental.pallas import tpu as pltpu
from jax.sharding import PartitionSpec as P

AGG = 128
LANES = 128
SUB = 8
HALO = 4
WIDTHS = (4, 3, 3)
POST = 4
KC = 8
OMEGA_FINE = 0.8
OMEGA_COARSE = 0.7
F32 = jnp.float32
BF16 = jnp.bfloat16
VMEM = pl.BlockSpec(memory_space=pltpu.VMEM)
IX, PARITY, X_LOW, X_HIGH, Y_LOW, Y_HIGH, Z_LOW, Z_HIGH = range(8)


def places():
    (ix, n_x), (iy, n_y), (iz, n_z) = ((lax.axis_index(a), lax.axis_size(a)) for a in ("gx", "gy", "gz"))
    flags = [ix, iy % 2, ix > 0, ix < n_x - 1, iy > 0, iy < n_y - 1, iz > 0, iz < n_z - 1]
    return [jnp.asarray(flag, jnp.int32) for flag in flags]


def call(kernel, outs, scratch=(), limit=16, flops=10**6, in_specs=None, aliases=None, out_specs=None):
    def placed(*refs):
        kernel(places(), *refs)

    def run(*arrays):
        return pl.pallas_call(
            placed,
            out_shape=outs,
            in_specs=in_specs or [VMEM] * len(arrays),
            out_specs=out_specs or jax.tree.map(lambda _: VMEM, outs),
            scratch_shapes=list(scratch),
            input_output_aliases=aliases or {},
            compiler_params=pltpu.CompilerParams(vmem_limit_bytes=limit * 2**20),
            cost_estimate=pl.CostEstimate(flops=flops, bytes_accessed=10**5, transcendentals=0),
        )(*arrays)

    return run


def shaped(*shape):
    return jax.ShapeDtypeStruct(shape, F32)


def lane_no(shape):
    return lax.broadcasted_iota(jnp.int32, shape, len(shape) - 1)


def row_no(shape):
    return lax.broadcasted_iota(jnp.int32, shape, len(shape) - 2)


def turned(values, shift, axis):
    if isinstance(shift, int):
        shift = shift % values.shape[axis]
        if shift == 0:
            return values
    return pltpu.roll(values, shift, axis)


def batched(low, high, step, carry, size=6):
    def some(i, carry):
        return step([low + i * size + k for k in range(size)], carry)

    carry = lax.fori_loop(0, (high - low) // size, some, carry)
    rest = (high - low) % size
    return step(list(range(high - rest, high)), carry) if rest else carry


def picked(values, index):
    return jnp.take_along_axis(values, index, axis=1, mode="promise_in_bounds")


class Frame:
    def __init__(self, nx, ny):
        self.nx, self.ny = nx, ny
        self.wide, self.tall = nx + 2 * HALO, ny + 2 * HALO
        self.rows = self.tall + 2 * SUB
        self.span = pl.ds(SUB, self.tall)
        self.own = SUB + HALO
        self.main = (self.wide, self.rows, LANES)
        self.ends = (2, self.rows, LANES)


def bases(widths):
    return [sum(widths[:f]) for f in range(len(widths) + 1)]


def copied(pairs, sems):
    copies = [pltpu.make_async_copy(src, dst, sems.at[n]) for n, (src, dst) in enumerate(pairs)]
    for copy in copies:
        copy.start()
    return copies


def pack_kernel(count, widths, flags, *refs):
    fields = len(widths)
    n_x = 1 if count == 2 else 2
    ins, kept = refs[: fields + 1], refs[fields + 1 : 2 * fields + 2]
    outs, sems = refs[2 * fields + 2 : -1], refs[-1]
    x_outs, y_outs, corner_outs = outs[:n_x], outs[n_x : n_x + 2], outs[n_x + 2 :]
    nx, ny = ins[0].shape[0], ins[0].shape[1]
    nb, half, width = ins[-1].shape
    thirds = 3
    copies = []
    for ref, out in zip(ins, kept):
        for t in range(thirds):
            size = ref.shape[0] // thirds
            rows = pl.ds(t * size, size)
            copies.append(pltpu.make_async_copy(ref.at[rows], out.at[rows], sems.at[len(copies)]))
    for copy in copies:
        copy.start()
    for out in (*x_outs, *y_outs):
        out[...] = jnp.zeros(out.shape, F32)
    for copy in copies:
        copy.wait()
    base = bases(widths)
    labels = kept[-1]
    for s, out in enumerate(x_outs):

        def place(size, thick, s=s):
            if count == 2:
                return jnp.where(flags[IX] == 0, size - thick, 0)
            return (size - thick, 0)[s]

        for f, thick in enumerate(widths):
            at = place(nx, thick)
            for k in range(thick):
                slab = kept[f][at + k]
                out[base[f] + k] = slab
                row = (sum(w * w for w in widths[:f])) + k * thick
                corner_outs[2 * s][row : row + thick] = slab[ny - thick :]
                corner_outs[2 * s + 1][row : row + thick] = slab[:thick]
        out[base[-1], :half, :width] = labels[place(nb, 1)].astype(F32)
    for out, high in zip(y_outs, (True, False)):
        for f, thick in enumerate(widths):
            for x in range(nx):
                row = base[f] * nx + x * thick
                out[row : row + thick] = kept[f][x, ny - thick :] if high else kept[f][x, :thick]
        row = base[-1] * nx
        for b in range(nb):
            line = labels[b, half - 1 :] if high else labels[b, :1]
            out[row + b : row + b + 1, :width] = line.astype(F32)


def slab_of(own, low, high, base, width, x):
    nx = own.shape[0]
    if HALO <= x < HALO + nx:
        return own[x - HALO]
    if x < HALO:
        at = x - (HALO - width)
        return low[base + at] if at >= 0 else None
    at = x - HALO - nx
    return high[base + at] if at < width else None


def pack_y_kernel(fields, flags, *refs):
    ins, rider = refs[:fields], refs[fields]
    low, high, to_high, to_low = refs[fields + 1 :]
    nx, ny = ins[0].shape[0], ins[0].shape[1]
    wide = nx + 2 * HALO
    for f in range(fields):
        for x in range(wide):
            slab = slab_of(ins[f], low, high, HALO * f, HALO, x)
            at = (f * wide + x) * HALO
            to_high[at : at + HALO] = slab[ny - HALO :]
            to_low[at : at + HALO] = slab[:HALO]
    at = fields * wide * HALO
    to_high[at:], to_low[at:] = rider[...], rider[...]


def packed_lanes(wide_ref, f, frame, rows, to_high, to_low):
    group = lane_no((1, LANES)) // HALO
    nothing = jnp.ones((rows.size, LANES), F32)
    high, low = nothing, nothing
    for x in range(frame.wide):
        moved = turned(wide_ref[f, x, rows], HALO * (x + 1), 1)
        high = jnp.where(group == x, moved, high)
        low = jnp.where(group == (x + 1) % frame.wide, moved, low)
    at = pl.ds(f * frame.tall + rows.start - SUB, rows.size)
    to_high[at] = high
    to_low[at] = turned(low, -HALO, 1)


def first_frame_kernel(count, widths, flags, *refs):
    fields = len(widths)
    ins, labels, refs = refs[:fields], refs[fields], refs[fields + 1 :]
    x_low, x_high, y_low, y_high = refs[:4]
    corners = refs[4:6] * 2 if count == 2 else refs[4:8]
    wide_ref, send_forth, send_back, to_high, to_low = refs[-5:]
    nx, ny = ins[0].shape[0], ins[0].shape[1]
    frame = Frame(nx, ny)
    base = bases(widths)
    tall, own = frame.tall, frame.own
    even = flags[PARITY] == 0
    ones = jnp.ones((frame.rows, LANES), F32)
    for f, thick in enumerate(widths):
        for x in range(frame.wide):
            slab = slab_of(ins[f], x_low, x_high, base[f], thick, x)
            if slab is None:
                wide_ref[f, x] = ones
                continue
            edge = ones[: SUB + HALO]
            wide_ref[f, x, :own] = edge
            wide_ref[f, x, own + ny :] = edge
            wide_ref[f, x, own : own + ny] = slab
            if HALO <= x < HALO + nx:
                low, high, row = y_low, y_high, base[f] * nx + (x - HALO) * thick
            else:
                above = x >= HALO
                low, high = corners[2 * above : 2 * above + 2]
                at = x - HALO - nx if above else x - (HALO - thick)
                row = sum(w * w for w in widths[:f]) + at * thick
            wide_ref[f, x, own - thick : own] = low[row : row + thick]
            wide_ref[f, x, own + ny : own + ny + thick] = high[row : row + thick]
        packed_lanes(wide_ref, f, frame, pl.ds(SUB, tall), to_high, to_low)
    high, low = to_high[...], to_low[...]
    size = fields * tall
    send_forth[:size], send_back[:size] = jnp.where(even, high, low), jnp.where(even, low, high)
    nb, rows, width = labels.shape
    lane = lane_no((rows, LANES))
    high = low = jnp.zeros((rows, LANES), F32)
    for b in range(nb):
        slab = labels[b].astype(F32)
        high = jnp.where(lane == b, slab[:, width - 1 :], high)
        low = jnp.where(lane == b, slab[:, :1], low)
    send_forth[size:], send_back[size:] = jnp.where(even, high, low), jnp.where(even, low, high)


def frame_kernel(fields, flags, *refs):
    ins = refs[:fields]
    x_low, x_high, _ = refs[fields : fields + 3]
    wide_ref, to_high, to_low = refs[fields + 3 :]
    nx, ny = ins[0].shape[0], ins[0].shape[1]
    frame = Frame(nx, ny)
    spare = jnp.ones((SUB, LANES), F32)
    for f in range(fields):
        for x in range(frame.wide):
            wide_ref[f, x, frame.own : frame.own + ny] = slab_of(ins[f], x_low, x_high, HALO * f, HALO, x)
            wide_ref[f, x, :SUB] = spare
            wide_ref[f, x, SUB + frame.tall :] = spare
        packed_lanes(wide_ref, f, frame, pl.ds(2 * SUB, frame.tall - 2 * SUB), to_high, to_low)


def pack_z_kernel(fields, flags, wide_in, high_in, low_in, from_low, from_high, rider, *refs):
    wide_ref, send_forth, send_back, to_high, to_low = refs
    frame = Frame(wide_ref.shape[1] - 2 * HALO, wide_ref.shape[2] - 2 * (SUB + HALO))
    ny, tall, own = frame.ny, frame.tall, frame.own
    even = flags[PARITY] == 0
    for f in range(fields):
        for x in range(frame.wide):
            at = (f * frame.wide + x) * HALO
            wide_ref[f, x, SUB:own] = from_low[at : at + HALO]
            wide_ref[f, x, own + ny : own + ny + HALO] = from_high[at : at + HALO]
    size = fields * tall
    to_high[...], to_low[...] = high_in[...], low_in[...]
    for f in range(fields):
        for start in (SUB, tall):
            packed_lanes(wide_ref, f, frame, pl.ds(start, SUB), to_high, to_low)
    high, low = to_high[...], to_low[...]
    send_forth[:size], send_back[:size] = jnp.where(even, high, low), jnp.where(even, low, high)
    send_forth[size:], send_back[size:] = rider[...], rider[...]


class Links:
    def __init__(self, mesh):
        self.sizes = [mesh.shape[a] for a in ("gx", "gy", "gz")]
        n_x, n_y, n_z = self.sizes

        def at(i, j, k):
            return (i % n_x * n_y + j % n_y) * n_z + k

        every = [(i, j, k) for i in range(n_x) for j in range(n_y) for k in range(n_z)]
        self.ring_x = [(i, (i + 1) % n_x) for i in range(n_x)]
        self.corner = {d: [(at(i, j, k), at(i + d, j + 1, k)) for i, j, k in every] for d in (1, -1)}
        self.snake = []
        for i in range(n_x):
            for j in range(0, n_y, 2):
                nodes = [at(i, j, k) for k in range(n_z)] + [at(i, j + 1, k) for k in reversed(range(n_z))]
                self.snake += [(nodes[m], nodes[(m + 1) % len(nodes)]) for m in range(len(nodes))]

    @staticmethod
    def back(pairs):
        return [(b, a) for a, b in pairs]

    @staticmethod
    def send(values, pairs):
        return lax.ppermute(values, ("gx", "gy", "gz"), pairs)

    def x(self, sends):
        if self.sizes[0] == 2:
            return (lax.ppermute(sends[0], "gx", self.ring_x),)
        return lax.ppermute(sends[0], "gx", self.ring_x), lax.ppermute(sends[1], "gx", self.back(self.ring_x))

    def near(self, values, x=None, y=None, z=None):
        forth, back = self.z(*(z or (values, values)))
        from_x = self.x(x or (values, values))
        return (forth, back, *from_x, *self.ring_y(*(y or (values, values))))

    def ring_y(self, to_high, to_low):
        ring = [(j, (j + 1) % self.sizes[1]) for j in range(self.sizes[1])]
        return lax.ppermute(to_high, "gy", ring), lax.ppermute(to_low, "gy", self.back(ring))

    def corners(self, sends):
        if self.sizes[0] == 2:
            return self.send(sends[0], self.corner[1]), self.send(sends[1], self.back(self.corner[1]))
        return (
            self.send(sends[0], self.corner[1]),
            self.send(sends[1], self.back(self.corner[-1])),
            self.send(sends[2], self.corner[-1]),
            self.send(sends[3], self.back(self.corner[1])),
        )

    def z(self, forth, back):
        return self.send(forth, self.snake), self.send(back, self.back(self.snake))


def send_y(arrays, rider, from_x):
    nx, ny, nz = arrays[0].shape
    rows = len(arrays) * Frame(nx, ny).wide * HALO + SUB
    kernel = functools.partial(pack_y_kernel, len(arrays))
    return call(kernel, [shaped(rows, nz)] * 2)(*arrays, rider, from_x[0], from_x[-1])


def framed(arrays, from_x, sent):
    nx, ny, nz = arrays[0].shape
    frame, fields = Frame(nx, ny), len(arrays)
    outs = [shaped(fields, *frame.main)] + [shaped(fields * frame.tall, nz)] * 2
    return call(functools.partial(frame_kernel, fields), outs)(*arrays, from_x[0], from_x[-1], sent)


def send_z(frames, from_y, rider):
    wide, high, _ = frames
    return call(
        functools.partial(pack_z_kernel, wide.shape[0]),
        [shaped(*wide.shape)] + [shaped(high.shape[0] + SUB, LANES)] * 2,
        [pltpu.VMEM(high.shape, F32)] * 2,
        aliases={0: 0},
    )(*frames, *from_y, rider)


def sides(flags, forth, back):
    even = flags[PARITY] == 0
    return jnp.where(even, forth, back), jnp.where(even, back, forth)


def weight(one, two):
    return 2.0 * (one * two) / (one + two)


def lane_mask(x):
    return ((lane_no((1, LANES)) - (HALO * x + HALO - 1)) & (LANES - 1)) < 2


def edge_step(here, x, edges):
    return jnp.where(lane_mask(x), turned(here, HALO * x + HALO, 1), edges)


def joined(below, above):
    lane = lane_no((1, LANES))
    return jnp.where(lane % HALO == HALO - 1, turned(above, HALO - 1, 1), turned(below, 1, 1))


def at_edges(join, x):
    lane = lane_no((1, LANES))
    return jnp.where((lane == 0) | (lane == LANES - 1), turned(join, (LANES - HALO) - HALO * x, 1), 0.0)


def ends_near(below, above, edges):
    layer = lane_no((1, LANES)) % HALO
    return (
        jnp.where(layer == HALO - 1, turned(edges, -1, 1), turned(below, -1, 1)),
        turned(below, 1, 1),
        turned(above, -1, 1),
        jnp.where(layer == 0, turned(edges, 1 - HALO, 1), turned(above, 1, 1)),
    )


def main_sums(frame, field, xs, join, wx, wy, wz):
    span = frame.span
    slabs = [field[xs[0] - 1 + k, span] for k in range(len(xs) + 2)]
    faces = [wx[xs[0] - 1 + k, span] for k in range(len(xs) + 1)]
    totals = []
    for k, x in enumerate(xs):
        here, face_y, face_z = slabs[k + 1], wy[x, span], wz[x, span]
        total = faces[k + 1] * slabs[k + 2] + faces[k] * slabs[k]
        total = total + face_y * turned(here, -1, 0) + turned(face_y * here, 1, 0)
        total = total + face_z * turned(here, -1, 1) + turned(face_z * here, 1, 1)
        totals.append(total + at_edges(join, x))
    return slabs[1:-1], totals


def ends_sum(frame, ends, s, upper, lower, wx, wy, wz_up, wz_low):
    span, down = frame.span, pl.ds(SUB - 1, frame.tall)
    here = ends[s, span]
    total = wx[s, span] * turned(here, -HALO, 1) + turned(wx[s, span] * here, HALO, 1)
    total = total + wy[s, span] * ends[s, pl.ds(SUB + 1, frame.tall)] + wy[s, down] * ends[s, down]
    return total + wz_up[s, span] * upper + wz_low[s, span] * lower


def clear_spares(ref, frame):
    for x in range(ref.shape[0]):
        ref[x, :SUB] = jnp.zeros((SUB, LANES), F32)
        ref[x, SUB + frame.tall :] = jnp.zeros((SUB, LANES), F32)


def pack_rows(values):
    half = values.shape[0] // 2
    lane = lane_no((half, LANES))
    return jnp.where(lane < LANES // 2, values[:half], turned(values[half:], LANES // 2, 1))


def lane_total(values):
    return jnp.broadcast_to(jnp.sum(values.T, axis=0, keepdims=True), (SUB, LANES))


def paired(values):
    even = 2 * (lane_no(values.shape) % (LANES // 2))
    return picked(values + turned(values, -1, 1), even)


def faces_y_kept(flags, frame):
    row = row_no((frame.tall, LANES))
    at_low, at_high = row == HALO - 1, row == HALO + frame.ny - 1
    return jnp.where(at_low, flags[Y_LOW], jnp.where(at_high, flags[Y_HIGH], 1)).astype(F32)


def face_rows(count, flags, nb):
    x = [(jnp.where(flags[IX] == 0, 1, 0), SUB)] if count == 2 else [(0, SUB), (1, SUB)]
    return x + [(2, nb // 2), (3, nb // 2), (4, 2), (5, 2)]


def add_rows(total, labels, b, values, c, rows=SUB):
    iota = row_no((AGG, LANES)).astype(F32)
    for r in range(rows):
        row = pl.ds(r, 1)
        total = total + jnp.where(labels[b, row] == iota, values[c, row], 0.0)
    return total


def pack_lanes(values):
    lane = lane_no((2, LANES))
    packed = values[:2]
    for g in range(1, SUB):
        packed = jnp.where(lane // 16 == g, turned(values[2 * g : 2 * g + 2], 16 * g, 1), packed)
    return packed


def fields_kernel(count, flags, wide_ref, block_label, inner, face_label, wx, wy, wz, partial, cond_edges, face_weight, diag):
    frame = Frame(wx.shape[0] - 2 * HALO, wx.shape[1] - 2 * (SUB + HALO))
    wide, tall, span = frame.wide, frame.tall, frame.span
    last = HALO + frame.nx
    keep_y = faces_y_kept(flags, frame)
    inside = jnp.where(lane_no((1, LANES)) == LANES - 1, 0.0, 1.0)

    def fields(xs, carry):
        before, edges = carry
        stores = []
        for x in xs:
            here = wide_ref[0, x, span]
            keep = jnp.where(x == HALO - 1, flags[X_LOW], jnp.where(x == last - 1, flags[X_HIGH], 1)).astype(F32)
            face_x = keep * weight(here, wide_ref[0, jnp.minimum(x + 1, wide - 1), span])
            face_y = keep_y * weight(here, wide_ref[0, x, pl.ds(SUB + 1, tall)])
            face_z = inside * weight(here, turned(here, -1, 1))
            total = wide_ref[2, x, span] + face_x + before + face_y + turned(face_y, 1, 0)
            total = total + face_z + turned(face_z, 1, 1)
            stores.append((x, (face_x, face_y, face_z, total)))
            edges = edge_step(here, x, edges)
            before = face_x
        for x, values in stores:
            for ref, value in zip((wx, wy, wz, partial), values):
                ref[x, span] = value
        return before, edges

    nothing = jnp.zeros((tall, LANES), F32)
    cond_edges[...] = batched(0, wide, fields, (nothing, nothing + 1.0), 4)[1]
    nb, ny = frame.nx // 2, frame.ny
    for s, x in enumerate((HALO - 1, last - 1)):
        rows = [wx[x, pl.ds(frame.own + c, ny // 2, stride=2)] for c in range(2)]
        face_weight[s] = pack_rows(paired(rows[0] + rows[1]))
    for s, at in ((2, frame.own - 1), (3, frame.own + ny - 1)):
        lines = [wy[HALO + 2 * b, at : at + 1] + wy[HALO + 2 * b + 1, at : at + 1] for b in range(nb)]
        face_weight[s, : nb // 2] = pack_rows(paired(jnp.concatenate(lines, axis=0)))
    around = jnp.zeros((AGG, LANES), F32)
    around = lax.fori_loop(0, nb, lambda b, around: add_rows(around, block_label, b, inner, b), around)
    for s, rows in face_rows(count, flags, nb)[:-2]:
        around = add_rows(around, face_label, s, face_weight, s, rows)
    diag[...] = lane_total(around)


def fine_kernel(flags, wide_ref, forth, back, wx, wy, wz, partial, cond_edges, block_label, face_label, some_diag,
                *refs):
    inv_diag, start = refs[:2]
    ends = refs[2:8]
    pre, face_weight, scaled_rhs, scale, once, once_ends, res, diag, block_res = refs[8:]
    ex, ey, ez_up, ez_low, inv_ends, start_ends = ends
    nx, ny = pre.shape[0], pre.shape[1]
    frame = Frame(nx, ny)
    wide, tall, span = frame.wide, frame.tall, frame.span
    last = HALO + nx
    got = [sides(flags, forth[f * tall : (f + 1) * tall], back[f * tall : (f + 1) * tall]) for f in range(3)]
    (cond_below, cond_above), rhs_ends, absorb_ends = got
    for ref in (ey, start_ends, once_ends):
        clear_spares(ref, frame)

    lane = lane_no((1, LANES))
    keep_y = faces_y_kept(flags, frame)
    keep_low, keep_high = flags[Z_LOW].astype(F32), flags[Z_HIGH].astype(F32)
    near = ends_near(cond_below, cond_above, cond_edges[...])
    slab = lane // HALO
    keep_x = jnp.where(
        slab == HALO - 1, flags[X_LOW], jnp.where(slab == last - 1, flags[X_HIGH], 1)
    ).astype(F32)
    layer = lane % HALO
    for s, here in enumerate((cond_below, cond_above)):
        up, low = weight(here, near[2 * s]), weight(here, near[2 * s + 1])
        if s == 0:
            up = up * jnp.where(layer == HALO - 1, keep_low, 1.0)
        else:
            low = low * jnp.where(layer == 0, keep_high, 1.0)
        face_x = keep_x * weight(here, turned(here, -HALO, 1))
        face_y = keep_y * weight(here, turned(here, -1, 0))
        ex[s, span], ey[s, span], ez_up[s, span], ez_low[s, span] = face_x, face_y, up, low
        total = absorb_ends[s] + face_x + turned(face_x, HALO, 1) + face_y + turned(face_y, 1, 0) + up + low
        inverse = OMEGA_FINE / total
        inv_ends[s, span] = inverse
        start_ends[s, span] = inverse * rhs_ends[s]

    end_low, end_high = ez_up[0, span], ez_low[1, span]
    join_faces = joined(end_low, end_high)

    def first_sweep(xs, edges):
        stores = []
        for x in xs:
            total = partial[x, span] + at_edges(join_faces, x)
            inverse = OMEGA_FINE / total
            begin = inverse * wide_ref[1, x, span]
            stores.append((x, (total, inverse, begin)))
            edges = edge_step(begin, x, edges)
        for x, values in stores:
            for ref, value in zip((diag, inv_diag, start), values):
                ref[x, span] = value
        return edges

    edges = batched(0, wide, first_sweep, jnp.zeros((tall, LANES), F32), 4)

    join = joined(end_low * start_ends[0, span], end_high * start_ends[1, span])
    near = ends_near(start_ends[0, span], start_ends[1, span], edges)
    for s in range(2):
        total = ends_sum(frame, start_ends, s, near[2 * s], near[2 * s + 1], ex, ey, ez_up, ez_low)
        once_ends[s, span] = (2.0 - OMEGA_FINE) * start_ends[s, span] + inv_ends[s, span] * total

    def second(xs, carry):
        news = []
        for x, here, total in zip(xs, *main_sums(frame, start, xs, join, wx, wy, wz)):
            news.append((2.0 - OMEGA_FINE) * here + inv_diag[x, span] * total)
        for x, new in zip(xs, news):
            once[x, span] = new
        return carry

    batched(HALO - 1, last + 1, second, 0, 13 if (nx + 2) % 13 == 0 else 6)
    join2 = joined(end_low * once_ends[0, span], end_high * once_ends[1, span])

    def remainder(xs, carry):
        news = []
        for x, here, total in zip(xs, *main_sums(frame, once, xs, join2, wx, wy, wz)):
            news.append(wide_ref[1, x, span] - diag[x, span] * here + total)
        for x, new in zip(xs, news):
            res[x - HALO, span] = new
        for x in xs:
            pre[x - HALO] = once[x, pl.ds(frame.own, ny)]
        return carry

    batched(HALO, last, remainder, 0, 8)

    nb, half = nx // 2, ny // 2

    def rows_at(ref, x, off):
        return ref[x, pl.ds(frame.own + off, half, stride=2)]

    def to_blocks(bs, carry):
        for b in bs:
            four = sum(rows_at(res, 2 * b + a, c) for a in range(2) for c in range(2))
            block_res[b] = pack_rows(paired(four))
        return carry

    batched(0, nb, to_blocks, 0)
    zeros = jnp.zeros((AGG, LANES), F32)
    sums = lax.fori_loop(0, nb, lambda b, total: add_rows(total, block_label, b, block_res, b), zeros)

    lane = lane_no((half, LANES))
    around = zeros
    for s, (ref, side, layer_at) in enumerate(((ez_up, 0, HALO - 1), (ez_low, 1, 0))):
        values = rows_at(ref, side, 0) + rows_at(ref, side, 1)
        values = values + turned(values, -HALO, 1)
        spot = jnp.minimum(2 * HALO * lane + HALO * HALO + layer_at, LANES - 1)
        face_weight[s, :2] = pack_lanes(jnp.where(lane < nb, picked(values, spot), 0.0))
        around = add_rows(around, face_label, 4 + s, face_weight, s, 2)
    scale[...] = OMEGA_COARSE / (some_diag[...] + lane_total(around))
    scaled_rhs[...] = scale[...] * lane_total(sums)


def tile_sum(tile, rows, label_at, pairs_at, group=4):
    iota = row_no((AGG, LANES)).astype(F32)
    for first in range(0, rows, group):
        places, highs, lows = [], [], []
        for r in range(first, min(first + group, rows)):
            places.append(jnp.where(label_at(r) == iota, 1.0, 0.0).astype(BF16))
            held = sum(jnp.where(near == iota, w, 0.0) for near, w in pairs_at(r))
            highs.append(held.astype(BF16))
            lows.append((held - highs[-1].astype(F32)).astype(BF16))
        left = jnp.concatenate(places, axis=1)
        right = jnp.concatenate([jnp.concatenate(highs, axis=1), jnp.concatenate(lows, axis=1)], axis=0)
        tile = tile + lax.dot_general(left, right, (((1,), (1,)), ((), ())), preferred_element_type=F32)
    return tile


def both_halves(tile):
    return tile[:, :AGG] + tile[:, AGG:]


def keep_tile(out, t, tile):
    high = tile.astype(BF16)
    rows = pl.ds(t * AGG, AGG)
    out[rows, :AGG] = high
    out[rows, AGG:] = (tile - high.astype(F32)).astype(BF16)


def blocks_kernel(flags, cond, absorb, block_agg, _, block_label, near, weights, inner, face_label, fine_label,
                  part, line):
    nx, ny = cond.shape[0], cond.shape[1]
    nb, half, width = nx // 2, ny // 2, LANES // 2
    lane, row = lane_no((half, LANES)), row_no((half, LANES))

    def halves(values, slot):
        part[slot] = values
        return part[slot, pl.ds(0, half, stride=2)], part[slot, pl.ds(1, half, stride=2)]

    def label_at(b):
        values = block_agg[b].astype(F32)
        return jnp.concatenate([values, values], axis=1)

    def upper_x(b, slot):
        x = jnp.maximum(2 * b, 0)
        faces = weight(cond[x + 1], cond[jnp.minimum(x + 2, nx - 1)])
        return jnp.where((b == nb - 1) | (b < 0), 0.0, paired(sum(halves(faces, slot))))

    def step(bs, carry):
        low_x = upper_x(bs[0] - 1, 0)
        for k, b in enumerate(bs):
            x = 2 * b
            slot = 4 * k + 1
            one, two = cond[x], cond[x + 1]
            both_y = weight(one, turned(one, -1, 0)) + weight(two, turned(two, -1, 0))
            both_z = weight(one, turned(one, -1, 1)) + weight(two, turned(two, -1, 1))
            high_x = upper_x(b, slot)
            high_y = jnp.where(row == half - 1, 0.0, paired(halves(both_y, slot + 1)[1]))
            high_z = picked(sum(halves(both_z, slot + 2)), 2 * (lane % width) + 1)
            high_z = jnp.where(lane % width == width - 1, 0.0, high_z)
            low_y, low_z = turned(high_y, 1, 0), turned(high_z, 1, 1)
            own = label_at(b)
            near_x, past_x = label_at(jnp.minimum(b + 1, nb - 1)), label_at(jnp.maximum(b - 1, 0))
            near_y, past_y = turned(own, -1, 0), turned(own, 1, 0)
            near_z, past_z = turned(own, -1, 1), turned(own, 1, 1)
            total = paired(sum(halves(absorb[x] + absorb[x + 1], slot + 3)))
            for d, (beside, values) in enumerate((
                (near_x, high_x), (past_x, low_x), (near_y, high_y), (past_y, low_y), (near_z, high_z), (past_z, low_z)
            )):
                leaving = jnp.where(beside != own, values, 0.0)
                total = total + leaving
                near[d, b], weights[d, b] = pack_rows(beside).astype(jnp.int32), pack_rows(leaving)
            block_label[b] = pack_rows(own)
            inner[b] = pack_rows(total)
            spread = picked(own, lane // 2)
            for a in range(2):
                for c in range(2):
                    fine_label[x + a, pl.ds(c, half, stride=2)] = spread
            low_x = high_x
        return carry

    batched(0, nb, step, 0, 4)
    line[...] = jnp.zeros(line.shape, F32)
    low, high = jnp.zeros((half, LANES), F32), jnp.zeros((half, LANES), F32)
    for b in range(nb):
        own = label_at(b)
        line[0, b : b + 1], line[1, b : b + 1] = own[:1], own[half - 1 :]
        low = jnp.where(lane == b, own[:, :1], low)
        high = jnp.where(lane == b, own[:, width - 1 : width], high)
    face_label[0], face_label[1] = block_label[0], block_label[nb - 1]
    for s in range(2):
        face_label[2 + s, : nb // 2] = pack_rows(line[s, :nb])
        face_label[4 + s, :2] = pack_lanes((low, high)[s])


def own_turn_kernel(flags, block_label, near, weights, coarse, out, values):
    table = jnp.broadcast_to(coarse[:1], (SUB, LANES))
    nb = block_label.shape[0]

    def sums(bs, carry):
        news = [sum(weights[d, b] * picked(table, near[d, b]) for d in range(6)) for b in bs]
        for b, new in zip(bs, news):
            values[b] = new
        return carry

    batched(0, nb, sums, 0)
    total = jnp.zeros((AGG, LANES), F32)
    total = lax.fori_loop(0, nb, lambda b, total: add_rows(total, block_label, b, values, b), total)
    out[...] = lane_total(total)


def faces_kernel(count, nb, flags, face_label, weight_xy, weight_z, x_low, x_high, y_low, y_high, forth, back, out,
                 near, weights):
    at, half = x_low.shape[0] - 1, x_low.shape[1] // 2
    near[0], near[1] = pack_rows(x_low[at, :half]), pack_rows(x_high[at, :half])
    at = sum(WIDTHS) * 2 * nb
    for s, ref in enumerate((y_low, y_high)):
        near[2 + s, : nb // 2] = pack_rows(ref[at : at + nb])
    at = forth.shape[0] - half
    for s, values in enumerate(sides(flags, forth[at:], back[at:])):
        near[4 + s, :2] = pack_lanes(values)
    weights[:4], weights[4:] = weight_xy[...], weight_z[...]
    for t, (s, rows) in enumerate(face_rows(count, flags, nb)):
        tile = tile_sum(
            jnp.zeros((AGG, 2 * AGG), F32),
            rows,
            lambda r, s=s: near[s, pl.ds(r, 1)],
            lambda r, s=s: [(face_label[s, pl.ds(r, 1)], weights[s, pl.ds(r, 1)])],
        )
        keep_tile(out, t, both_halves(tile))


def turn_kernel(flags, tiles, scaled_rhs, scale, own, inside, *refs):
    forth, back, *others, out = refs
    got = [ref[ref.shape[0] - 1, :SUB] if len(ref.shape) == 3 else ref[ref.shape[0] - SUB :] for ref in (*others, forth, back)]
    vectors = [*got[:-2], *sides(flags, *got[-2:])]
    row = row_no((SUB, AGG))
    parts = []
    for v in vectors:
        high = v.astype(BF16).astype(F32)
        parts.append(jnp.where(row == 0, high, jnp.where(row == 1, v - high, 0.0)).astype(BF16))
    got = jnp.dot(jnp.concatenate(parts, axis=1), tiles[...], preferred_element_type=F32)
    applied = jnp.sum(got[:, :AGG] + got[:, AGG:], axis=0, keepdims=True)
    out[...] = (1.0 - OMEGA_COARSE) * own[...] + scaled_rhs[...] + scale[...] * (inside[...] + applied)


def ride_kernel(count, flags, pre, fine_label, coarse, *outs):
    nx = pre.shape[0]
    for s, out in enumerate(outs):
        at = jnp.where(flags[IX] == 0, nx - HALO, 0) if count == 2 else (nx - HALO, 0)[s]
        for f, field in enumerate((pre, fine_label)):
            for x in range(HALO):
                out[HALO * f + x] = field[at + x]
        out[2 * HALO] = jnp.zeros(out.shape[1:], F32)
        out[2 * HALO, :SUB] = coarse[...]


def three_kernel(flags, low, mid, high, out):
    row = row_no(out.shape)
    out[...] = jnp.where(row == 0, low[...], jnp.where(row == 1, mid[...], high[...]))


def nine_kernel(flags, low, mid, high, out):
    out[...] = jnp.zeros(out.shape, F32)
    for n, ref in enumerate((low, mid, high)):
        out[3 * n : 3 * n + 3] = ref[:3]


def lift_kernel(flags, wide_ref, forth, back, main, ends):
    frame = Frame(wide_ref.shape[1] - 2 * HALO, wide_ref.shape[2] - 2 * (SUB + HALO))
    tall = frame.tall
    for b in range(frame.wide // 2):
        main[b] = wide_ref[1, 2 * b, frame.span].astype(jnp.int32)
    rows = pl.ds(tall, tall)
    for s, values in enumerate(sides(flags, forth[rows], back[rows])):
        ends[s] = values.astype(jnp.int32)


def post_kernel(flags, table, table_forth, table_back, labels, end_labels, wide_ref, forth, back, *refs):
    (wx, wy, wz, inv_diag, start), ends = refs[:5], refs[5:11]
    out, one, two, one_ends, two_ends, kept_out, sems = refs[11:]
    nx, ny = out.shape[0], out.shape[1]
    frame = Frame(nx, ny)
    wide, tall, span = frame.wide, frame.tall, frame.span
    ex, ey, ez_up, ez_low, inv_ends, start_ends = ends
    for ref in (one_ends, two_ends):
        clear_spares(ref, frame)
    row, lane = row_no((tall, LANES)), lane_no((tall, LANES))
    under, over = sides(flags, table_forth[...], table_back[...])
    tables = {-1: under, 0: table[...], 1: over}

    def table_at(dx, dz):
        low, mid, high = (tables[dz][3 * n + dx + 1 : 3 * n + dx + 2] for n in range(3))
        return jnp.where(row < HALO, low, jnp.where(row < HALO + ny, mid, high))

    for x_from, x_to, dx in ((0, HALO, -1), (HALO, HALO + nx, 0), (HALO + nx, wide, 1)):
        values = table_at(dx, 0)

        def lift(bs, carry, values=values):
            news = [picked(values, labels[b]) for b in bs]
            for b, new in zip(bs, news):
                for a in range(2):
                    two[2 * b + a, span] = wide_ref[0, 2 * b + a, span] + new
            return carry

        batched(x_from // 2, x_to // 2, lift, 0, 4)
    for s, (dz, base) in enumerate(zip((-1, 1), sides(flags, forth[:tall], back[:tall]))):
        below, inside, above = (picked(table_at(dx, dz), end_labels[s]) for dx in (-1, 0, 1))
        spot = lane // HALO
        lifted = jnp.where(spot < HALO, below, jnp.where(spot < HALO + nx, inside, above))
        two_ends[s, span] = base + lifted
    kept = 1.0 - OMEGA_FINE

    def result(at, count):
        rows = pl.ds(at, count)
        return pltpu.make_async_copy(kept_out.at[rows], out.at[rows], sems.at[at // count])

    buffers = ((two, two_ends), (one, one_ends), (two, two_ends), (one, one_ends))
    for s in range(POST):
        src, src_ends = buffers[s]
        join = joined(ez_up[0, span] * src_ends[0, span], ez_low[1, span] * src_ends[1, span])
        final = s == POST - 1
        dst, dst_ends = (None, None) if final else buffers[s + 1]

        def step(xs, edges, src=src, join=join, dst=dst, final=final):
            news = []
            for x, here, total in zip(xs, *main_sums(frame, src, xs, join, wx, wy, wz)):
                news.append(kept * here + start[x, span] + inv_diag[x, span] * total)
                if not final:
                    edges = edge_step(here, x, edges)
            for x, new in zip(xs, news):
                if final:
                    kept_out[x - HALO] = new[HALO : HALO + ny]
                else:
                    dst[x, span] = new
            if final:
                result(xs[0] - HALO, len(xs)).start()
            return edges

        size = 8 if final else 10
        edges = batched(s + 1, wide - s - 1, step, jnp.zeros((tall, LANES), F32), size)
        if not final:
            near = ends_near(src_ends[0, span], src_ends[1, span], edges)
            news = []
            for e in range(2):
                total = ends_sum(frame, src_ends, e, near[2 * e], near[2 * e + 1], ex, ey, ez_up, ez_low)
                news.append(kept * src_ends[e, span] + start_ends[e, span] + inv_ends[e, span] * total)
            dst_ends[0, span], dst_ends[1, span] = news
    for n in range(nx // 8):
        result(8 * n, 8).wait()


def body(links, right_side, conductance, absorption, block_agg):
    nx, ny, nz = right_side.shape
    frame = Frame(nx, ny)
    nb = nx // 2
    n_x = links.sizes[0]
    arrays = (conductance, right_side, absorption, block_agg)
    n_send = 1 if n_x == 2 else 2
    pinned = [pltpu.with_memory_space_constraint(a, pltpu.HBM) for a in arrays]
    outs = [jax.ShapeDtypeStruct(a.shape, a.dtype) for a in arrays]
    outs += [shaped(sum(WIDTHS) + 1, ny, nz)] * n_send + [shaped(sum(WIDTHS) * nx + 16, nz)] * 2
    outs += [shaped(-(-sum(w * w for w in WIDTHS) // SUB) * SUB, nz)] * (2 * n_send)
    got = call(
        functools.partial(pack_kernel, n_x, WIDTHS),
        outs,
        [pltpu.SemaphoreType.DMA((3 * 4,))],
        in_specs=[pl.BlockSpec(memory_space=pltpu.HBM)] * 4,
    )(*pinned)
    arrays, sends = got[:4], got[4:]
    from_x = links.x(sends[:n_send])
    from_y = links.ring_y(*sends[n_send : n_send + 2])
    from_corners = links.corners(sends[n_send + 2 :])
    size = len(WIDTHS) * frame.tall
    wide, *sends = call(
        functools.partial(first_frame_kernel, n_x, WIDTHS),
        [shaped(len(WIDTHS), *frame.main)] + [shaped(size + ny // 2, nz)] * 2,
        [pltpu.VMEM((size, nz), F32)] * 2,
    )(*arrays, from_x[0], from_x[-1], *from_y, *from_corners)
    blocks = (nb, SUB, LANES)
    outs = [shaped(*blocks), jax.ShapeDtypeStruct((6, *blocks), jnp.int32), shaped(6, *blocks), shaped(*blocks)]
    outs += [shaped(6, SUB, LANES), shaped(nx, ny, nz)]
    scratch = [pltpu.VMEM((17, ny, LANES), F32), pltpu.VMEM((2, ny // 2, LANES), F32)]
    *rows, inner, face_label, fine_label = call(blocks_kernel, outs, scratch)(
        arrays[0], arrays[2], arrays[3], sends[0]
    )
    block_label = rows[0]
    outs = [shaped(*frame.main)] * 4 + [shaped(frame.tall, nz), shaped(4, SUB, LANES), shaped(SUB, AGG)]
    *fields, weight_xy, some_diag = call(functools.partial(fields_kernel, n_x), outs, limit=24)(
        wide, block_label, inner, face_label
    )
    halo = (wide, *links.z(*sends))
    outs = [shaped(*frame.main)] * 2 + [shaped(*frame.ends)] * 6 + [shaped(nx, ny, nz)]
    outs += [shaped(2, SUB, LANES)] + [shaped(SUB, AGG)] * 2
    scratch = [pltpu.VMEM(frame.main, F32), pltpu.VMEM(frame.ends, F32), pltpu.VMEM((nx, frame.rows, LANES), F32)]
    scratch += [pltpu.VMEM(frame.main, F32), pltpu.VMEM(blocks, F32)]
    got = call(fine_kernel, outs, scratch, limit=28)(
        *halo, *fields, block_label, face_label, some_diag
    )
    fields, pre = (*fields[:3], *got[:8]), got[8]
    weight_z, scaled_rhs, scale = got[9:]
    tiles = call(
        functools.partial(faces_kernel, n_x, nb),
        jax.ShapeDtypeStruct(((n_send + 4) * AGG, 2 * AGG), BF16),
        [pltpu.VMEM((6, SUB, LANES), F32)] * 2,
    )(face_label, weight_xy, weight_z, from_x[0], from_x[-1], *from_y, *halo[1:])
    coarse = scaled_rhs

    def turn(**more):
        near = links.near(coarse, **more)
        inside = call(own_turn_kernel, shaped(SUB, AGG), [pltpu.VMEM(blocks, F32)])(*rows, coarse)
        return call(turn_kernel, shaped(SUB, AGG))(tiles, scaled_rhs, scale, coarse, inside, *near), near

    both = (pre, fine_label)
    rides = call(functools.partial(ride_kernel, n_x), [shaped(2 * HALO + 1, ny, nz)] * n_send)(*both, coarse)
    coarse, near = turn(x=rides)
    from_x = near[2:-2]
    rides = send_y(both, coarse, from_x)
    frames = framed(both, from_x, rides[0])
    coarse, near = turn(y=rides)
    wide, *rides = send_z(frames, near[-2:], coarse)
    coarse, near = turn(z=rides)
    halo = (wide, *near[:2])
    outs = [jax.ShapeDtypeStruct((frame.wide // 2, frame.tall, nz), jnp.int32)]
    outs += [jax.ShapeDtypeStruct((2, frame.tall, nz), jnp.int32)]
    lifts = call(lift_kernel, outs)(*halo)
    for _ in range(KC - 4):
        coarse, _ = turn()
    from_x = links.x([coarse] * n_send)
    three = call(three_kernel, shaped(SUB, AGG))(from_x[0], coarse, from_x[-1])
    low, high = links.ring_y(three, three)
    nine = call(nine_kernel, shaped(2 * SUB, AGG))(low, three, high)
    tables = (nine, *links.z(nine, nine))
    scratch = [pltpu.VMEM(frame.main, F32)] * 2 + [pltpu.VMEM(frame.ends, F32)] * 2
    scratch += [pltpu.VMEM((nx, ny, nz), F32), pltpu.SemaphoreType.DMA((nx // 8,))]
    return call(post_kernel, shaped(nx, ny, nz), scratch, limit=24, out_specs=pl.BlockSpec(memory_space=pl.ANY))(
        *tables, *lifts, *halo, *fields
    )


def solution(mesh):
    spec = P("gx", "gy", "gz")
    return jax.shard_map(
        functools.partial(body, Links(mesh)), mesh=mesh, in_specs=(spec,) * 4, out_specs=spec, check_vma=False
    )
```

```python
import functools

import jax
import jax.numpy as jnp
from jax import lax
from jax.experimental import pallas as pl
from jax.experimental.pallas import tpu as pltpu
from jax.sharding import PartitionSpec as P

AGG = 128
LANES = 128
SUB = 8
HALO = 4
WIDTHS = (4, 3, 3)
POST = 4
KC = 8
OMEGA_FINE = 0.8
OMEGA_COARSE = 0.7
F32 = jnp.float32
BF16 = jnp.bfloat16
VMEM = pl.BlockSpec(memory_space=pltpu.VMEM)
IX, PARITY, X_LOW, X_HIGH, Y_LOW, Y_HIGH, Z_LOW, Z_HIGH = range(8)


def places():
    (ix, n_x), (iy, n_y), (iz, n_z) = ((lax.axis_index(a), lax.axis_size(a)) for a in ("gx", "gy", "gz"))
    flags = [ix, iy % 2, ix > 0, ix < n_x - 1, iy > 0, iy < n_y - 1, iz > 0, iz < n_z - 1]
    return [jnp.asarray(flag, jnp.int32) for flag in flags]


def call(kernel, outs, scratch=(), limit=16, flops=10**6, in_specs=None, aliases=None, out_specs=None):
    def placed(*refs):
        kernel(places(), *refs)

    def run(*arrays):
        return pl.pallas_call(
            placed,
            out_shape=outs,
            in_specs=in_specs or [VMEM] * len(arrays),
            out_specs=out_specs or jax.tree.map(lambda _: VMEM, outs),
            scratch_shapes=list(scratch),
            input_output_aliases=aliases or {},
            compiler_params=pltpu.CompilerParams(vmem_limit_bytes=limit * 2**20),
            cost_estimate=pl.CostEstimate(flops=flops, bytes_accessed=10**5, transcendentals=0),
        )(*arrays)

    return run


def shaped(*shape):
    return jax.ShapeDtypeStruct(shape, F32)


def lane_no(shape):
    return lax.broadcasted_iota(jnp.int32, shape, len(shape) - 1)


def row_no(shape):
    return lax.broadcasted_iota(jnp.int32, shape, len(shape) - 2)


def turned(values, shift, axis):
    if isinstance(shift, int):
        shift = shift % values.shape[axis]
        if shift == 0:
            return values
    return pltpu.roll(values, shift, axis)


def batched(low, high, step, carry, size=6):
    def some(i, carry):
        return step([low + i * size + k for k in range(size)], carry)

    carry = lax.fori_loop(0, (high - low) // size, some, carry)
    rest = (high - low) % size
    return step(list(range(high - rest, high)), carry) if rest else carry


def picked(values, index):
    return jnp.take_along_axis(values, index, axis=1, mode="promise_in_bounds")


class Frame:
    def __init__(self, nx, ny):
        self.nx, self.ny = nx, ny
        self.wide, self.tall = nx + 2 * HALO, ny + 2 * HALO
        self.rows = self.tall + 2 * SUB
        self.span = pl.ds(SUB, self.tall)
        self.own = SUB + HALO
        self.main = (self.wide, self.rows, LANES)
        self.ends = (2, self.rows, LANES)


def bases(widths):
    return [sum(widths[:f]) for f in range(len(widths) + 1)]


def copied(pairs, sems):
    copies = [pltpu.make_async_copy(src, dst, sems.at[n]) for n, (src, dst) in enumerate(pairs)]
    for copy in copies:
        copy.start()
    return copies


def pack_kernel(count, widths, flags, *refs):
    fields = len(widths)
    n_x = 1 if count == 2 else 2
    ins, kept = refs[: fields + 1], refs[fields + 1 : 2 * fields + 2]
    outs, sems = refs[2 * fields + 2 : -1], refs[-1]
    x_outs, y_outs, corner_outs = outs[:n_x], outs[n_x : n_x + 2], outs[n_x + 2 :]
    nx, ny = ins[0].shape[0], ins[0].shape[1]
    nb, half, width = ins[-1].shape
    thirds = 3
    copies = []
    for ref, out in zip(ins, kept):
        for t in range(thirds):
            size = ref.shape[0] // thirds
            rows = pl.ds(t * size, size)
            copies.append(pltpu.make_async_copy(ref.at[rows], out.at[rows], sems.at[len(copies)]))
    for copy in copies:
        copy.start()
    for out in (*x_outs, *y_outs):
        out[...] = jnp.zeros(out.shape, F32)
    for copy in copies:
        copy.wait()
    base = bases(widths)
    labels = kept[-1]
    for s, out in enumerate(x_outs):

        def place(size, thick, s=s):
            if count == 2:
                return jnp.where(flags[IX] == 0, size - thick, 0)
            return (size - thick, 0)[s]

        for f, thick in enumerate(widths):
            at = place(nx, thick)
            for k in range(thick):
                slab = kept[f][at + k]
                out[base[f] + k] = slab
                row = (sum(w * w for w in widths[:f])) + k * thick
                corner_outs[2 * s][row : row + thick] = slab[ny - thick :]
                corner_outs[2 * s + 1][row : row + thick] = slab[:thick]
        out[base[-1], :half, :width] = labels[place(nb, 1)].astype(F32)
    for out, high in zip(y_outs, (True, False)):
        for f, thick in enumerate(widths):
            for x in range(nx):
                row = base[f] * nx + x * thick
                out[row : row + thick] = kept[f][x, ny - thick :] if high else kept[f][x, :thick]
        row = base[-1] * nx
        for b in range(nb):
            line = labels[b, half - 1 :] if high else labels[b, :1]
            out[row + b : row + b + 1, :width] = line.astype(F32)


def slab_of(own, low, high, base, width, x):
    nx = own.shape[0]
    if HALO <= x < HALO + nx:
        return own[x - HALO]
    if x < HALO:
        at = x - (HALO - width)
        return low[base + at] if at >= 0 else None
    at = x - HALO - nx
    return high[base + at] if at < width else None


def pack_y_kernel(fields, flags, *refs):
    ins, rider = refs[:fields], refs[fields]
    low, high, to_high, to_low = refs[fields + 1 :]
    nx, ny = ins[0].shape[0], ins[0].shape[1]
    wide = nx + 2 * HALO
    for f in range(fields):
        for x in range(wide):
            slab = slab_of(ins[f], low, high, HALO * f, HALO, x)
            at = (f * wide + x) * HALO
            to_high[at : at + HALO] = slab[ny - HALO :]
            to_low[at : at + HALO] = slab[:HALO]
    at = fields * wide * HALO
    to_high[at:], to_low[at:] = rider[...], rider[...]


def packed_lanes(wide_ref, f, frame, rows, to_high, to_low):
    group = lane_no((1, LANES)) // HALO
    nothing = jnp.ones((rows.size, LANES), F32)
    high, low = nothing, nothing
    for x in range(frame.wide):
        moved = turned(wide_ref[f, x, rows], HALO * (x + 1), 1)
        high = jnp.where(group == x, moved, high)
        low = jnp.where(group == (x + 1) % frame.wide, moved, low)
    at = pl.ds(f * frame.tall + rows.start - SUB, rows.size)
    to_high[at] = high
    to_low[at] = turned(low, -HALO, 1)


def first_frame_kernel(count, widths, flags, *refs):
    fields = len(widths)
    ins, labels, refs = refs[:fields], refs[fields], refs[fields + 1 :]
    x_low, x_high, y_low, y_high = refs[:4]
    corners = refs[4:6] * 2 if count == 2 else refs[4:8]
    wide_ref, send_forth, send_back, to_high, to_low = refs[-5:]
    nx, ny = ins[0].shape[0], ins[0].shape[1]
    frame = Frame(nx, ny)
    base = bases(widths)
    tall, own = frame.tall, frame.own
    even = flags[PARITY] == 0
    ones = jnp.ones((frame.rows, LANES), F32)
    for f, thick in enumerate(widths):
        for x in range(frame.wide):
            slab = slab_of(ins[f], x_low, x_high, base[f], thick, x)
            if slab is None:
                wide_ref[f, x] = ones
                continue
            edge = ones[: SUB + HALO]
            wide_ref[f, x, :own] = edge
            wide_ref[f, x, own + ny :] = edge
            wide_ref[f, x, own : own + ny] = slab
            if HALO <= x < HALO + nx:
                low, high, row = y_low, y_high, base[f] * nx + (x - HALO) * thick
            else:
                above = x >= HALO
                low, high = corners[2 * above : 2 * above + 2]
                at = x - HALO - nx if above else x - (HALO - thick)
                row = sum(w * w for w in widths[:f]) + at * thick
            wide_ref[f, x, own - thick : own] = low[row : row + thick]
            wide_ref[f, x, own + ny : own + ny + thick] = high[row : row + thick]
        packed_lanes(wide_ref, f, frame, pl.ds(SUB, tall), to_high, to_low)
    high, low = to_high[...], to_low[...]
    size = fields * tall
    send_forth[:size], send_back[:size] = jnp.where(even, high, low), jnp.where(even, low, high)
    nb, rows, width = labels.shape
    lane = lane_no((rows, LANES))
    high = low = jnp.zeros((rows, LANES), F32)
    for b in range(nb):
        slab = labels[b].astype(F32)
        high = jnp.where(lane == b, slab[:, width - 1 :], high)
        low = jnp.where(lane == b, slab[:, :1], low)
    send_forth[size:], send_back[size:] = jnp.where(even, high, low), jnp.where(even, low, high)


def frame_kernel(fields, flags, *refs):
    ins = refs[:fields]
    x_low, x_high, _ = refs[fields : fields + 3]
    wide_ref, to_high, to_low = refs[fields + 3 :]
    nx, ny = ins[0].shape[0], ins[0].shape[1]
    frame = Frame(nx, ny)
    spare = jnp.ones((SUB, LANES), F32)
    for f in range(fields):
        for x in range(frame.wide):
            wide_ref[f, x, frame.own : frame.own + ny] = slab_of(ins[f], x_low, x_high, HALO * f, HALO, x)
            wide_ref[f, x, :SUB] = spare
            wide_ref[f, x, SUB + frame.tall :] = spare
        packed_lanes(wide_ref, f, frame, pl.ds(2 * SUB, frame.tall - 2 * SUB), to_high, to_low)


def pack_z_kernel(fields, flags, wide_in, high_in, low_in, from_low, from_high, rider, *refs):
    wide_ref, send_forth, send_back, to_high, to_low = refs
    frame = Frame(wide_ref.shape[1] - 2 * HALO, wide_ref.shape[2] - 2 * (SUB + HALO))
    ny, tall, own = frame.ny, frame.tall, frame.own
    even = flags[PARITY] == 0
    for f in range(fields):
        for x in range(frame.wide):
            at = (f * frame.wide + x) * HALO
            wide_ref[f, x, SUB:own] = from_low[at : at + HALO]
            wide_ref[f, x, own + ny : own + ny + HALO] = from_high[at : at + HALO]
    size = fields * tall
    to_high[...], to_low[...] = high_in[...], low_in[...]
    for f in range(fields):
        for start in (SUB, tall):
            packed_lanes(wide_ref, f, frame, pl.ds(start, SUB), to_high, to_low)
    high, low = to_high[...], to_low[...]
    send_forth[:size], send_back[:size] = jnp.where(even, high, low), jnp.where(even, low, high)
    send_forth[size:], send_back[size:] = rider[...], rider[...]


class Links:
    def __init__(self, mesh):
        self.sizes = [mesh.shape[a] for a in ("gx", "gy", "gz")]
        n_x, n_y, n_z = self.sizes

        def at(i, j, k):
            return (i % n_x * n_y + j % n_y) * n_z + k

        every = [(i, j, k) for i in range(n_x) for j in range(n_y) for k in range(n_z)]
        self.ring_x = [(i, (i + 1) % n_x) for i in range(n_x)]
        self.corner = {d: [(at(i, j, k), at(i + d, j + 1, k)) for i, j, k in every] for d in (1, -1)}
        self.snake = []
        for i in range(n_x):
            for j in range(0, n_y, 2):
                nodes = [at(i, j, k) for k in range(n_z)] + [at(i, j + 1, k) for k in reversed(range(n_z))]
                self.snake += [(nodes[m], nodes[(m + 1) % len(nodes)]) for m in range(len(nodes))]

    @staticmethod
    def back(pairs):
        return [(b, a) for a, b in pairs]

    @staticmethod
    def send(values, pairs):
        return lax.ppermute(values, ("gx", "gy", "gz"), pairs)

    def x(self, sends):
        if self.sizes[0] == 2:
            return (lax.ppermute(sends[0], "gx", self.ring_x),)
        return lax.ppermute(sends[0], "gx", self.ring_x), lax.ppermute(sends[1], "gx", self.back(self.ring_x))

    def near(self, values, x=None, y=None, z=None):
        forth, back = self.z(*(z or (values, values)))
        from_x = self.x(x or (values, values))
        return (forth, back, *from_x, *self.ring_y(*(y or (values, values))))

    def ring_y(self, to_high, to_low):
        ring = [(j, (j + 1) % self.sizes[1]) for j in range(self.sizes[1])]
        return lax.ppermute(to_high, "gy", ring), lax.ppermute(to_low, "gy", self.back(ring))

    def corners(self, sends):
        if self.sizes[0] == 2:
            return self.send(sends[0], self.corner[1]), self.send(sends[1], self.back(self.corner[1]))
        return (
            self.send(sends[0], self.corner[1]),
            self.send(sends[1], self.back(self.corner[-1])),
            self.send(sends[2], self.corner[-1]),
            self.send(sends[3], self.back(self.corner[1])),
        )

    def z(self, forth, back):
        return self.send(forth, self.snake), self.send(back, self.back(self.snake))


def send_y(arrays, rider, from_x):
    nx, ny, nz = arrays[0].shape
    rows = len(arrays) * Frame(nx, ny).wide * HALO + SUB
    kernel = functools.partial(pack_y_kernel, len(arrays))
    return call(kernel, [shaped(rows, nz)] * 2)(*arrays, rider, from_x[0], from_x[-1])


def framed(arrays, from_x, sent):
    nx, ny, nz = arrays[0].shape
    frame, fields = Frame(nx, ny), len(arrays)
    outs = [shaped(fields, *frame.main)] + [shaped(fields * frame.tall, nz)] * 2
    return call(functools.partial(frame_kernel, fields), outs)(*arrays, from_x[0], from_x[-1], sent)


def send_z(frames, from_y, rider):
    wide, high, _ = frames
    return call(
        functools.partial(pack_z_kernel, wide.shape[0]),
        [shaped(*wide.shape)] + [shaped(high.shape[0] + SUB, LANES)] * 2,
        [pltpu.VMEM(high.shape, F32)] * 2,
        aliases={0: 0},
    )(*frames, *from_y, rider)


def sides(flags, forth, back):
    even = flags[PARITY] == 0
    return jnp.where(even, forth, back), jnp.where(even, back, forth)


def weight(one, two):
    return 2.0 * (one * two) / (one + two)


def lane_mask(x):
    return ((lane_no((1, LANES)) - (HALO * x + HALO - 1)) & (LANES - 1)) < 2


def edge_step(here, x, edges):
    return jnp.where(lane_mask(x), turned(here, HALO * x + HALO, 1), edges)


def joined(below, above):
    lane = lane_no((1, LANES))
    return jnp.where(lane % HALO == HALO - 1, turned(above, HALO - 1, 1), turned(below, 1, 1))


def at_edges(join, x):
    lane = lane_no((1, LANES))
    return jnp.where((lane == 0) | (lane == LANES - 1), turned(join, (LANES - HALO) - HALO * x, 1), 0.0)


def ends_near(below, above, edges):
    layer = lane_no((1, LANES)) % HALO
    return (
        jnp.where(layer == HALO - 1, turned(edges, -1, 1), turned(below, -1, 1)),
        turned(below, 1, 1),
        turned(above, -1, 1),
        jnp.where(layer == 0, turned(edges, 1 - HALO, 1), turned(above, 1, 1)),
    )


def main_sums(frame, field, xs, join, wx, wy, wz):
    span = frame.span
    slabs = [field[xs[0] - 1 + k, span] for k in range(len(xs) + 2)]
    faces = [wx[xs[0] - 1 + k, span] for k in range(len(xs) + 1)]
    totals = []
    for k, x in enumerate(xs):
        here, face_y, face_z = slabs[k + 1], wy[x, span], wz[x, span]
        total = faces[k + 1] * slabs[k + 2] + faces[k] * slabs[k]
        total = total + face_y * turned(here, -1, 0) + turned(face_y * here, 1, 0)
        total = total + face_z * turned(here, -1, 1) + turned(face_z * here, 1, 1)
        totals.append(total + at_edges(join, x))
    return slabs[1:-1], totals


def ends_sum(frame, ends, s, upper, lower, wx, wy, wz_up, wz_low):
    span, down = frame.span, pl.ds(SUB - 1, frame.tall)
    here = ends[s, span]
    total = wx[s, span] * turned(here, -HALO, 1) + turned(wx[s, span] * here, HALO, 1)
    total = total + wy[s, span] * ends[s, pl.ds(SUB + 1, frame.tall)] + wy[s, down] * ends[s, down]
    return total + wz_up[s, span] * upper + wz_low[s, span] * lower


def clear_spares(ref, frame):
    for x in range(ref.shape[0]):
        ref[x, :SUB] = jnp.zeros((SUB, LANES), F32)
        ref[x, SUB + frame.tall :] = jnp.zeros((SUB, LANES), F32)


def pack_rows(values):
    half = values.shape[0] // 2
    lane = lane_no((half, LANES))
    return jnp.where(lane < LANES // 2, values[:half], turned(values[half:], LANES // 2, 1))


def lane_total(values):
    return jnp.broadcast_to(jnp.sum(values.T, axis=0, keepdims=True), (SUB, LANES))


def paired(values):
    even = 2 * (lane_no(values.shape) % (LANES // 2))
    return picked(values + turned(values, -1, 1), even)


def faces_y_kept(flags, frame):
    row = row_no((frame.tall, LANES))
    at_low, at_high = row == HALO - 1, row == HALO + frame.ny - 1
    return jnp.where(at_low, flags[Y_LOW], jnp.where(at_high, flags[Y_HIGH], 1)).astype(F32)


def face_rows(count, flags, nb):
    x = [(jnp.where(flags[IX] == 0, 1, 0), SUB)] if count == 2 else [(0, SUB), (1, SUB)]
    return x + [(2, nb // 2), (3, nb // 2), (4, 2), (5, 2)]


def add_rows(total, labels, b, values, c, rows=SUB):
    iota = row_no((AGG, LANES)).astype(F32)
    for r in range(rows):
        row = pl.ds(r, 1)
        total = total + jnp.where(labels[b, row] == iota, values[c, row], 0.0)
    return total


def pack_lanes(values):
    lane = lane_no((2, LANES))
    packed = values[:2]
    for g in range(1, SUB):
        packed = jnp.where(lane // 16 == g, turned(values[2 * g : 2 * g + 2], 16 * g, 1), packed)
    return packed


def fields_kernel(count, flags, wide_ref, block_label, inner, face_label, wx, wy, wz, partial, cond_edges, face_weight, diag):
    frame = Frame(wx.shape[0] - 2 * HALO, wx.shape[1] - 2 * (SUB + HALO))
    wide, tall, span = frame.wide, frame.tall, frame.span
    last = HALO + frame.nx
    keep_y = faces_y_kept(flags, frame)
    inside = jnp.where(lane_no((1, LANES)) == LANES - 1, 0.0, 1.0)

    def fields(xs, carry):
        before, edges = carry
        stores = []
        for x in xs:
            here = wide_ref[0, x, span]
            keep = jnp.where(x == HALO - 1, flags[X_LOW], jnp.where(x == last - 1, flags[X_HIGH], 1)).astype(F32)
            face_x = keep * weight(here, wide_ref[0, jnp.minimum(x + 1, wide - 1), span])
            face_y = keep_y * weight(here, wide_ref[0, x, pl.ds(SUB + 1, tall)])
            face_z = inside * weight(here, turned(here, -1, 1))
            total = wide_ref[2, x, span] + face_x + before + face_y + turned(face_y, 1, 0)
            total = total + face_z + turned(face_z, 1, 1)
            stores.append((x, (face_x, face_y, face_z, total)))
            edges = edge_step(here, x, edges)
            before = face_x
        for x, values in stores:
            for ref, value in zip((wx, wy, wz, partial), values):
                ref[x, span] = value
        return before, edges

    nothing = jnp.zeros((tall, LANES), F32)
    cond_edges[...] = batched(0, wide, fields, (nothing, nothing + 1.0), 4)[1]
    nb, ny = frame.nx // 2, frame.ny
    for s, x in enumerate((HALO - 1, last - 1)):
        rows = [wx[x, pl.ds(frame.own + c, ny // 2, stride=2)] for c in range(2)]
        face_weight[s] = pack_rows(paired(rows[0] + rows[1]))
    for s, at in ((2, frame.own - 1), (3, frame.own + ny - 1)):
        lines = [wy[HALO + 2 * b, at : at + 1] + wy[HALO + 2 * b + 1, at : at + 1] for b in range(nb)]
        face_weight[s, : nb // 2] = pack_rows(paired(jnp.concatenate(lines, axis=0)))
    around = jnp.zeros((AGG, LANES), F32)
    around = lax.fori_loop(0, nb, lambda b, around: add_rows(around, block_label, b, inner, b), around)
    for s, rows in face_rows(count, flags, nb)[:-2]:
        around = add_rows(around, face_label, s, face_weight, s, rows)
    diag[...] = lane_total(around)


def fine_kernel(flags, wide_ref, forth, back, wx, wy, wz, partial, cond_edges, block_label, face_label, some_diag,
                *refs):
    inv_diag, start = refs[:2]
    ends = refs[2:8]
    pre, face_weight, scaled_rhs, scale, once, once_ends, res, diag, block_res = refs[8:]
    ex, ey, ez_up, ez_low, inv_ends, start_ends = ends
    nx, ny = pre.shape[0], pre.shape[1]
    frame = Frame(nx, ny)
    wide, tall, span = frame.wide, frame.tall, frame.span
    last = HALO + nx
    got = [sides(flags, forth[f * tall : (f + 1) * tall], back[f * tall : (f + 1) * tall]) for f in range(3)]
    (cond_below, cond_above), rhs_ends, absorb_ends = got
    for ref in (ey, start_ends, once_ends):
        clear_spares(ref, frame)

    lane = lane_no((1, LANES))
    keep_y = faces_y_kept(flags, frame)
    keep_low, keep_high = flags[Z_LOW].astype(F32), flags[Z_HIGH].astype(F32)
    near = ends_near(cond_below, cond_above, cond_edges[...])
    slab = lane // HALO
    keep_x = jnp.where(
        slab == HALO - 1, flags[X_LOW], jnp.where(slab == last - 1, flags[X_HIGH], 1)
    ).astype(F32)
    layer = lane % HALO
    for s, here in enumerate((cond_below, cond_above)):
        up, low = weight(here, near[2 * s]), weight(here, near[2 * s + 1])
        if s == 0:
            up = up * jnp.where(layer == HALO - 1, keep_low, 1.0)
        else:
            low = low * jnp.where(layer == 0, keep_high, 1.0)
        face_x = keep_x * weight(here, turned(here, -HALO, 1))
        face_y = keep_y * weight(here, turned(here, -1, 0))
        ex[s, span], ey[s, span], ez_up[s, span], ez_low[s, span] = face_x, face_y, up, low
        total = absorb_ends[s] + face_x + turned(face_x, HALO, 1) + face_y + turned(face_y, 1, 0) + up + low
        inverse = OMEGA_FINE / total
        inv_ends[s, span] = inverse
        start_ends[s, span] = inverse * rhs_ends[s]

    end_low, end_high = ez_up[0, span], ez_low[1, span]
    join_faces = joined(end_low, end_high)

    def first_sweep(xs, edges):
        stores = []
        for x in xs:
            total = partial[x, span] + at_edges(join_faces, x)
            inverse = OMEGA_FINE / total
            begin = inverse * wide_ref[1, x, span]
            stores.append((x, (total, inverse, begin)))
            edges = edge_step(begin, x, edges)
        for x, values in stores:
            for ref, value in zip((diag, inv_diag, start), values):
                ref[x, span] = value
        return edges

    edges = batched(0, wide, first_sweep, jnp.zeros((tall, LANES), F32), 4)

    join = joined(end_low * start_ends[0, span], end_high * start_ends[1, span])
    near = ends_near(start_ends[0, span], start_ends[1, span], edges)
    for s in range(2):
        total = ends_sum(frame, start_ends, s, near[2 * s], near[2 * s + 1], ex, ey, ez_up, ez_low)
        once_ends[s, span] = (2.0 - OMEGA_FINE) * start_ends[s, span] + inv_ends[s, span] * total

    def second(xs, carry):
        news = []
        for x, here, total in zip(xs, *main_sums(frame, start, xs, join, wx, wy, wz)):
            news.append((2.0 - OMEGA_FINE) * here + inv_diag[x, span] * total)
        for x, new in zip(xs, news):
            once[x, span] = new
        return carry

    batched(HALO - 1, last + 1, second, 0, 13 if (nx + 2) % 13 == 0 else 6)
    join2 = joined(end_low * once_ends[0, span], end_high * once_ends[1, span])

    def remainder(xs, carry):
        news = []
        for x, here, total in zip(xs, *main_sums(frame, once, xs, join2, wx, wy, wz)):
            news.append(wide_ref[1, x, span] - diag[x, span] * here + total)
        for x, new in zip(xs, news):
            res[x - HALO, span] = new
        for x in xs:
            pre[x - HALO] = once[x, pl.ds(frame.own, ny)]
        return carry

    batched(HALO, last, remainder, 0, 8)

    nb, half = nx // 2, ny // 2

    def rows_at(ref, x, off):
        return ref[x, pl.ds(frame.own + off, half, stride=2)]

    def to_blocks(bs, carry):
        for b in bs:
            four = sum(rows_at(res, 2 * b + a, c) for a in range(2) for c in range(2))
            block_res[b] = pack_rows(paired(four))
        return carry

    batched(0, nb, to_blocks, 0)
    zeros = jnp.zeros((AGG, LANES), F32)
    sums = lax.fori_loop(0, nb, lambda b, total: add_rows(total, block_label, b, block_res, b), zeros)

    lane = lane_no((half, LANES))
    around = zeros
    for s, (ref, side, layer_at) in enumerate(((ez_up, 0, HALO - 1), (ez_low, 1, 0))):
        values = rows_at(ref, side, 0) + rows_at(ref, side, 1)
        values = values + turned(values, -HALO, 1)
        spot = jnp.minimum(2 * HALO * lane + HALO * HALO + layer_at, LANES - 1)
        face_weight[s, :2] = pack_lanes(jnp.where(lane < nb, picked(values, spot), 0.0))
        around = add_rows(around, face_label, 4 + s, face_weight, s, 2)
    scale[...] = OMEGA_COARSE / (some_diag[...] + lane_total(around))
    scaled_rhs[...] = scale[...] * lane_total(sums)


def tile_sum(tile, rows, label_at, pairs_at, group=4):
    iota = row_no((AGG, LANES)).astype(F32)
    for first in range(0, rows, group):
        places, highs, lows = [], [], []
        for r in range(first, min(first + group, rows)):
            places.append(jnp.where(label_at(r) == iota, 1.0, 0.0).astype(BF16))
            held = sum(jnp.where(near == iota, w, 0.0) for near, w in pairs_at(r))
            highs.append(held.astype(BF16))
            lows.append((held - highs[-1].astype(F32)).astype(BF16))
        left = jnp.concatenate(places, axis=1)
        right = jnp.concatenate([jnp.concatenate(highs, axis=1), jnp.concatenate(lows, axis=1)], axis=0)
        tile = tile + lax.dot_general(left, right, (((1,), (1,)), ((), ())), preferred_element_type=F32)
    return tile


def both_halves(tile):
    return tile[:, :AGG] + tile[:, AGG:]


def keep_tile(out, t, tile):
    high = tile.astype(BF16)
    rows = pl.ds(t * AGG, AGG)
    out[rows, :AGG] = high
    out[rows, AGG:] = (tile - high.astype(F32)).astype(BF16)


def blocks_kernel(flags, cond, absorb, block_agg, _, block_label, near, weights, inner, face_label, fine_label,
                  part, line):
    nx, ny = cond.shape[0], cond.shape[1]
    nb, half, width = nx // 2, ny // 2, LANES // 2
    lane, row = lane_no((half, LANES)), row_no((half, LANES))

    def halves(values, slot):
        part[slot] = values
        return part[slot, pl.ds(0, half, stride=2)], part[slot, pl.ds(1, half, stride=2)]

    def label_at(b):
        values = block_agg[b].astype(F32)
        return jnp.concatenate([values, values], axis=1)

    def upper_x(b, slot):
        x = jnp.maximum(2 * b, 0)
        faces = weight(cond[x + 1], cond[jnp.minimum(x + 2, nx - 1)])
        return jnp.where((b == nb - 1) | (b < 0), 0.0, paired(sum(halves(faces, slot))))

    def step(bs, carry):
        low_x = upper_x(bs[0] - 1, 0)
        for k, b in enumerate(bs):
            x = 2 * b
            slot = 4 * k + 1
            one, two = cond[x], cond[x + 1]
            both_y = weight(one, turned(one, -1, 0)) + weight(two, turned(two, -1, 0))
            both_z = weight(one, turned(one, -1, 1)) + weight(two, turned(two, -1, 1))
            high_x = upper_x(b, slot)
            high_y = jnp.where(row == half - 1, 0.0, paired(halves(both_y, slot + 1)[1]))
            high_z = picked(sum(halves(both_z, slot + 2)), 2 * (lane % width) + 1)
            high_z = jnp.where(lane % width == width - 1, 0.0, high_z)
            low_y, low_z = turned(high_y, 1, 0), turned(high_z, 1, 1)
            own = label_at(b)
            near_x, past_x = label_at(jnp.minimum(b + 1, nb - 1)), label_at(jnp.maximum(b - 1, 0))
            near_y, past_y = turned(own, -1, 0), turned(own, 1, 0)
            near_z, past_z = turned(own, -1, 1), turned(own, 1, 1)
            total = paired(sum(halves(absorb[x] + absorb[x + 1], slot + 3)))
            for d, (beside, values) in enumerate((
                (near_x, high_x), (past_x, low_x), (near_y, high_y), (past_y, low_y), (near_z, high_z), (past_z, low_z)
            )):
                leaving = jnp.where(beside != own, values, 0.0)
                total = total + leaving
                near[d, b], weights[d, b] = pack_rows(beside).astype(jnp.int32), pack_rows(leaving)
            block_label[b] = pack_rows(own)
            inner[b] = pack_rows(total)
            spread = picked(own, lane // 2)
            for a in range(2):
                for c in range(2):
                    fine_label[x + a, pl.ds(c, half, stride=2)] = spread
            low_x = high_x
        return carry

    batched(0, nb, step, 0, 4)
    line[...] = jnp.zeros(line.shape, F32)
    low, high = jnp.zeros((half, LANES), F32), jnp.zeros((half, LANES), F32)
    for b in range(nb):
        own = label_at(b)
        line[0, b : b + 1], line[1, b : b + 1] = own[:1], own[half - 1 :]
        low = jnp.where(lane == b, own[:, :1], low)
        high = jnp.where(lane == b, own[:, width - 1 : width], high)
    face_label[0], face_label[1] = block_label[0], block_label[nb - 1]
    for s in range(2):
        face_label[2 + s, : nb // 2] = pack_rows(line[s, :nb])
        face_label[4 + s, :2] = pack_lanes((low, high)[s])


def own_turn_kernel(flags, block_label, near, weights, coarse, out, values):
    table = jnp.broadcast_to(coarse[:1], (SUB, LANES))
    nb = block_label.shape[0]

    def sums(bs, carry):
        news = [sum(weights[d, b] * picked(table, near[d, b]) for d in range(6)) for b in bs]
        for b, new in zip(bs, news):
            values[b] = new
        return carry

    batched(0, nb, sums, 0)
    total = jnp.zeros((AGG, LANES), F32)
    total = lax.fori_loop(0, nb, lambda b, total: add_rows(total, block_label, b, values, b), total)
    out[...] = lane_total(total)


def faces_kernel(count, nb, flags, face_label, weight_xy, weight_z, x_low, x_high, y_low, y_high, forth, back, out,
                 near, weights):
    at, half = x_low.shape[0] - 1, x_low.shape[1] // 2
    near[0], near[1] = pack_rows(x_low[at, :half]), pack_rows(x_high[at, :half])
    at = sum(WIDTHS) * 2 * nb
    for s, ref in enumerate((y_low, y_high)):
        near[2 + s, : nb // 2] = pack_rows(ref[at : at + nb])
    at = forth.shape[0] - half
    for s, values in enumerate(sides(flags, forth[at:], back[at:])):
        near[4 + s, :2] = pack_lanes(values)
    weights[:4], weights[4:] = weight_xy[...], weight_z[...]
    for t, (s, rows) in enumerate(face_rows(count, flags, nb)):
        tile = tile_sum(
            jnp.zeros((AGG, 2 * AGG), F32),
            rows,
            lambda r, s=s: near[s, pl.ds(r, 1)],
            lambda r, s=s: [(face_label[s, pl.ds(r, 1)], weights[s, pl.ds(r, 1)])],
        )
        keep_tile(out, t, both_halves(tile))


def turn_kernel(flags, tiles, scaled_rhs, scale, own, inside, *refs):
    forth, back, *others, out = refs
    got = [ref[ref.shape[0] - 1, :SUB] if len(ref.shape) == 3 else ref[ref.shape[0] - SUB :] for ref in (*others, forth, back)]
    vectors = [*got[:-2], *sides(flags, *got[-2:])]
    row = row_no((SUB, AGG))
    parts = []
    for v in vectors:
        high = v.astype(BF16).astype(F32)
        parts.append(jnp.where(row == 0, high, jnp.where(row == 1, v - high, 0.0)).astype(BF16))
    got = jnp.dot(jnp.concatenate(parts, axis=1), tiles[...], preferred_element_type=F32)
    applied = jnp.sum(got[:, :AGG] + got[:, AGG:], axis=0, keepdims=True)
    out[...] = (1.0 - OMEGA_COARSE) * own[...] + scaled_rhs[...] + scale[...] * (inside[...] + applied)


def ride_kernel(count, flags, pre, fine_label, coarse, *outs):
    nx = pre.shape[0]
    for s, out in enumerate(outs):
        at = jnp.where(flags[IX] == 0, nx - HALO, 0) if count == 2 else (nx - HALO, 0)[s]
        for f, field in enumerate((pre, fine_label)):
            for x in range(HALO):
                out[HALO * f + x] = field[at + x]
        out[2 * HALO] = jnp.zeros(out.shape[1:], F32)
        out[2 * HALO, :SUB] = coarse[...]


def three_kernel(flags, low, mid, high, out):
    row = row_no(out.shape)
    out[...] = jnp.where(row == 0, low[...], jnp.where(row == 1, mid[...], high[...]))


def nine_kernel(flags, low, mid, high, out):
    out[...] = jnp.zeros(out.shape, F32)
    for n, ref in enumerate((low, mid, high)):
        out[3 * n : 3 * n + 3] = ref[:3]


def lift_kernel(flags, wide_ref, forth, back, main, ends):
    frame = Frame(wide_ref.shape[1] - 2 * HALO, wide_ref.shape[2] - 2 * (SUB + HALO))
    tall = frame.tall
    for b in range(frame.wide // 2):
        main[b] = wide_ref[1, 2 * b, frame.span].astype(jnp.int32)
    rows = pl.ds(tall, tall)
    for s, values in enumerate(sides(flags, forth[rows], back[rows])):
        ends[s] = values.astype(jnp.int32)


def own_lift_kernel(flags, wide_ref, labels, coarse, lifted):
    frame = Frame(wide_ref.shape[1] - 2 * HALO, wide_ref.shape[2] - 2 * (SUB + HALO))
    table = jnp.broadcast_to(coarse[:1], (frame.tall, LANES))

    def lift(bs, carry):
        news = [picked(table, labels[b]) for b in bs]
        for b, new in zip(bs, news):
            for a in range(2):
                lifted[2 * b + a, frame.span] = wide_ref[0, 2 * b + a, frame.span] + new
        return carry

    batched(HALO // 2, (HALO + frame.nx) // 2, lift, 0, 4)


def post_kernel(flags, own_lifted, table, table_forth, table_back, labels, end_labels, wide_ref, forth, back, *refs):
    (wx, wy, wz, inv_diag, start), ends = refs[:5], refs[5:11]
    out, lifted, one, two, one_ends, two_ends, kept_out, sems = refs[11:]
    nx, ny = out.shape[0], out.shape[1]
    frame = Frame(nx, ny)
    wide, tall, span = frame.wide, frame.tall, frame.span
    ex, ey, ez_up, ez_low, inv_ends, start_ends = ends
    for ref in (one_ends, two_ends):
        clear_spares(ref, frame)
    row, lane = row_no((tall, LANES)), lane_no((tall, LANES))
    under, over = sides(flags, table_forth[...], table_back[...])
    tables = {-1: under, 0: table[...], 1: over}

    def table_at(dx, dz):
        low, mid, high = (tables[dz][3 * n + dx + 1 : 3 * n + dx + 2] for n in range(3))
        return jnp.where(row < HALO, low, jnp.where(row < HALO + ny, mid, high))

    def lift(x, values, at):
        rows = pl.ds(SUB + at.start, at.size)
        lifted[x, rows] = wide_ref[0, x, rows] + picked(values[at.start : at.start + at.size], labels[x // 2, at])

    for x in range(wide):
        if HALO <= x < HALO + nx:
            continue
        lift(x, table_at(-1 if x < HALO else 1, 0), pl.ds(0, tall))
    mid = table_at(0, 0)

    def ends_of_rows(xs, carry):
        for x in xs:
            for at in (pl.ds(0, SUB), pl.ds(tall - SUB, SUB)):
                lift(x, mid, at)
        return carry

    batched(HALO, HALO + nx, ends_of_rows, 0, 6)
    for s, (dz, base) in enumerate(zip((-1, 1), sides(flags, forth[:tall], back[:tall]))):
        below, inside, above = (picked(table_at(dx, dz), end_labels[s]) for dx in (-1, 0, 1))
        spot = lane // HALO
        two_ends[s, span] = base + jnp.where(spot < HALO, below, jnp.where(spot < HALO + nx, inside, above))
    kept = 1.0 - OMEGA_FINE

    def result(at, count):
        rows = pl.ds(at, count)
        return pltpu.make_async_copy(kept_out.at[rows], out.at[rows], sems.at[at // count])

    buffers = ((lifted, two_ends), (one, one_ends), (two, two_ends), (one, one_ends))
    for s in range(POST):
        src, src_ends = buffers[s]
        join = joined(ez_up[0, span] * src_ends[0, span], ez_low[1, span] * src_ends[1, span])
        final = s == POST - 1
        dst, dst_ends = (None, None) if final else buffers[s + 1]

        def step(xs, edges, src=src, join=join, dst=dst, final=final):
            news = []
            for x, here, total in zip(xs, *main_sums(frame, src, xs, join, wx, wy, wz)):
                news.append(kept * here + start[x, span] + inv_diag[x, span] * total)
                if not final:
                    edges = edge_step(here, x, edges)
            for x, new in zip(xs, news):
                if final:
                    kept_out[x - HALO] = new[HALO : HALO + ny]
                else:
                    dst[x, span] = new
            if final:
                result(xs[0] - HALO, len(xs)).start()
            return edges

        size = 8 if final else 10
        edges = batched(s + 1, wide - s - 1, step, jnp.zeros((tall, LANES), F32), size)
        if not final:
            near = ends_near(src_ends[0, span], src_ends[1, span], edges)
            news = []
            for e in range(2):
                total = ends_sum(frame, src_ends, e, near[2 * e], near[2 * e + 1], ex, ey, ez_up, ez_low)
                news.append(kept * src_ends[e, span] + start_ends[e, span] + inv_ends[e, span] * total)
            dst_ends[0, span], dst_ends[1, span] = news
    for n in range(nx // 8):
        result(8 * n, 8).wait()


def body(links, right_side, conductance, absorption, block_agg):
    nx, ny, nz = right_side.shape
    frame = Frame(nx, ny)
    nb = nx // 2
    n_x = links.sizes[0]
    arrays = (conductance, right_side, absorption, block_agg)
    n_send = 1 if n_x == 2 else 2
    pinned = [pltpu.with_memory_space_constraint(a, pltpu.HBM) for a in arrays]
    outs = [jax.ShapeDtypeStruct(a.shape, a.dtype) for a in arrays]
    outs += [shaped(sum(WIDTHS) + 1, ny, nz)] * n_send + [shaped(sum(WIDTHS) * nx + 16, nz)] * 2
    outs += [shaped(-(-sum(w * w for w in WIDTHS) // SUB) * SUB, nz)] * (2 * n_send)
    got = call(
        functools.partial(pack_kernel, n_x, WIDTHS),
        outs,
        [pltpu.SemaphoreType.DMA((3 * 4,))],
        in_specs=[pl.BlockSpec(memory_space=pltpu.HBM)] * 4,
    )(*pinned)
    arrays, sends = got[:4], got[4:]
    from_x = links.x(sends[:n_send])
    from_y = links.ring_y(*sends[n_send : n_send + 2])
    from_corners = links.corners(sends[n_send + 2 :])
    blocks = (nb, SUB, LANES)
    outs = [shaped(*blocks), jax.ShapeDtypeStruct((6, *blocks), jnp.int32), shaped(6, *blocks), shaped(*blocks)]
    outs += [shaped(6, SUB, LANES), shaped(nx, ny, nz)]
    scratch = [pltpu.VMEM((17, ny, LANES), F32), pltpu.VMEM((2, ny // 2, LANES), F32)]
    *rows, inner, face_label, fine_label = call(blocks_kernel, outs, scratch)(
        arrays[0], arrays[2], arrays[3], sends[0]
    )
    got = lax.optimization_barrier((*from_x, *from_y, *from_corners, inner))
    from_x, from_y, from_corners, inner = got[:n_send], got[n_send : n_send + 2], got[n_send + 2 : -1], got[-1]
    block_label = rows[0]
    size = len(WIDTHS) * frame.tall
    wide, *sends = call(
        functools.partial(first_frame_kernel, n_x, WIDTHS),
        [shaped(len(WIDTHS), *frame.main)] + [shaped(size + ny // 2, nz)] * 2,
        [pltpu.VMEM((size, nz), F32)] * 2,
    )(*arrays, from_x[0], from_x[-1], *from_y, *from_corners)
    outs = [shaped(*frame.main)] * 4 + [shaped(frame.tall, nz), shaped(4, SUB, LANES), shaped(SUB, AGG)]
    *fields, weight_xy, some_diag = call(functools.partial(fields_kernel, n_x), outs, limit=24)(
        wide, block_label, inner, face_label
    )
    halo = (wide, *links.z(*sends))
    outs = [shaped(*frame.main)] * 2 + [shaped(*frame.ends)] * 6 + [shaped(nx, ny, nz)]
    outs += [shaped(2, SUB, LANES)] + [shaped(SUB, AGG)] * 2
    scratch = [pltpu.VMEM(frame.main, F32), pltpu.VMEM(frame.ends, F32), pltpu.VMEM((nx, frame.rows, LANES), F32)]
    scratch += [pltpu.VMEM(frame.main, F32), pltpu.VMEM(blocks, F32)]
    got = call(fine_kernel, outs, scratch, limit=28)(
        *halo, *fields, block_label, face_label, some_diag
    )
    fields, pre = (*fields[:3], *got[:8]), got[8]
    weight_z, scaled_rhs, scale = got[9:]
    tiles = call(
        functools.partial(faces_kernel, n_x, nb),
        jax.ShapeDtypeStruct(((n_send + 4) * AGG, 2 * AGG), BF16),
        [pltpu.VMEM((6, SUB, LANES), F32)] * 2,
    )(face_label, weight_xy, weight_z, from_x[0], from_x[-1], *from_y, *halo[1:])
    coarse = scaled_rhs

    def turn(**more):
        near = links.near(coarse, **more)
        inside = call(own_turn_kernel, shaped(SUB, AGG), [pltpu.VMEM(blocks, F32)])(*rows, coarse)
        return call(turn_kernel, shaped(SUB, AGG))(tiles, scaled_rhs, scale, coarse, inside, *near), near

    both = (pre, fine_label)
    rides = call(functools.partial(ride_kernel, n_x), [shaped(2 * HALO + 1, ny, nz)] * n_send)(*both, coarse)
    coarse, near = turn(x=rides)
    from_x = near[2:-2]
    rides = send_y(both, coarse, from_x)
    frames = framed(both, from_x, rides[0])
    coarse, near = turn(y=rides)
    wide, *rides = send_z(frames, near[-2:], coarse)
    coarse, near = turn(z=rides)
    halo = (wide, *near[:2])
    outs = [jax.ShapeDtypeStruct((frame.wide // 2, frame.tall, nz), jnp.int32)]
    outs += [jax.ShapeDtypeStruct((2, frame.tall, nz), jnp.int32)]
    lifts = call(lift_kernel, outs)(*halo)
    for _ in range(KC - 4):
        coarse, _ = turn()
    from_x = links.x([coarse] * n_send)
    own_lifted = call(own_lift_kernel, shaped(*frame.main))(halo[0], lifts[0], coarse)
    three = call(three_kernel, shaped(SUB, AGG))(from_x[0], coarse, from_x[-1])
    low, high = links.ring_y(three, three)
    nine = call(nine_kernel, shaped(2 * SUB, AGG))(low, three, high)
    tables = (nine, *links.z(nine, nine))
    scratch = [pltpu.VMEM(frame.main, F32)] * 2 + [pltpu.VMEM(frame.ends, F32)] * 2
    scratch += [pltpu.VMEM((nx, ny, nz), F32), pltpu.SemaphoreType.DMA((nx // 8,))]
    outs, out_specs = [shaped(nx, ny, nz), shaped(*frame.main)], [pl.BlockSpec(memory_space=pl.ANY), VMEM]
    return call(post_kernel, outs, scratch, limit=24, out_specs=out_specs, aliases={0: 1})(
        own_lifted, *tables, *lifts, *halo, *fields
    )[0]


def solution(mesh):
    spec = P("gx", "gy", "gz")
    return jax.shard_map(
        functools.partial(body, Links(mesh)), mesh=mesh, in_specs=(spec,) * 4, out_specs=spec, check_vma=False
    )
```

```python
import functools

import jax
import jax.numpy as jnp
from jax import lax
from jax.experimental import pallas as pl
from jax.experimental.pallas import tpu as pltpu
from jax.sharding import PartitionSpec as P

AGG = 128
LANES = 128
SUB = 8
HALO = 4
WIDTHS = (4, 3, 3)
POST = 4
KC = 8
OMEGA_FINE = 0.8
OMEGA_COARSE = 0.7
F32 = jnp.float32
BF16 = jnp.bfloat16
VMEM = pl.BlockSpec(memory_space=pltpu.VMEM)
IX, PARITY, X_LOW, X_HIGH, Y_LOW, Y_HIGH, Z_LOW, Z_HIGH = range(8)


def places():
    (ix, n_x), (iy, n_y), (iz, n_z) = ((lax.axis_index(a), lax.axis_size(a)) for a in ("gx", "gy", "gz"))
    flags = [ix, iy % 2, ix > 0, ix < n_x - 1, iy > 0, iy < n_y - 1, iz > 0, iz < n_z - 1]
    return [jnp.asarray(flag, jnp.int32) for flag in flags]


def call(kernel, outs, scratch=(), limit=16, flops=10**6, in_specs=None, aliases=None, out_specs=None):
    def placed(*refs):
        kernel(places(), *refs)

    def run(*arrays):
        return pl.pallas_call(
            placed,
            out_shape=outs,
            in_specs=in_specs or [VMEM] * len(arrays),
            out_specs=out_specs or jax.tree.map(lambda _: VMEM, outs),
            scratch_shapes=list(scratch),
            input_output_aliases=aliases or {},
            compiler_params=pltpu.CompilerParams(vmem_limit_bytes=limit * 2**20),
            cost_estimate=pl.CostEstimate(flops=flops, bytes_accessed=10**5, transcendentals=0),
        )(*arrays)

    return run


def shaped(*shape):
    return jax.ShapeDtypeStruct(shape, F32)


def lane_no(shape):
    return lax.broadcasted_iota(jnp.int32, shape, len(shape) - 1)


def row_no(shape):
    return lax.broadcasted_iota(jnp.int32, shape, len(shape) - 2)


def turned(values, shift, axis):
    if isinstance(shift, int):
        shift = shift % values.shape[axis]
        if shift == 0:
            return values
    return pltpu.roll(values, shift, axis)


def batched(low, high, step, carry, size=6):
    def some(i, carry):
        return step([low + i * size + k for k in range(size)], carry)

    carry = lax.fori_loop(0, (high - low) // size, some, carry)
    rest = (high - low) % size
    return step(list(range(high - rest, high)), carry) if rest else carry


def picked(values, index):
    return jnp.take_along_axis(values, index, axis=1, mode="promise_in_bounds")


class Frame:
    def __init__(self, nx, ny):
        self.nx, self.ny = nx, ny
        self.wide, self.tall = nx + 2 * HALO, ny + 2 * HALO
        self.rows = self.tall + 2 * SUB
        self.span = pl.ds(SUB, self.tall)
        self.own = SUB + HALO
        self.main = (self.wide, self.rows, LANES)
        self.ends = (2, self.rows, LANES)


def bases(widths):
    return [sum(widths[:f]) for f in range(len(widths) + 1)]


def copied(pairs, sems):
    copies = [pltpu.make_async_copy(src, dst, sems.at[n]) for n, (src, dst) in enumerate(pairs)]
    for copy in copies:
        copy.start()
    return copies


def pack_kernel(count, widths, flags, *refs):
    fields = len(widths)
    n_x = 1 if count == 2 else 2
    ins, kept = refs[: fields + 1], refs[fields + 1 : 2 * fields + 2]
    outs, sems = refs[2 * fields + 2 : -1], refs[-1]
    x_outs, y_outs, corner_outs = outs[:n_x], outs[n_x : n_x + 2], outs[n_x + 2 :]
    nx, ny = ins[0].shape[0], ins[0].shape[1]
    nb, half, width = ins[-1].shape
    thirds = 3
    copies = []
    for ref, out in zip(ins, kept):
        for t in range(thirds):
            size = ref.shape[0] // thirds
            rows = pl.ds(t * size, size)
            copies.append(pltpu.make_async_copy(ref.at[rows], out.at[rows], sems.at[len(copies)]))
    for copy in copies:
        copy.start()
    for out in (*x_outs, *y_outs):
        out[...] = jnp.zeros(out.shape, F32)
    for copy in copies:
        copy.wait()
    base = bases(widths)
    labels = kept[-1]
    for s, out in enumerate(x_outs):

        def place(size, thick, s=s):
            if count == 2:
                return jnp.where(flags[IX] == 0, size - thick, 0)
            return (size - thick, 0)[s]

        for f, thick in enumerate(widths):
            at = place(nx, thick)
            for k in range(thick):
                slab = kept[f][at + k]
                out[base[f] + k] = slab
                row = (sum(w * w for w in widths[:f])) + k * thick
                corner_outs[2 * s][row : row + thick] = slab[ny - thick :]
                corner_outs[2 * s + 1][row : row + thick] = slab[:thick]
        out[base[-1], :half, :width] = labels[place(nb, 1)].astype(F32)
    for out, high in zip(y_outs, (True, False)):
        for f, thick in enumerate(widths):
            for x in range(nx):
                row = base[f] * nx + x * thick
                out[row : row + thick] = kept[f][x, ny - thick :] if high else kept[f][x, :thick]
        row = base[-1] * nx
        for b in range(nb):
            line = labels[b, half - 1 :] if high else labels[b, :1]
            out[row + b : row + b + 1, :width] = line.astype(F32)


def slab_of(own, low, high, base, width, x):
    nx = own.shape[0]
    if HALO <= x < HALO + nx:
        return own[x - HALO]
    if x < HALO:
        at = x - (HALO - width)
        return low[base + at] if at >= 0 else None
    at = x - HALO - nx
    return high[base + at] if at < width else None


def pack_y_kernel(fields, flags, *refs):
    ins, rider = refs[:fields], refs[fields]
    low, high, to_high, to_low = refs[fields + 1 :]
    nx, ny = ins[0].shape[0], ins[0].shape[1]
    wide = nx + 2 * HALO
    for f in range(fields):
        for x in range(wide):
            slab = slab_of(ins[f], low, high, HALO * f, HALO, x)
            at = (f * wide + x) * HALO
            to_high[at : at + HALO] = slab[ny - HALO :]
            to_low[at : at + HALO] = slab[:HALO]
    at = fields * wide * HALO
    to_high[at:], to_low[at:] = rider[...], rider[...]


def packed_lanes(wide_ref, f, frame, rows, to_high, to_low):
    group = lane_no((1, LANES)) // HALO
    nothing = jnp.ones((rows.size, LANES), F32)
    high, low = nothing, nothing
    for x in range(frame.wide):
        moved = turned(wide_ref[f, x, rows], HALO * (x + 1), 1)
        high = jnp.where(group == x, moved, high)
        low = jnp.where(group == (x + 1) % frame.wide, moved, low)
    at = pl.ds(f * frame.tall + rows.start - SUB, rows.size)
    to_high[at] = high
    to_low[at] = turned(low, -HALO, 1)


def first_frame_kernel(count, widths, flags, *refs):
    fields = len(widths)
    ins, labels, refs = refs[:fields], refs[fields], refs[fields + 1 :]
    x_low, x_high, y_low, y_high = refs[:4]
    corners = refs[4:6] * 2 if count == 2 else refs[4:8]
    wide_ref, send_forth, send_back, to_high, to_low = refs[-5:]
    nx, ny = ins[0].shape[0], ins[0].shape[1]
    frame = Frame(nx, ny)
    base = bases(widths)
    tall, own = frame.tall, frame.own
    even = flags[PARITY] == 0
    ones = jnp.ones((frame.rows, LANES), F32)
    for f, thick in enumerate(widths):
        for x in range(frame.wide):
            slab = slab_of(ins[f], x_low, x_high, base[f], thick, x)
            if slab is None:
                wide_ref[f, x] = ones
                continue
            edge = ones[: SUB + HALO]
            wide_ref[f, x, :own] = edge
            wide_ref[f, x, own + ny :] = edge
            wide_ref[f, x, own : own + ny] = slab
            if HALO <= x < HALO + nx:
                low, high, row = y_low, y_high, base[f] * nx + (x - HALO) * thick
            else:
                above = x >= HALO
                low, high = corners[2 * above : 2 * above + 2]
                at = x - HALO - nx if above else x - (HALO - thick)
                row = sum(w * w for w in widths[:f]) + at * thick
            wide_ref[f, x, own - thick : own] = low[row : row + thick]
            wide_ref[f, x, own + ny : own + ny + thick] = high[row : row + thick]
        packed_lanes(wide_ref, f, frame, pl.ds(SUB, tall), to_high, to_low)
    high, low = to_high[...], to_low[...]
    size = fields * tall
    send_forth[:size], send_back[:size] = jnp.where(even, high, low), jnp.where(even, low, high)
    nb, rows, width = labels.shape
    lane = lane_no((rows, LANES))
    high = low = jnp.zeros((rows, LANES), F32)
    for b in range(nb):
        slab = labels[b].astype(F32)
        high = jnp.where(lane == b, slab[:, width - 1 :], high)
        low = jnp.where(lane == b, slab[:, :1], low)
    send_forth[size:], send_back[size:] = jnp.where(even, high, low), jnp.where(even, low, high)


def frame_kernel(fields, flags, *refs):
    ins = refs[:fields]
    x_low, x_high, _ = refs[fields : fields + 3]
    wide_ref, to_high, to_low = refs[fields + 3 :]
    nx, ny = ins[0].shape[0], ins[0].shape[1]
    frame = Frame(nx, ny)
    spare = jnp.ones((SUB, LANES), F32)
    for f in range(fields):
        for x in range(frame.wide):
            wide_ref[f, x, frame.own : frame.own + ny] = slab_of(ins[f], x_low, x_high, HALO * f, HALO, x)
            wide_ref[f, x, :SUB] = spare
            wide_ref[f, x, SUB + frame.tall :] = spare
        packed_lanes(wide_ref, f, frame, pl.ds(2 * SUB, frame.tall - 2 * SUB), to_high, to_low)


def pack_z_kernel(fields, flags, wide_in, high_in, low_in, from_low, from_high, rider, *refs):
    wide_ref, send_forth, send_back, to_high, to_low = refs
    frame = Frame(wide_ref.shape[1] - 2 * HALO, wide_ref.shape[2] - 2 * (SUB + HALO))
    ny, tall, own = frame.ny, frame.tall, frame.own
    even = flags[PARITY] == 0
    for f in range(fields):
        for x in range(frame.wide):
            at = (f * frame.wide + x) * HALO
            wide_ref[f, x, SUB:own] = from_low[at : at + HALO]
            wide_ref[f, x, own + ny : own + ny + HALO] = from_high[at : at + HALO]
    size = fields * tall
    to_high[...], to_low[...] = high_in[...], low_in[...]
    for f in range(fields):
        for start in (SUB, tall):
            packed_lanes(wide_ref, f, frame, pl.ds(start, SUB), to_high, to_low)
    high, low = to_high[...], to_low[...]
    send_forth[:size], send_back[:size] = jnp.where(even, high, low), jnp.where(even, low, high)
    send_forth[size:], send_back[size:] = rider[...], rider[...]


class Links:
    def __init__(self, mesh):
        self.sizes = [mesh.shape[a] for a in ("gx", "gy", "gz")]
        n_x, n_y, n_z = self.sizes

        def at(i, j, k):
            return (i % n_x * n_y + j % n_y) * n_z + k

        every = [(i, j, k) for i in range(n_x) for j in range(n_y) for k in range(n_z)]
        self.ring_x = [(i, (i + 1) % n_x) for i in range(n_x)]
        self.corner = {d: [(at(i, j, k), at(i + d, j + 1, k)) for i, j, k in every] for d in (1, -1)}
        self.snake = []
        for i in range(n_x):
            for j in range(0, n_y, 2):
                nodes = [at(i, j, k) for k in range(n_z)] + [at(i, j + 1, k) for k in reversed(range(n_z))]
                self.snake += [(nodes[m], nodes[(m + 1) % len(nodes)]) for m in range(len(nodes))]

    @staticmethod
    def back(pairs):
        return [(b, a) for a, b in pairs]

    @staticmethod
    def send(values, pairs):
        return lax.ppermute(values, ("gx", "gy", "gz"), pairs)

    def x(self, sends):
        if self.sizes[0] == 2:
            return (lax.ppermute(sends[0], "gx", self.ring_x),)
        return lax.ppermute(sends[0], "gx", self.ring_x), lax.ppermute(sends[1], "gx", self.back(self.ring_x))

    def near(self, values, x=None, y=None, z=None):
        forth, back = self.z(*(z or (values, values)))
        from_x = self.x(x or (values, values))
        return (forth, back, *from_x, *self.ring_y(*(y or (values, values))))

    def ring_y(self, to_high, to_low):
        ring = [(j, (j + 1) % self.sizes[1]) for j in range(self.sizes[1])]
        return lax.ppermute(to_high, "gy", ring), lax.ppermute(to_low, "gy", self.back(ring))

    def corners(self, sends):
        if self.sizes[0] == 2:
            return self.send(sends[0], self.corner[1]), self.send(sends[1], self.back(self.corner[1]))
        return (
            self.send(sends[0], self.corner[1]),
            self.send(sends[1], self.back(self.corner[-1])),
            self.send(sends[2], self.corner[-1]),
            self.send(sends[3], self.back(self.corner[1])),
        )

    def z(self, forth, back):
        return self.send(forth, self.snake), self.send(back, self.back(self.snake))


def send_y(arrays, rider, from_x):
    nx, ny, nz = arrays[0].shape
    rows = len(arrays) * Frame(nx, ny).wide * HALO + SUB
    kernel = functools.partial(pack_y_kernel, len(arrays))
    return call(kernel, [shaped(rows, nz)] * 2)(*arrays, rider, from_x[0], from_x[-1])


def framed(arrays, from_x, sent):
    nx, ny, nz = arrays[0].shape
    frame, fields = Frame(nx, ny), len(arrays)
    outs = [shaped(fields, *frame.main)] + [shaped(fields * frame.tall, nz)] * 2
    return call(functools.partial(frame_kernel, fields), outs)(*arrays, from_x[0], from_x[-1], sent)


def send_z(frames, from_y, rider):
    wide, high, _ = frames
    return call(
        functools.partial(pack_z_kernel, wide.shape[0]),
        [shaped(*wide.shape)] + [shaped(high.shape[0] + SUB, LANES)] * 2,
        [pltpu.VMEM(high.shape, F32)] * 2,
        aliases={0: 0},
    )(*frames, *from_y, rider)


def sides(flags, forth, back):
    even = flags[PARITY] == 0
    return jnp.where(even, forth, back), jnp.where(even, back, forth)


def weight(one, two):
    return 2.0 * (one * two) / (one + two)


def lane_mask(x):
    return ((lane_no((1, LANES)) - (HALO * x + HALO - 1)) & (LANES - 1)) < 2


def edge_step(here, x, edges):
    return jnp.where(lane_mask(x), turned(here, HALO * x + HALO, 1), edges)


def joined(below, above):
    lane = lane_no((1, LANES))
    return jnp.where(lane % HALO == HALO - 1, turned(above, HALO - 1, 1), turned(below, 1, 1))


def at_edges(join, x):
    lane = lane_no((1, LANES))
    return jnp.where((lane == 0) | (lane == LANES - 1), turned(join, (LANES - HALO) - HALO * x, 1), 0.0)


def ends_near(below, above, edges):
    layer = lane_no((1, LANES)) % HALO
    return (
        jnp.where(layer == HALO - 1, turned(edges, -1, 1), turned(below, -1, 1)),
        turned(below, 1, 1),
        turned(above, -1, 1),
        jnp.where(layer == 0, turned(edges, 1 - HALO, 1), turned(above, 1, 1)),
    )


def main_sums(frame, field, xs, join, wx, wy, wz):
    span = frame.span
    slabs = [field[xs[0] - 1 + k, span] for k in range(len(xs) + 2)]
    faces = [wx[xs[0] - 1 + k, span] for k in range(len(xs) + 1)]
    totals = []
    for k, x in enumerate(xs):
        here, face_y, face_z = slabs[k + 1], wy[x, span], wz[x, span]
        total = faces[k + 1] * slabs[k + 2] + faces[k] * slabs[k]
        total = total + face_y * turned(here, -1, 0) + turned(face_y * here, 1, 0)
        total = total + face_z * turned(here, -1, 1) + turned(face_z * here, 1, 1)
        totals.append(total + at_edges(join, x))
    return slabs[1:-1], totals


def ends_sum(frame, ends, s, upper, lower, wx, wy, wz_up, wz_low):
    span, down = frame.span, pl.ds(SUB - 1, frame.tall)
    here = ends[s, span]
    total = wx[s, span] * turned(here, -HALO, 1) + turned(wx[s, span] * here, HALO, 1)
    total = total + wy[s, span] * ends[s, pl.ds(SUB + 1, frame.tall)] + wy[s, down] * ends[s, down]
    return total + wz_up[s, span] * upper + wz_low[s, span] * lower


def clear_spares(ref, frame):
    for x in range(ref.shape[0]):
        ref[x, :SUB] = jnp.zeros((SUB, LANES), F32)
        ref[x, SUB + frame.tall :] = jnp.zeros((SUB, LANES), F32)


def pack_rows(values):
    half = values.shape[0] // 2
    lane = lane_no((half, LANES))
    return jnp.where(lane < LANES // 2, values[:half], turned(values[half:], LANES // 2, 1))


def lane_total(values):
    return jnp.broadcast_to(jnp.sum(values.T, axis=0, keepdims=True), (SUB, LANES))


def paired(values):
    even = 2 * (lane_no(values.shape) % (LANES // 2))
    return picked(values + turned(values, -1, 1), even)


def faces_y_kept(flags, frame):
    row = row_no((frame.tall, LANES))
    at_low, at_high = row == HALO - 1, row == HALO + frame.ny - 1
    return jnp.where(at_low, flags[Y_LOW], jnp.where(at_high, flags[Y_HIGH], 1)).astype(F32)


def face_rows(count, flags, nb):
    x = [(jnp.where(flags[IX] == 0, 1, 0), SUB)] if count == 2 else [(0, SUB), (1, SUB)]
    return x + [(2, nb // 2), (3, nb // 2), (4, 2), (5, 2)]


def add_rows(total, labels, b, values, c, rows=SUB):
    iota = row_no((AGG, LANES)).astype(F32)
    for r in range(rows):
        row = pl.ds(r, 1)
        total = total + jnp.where(labels[b, row] == iota, values[c, row], 0.0)
    return total


def pack_lanes(values):
    lane = lane_no((2, LANES))
    packed = values[:2]
    for g in range(1, SUB):
        packed = jnp.where(lane // 16 == g, turned(values[2 * g : 2 * g + 2], 16 * g, 1), packed)
    return packed


def fields_kernel(count, flags, wide_ref, block_label, inner, face_label, wx, wy, wz, partial, cond_edges, face_weight, diag):
    frame = Frame(wx.shape[0] - 2 * HALO, wx.shape[1] - 2 * (SUB + HALO))
    wide, tall, span = frame.wide, frame.tall, frame.span
    last = HALO + frame.nx
    keep_y = faces_y_kept(flags, frame)
    inside = jnp.where(lane_no((1, LANES)) == LANES - 1, 0.0, 1.0)

    def fields(xs, carry):
        before, edges = carry
        stores = []
        for x in xs:
            here = wide_ref[0, x, span]
            keep = jnp.where(x == HALO - 1, flags[X_LOW], jnp.where(x == last - 1, flags[X_HIGH], 1)).astype(F32)
            face_x = keep * weight(here, wide_ref[0, jnp.minimum(x + 1, wide - 1), span])
            face_y = keep_y * weight(here, wide_ref[0, x, pl.ds(SUB + 1, tall)])
            face_z = inside * weight(here, turned(here, -1, 1))
            total = wide_ref[2, x, span] + face_x + before + face_y + turned(face_y, 1, 0)
            total = total + face_z + turned(face_z, 1, 1)
            stores.append((x, (face_x, face_y, face_z, total)))
            edges = edge_step(here, x, edges)
            before = face_x
        for x, values in stores:
            for ref, value in zip((wx, wy, wz, partial), values):
                ref[x, span] = value
        return before, edges

    nothing = jnp.zeros((tall, LANES), F32)
    cond_edges[...] = batched(0, wide, fields, (nothing, nothing + 1.0), 4)[1]
    nb, ny = frame.nx // 2, frame.ny
    for s, x in enumerate((HALO - 1, last - 1)):
        rows = [wx[x, pl.ds(frame.own + c, ny // 2, stride=2)] for c in range(2)]
        face_weight[s] = pack_rows(paired(rows[0] + rows[1]))
    for s, at in ((2, frame.own - 1), (3, frame.own + ny - 1)):
        lines = [wy[HALO + 2 * b, at : at + 1] + wy[HALO + 2 * b + 1, at : at + 1] for b in range(nb)]
        face_weight[s, : nb // 2] = pack_rows(paired(jnp.concatenate(lines, axis=0)))
    around = jnp.zeros((AGG, LANES), F32)
    around = lax.fori_loop(0, nb, lambda b, around: add_rows(around, block_label, b, inner, b), around)
    for s, rows in face_rows(count, flags, nb)[:-2]:
        around = add_rows(around, face_label, s, face_weight, s, rows)
    diag[...] = lane_total(around)


def fine_kernel(flags, wide_ref, forth, back, wx, wy, wz, partial, cond_edges, block_label, face_label, some_diag,
                *refs):
    inv_diag, start = refs[:2]
    ends = refs[2:8]
    pre, face_weight, scaled_rhs, scale, once, once_ends, res, diag, block_res = refs[8:]
    ex, ey, ez_up, ez_low, inv_ends, start_ends = ends
    nx, ny = pre.shape[0], pre.shape[1]
    frame = Frame(nx, ny)
    wide, tall, span = frame.wide, frame.tall, frame.span
    last = HALO + nx
    got = [sides(flags, forth[f * tall : (f + 1) * tall], back[f * tall : (f + 1) * tall]) for f in range(3)]
    (cond_below, cond_above), rhs_ends, absorb_ends = got
    for ref in (ey, start_ends, once_ends):
        clear_spares(ref, frame)

    lane = lane_no((1, LANES))
    keep_y = faces_y_kept(flags, frame)
    keep_low, keep_high = flags[Z_LOW].astype(F32), flags[Z_HIGH].astype(F32)
    near = ends_near(cond_below, cond_above, cond_edges[...])
    slab = lane // HALO
    keep_x = jnp.where(
        slab == HALO - 1, flags[X_LOW], jnp.where(slab == last - 1, flags[X_HIGH], 1)
    ).astype(F32)
    layer = lane % HALO
    for s, here in enumerate((cond_below, cond_above)):
        up, low = weight(here, near[2 * s]), weight(here, near[2 * s + 1])
        if s == 0:
            up = up * jnp.where(layer == HALO - 1, keep_low, 1.0)
        else:
            low = low * jnp.where(layer == 0, keep_high, 1.0)
        face_x = keep_x * weight(here, turned(here, -HALO, 1))
        face_y = keep_y * weight(here, turned(here, -1, 0))
        ex[s, span], ey[s, span], ez_up[s, span], ez_low[s, span] = face_x, face_y, up, low
        total = absorb_ends[s] + face_x + turned(face_x, HALO, 1) + face_y + turned(face_y, 1, 0) + up + low
        inverse = OMEGA_FINE / total
        inv_ends[s, span] = inverse
        start_ends[s, span] = inverse * rhs_ends[s]

    end_low, end_high = ez_up[0, span], ez_low[1, span]
    join_faces = joined(end_low, end_high)

    def first_sweep(xs, edges):
        stores = []
        for x in xs:
            total = partial[x, span] + at_edges(join_faces, x)
            inverse = OMEGA_FINE / total
            begin = inverse * wide_ref[1, x, span]
            stores.append((x, (total, inverse, begin)))
            edges = edge_step(begin, x, edges)
        for x, values in stores:
            for ref, value in zip((diag, inv_diag, start), values):
                ref[x, span] = value
        return edges

    edges = batched(0, wide, first_sweep, jnp.zeros((tall, LANES), F32), 8)

    join = joined(end_low * start_ends[0, span], end_high * start_ends[1, span])
    near = ends_near(start_ends[0, span], start_ends[1, span], edges)
    for s in range(2):
        total = ends_sum(frame, start_ends, s, near[2 * s], near[2 * s + 1], ex, ey, ez_up, ez_low)
        once_ends[s, span] = (2.0 - OMEGA_FINE) * start_ends[s, span] + inv_ends[s, span] * total

    def second(xs, carry):
        news = []
        for x, here, total in zip(xs, *main_sums(frame, start, xs, join, wx, wy, wz)):
            news.append((2.0 - OMEGA_FINE) * here + inv_diag[x, span] * total)
        for x, new in zip(xs, news):
            once[x, span] = new
        return carry

    batched(HALO - 1, last + 1, second, 0, 13 if (nx + 2) % 13 == 0 else 6)
    join2 = joined(end_low * once_ends[0, span], end_high * once_ends[1, span])

    def remainder(xs, carry):
        news = []
        for x, here, total in zip(xs, *main_sums(frame, once, xs, join2, wx, wy, wz)):
            news.append(wide_ref[1, x, span] - diag[x, span] * here + total)
        for x, new in zip(xs, news):
            res[x - HALO, span] = new
        for x in xs:
            pre[x - HALO] = once[x, pl.ds(frame.own, ny)]
        return carry

    batched(HALO, last, remainder, 0, 8)

    nb, half = nx // 2, ny // 2

    def rows_at(ref, x, off):
        return ref[x, pl.ds(frame.own + off, half, stride=2)]

    def to_blocks(bs, carry):
        for b in bs:
            four = sum(rows_at(res, 2 * b + a, c) for a in range(2) for c in range(2))
            block_res[b] = pack_rows(paired(four))
        return carry

    batched(0, nb, to_blocks, 0)
    zeros = jnp.zeros((AGG, LANES), F32)
    sums = lax.fori_loop(0, nb, lambda b, total: add_rows(total, block_label, b, block_res, b), zeros)

    lane = lane_no((half, LANES))
    around = zeros
    for s, (ref, side, layer_at) in enumerate(((ez_up, 0, HALO - 1), (ez_low, 1, 0))):
        values = rows_at(ref, side, 0) + rows_at(ref, side, 1)
        values = values + turned(values, -HALO, 1)
        spot = jnp.minimum(2 * HALO * lane + HALO * HALO + layer_at, LANES - 1)
        face_weight[s, :2] = pack_lanes(jnp.where(lane < nb, picked(values, spot), 0.0))
        around = add_rows(around, face_label, 4 + s, face_weight, s, 2)
    scale[...] = OMEGA_COARSE / (some_diag[...] + lane_total(around))
    scaled_rhs[...] = scale[...] * lane_total(sums)


def tile_sum(tile, rows, label_at, pairs_at, group=4):
    iota = row_no((AGG, LANES)).astype(F32)
    for first in range(0, rows, group):
        places, highs, lows = [], [], []
        for r in range(first, min(first + group, rows)):
            places.append(jnp.where(label_at(r) == iota, 1.0, 0.0).astype(BF16))
            held = sum(jnp.where(near == iota, w, 0.0) for near, w in pairs_at(r))
            highs.append(held.astype(BF16))
            lows.append((held - highs[-1].astype(F32)).astype(BF16))
        left = jnp.concatenate(places, axis=1)
        right = jnp.concatenate([jnp.concatenate(highs, axis=1), jnp.concatenate(lows, axis=1)], axis=0)
        tile = tile + lax.dot_general(left, right, (((1,), (1,)), ((), ())), preferred_element_type=F32)
    return tile


def both_halves(tile):
    return tile[:, :AGG] + tile[:, AGG:]


def keep_tile(out, t, tile):
    high = tile.astype(BF16)
    rows = pl.ds(t * AGG, AGG)
    out[rows, :AGG] = high
    out[rows, AGG:] = (tile - high.astype(F32)).astype(BF16)


def blocks_kernel(flags, cond, absorb, block_agg, _, block_label, near, weights, inner, face_label, fine_label,
                  part, line):
    nx, ny = cond.shape[0], cond.shape[1]
    nb, half, width = nx // 2, ny // 2, LANES // 2
    lane, row = lane_no((half, LANES)), row_no((half, LANES))

    def halves(values, slot):
        part[slot] = values
        return part[slot, pl.ds(0, half, stride=2)], part[slot, pl.ds(1, half, stride=2)]

    def label_at(b):
        values = block_agg[b].astype(F32)
        return jnp.concatenate([values, values], axis=1)

    def upper_x(b, slot):
        x = jnp.maximum(2 * b, 0)
        faces = weight(cond[x + 1], cond[jnp.minimum(x + 2, nx - 1)])
        return jnp.where((b == nb - 1) | (b < 0), 0.0, paired(sum(halves(faces, slot))))

    def step(bs, carry):
        low_x = upper_x(bs[0] - 1, 0)
        for k, b in enumerate(bs):
            x = 2 * b
            slot = 4 * k + 1
            one, two = cond[x], cond[x + 1]
            both_y = weight(one, turned(one, -1, 0)) + weight(two, turned(two, -1, 0))
            both_z = weight(one, turned(one, -1, 1)) + weight(two, turned(two, -1, 1))
            high_x = upper_x(b, slot)
            high_y = jnp.where(row == half - 1, 0.0, paired(halves(both_y, slot + 1)[1]))
            high_z = picked(sum(halves(both_z, slot + 2)), 2 * (lane % width) + 1)
            high_z = jnp.where(lane % width == width - 1, 0.0, high_z)
            low_y, low_z = turned(high_y, 1, 0), turned(high_z, 1, 1)
            own = label_at(b)
            near_x, past_x = label_at(jnp.minimum(b + 1, nb - 1)), label_at(jnp.maximum(b - 1, 0))
            near_y, past_y = turned(own, -1, 0), turned(own, 1, 0)
            near_z, past_z = turned(own, -1, 1), turned(own, 1, 1)
            total = paired(sum(halves(absorb[x] + absorb[x + 1], slot + 3)))
            for d, (beside, values) in enumerate((
                (near_x, high_x), (past_x, low_x), (near_y, high_y), (past_y, low_y), (near_z, high_z), (past_z, low_z)
            )):
                leaving = jnp.where(beside != own, values, 0.0)
                total = total + leaving
                near[d, b], weights[d, b] = pack_rows(beside).astype(jnp.int32), pack_rows(leaving)
            block_label[b] = pack_rows(own)
            inner[b] = pack_rows(total)
            spread = picked(own, lane // 2)
            for a in range(2):
                for c in range(2):
                    fine_label[x + a, pl.ds(c, half, stride=2)] = spread
            low_x = high_x
        return carry

    batched(0, nb, step, 0, 4)
    line[...] = jnp.zeros(line.shape, F32)
    low, high = jnp.zeros((half, LANES), F32), jnp.zeros((half, LANES), F32)
    for b in range(nb):
        own = label_at(b)
        line[0, b : b + 1], line[1, b : b + 1] = own[:1], own[half - 1 :]
        low = jnp.where(lane == b, own[:, :1], low)
        high = jnp.where(lane == b, own[:, width - 1 : width], high)
    face_label[0], face_label[1] = block_label[0], block_label[nb - 1]
    for s in range(2):
        face_label[2 + s, : nb // 2] = pack_rows(line[s, :nb])
        face_label[4 + s, :2] = pack_lanes((low, high)[s])


def own_turn_kernel(flags, block_label, near, weights, coarse, out, values):
    table = jnp.broadcast_to(coarse[:1], (SUB, LANES))
    nb = block_label.shape[0]

    def sums(bs, carry):
        news = [sum(weights[d, b] * picked(table, near[d, b]) for d in range(6)) for b in bs]
        for b, new in zip(bs, news):
            values[b] = new
        return carry

    batched(0, nb, sums, 0)
    total = jnp.zeros((AGG, LANES), F32)
    total = lax.fori_loop(0, nb, lambda b, total: add_rows(total, block_label, b, values, b), total)
    out[...] = lane_total(total)


def faces_kernel(count, nb, flags, face_label, weight_xy, weight_z, x_low, x_high, y_low, y_high, forth, back, out,
                 near, weights):
    at, half = x_low.shape[0] - 1, x_low.shape[1] // 2
    near[0], near[1] = pack_rows(x_low[at, :half]), pack_rows(x_high[at, :half])
    at = sum(WIDTHS) * 2 * nb
    for s, ref in enumerate((y_low, y_high)):
        near[2 + s, : nb // 2] = pack_rows(ref[at : at + nb])
    at = forth.shape[0] - half
    for s, values in enumerate(sides(flags, forth[at:], back[at:])):
        near[4 + s, :2] = pack_lanes(values)
    weights[:4], weights[4:] = weight_xy[...], weight_z[...]
    for t, (s, rows) in enumerate(face_rows(count, flags, nb)):
        tile = tile_sum(
            jnp.zeros((AGG, 2 * AGG), F32),
            rows,
            lambda r, s=s: near[s, pl.ds(r, 1)],
            lambda r, s=s: [(face_label[s, pl.ds(r, 1)], weights[s, pl.ds(r, 1)])],
        )
        keep_tile(out, t, both_halves(tile))


def turn_kernel(flags, tiles, scaled_rhs, scale, own, inside, *refs):
    forth, back, *others, out = refs
    got = [ref[ref.shape[0] - 1, :SUB] if len(ref.shape) == 3 else ref[ref.shape[0] - SUB :] for ref in (*others, forth, back)]
    vectors = [*got[:-2], *sides(flags, *got[-2:])]
    row = row_no((SUB, AGG))
    parts = []
    for v in vectors:
        high = v.astype(BF16).astype(F32)
        parts.append(jnp.where(row == 0, high, jnp.where(row == 1, v - high, 0.0)).astype(BF16))
    got = jnp.dot(jnp.concatenate(parts, axis=1), tiles[...], preferred_element_type=F32)
    applied = jnp.sum(got[:, :AGG] + got[:, AGG:], axis=0, keepdims=True)
    out[...] = (1.0 - OMEGA_COARSE) * own[...] + scaled_rhs[...] + scale[...] * (inside[...] + applied)


def ride_kernel(count, flags, pre, fine_label, coarse, *outs):
    nx = pre.shape[0]
    for s, out in enumerate(outs):
        at = jnp.where(flags[IX] == 0, nx - HALO, 0) if count == 2 else (nx - HALO, 0)[s]
        for f, field in enumerate((pre, fine_label)):
            for x in range(HALO):
                out[HALO * f + x] = field[at + x]
        out[2 * HALO] = jnp.zeros(out.shape[1:], F32)
        out[2 * HALO, :SUB] = coarse[...]


def three_kernel(flags, low, mid, high, out):
    row = row_no(out.shape)
    out[...] = jnp.where(row == 0, low[...], jnp.where(row == 1, mid[...], high[...]))


def nine_kernel(flags, low, mid, high, out):
    out[...] = jnp.zeros(out.shape, F32)
    for n, ref in enumerate((low, mid, high)):
        out[3 * n : 3 * n + 3] = ref[:3]


def lift_kernel(flags, wide_ref, forth, back, main, ends):
    frame = Frame(wide_ref.shape[1] - 2 * HALO, wide_ref.shape[2] - 2 * (SUB + HALO))
    tall = frame.tall
    for b in range(frame.wide // 2):
        main[b] = wide_ref[1, 2 * b, frame.span].astype(jnp.int32)
    rows = pl.ds(tall, tall)
    for s, values in enumerate(sides(flags, forth[rows], back[rows])):
        ends[s] = values.astype(jnp.int32)


def rows_of(frame, table, dx):
    row = row_no((frame.tall, LANES))
    low, mid, high = (table[3 * n + dx + 1 : 3 * n + dx + 2] for n in range(3))
    return jnp.where(row < HALO, low, jnp.where(row < HALO + frame.ny, mid, high))


def lift_main_kernel(flags, table, labels, wide_ref, lifted):
    frame = Frame(wide_ref.shape[1] - 2 * HALO, wide_ref.shape[2] - 2 * (SUB + HALO))
    last = HALO + frame.nx
    for first, stop, dx in ((0, HALO, -1), (HALO, last, 0), (last, frame.wide, 1)):
        values = rows_of(frame, table[...], dx)

        def lift(bs, carry, values=values):
            news = [picked(values, labels[b]) for b in bs]
            for b, new in zip(bs, news):
                for a in range(2):
                    lifted[2 * b + a, frame.span] = wide_ref[0, 2 * b + a, frame.span] + new
            return carry

        batched(first // 2, stop // 2, lift, 0, 6)


def post_kernel(flags, lifted, table_forth, table_back, end_labels, forth, back, *refs):
    (wx, wy, wz, inv_diag, start), ends = refs[:5], refs[5:11]
    out, one, two, one_ends, two_ends, kept_out, sems = refs[11:]
    nx, ny = out.shape[0], out.shape[1]
    frame = Frame(nx, ny)
    wide, tall, span = frame.wide, frame.tall, frame.span
    ex, ey, ez_up, ez_low, inv_ends, start_ends = ends
    for ref in (one_ends, two_ends):
        clear_spares(ref, frame)
    lane = lane_no((tall, LANES))
    tables = sides(flags, table_forth[...], table_back[...])
    for s, (table, base) in enumerate(zip(tables, sides(flags, forth[:tall], back[:tall]))):
        below, inside, above = (picked(rows_of(frame, table, dx), end_labels[s]) for dx in (-1, 0, 1))
        spot = lane // HALO
        two_ends[s, span] = base + jnp.where(spot < HALO, below, jnp.where(spot < HALO + nx, inside, above))
    kept = 1.0 - OMEGA_FINE

    def result(at, count):
        rows = pl.ds(at, count)
        return pltpu.make_async_copy(kept_out.at[rows], out.at[rows], sems.at[at // count])

    buffers = ((lifted, two_ends), (one, one_ends), (two, two_ends), (one, one_ends))
    for s in range(POST):
        src, src_ends = buffers[s]
        join = joined(ez_up[0, span] * src_ends[0, span], ez_low[1, span] * src_ends[1, span])
        final = s == POST - 1
        dst, dst_ends = (None, None) if final else buffers[s + 1]

        def step(xs, edges, src=src, join=join, dst=dst, final=final):
            news = []
            for x, here, total in zip(xs, *main_sums(frame, src, xs, join, wx, wy, wz)):
                news.append(kept * here + start[x, span] + inv_diag[x, span] * total)
                if not final:
                    edges = edge_step(here, x, edges)
            for x, new in zip(xs, news):
                if final:
                    kept_out[x - HALO] = new[HALO : HALO + ny]
                else:
                    dst[x, span] = new
            if final:
                result(xs[0] - HALO, len(xs)).start()
            return edges

        size = 8 if final else 10
        edges = batched(s + 1, wide - s - 1, step, jnp.zeros((tall, LANES), F32), size)
        if not final:
            near = ends_near(src_ends[0, span], src_ends[1, span], edges)
            news = []
            for e in range(2):
                total = ends_sum(frame, src_ends, e, near[2 * e], near[2 * e + 1], ex, ey, ez_up, ez_low)
                news.append(kept * src_ends[e, span] + start_ends[e, span] + inv_ends[e, span] * total)
            dst_ends[0, span], dst_ends[1, span] = news
    for n in range(nx // 8):
        result(8 * n, 8).wait()


def body(links, right_side, conductance, absorption, block_agg):
    nx, ny, nz = right_side.shape
    frame = Frame(nx, ny)
    nb = nx // 2
    n_x = links.sizes[0]
    arrays = (conductance, right_side, absorption, block_agg)
    n_send = 1 if n_x == 2 else 2
    pinned = [pltpu.with_memory_space_constraint(a, pltpu.HBM) for a in arrays]
    outs = [jax.ShapeDtypeStruct(a.shape, a.dtype) for a in arrays]
    outs += [shaped(sum(WIDTHS) + 1, ny, nz)] * n_send + [shaped(sum(WIDTHS) * nx + 16, nz)] * 2
    outs += [shaped(-(-sum(w * w for w in WIDTHS) // SUB) * SUB, nz)] * (2 * n_send)
    got = call(
        functools.partial(pack_kernel, n_x, WIDTHS),
        outs,
        [pltpu.SemaphoreType.DMA((3 * 4,))],
        in_specs=[pl.BlockSpec(memory_space=pltpu.HBM)] * 4,
    )(*pinned)
    arrays, sends = got[:4], got[4:]
    from_x = links.x(sends[:n_send])
    from_y = links.ring_y(*sends[n_send : n_send + 2])
    from_corners = links.corners(sends[n_send + 2 :])
    blocks = (nb, SUB, LANES)
    outs = [shaped(*blocks), jax.ShapeDtypeStruct((6, *blocks), jnp.int32), shaped(6, *blocks), shaped(*blocks)]
    outs += [shaped(6, SUB, LANES), shaped(nx, ny, nz)]
    scratch = [pltpu.VMEM((17, ny, LANES), F32), pltpu.VMEM((2, ny // 2, LANES), F32)]
    *rows, inner, face_label, fine_label = call(blocks_kernel, outs, scratch)(
        arrays[0], arrays[2], arrays[3], sends[0]
    )
    got = lax.optimization_barrier((*from_x, *from_y, *from_corners, inner))
    from_x, from_y, from_corners, inner = got[:n_send], got[n_send : n_send + 2], got[n_send + 2 : -1], got[-1]
    block_label = rows[0]
    size = len(WIDTHS) * frame.tall
    wide, *sends = call(
        functools.partial(first_frame_kernel, n_x, WIDTHS),
        [shaped(len(WIDTHS), *frame.main)] + [shaped(size + ny // 2, nz)] * 2,
        [pltpu.VMEM((size, nz), F32)] * 2,
    )(*arrays, from_x[0], from_x[-1], *from_y, *from_corners)
    outs = [shaped(*frame.main)] * 4 + [shaped(frame.tall, nz), shaped(4, SUB, LANES), shaped(SUB, AGG)]
    *fields, weight_xy, some_diag = call(functools.partial(fields_kernel, n_x), outs, limit=24)(
        wide, block_label, inner, face_label
    )
    halo = (wide, *links.z(*sends))
    outs = [shaped(*frame.main)] * 2 + [shaped(*frame.ends)] * 6 + [shaped(nx, ny, nz)]
    outs += [shaped(2, SUB, LANES)] + [shaped(SUB, AGG)] * 2
    scratch = [pltpu.VMEM(frame.main, F32), pltpu.VMEM(frame.ends, F32), pltpu.VMEM((nx, frame.rows, LANES), F32)]
    scratch += [pltpu.VMEM(frame.main, F32), pltpu.VMEM(blocks, F32)]
    got = call(fine_kernel, outs, scratch, limit=28)(
        *halo, *fields, block_label, face_label, some_diag
    )
    fields, pre = (*fields[:3], *got[:8]), got[8]
    weight_z, scaled_rhs, scale = got[9:]
    tiles = call(
        functools.partial(faces_kernel, n_x, nb),
        jax.ShapeDtypeStruct(((n_send + 4) * AGG, 2 * AGG), BF16),
        [pltpu.VMEM((6, SUB, LANES), F32)] * 2,
    )(face_label, weight_xy, weight_z, from_x[0], from_x[-1], *from_y, *halo[1:])
    coarse = scaled_rhs

    def turn(**more):
        near = links.near(coarse, **more)
        inside = call(own_turn_kernel, shaped(SUB, AGG), [pltpu.VMEM(blocks, F32)])(*rows, coarse)
        return call(turn_kernel, shaped(SUB, AGG))(tiles, scaled_rhs, scale, coarse, inside, *near), near

    both = (pre, fine_label)
    rides = call(functools.partial(ride_kernel, n_x), [shaped(2 * HALO + 1, ny, nz)] * n_send)(*both, coarse)
    coarse, near = turn(x=rides)
    from_x = near[2:-2]
    rides = send_y(both, coarse, from_x)
    frames = framed(both, from_x, rides[0])
    coarse, near = turn(y=rides)
    wide, *rides = send_z(frames, near[-2:], coarse)
    coarse, near = turn(z=rides)
    halo = (wide, *near[:2])
    outs = [jax.ShapeDtypeStruct((frame.wide // 2, frame.tall, nz), jnp.int32)]
    outs += [jax.ShapeDtypeStruct((2, frame.tall, nz), jnp.int32)]
    lifts = call(lift_kernel, outs)(*halo)
    for _ in range(KC - 4):
        coarse, _ = turn()
    from_x = links.x([coarse] * n_send)
    three = call(three_kernel, shaped(SUB, AGG))(from_x[0], coarse, from_x[-1])
    low, high = links.ring_y(three, three)
    nine = call(nine_kernel, shaped(2 * SUB, AGG))(low, three, high)
    tables = links.z(nine, nine)
    lifted = call(lift_main_kernel, shaped(*frame.main))(nine, lifts[0], halo[0])
    scratch = [pltpu.VMEM(frame.main, F32)] * 2 + [pltpu.VMEM(frame.ends, F32)] * 2
    scratch += [pltpu.VMEM((nx, ny, nz), F32), pltpu.SemaphoreType.DMA((nx // 8,))]
    return call(post_kernel, shaped(nx, ny, nz), scratch, limit=24, out_specs=pl.BlockSpec(memory_space=pl.ANY))(
        lifted, *tables, lifts[1], *halo[1:], *fields
    )


def solution(mesh):
    spec = P("gx", "gy", "gz")
    return jax.shard_map(
        functools.partial(body, Links(mesh)), mesh=mesh, in_specs=(spec,) * 4, out_specs=spec, check_vma=False
    )
```

```python
import functools

import jax
import jax.numpy as jnp
from jax import lax
from jax.experimental import pallas as pl
from jax.experimental.pallas import tpu as pltpu
from jax.sharding import PartitionSpec as P

AGG = 128
LANES = 128
SUB = 8
HALO = 4
WIDTHS = (4, 3, 3)
POST = 4
KC = 8
OMEGA_FINE = 0.8
OMEGA_COARSE = 0.7
F32 = jnp.float32
BF16 = jnp.bfloat16
VMEM = pl.BlockSpec(memory_space=pltpu.VMEM)
IX, PARITY, X_LOW, X_HIGH, Y_LOW, Y_HIGH, Z_LOW, Z_HIGH = range(8)


def places():
    (ix, n_x), (iy, n_y), (iz, n_z) = ((lax.axis_index(a), lax.axis_size(a)) for a in ("gx", "gy", "gz"))
    flags = [ix, iy % 2, ix > 0, ix < n_x - 1, iy > 0, iy < n_y - 1, iz > 0, iz < n_z - 1]
    return [jnp.asarray(flag, jnp.int32) for flag in flags]


def call(kernel, outs, scratch=(), limit=16, flops=10**6, in_specs=None, aliases=None, out_specs=None):
    def placed(*refs):
        kernel(places(), *refs)

    def run(*arrays):
        return pl.pallas_call(
            placed,
            out_shape=outs,
            in_specs=in_specs or [VMEM] * len(arrays),
            out_specs=out_specs or jax.tree.map(lambda _: VMEM, outs),
            scratch_shapes=list(scratch),
            input_output_aliases=aliases or {},
            compiler_params=pltpu.CompilerParams(vmem_limit_bytes=limit * 2**20),
            cost_estimate=pl.CostEstimate(flops=flops, bytes_accessed=10**5, transcendentals=0),
        )(*arrays)

    return run


def shaped(*shape):
    return jax.ShapeDtypeStruct(shape, F32)


def lane_no(shape):
    return lax.broadcasted_iota(jnp.int32, shape, len(shape) - 1)


def row_no(shape):
    return lax.broadcasted_iota(jnp.int32, shape, len(shape) - 2)


def turned(values, shift, axis):
    if isinstance(shift, int):
        shift = shift % values.shape[axis]
        if shift == 0:
            return values
    return pltpu.roll(values, shift, axis)


def batched(low, high, step, carry, size=6):
    def some(i, carry):
        return step([low + i * size + k for k in range(size)], carry)

    carry = lax.fori_loop(0, (high - low) // size, some, carry)
    rest = (high - low) % size
    return step(list(range(high - rest, high)), carry) if rest else carry


def picked(values, index):
    return jnp.take_along_axis(values, index, axis=1, mode="promise_in_bounds")


class Frame:
    def __init__(self, nx, ny):
        self.nx, self.ny = nx, ny
        self.wide, self.tall = nx + 2 * HALO, ny + 2 * HALO
        self.rows = self.tall + 2 * SUB
        self.span = pl.ds(SUB, self.tall)
        self.own = SUB + HALO
        self.main = (self.wide, self.rows, LANES)
        self.ends = (2, self.rows, LANES)


def bases(widths):
    return [sum(widths[:f]) for f in range(len(widths) + 1)]


def copied(pairs, sems):
    copies = [pltpu.make_async_copy(src, dst, sems.at[n]) for n, (src, dst) in enumerate(pairs)]
    for copy in copies:
        copy.start()
    return copies


def pack_kernel(count, widths, flags, *refs):
    fields = len(widths)
    n_x = 1 if count == 2 else 2
    ins, kept = refs[: fields + 1], refs[fields + 1 : 2 * fields + 2]
    outs, sems = refs[2 * fields + 2 : -1], refs[-1]
    x_outs, y_outs, corner_outs = outs[:n_x], outs[n_x : n_x + 2], outs[n_x + 2 :]
    nx, ny = ins[0].shape[0], ins[0].shape[1]
    nb, half, width = ins[-1].shape
    thirds = 3
    copies = []
    for ref, out in zip(ins, kept):
        for t in range(thirds):
            size = ref.shape[0] // thirds
            rows = pl.ds(t * size, size)
            copies.append(pltpu.make_async_copy(ref.at[rows], out.at[rows], sems.at[len(copies)]))
    for copy in copies:
        copy.start()
    for out in (*x_outs, *y_outs):
        out[...] = jnp.zeros(out.shape, F32)
    for copy in copies:
        copy.wait()
    base = bases(widths)
    labels = kept[-1]
    for s, out in enumerate(x_outs):

        def place(size, thick, s=s):
            if count == 2:
                return jnp.where(flags[IX] == 0, size - thick, 0)
            return (size - thick, 0)[s]

        for f, thick in enumerate(widths):
            at = place(nx, thick)
            for k in range(thick):
                slab = kept[f][at + k]
                out[base[f] + k] = slab
                row = (sum(w * w for w in widths[:f])) + k * thick
                corner_outs[2 * s][row : row + thick] = slab[ny - thick :]
                corner_outs[2 * s + 1][row : row + thick] = slab[:thick]
        out[base[-1], :half, :width] = labels[place(nb, 1)].astype(F32)
    for out, high in zip(y_outs, (True, False)):
        for f, thick in enumerate(widths):
            for x in range(nx):
                row = base[f] * nx + x * thick
                out[row : row + thick] = kept[f][x, ny - thick :] if high else kept[f][x, :thick]
        row = base[-1] * nx
        for b in range(nb):
            line = labels[b, half - 1 :] if high else labels[b, :1]
            out[row + b : row + b + 1, :width] = line.astype(F32)


def slab_of(own, low, high, base, width, x):
    nx = own.shape[0]
    if HALO <= x < HALO + nx:
        return own[x - HALO]
    if x < HALO:
        at = x - (HALO - width)
        return low[base + at] if at >= 0 else None
    at = x - HALO - nx
    return high[base + at] if at < width else None


def pack_y_kernel(fields, flags, *refs):
    ins, rider = refs[:fields], refs[fields]
    low, high, to_high, to_low = refs[fields + 1 :]
    nx, ny = ins[0].shape[0], ins[0].shape[1]
    wide = nx + 2 * HALO
    for f in range(fields):
        for x in range(wide):
            slab = slab_of(ins[f], low, high, HALO * f, HALO, x)
            at = (f * wide + x) * HALO
            to_high[at : at + HALO] = slab[ny - HALO :]
            to_low[at : at + HALO] = slab[:HALO]
    at = fields * wide * HALO
    to_high[at:], to_low[at:] = rider[...], rider[...]


def packed_lanes(wide_ref, f, frame, rows, to_high, to_low):
    group = lane_no((1, LANES)) // HALO
    nothing = jnp.ones((rows.size, LANES), F32)
    high, low = nothing, nothing
    for x in range(frame.wide):
        moved = turned(wide_ref[f, x, rows], HALO * (x + 1), 1)
        high = jnp.where(group == x, moved, high)
        low = jnp.where(group == (x + 1) % frame.wide, moved, low)
    at = pl.ds(f * frame.tall + rows.start - SUB, rows.size)
    to_high[at] = high
    to_low[at] = turned(low, -HALO, 1)


def first_frame_kernel(count, widths, flags, *refs):
    fields = len(widths)
    ins, labels, refs = refs[:fields], refs[fields], refs[fields + 1 :]
    x_low, x_high, y_low, y_high = refs[:4]
    corners = refs[4:6] * 2 if count == 2 else refs[4:8]
    wide_ref, send_forth, send_back, to_high, to_low = refs[-5:]
    nx, ny = ins[0].shape[0], ins[0].shape[1]
    frame = Frame(nx, ny)
    base = bases(widths)
    tall, own = frame.tall, frame.own
    even = flags[PARITY] == 0
    ones = jnp.ones((frame.rows, LANES), F32)
    for f, thick in enumerate(widths):
        for x in range(frame.wide):
            slab = slab_of(ins[f], x_low, x_high, base[f], thick, x)
            if slab is None:
                wide_ref[f, x] = ones
                continue
            edge = ones[: SUB + HALO]
            wide_ref[f, x, :own] = edge
            wide_ref[f, x, own + ny :] = edge
            wide_ref[f, x, own : own + ny] = slab
            if HALO <= x < HALO + nx:
                low, high, row = y_low, y_high, base[f] * nx + (x - HALO) * thick
            else:
                above = x >= HALO
                low, high = corners[2 * above : 2 * above + 2]
                at = x - HALO - nx if above else x - (HALO - thick)
                row = sum(w * w for w in widths[:f]) + at * thick
            wide_ref[f, x, own - thick : own] = low[row : row + thick]
            wide_ref[f, x, own + ny : own + ny + thick] = high[row : row + thick]
        packed_lanes(wide_ref, f, frame, pl.ds(SUB, tall), to_high, to_low)
    high, low = to_high[...], to_low[...]
    size = fields * tall
    send_forth[:size], send_back[:size] = jnp.where(even, high, low), jnp.where(even, low, high)
    nb, rows, width = labels.shape
    lane = lane_no((rows, LANES))
    high = low = jnp.zeros((rows, LANES), F32)
    for b in range(nb):
        slab = labels[b].astype(F32)
        high = jnp.where(lane == b, slab[:, width - 1 :], high)
        low = jnp.where(lane == b, slab[:, :1], low)
    send_forth[size:], send_back[size:] = jnp.where(even, high, low), jnp.where(even, low, high)


def frame_kernel(fields, flags, *refs):
    ins = refs[:fields]
    x_low, x_high, _ = refs[fields : fields + 3]
    wide_ref, to_high, to_low = refs[fields + 3 :]
    nx, ny = ins[0].shape[0], ins[0].shape[1]
    frame = Frame(nx, ny)
    spare = jnp.ones((SUB, LANES), F32)
    for f in range(fields):
        for x in range(frame.wide):
            wide_ref[f, x, frame.own : frame.own + ny] = slab_of(ins[f], x_low, x_high, HALO * f, HALO, x)
            wide_ref[f, x, :SUB] = spare
            wide_ref[f, x, SUB + frame.tall :] = spare
        packed_lanes(wide_ref, f, frame, pl.ds(2 * SUB, frame.tall - 2 * SUB), to_high, to_low)


def pack_z_kernel(fields, flags, wide_in, high_in, low_in, from_low, from_high, rider, *refs):
    wide_ref, send_forth, send_back, to_high, to_low = refs
    frame = Frame(wide_ref.shape[1] - 2 * HALO, wide_ref.shape[2] - 2 * (SUB + HALO))
    ny, tall, own = frame.ny, frame.tall, frame.own
    even = flags[PARITY] == 0
    for f in range(fields):
        for x in range(frame.wide):
            at = (f * frame.wide + x) * HALO
            wide_ref[f, x, SUB:own] = from_low[at : at + HALO]
            wide_ref[f, x, own + ny : own + ny + HALO] = from_high[at : at + HALO]
    size = fields * tall
    to_high[...], to_low[...] = high_in[...], low_in[...]
    for f in range(fields):
        for start in (SUB, tall):
            packed_lanes(wide_ref, f, frame, pl.ds(start, SUB), to_high, to_low)
    high, low = to_high[...], to_low[...]
    send_forth[:size], send_back[:size] = jnp.where(even, high, low), jnp.where(even, low, high)
    send_forth[size:], send_back[size:] = rider[...], rider[...]


class Links:
    def __init__(self, mesh):
        self.sizes = [mesh.shape[a] for a in ("gx", "gy", "gz")]
        n_x, n_y, n_z = self.sizes

        def at(i, j, k):
            return (i % n_x * n_y + j % n_y) * n_z + k

        every = [(i, j, k) for i in range(n_x) for j in range(n_y) for k in range(n_z)]
        self.ring_x = [(i, (i + 1) % n_x) for i in range(n_x)]
        self.corner = {d: [(at(i, j, k), at(i + d, j + 1, k)) for i, j, k in every] for d in (1, -1)}
        self.snake = []
        for i in range(n_x):
            for j in range(0, n_y, 2):
                nodes = [at(i, j, k) for k in range(n_z)] + [at(i, j + 1, k) for k in reversed(range(n_z))]
                self.snake += [(nodes[m], nodes[(m + 1) % len(nodes)]) for m in range(len(nodes))]

    @staticmethod
    def back(pairs):
        return [(b, a) for a, b in pairs]

    @staticmethod
    def send(values, pairs):
        return lax.ppermute(values, ("gx", "gy", "gz"), pairs)

    def x(self, sends):
        if self.sizes[0] == 2:
            return (lax.ppermute(sends[0], "gx", self.ring_x),)
        return lax.ppermute(sends[0], "gx", self.ring_x), lax.ppermute(sends[1], "gx", self.back(self.ring_x))

    def near(self, values, x=None, y=None, z=None):
        forth, back = self.z(*(z or (values, values)))
        from_x = self.x(x or (values, values))
        return (forth, back, *from_x, *self.ring_y(*(y or (values, values))))

    def ring_y(self, to_high, to_low):
        ring = [(j, (j + 1) % self.sizes[1]) for j in range(self.sizes[1])]
        return lax.ppermute(to_high, "gy", ring), lax.ppermute(to_low, "gy", self.back(ring))

    def corners(self, sends):
        if self.sizes[0] == 2:
            return self.send(sends[0], self.corner[1]), self.send(sends[1], self.back(self.corner[1]))
        return (
            self.send(sends[0], self.corner[1]),
            self.send(sends[1], self.back(self.corner[-1])),
            self.send(sends[2], self.corner[-1]),
            self.send(sends[3], self.back(self.corner[1])),
        )

    def z(self, forth, back):
        return self.send(forth, self.snake), self.send(back, self.back(self.snake))


def send_y(arrays, rider, from_x):
    nx, ny, nz = arrays[0].shape
    rows = len(arrays) * Frame(nx, ny).wide * HALO + SUB
    kernel = functools.partial(pack_y_kernel, len(arrays))
    return call(kernel, [shaped(rows, nz)] * 2)(*arrays, rider, from_x[0], from_x[-1])


def framed(arrays, from_x, sent):
    nx, ny, nz = arrays[0].shape
    frame, fields = Frame(nx, ny), len(arrays)
    outs = [shaped(fields, *frame.main)] + [shaped(fields * frame.tall, nz)] * 2
    return call(functools.partial(frame_kernel, fields), outs)(*arrays, from_x[0], from_x[-1], sent)


def send_z(frames, from_y, rider):
    wide, high, _ = frames
    return call(
        functools.partial(pack_z_kernel, wide.shape[0]),
        [shaped(*wide.shape)] + [shaped(high.shape[0] + SUB, LANES)] * 2,
        [pltpu.VMEM(high.shape, F32)] * 2,
        aliases={0: 0},
    )(*frames, *from_y, rider)


def sides(flags, forth, back):
    even = flags[PARITY] == 0
    return jnp.where(even, forth, back), jnp.where(even, back, forth)


def weight(one, two):
    return 2.0 * (one * two) / (one + two)


def lane_mask(x):
    return ((lane_no((1, LANES)) - (HALO * x + HALO - 1)) & (LANES - 1)) < 2


def edge_step(here, x, edges):
    return jnp.where(lane_mask(x), turned(here, HALO * x + HALO, 1), edges)


def joined(below, above):
    lane = lane_no((1, LANES))
    return jnp.where(lane % HALO == HALO - 1, turned(above, HALO - 1, 1), turned(below, 1, 1))


def at_edges(join, x):
    lane = lane_no((1, LANES))
    return jnp.where((lane == 0) | (lane == LANES - 1), turned(join, (LANES - HALO) - HALO * x, 1), 0.0)


def ends_near(below, above, edges):
    layer = lane_no((1, LANES)) % HALO
    return (
        jnp.where(layer == HALO - 1, turned(edges, -1, 1), turned(below, -1, 1)),
        turned(below, 1, 1),
        turned(above, -1, 1),
        jnp.where(layer == 0, turned(edges, 1 - HALO, 1), turned(above, 1, 1)),
    )


def main_sums(frame, field, xs, join, wx, wy, wz):
    span = frame.span
    slabs = [field[xs[0] - 1 + k, span] for k in range(len(xs) + 2)]
    faces = [wx[xs[0] - 1 + k, span] for k in range(len(xs) + 1)]
    totals = []
    for k, x in enumerate(xs):
        here, face_y, face_z = slabs[k + 1], wy[x, span], wz[x, span]
        total = faces[k + 1] * slabs[k + 2] + faces[k] * slabs[k]
        total = total + face_y * turned(here, -1, 0) + turned(face_y * here, 1, 0)
        total = total + face_z * turned(here, -1, 1) + turned(face_z * here, 1, 1)
        totals.append(total + at_edges(join, x))
    return slabs[1:-1], totals


def ends_sum(frame, ends, s, upper, lower, wx, wy, wz_up, wz_low):
    span, down = frame.span, pl.ds(SUB - 1, frame.tall)
    here = ends[s, span]
    total = wx[s, span] * turned(here, -HALO, 1) + turned(wx[s, span] * here, HALO, 1)
    total = total + wy[s, span] * ends[s, pl.ds(SUB + 1, frame.tall)] + wy[s, down] * ends[s, down]
    return total + wz_up[s, span] * upper + wz_low[s, span] * lower


def clear_spares(ref, frame):
    for x in range(ref.shape[0]):
        ref[x, :SUB] = jnp.zeros((SUB, LANES), F32)
        ref[x, SUB + frame.tall :] = jnp.zeros((SUB, LANES), F32)


def pack_rows(values):
    half = values.shape[0] // 2
    lane = lane_no((half, LANES))
    return jnp.where(lane < LANES // 2, values[:half], turned(values[half:], LANES // 2, 1))


def lane_total(values):
    return jnp.broadcast_to(jnp.sum(values.T, axis=0, keepdims=True), (SUB, LANES))


def paired(values):
    even = 2 * (lane_no(values.shape) % (LANES // 2))
    return picked(values + turned(values, -1, 1), even)


def faces_y_kept(flags, frame):
    row = row_no((frame.tall, LANES))
    at_low, at_high = row == HALO - 1, row == HALO + frame.ny - 1
    return jnp.where(at_low, flags[Y_LOW], jnp.where(at_high, flags[Y_HIGH], 1)).astype(F32)


def face_rows(count, flags, nb):
    x = [(jnp.where(flags[IX] == 0, 1, 0), SUB)] if count == 2 else [(0, SUB), (1, SUB)]
    return x + [(2, nb // 2), (3, nb // 2), (4, 2), (5, 2)]


def add_rows(total, labels, b, values, c, rows=SUB):
    iota = row_no((AGG, LANES)).astype(F32)
    for r in range(rows):
        row = pl.ds(r, 1)
        total = total + jnp.where(labels[b, row] == iota, values[c, row], 0.0)
    return total


def pack_lanes(values):
    lane = lane_no((2, LANES))
    packed = values[:2]
    for g in range(1, SUB):
        packed = jnp.where(lane // 16 == g, turned(values[2 * g : 2 * g + 2], 16 * g, 1), packed)
    return packed


def fields_kernel(count, flags, wide_ref, block_label, inner, face_label, wx, wy, wz, partial, cond_edges, face_weight, diag):
    frame = Frame(wx.shape[0] - 2 * HALO, wx.shape[1] - 2 * (SUB + HALO))
    wide, tall, span = frame.wide, frame.tall, frame.span
    last = HALO + frame.nx
    keep_y = faces_y_kept(flags, frame)
    inside = jnp.where(lane_no((1, LANES)) == LANES - 1, 0.0, 1.0)

    def fields(xs, carry):
        before, edges = carry
        stores = []
        for x in xs:
            here = wide_ref[0, x, span]
            keep = jnp.where(x == HALO - 1, flags[X_LOW], jnp.where(x == last - 1, flags[X_HIGH], 1)).astype(F32)
            face_x = keep * weight(here, wide_ref[0, jnp.minimum(x + 1, wide - 1), span])
            face_y = keep_y * weight(here, wide_ref[0, x, pl.ds(SUB + 1, tall)])
            face_z = inside * weight(here, turned(here, -1, 1))
            total = wide_ref[2, x, span] + face_x + before + face_y + turned(face_y, 1, 0)
            total = total + face_z + turned(face_z, 1, 1)
            stores.append((x, (face_x, face_y, face_z, total)))
            edges = edge_step(here, x, edges)
            before = face_x
        for x, values in stores:
            for ref, value in zip((wx, wy, wz, partial), values):
                ref[x, span] = value
        return before, edges

    nothing = jnp.zeros((tall, LANES), F32)
    cond_edges[...] = batched(0, wide, fields, (nothing, nothing + 1.0), 4)[1]
    nb, ny = frame.nx // 2, frame.ny
    for s, x in enumerate((HALO - 1, last - 1)):
        rows = [wx[x, pl.ds(frame.own + c, ny // 2, stride=2)] for c in range(2)]
        face_weight[s] = pack_rows(paired(rows[0] + rows[1]))
    for s, at in ((2, frame.own - 1), (3, frame.own + ny - 1)):
        lines = [wy[HALO + 2 * b, at : at + 1] + wy[HALO + 2 * b + 1, at : at + 1] for b in range(nb)]
        face_weight[s, : nb // 2] = pack_rows(paired(jnp.concatenate(lines, axis=0)))
    around = jnp.zeros((AGG, LANES), F32)
    around = lax.fori_loop(0, nb, lambda b, around: add_rows(around, block_label, b, inner, b), around)
    for s, rows in face_rows(count, flags, nb)[:-2]:
        around = add_rows(around, face_label, s, face_weight, s, rows)
    diag[...] = lane_total(around)


def fine_kernel(flags, wide_ref, forth, back, wx, wy, wz, partial, cond_edges, block_label, face_label, some_diag,
                *refs):
    inv_diag, start = refs[:2]
    ends = refs[2:8]
    pre, face_weight, scaled_rhs, scale, once, once_ends, res, diag, block_res = refs[8:]
    ex, ey, ez_up, ez_low, inv_ends, start_ends = ends
    nx, ny = pre.shape[0], pre.shape[1]
    frame = Frame(nx, ny)
    wide, tall, span = frame.wide, frame.tall, frame.span
    last = HALO + nx
    got = [sides(flags, forth[f * tall : (f + 1) * tall], back[f * tall : (f + 1) * tall]) for f in range(3)]
    (cond_below, cond_above), rhs_ends, absorb_ends = got
    for ref in (ey, start_ends, once_ends):
        clear_spares(ref, frame)

    lane = lane_no((1, LANES))
    keep_y = faces_y_kept(flags, frame)
    keep_low, keep_high = flags[Z_LOW].astype(F32), flags[Z_HIGH].astype(F32)
    near = ends_near(cond_below, cond_above, cond_edges[...])
    slab = lane // HALO
    keep_x = jnp.where(
        slab == HALO - 1, flags[X_LOW], jnp.where(slab == last - 1, flags[X_HIGH], 1)
    ).astype(F32)
    layer = lane % HALO
    for s, here in enumerate((cond_below, cond_above)):
        up, low = weight(here, near[2 * s]), weight(here, near[2 * s + 1])
        if s == 0:
            up = up * jnp.where(layer == HALO - 1, keep_low, 1.0)
        else:
            low = low * jnp.where(layer == 0, keep_high, 1.0)
        face_x = keep_x * weight(here, turned(here, -HALO, 1))
        face_y = keep_y * weight(here, turned(here, -1, 0))
        ex[s, span], ey[s, span], ez_up[s, span], ez_low[s, span] = face_x, face_y, up, low
        total = absorb_ends[s] + face_x + turned(face_x, HALO, 1) + face_y + turned(face_y, 1, 0) + up + low
        inverse = OMEGA_FINE / total
        inv_ends[s, span] = inverse
        start_ends[s, span] = inverse * rhs_ends[s]

    end_low, end_high = ez_up[0, span], ez_low[1, span]
    join_faces = joined(end_low, end_high)

    def first_sweep(xs, edges):
        stores = []
        for x in xs:
            total = partial[x, span] + at_edges(join_faces, x)
            inverse = OMEGA_FINE / total
            begin = inverse * wide_ref[1, x, span]
            stores.append((x, (total, inverse, begin)))
            edges = edge_step(begin, x, edges)
        for x, values in stores:
            for ref, value in zip((diag, inv_diag, start), values):
                ref[x, span] = value
        return edges

    edges = batched(0, wide, first_sweep, jnp.zeros((tall, LANES), F32), 8)

    join = joined(end_low * start_ends[0, span], end_high * start_ends[1, span])
    near = ends_near(start_ends[0, span], start_ends[1, span], edges)
    for s in range(2):
        total = ends_sum(frame, start_ends, s, near[2 * s], near[2 * s + 1], ex, ey, ez_up, ez_low)
        once_ends[s, span] = (2.0 - OMEGA_FINE) * start_ends[s, span] + inv_ends[s, span] * total

    def second(xs, carry):
        news = []
        for x, here, total in zip(xs, *main_sums(frame, start, xs, join, wx, wy, wz)):
            news.append((2.0 - OMEGA_FINE) * here + inv_diag[x, span] * total)
        for x, new in zip(xs, news):
            once[x, span] = new
        return carry

    batched(HALO - 1, last + 1, second, 0, 13 if (nx + 2) % 13 == 0 else 6)
    join2 = joined(end_low * once_ends[0, span], end_high * once_ends[1, span])

    def remainder(xs, carry):
        news = []
        for x, here, total in zip(xs, *main_sums(frame, once, xs, join2, wx, wy, wz)):
            news.append(wide_ref[1, x, span] - diag[x, span] * here + total)
        for x, new in zip(xs, news):
            res[x - HALO, span] = new
        for x in xs:
            pre[x - HALO] = once[x, pl.ds(frame.own, ny)]
        return carry

    batched(HALO, last, remainder, 0, 8)

    nb, half = nx // 2, ny // 2

    def rows_at(ref, x, off):
        return ref[x, pl.ds(frame.own + off, half, stride=2)]

    def to_blocks(bs, carry):
        for b in bs:
            four = sum(rows_at(res, 2 * b + a, c) for a in range(2) for c in range(2))
            block_res[b] = pack_rows(paired(four))
        return carry

    batched(0, nb, to_blocks, 0)
    zeros = jnp.zeros((AGG, LANES), F32)
    sums = lax.fori_loop(0, nb, lambda b, total: add_rows(total, block_label, b, block_res, b), zeros)

    lane = lane_no((half, LANES))
    around = zeros
    for s, (ref, side, layer_at) in enumerate(((ez_up, 0, HALO - 1), (ez_low, 1, 0))):
        values = rows_at(ref, side, 0) + rows_at(ref, side, 1)
        values = values + turned(values, -HALO, 1)
        spot = jnp.minimum(2 * HALO * lane + HALO * HALO + layer_at, LANES - 1)
        face_weight[s, :2] = pack_lanes(jnp.where(lane < nb, picked(values, spot), 0.0))
        around = add_rows(around, face_label, 4 + s, face_weight, s, 2)
    scale[...] = OMEGA_COARSE / (some_diag[...] + lane_total(around))
    scaled_rhs[...] = scale[...] * lane_total(sums)


def tile_sum(tile, rows, label_at, pairs_at, group=4):
    iota = row_no((AGG, LANES)).astype(F32)
    for first in range(0, rows, group):
        places, highs, lows = [], [], []
        for r in range(first, min(first + group, rows)):
            places.append(jnp.where(label_at(r) == iota, 1.0, 0.0).astype(BF16))
            held = sum(jnp.where(near == iota, w, 0.0) for near, w in pairs_at(r))
            highs.append(held.astype(BF16))
            lows.append((held - highs[-1].astype(F32)).astype(BF16))
        left = jnp.concatenate(places, axis=1)
        right = jnp.concatenate([jnp.concatenate(highs, axis=1), jnp.concatenate(lows, axis=1)], axis=0)
        tile = tile + lax.dot_general(left, right, (((1,), (1,)), ((), ())), preferred_element_type=F32)
    return tile


def both_halves(tile):
    return tile[:, :AGG] + tile[:, AGG:]


def keep_tile(out, t, tile):
    high = tile.astype(BF16)
    rows = pl.ds(t * AGG, AGG)
    out[rows, :AGG] = high
    out[rows, AGG:] = (tile - high.astype(F32)).astype(BF16)


def blocks_kernel(flags, cond, absorb, block_agg, _, block_label, near, weights, inner, part):
    nx, ny = cond.shape[0], cond.shape[1]
    nb, half, width = nx // 2, ny // 2, LANES // 2
    lane, row = lane_no((half, LANES)), row_no((half, LANES))

    def halves(values, slot):
        part[slot] = values
        return part[slot, pl.ds(0, half, stride=2)], part[slot, pl.ds(1, half, stride=2)]

    def label_at(b):
        values = block_agg[b].astype(F32)
        return jnp.concatenate([values, values], axis=1)

    def upper_x(b, slot):
        x = jnp.maximum(2 * b, 0)
        faces = weight(cond[x + 1], cond[jnp.minimum(x + 2, nx - 1)])
        return jnp.where((b == nb - 1) | (b < 0), 0.0, paired(sum(halves(faces, slot))))

    def step(bs, carry):
        low_x = upper_x(bs[0] - 1, 0)
        for k, b in enumerate(bs):
            x = 2 * b
            slot = 4 * k + 1
            one, two = cond[x], cond[x + 1]
            both_y = weight(one, turned(one, -1, 0)) + weight(two, turned(two, -1, 0))
            both_z = weight(one, turned(one, -1, 1)) + weight(two, turned(two, -1, 1))
            high_x = upper_x(b, slot)
            high_y = jnp.where(row == half - 1, 0.0, paired(halves(both_y, slot + 1)[1]))
            high_z = picked(sum(halves(both_z, slot + 2)), 2 * (lane % width) + 1)
            high_z = jnp.where(lane % width == width - 1, 0.0, high_z)
            low_y, low_z = turned(high_y, 1, 0), turned(high_z, 1, 1)
            own = label_at(b)
            near_x, past_x = label_at(jnp.minimum(b + 1, nb - 1)), label_at(jnp.maximum(b - 1, 0))
            near_y, past_y = turned(own, -1, 0), turned(own, 1, 0)
            near_z, past_z = turned(own, -1, 1), turned(own, 1, 1)
            total = paired(sum(halves(absorb[x] + absorb[x + 1], slot + 3)))
            for d, (beside, values) in enumerate((
                (near_x, high_x), (past_x, low_x), (near_y, high_y), (past_y, low_y), (near_z, high_z), (past_z, low_z)
            )):
                leaving = jnp.where(beside != own, values, 0.0)
                total = total + leaving
                near[d, b], weights[d, b] = pack_rows(beside).astype(jnp.int32), pack_rows(leaving)
            block_label[b] = pack_rows(own)
            inner[b] = pack_rows(total)
            low_x = high_x
        return carry

    batched(0, nb, step, 0, 4)


def labels_kernel(flags, block_agg, block_label, _, face_label, fine_label, line):
    nb, half, width = block_agg.shape
    lane = lane_no((half, LANES))
    line[...] = jnp.zeros(line.shape, F32)
    low, high = jnp.zeros((half, LANES), F32), jnp.zeros((half, LANES), F32)
    for b in range(nb):
        own = block_agg[b].astype(F32)
        own = jnp.concatenate([own, own], axis=1)
        line[0, b : b + 1], line[1, b : b + 1] = own[:1], own[half - 1 :]
        low = jnp.where(lane == b, own[:, :1], low)
        high = jnp.where(lane == b, own[:, width - 1 : width], high)
        spread = picked(own, lane // 2)
        for a in range(2):
            for c in range(2):
                fine_label[2 * b + a, pl.ds(c, half, stride=2)] = spread
    face_label[0], face_label[1] = block_label[0], block_label[nb - 1]
    for s in range(2):
        face_label[2 + s, : nb // 2] = pack_rows(line[s, :nb])
        face_label[4 + s, :2] = pack_lanes((low, high)[s])


def own_turn_kernel(flags, block_label, near, weights, coarse, out, values):
    table = jnp.broadcast_to(coarse[:1], (SUB, LANES))
    nb = block_label.shape[0]

    def sums(bs, carry):
        news = [sum(weights[d, b] * picked(table, near[d, b]) for d in range(6)) for b in bs]
        for b, new in zip(bs, news):
            values[b] = new
        return carry

    batched(0, nb, sums, 0)
    total = jnp.zeros((AGG, LANES), F32)
    total = lax.fori_loop(0, nb, lambda b, total: add_rows(total, block_label, b, values, b), total)
    out[...] = lane_total(total)


def faces_kernel(count, nb, flags, face_label, weight_xy, weight_z, x_low, x_high, y_low, y_high, forth, back, out,
                 near, weights):
    at, half = x_low.shape[0] - 1, x_low.shape[1] // 2
    near[0], near[1] = pack_rows(x_low[at, :half]), pack_rows(x_high[at, :half])
    at = sum(WIDTHS) * 2 * nb
    for s, ref in enumerate((y_low, y_high)):
        near[2 + s, : nb // 2] = pack_rows(ref[at : at + nb])
    at = forth.shape[0] - half
    for s, values in enumerate(sides(flags, forth[at:], back[at:])):
        near[4 + s, :2] = pack_lanes(values)
    weights[:4], weights[4:] = weight_xy[...], weight_z[...]
    for t, (s, rows) in enumerate(face_rows(count, flags, nb)):
        tile = tile_sum(
            jnp.zeros((AGG, 2 * AGG), F32),
            rows,
            lambda r, s=s: near[s, pl.ds(r, 1)],
            lambda r, s=s: [(face_label[s, pl.ds(r, 1)], weights[s, pl.ds(r, 1)])],
        )
        keep_tile(out, t, both_halves(tile))


def turn_kernel(flags, tiles, scaled_rhs, scale, own, inside, *refs):
    forth, back, *others, out = refs
    got = [ref[ref.shape[0] - 1, :SUB] if len(ref.shape) == 3 else ref[ref.shape[0] - SUB :] for ref in (*others, forth, back)]
    vectors = [*got[:-2], *sides(flags, *got[-2:])]
    row = row_no((SUB, AGG))
    parts = []
    for v in vectors:
        high = v.astype(BF16).astype(F32)
        parts.append(jnp.where(row == 0, high, jnp.where(row == 1, v - high, 0.0)).astype(BF16))
    got = jnp.dot(jnp.concatenate(parts, axis=1), tiles[...], preferred_element_type=F32)
    applied = jnp.sum(got[:, :AGG] + got[:, AGG:], axis=0, keepdims=True)
    out[...] = (1.0 - OMEGA_COARSE) * own[...] + scaled_rhs[...] + scale[...] * (inside[...] + applied)


def ride_kernel(count, flags, pre, fine_label, coarse, *outs):
    nx = pre.shape[0]
    for s, out in enumerate(outs):
        at = jnp.where(flags[IX] == 0, nx - HALO, 0) if count == 2 else (nx - HALO, 0)[s]
        for f, field in enumerate((pre, fine_label)):
            for x in range(HALO):
                out[HALO * f + x] = field[at + x]
        out[2 * HALO] = jnp.zeros(out.shape[1:], F32)
        out[2 * HALO, :SUB] = coarse[...]


def three_kernel(flags, low, mid, high, out):
    row = row_no(out.shape)
    out[...] = jnp.where(row == 0, low[...], jnp.where(row == 1, mid[...], high[...]))


def nine_kernel(flags, low, mid, high, out):
    out[...] = jnp.zeros(out.shape, F32)
    for n, ref in enumerate((low, mid, high)):
        out[3 * n : 3 * n + 3] = ref[:3]


def lift_kernel(flags, wide_ref, forth, back, main, ends):
    frame = Frame(wide_ref.shape[1] - 2 * HALO, wide_ref.shape[2] - 2 * (SUB + HALO))
    tall = frame.tall
    for b in range(frame.wide // 2):
        main[b] = wide_ref[1, 2 * b, frame.span].astype(jnp.int32)
    rows = pl.ds(tall, tall)
    for s, values in enumerate(sides(flags, forth[rows], back[rows])):
        ends[s] = values.astype(jnp.int32)


def rows_of(frame, table, dx):
    row = row_no((frame.tall, LANES))
    low, mid, high = (table[3 * n + dx + 1 : 3 * n + dx + 2] for n in range(3))
    return jnp.where(row < HALO, low, jnp.where(row < HALO + frame.ny, mid, high))


def lift_main_kernel(flags, table, labels, wide_ref, lifted):
    frame = Frame(wide_ref.shape[1] - 2 * HALO, wide_ref.shape[2] - 2 * (SUB + HALO))
    last = HALO + frame.nx
    for first, stop, dx in ((0, HALO, -1), (HALO, last, 0), (last, frame.wide, 1)):
        values = rows_of(frame, table[...], dx)

        def lift(bs, carry, values=values):
            news = [picked(values, labels[b]) for b in bs]
            for b, new in zip(bs, news):
                for a in range(2):
                    lifted[2 * b + a, frame.span] = wide_ref[0, 2 * b + a, frame.span] + new
            return carry

        batched(first // 2, stop // 2, lift, 0, 6)


def post_kernel(flags, lifted, table_forth, table_back, end_labels, forth, back, *refs):
    (wx, wy, wz, inv_diag, start), ends = refs[:5], refs[5:11]
    out, one, two, one_ends, two_ends, kept_out, sems = refs[11:]
    nx, ny = out.shape[0], out.shape[1]
    frame = Frame(nx, ny)
    wide, tall, span = frame.wide, frame.tall, frame.span
    ex, ey, ez_up, ez_low, inv_ends, start_ends = ends
    for ref in (one_ends, two_ends):
        clear_spares(ref, frame)
    lane = lane_no((tall, LANES))
    tables = sides(flags, table_forth[...], table_back[...])
    for s, (table, base) in enumerate(zip(tables, sides(flags, forth[:tall], back[:tall]))):
        below, inside, above = (picked(rows_of(frame, table, dx), end_labels[s]) for dx in (-1, 0, 1))
        spot = lane // HALO
        two_ends[s, span] = base + jnp.where(spot < HALO, below, jnp.where(spot < HALO + nx, inside, above))
    kept = 1.0 - OMEGA_FINE

    def result(at, count):
        rows = pl.ds(at, count)
        return pltpu.make_async_copy(kept_out.at[rows], out.at[rows], sems.at[at // count])

    buffers = ((lifted, two_ends), (one, one_ends), (two, two_ends), (one, one_ends))
    for s in range(POST):
        src, src_ends = buffers[s]
        join = joined(ez_up[0, span] * src_ends[0, span], ez_low[1, span] * src_ends[1, span])
        final = s == POST - 1
        dst, dst_ends = (None, None) if final else buffers[s + 1]

        def step(xs, edges, src=src, join=join, dst=dst, final=final):
            news = []
            for x, here, total in zip(xs, *main_sums(frame, src, xs, join, wx, wy, wz)):
                news.append(kept * here + start[x, span] + inv_diag[x, span] * total)
                if not final:
                    edges = edge_step(here, x, edges)
            for x, new in zip(xs, news):
                if final:
                    kept_out[x - HALO] = new[HALO : HALO + ny]
                else:
                    dst[x, span] = new
            if final:
                result(xs[0] - HALO, len(xs)).start()
            return edges

        size = 8 if final else 10
        edges = batched(s + 1, wide - s - 1, step, jnp.zeros((tall, LANES), F32), size)
        if not final:
            near = ends_near(src_ends[0, span], src_ends[1, span], edges)
            news = []
            for e in range(2):
                total = ends_sum(frame, src_ends, e, near[2 * e], near[2 * e + 1], ex, ey, ez_up, ez_low)
                news.append(kept * src_ends[e, span] + start_ends[e, span] + inv_ends[e, span] * total)
            dst_ends[0, span], dst_ends[1, span] = news
    for n in range(nx // 8):
        result(8 * n, 8).wait()


def body(links, right_side, conductance, absorption, block_agg):
    nx, ny, nz = right_side.shape
    frame = Frame(nx, ny)
    nb = nx // 2
    n_x = links.sizes[0]
    arrays = (conductance, right_side, absorption, block_agg)
    n_send = 1 if n_x == 2 else 2
    pinned = [pltpu.with_memory_space_constraint(a, pltpu.HBM) for a in arrays]
    outs = [jax.ShapeDtypeStruct(a.shape, a.dtype) for a in arrays]
    outs += [shaped(sum(WIDTHS) + 1, ny, nz)] * n_send + [shaped(sum(WIDTHS) * nx + 16, nz)] * 2
    outs += [shaped(-(-sum(w * w for w in WIDTHS) // SUB) * SUB, nz)] * (2 * n_send)
    got = call(
        functools.partial(pack_kernel, n_x, WIDTHS),
        outs,
        [pltpu.SemaphoreType.DMA((3 * 4,))],
        in_specs=[pl.BlockSpec(memory_space=pltpu.HBM)] * 4,
    )(*pinned)
    arrays, sends = got[:4], got[4:]
    from_x = links.x(sends[:n_send])
    from_y = links.ring_y(*sends[n_send : n_send + 2])
    from_corners = links.corners(sends[n_send + 2 :])
    blocks = (nb, SUB, LANES)
    outs = [shaped(*blocks), jax.ShapeDtypeStruct((6, *blocks), jnp.int32), shaped(6, *blocks), shaped(*blocks)]
    *rows, inner = call(blocks_kernel, outs, [pltpu.VMEM((17, ny, LANES), F32)])(
        arrays[0], arrays[2], arrays[3], sends[0]
    )
    got = lax.optimization_barrier((*from_x, *from_y, *from_corners, inner))
    from_x, from_y, from_corners, inner = got[:n_send], got[n_send : n_send + 2], got[n_send + 2 : -1], got[-1]
    block_label = rows[0]
    size = len(WIDTHS) * frame.tall
    wide, *sends = call(
        functools.partial(first_frame_kernel, n_x, WIDTHS),
        [shaped(len(WIDTHS), *frame.main)] + [shaped(size + ny // 2, nz)] * 2,
        [pltpu.VMEM((size, nz), F32)] * 2,
    )(*arrays, from_x[0], from_x[-1], *from_y, *from_corners)
    outs = [shaped(6, SUB, LANES), shaped(nx, ny, nz)]
    face_label, fine_label = call(labels_kernel, outs, [pltpu.VMEM((2, ny // 2, LANES), F32)])(
        arrays[3], block_label, sends[0]
    )
    outs = [shaped(*frame.main)] * 4 + [shaped(frame.tall, nz), shaped(4, SUB, LANES), shaped(SUB, AGG)]
    *fields, weight_xy, some_diag = call(functools.partial(fields_kernel, n_x), outs, limit=24)(
        wide, block_label, inner, face_label
    )
    halo = (wide, *links.z(*sends))
    outs = [shaped(*frame.main)] * 2 + [shaped(*frame.ends)] * 6 + [shaped(nx, ny, nz)]
    outs += [shaped(2, SUB, LANES)] + [shaped(SUB, AGG)] * 2
    scratch = [pltpu.VMEM(frame.main, F32), pltpu.VMEM(frame.ends, F32), pltpu.VMEM((nx, frame.rows, LANES), F32)]
    scratch += [pltpu.VMEM(frame.main, F32), pltpu.VMEM(blocks, F32)]
    got = call(fine_kernel, outs, scratch, limit=28)(
        *halo, *fields, block_label, face_label, some_diag
    )
    fields, pre = (*fields[:3], *got[:8]), got[8]
    weight_z, scaled_rhs, scale = got[9:]
    tiles = call(
        functools.partial(faces_kernel, n_x, nb),
        jax.ShapeDtypeStruct(((n_send + 4) * AGG, 2 * AGG), BF16),
        [pltpu.VMEM((6, SUB, LANES), F32)] * 2,
    )(face_label, weight_xy, weight_z, from_x[0], from_x[-1], *from_y, *halo[1:])
    coarse = scaled_rhs

    def turn(**more):
        near = links.near(coarse, **more)
        inside = call(own_turn_kernel, shaped(SUB, AGG), [pltpu.VMEM(blocks, F32)])(*rows, coarse)
        return call(turn_kernel, shaped(SUB, AGG))(tiles, scaled_rhs, scale, coarse, inside, *near), near

    both = (pre, fine_label)
    rides = call(functools.partial(ride_kernel, n_x), [shaped(2 * HALO + 1, ny, nz)] * n_send)(*both, coarse)
    coarse, near = turn(x=rides)
    from_x = near[2:-2]
    rides = send_y(both, coarse, from_x)
    frames = framed(both, from_x, rides[0])
    coarse, near = turn(y=rides)
    wide, *rides = send_z(frames, near[-2:], coarse)
    coarse, near = turn(z=rides)
    halo = (wide, *near[:2])
    outs = [jax.ShapeDtypeStruct((frame.wide // 2, frame.tall, nz), jnp.int32)]
    outs += [jax.ShapeDtypeStruct((2, frame.tall, nz), jnp.int32)]
    lifts = call(lift_kernel, outs)(*halo)
    for _ in range(KC - 4):
        coarse, _ = turn()
    from_x = links.x([coarse] * n_send)
    three = call(three_kernel, shaped(SUB, AGG))(from_x[0], coarse, from_x[-1])
    low, high = links.ring_y(three, three)
    nine = call(nine_kernel, shaped(2 * SUB, AGG))(low, three, high)
    tables = links.z(nine, nine)
    lifted = call(lift_main_kernel, shaped(*frame.main))(nine, lifts[0], halo[0])
    scratch = [pltpu.VMEM(frame.main, F32)] * 2 + [pltpu.VMEM(frame.ends, F32)] * 2
    scratch += [pltpu.VMEM((nx, ny, nz), F32), pltpu.SemaphoreType.DMA((nx // 8,))]
    return call(post_kernel, shaped(nx, ny, nz), scratch, limit=24, out_specs=pl.BlockSpec(memory_space=pl.ANY))(
        lifted, *tables, lifts[1], *halo[1:], *fields
    )


def solution(mesh):
    spec = P("gx", "gy", "gz")
    return jax.shard_map(
        functools.partial(body, Links(mesh)), mesh=mesh, in_specs=(spec,) * 4, out_specs=spec, check_vma=False
    )
```

```python
import functools

import jax
import jax.numpy as jnp
from jax import lax
from jax.experimental import pallas as pl
from jax.experimental.pallas import tpu as pltpu
from jax.sharding import PartitionSpec as P

AGG = 128
LANES = 128
SUB = 8
HALO = 4
WIDTHS = (4, 3, 3)
POST = 4
KC = 8
OMEGA_FINE = 0.8
OMEGA_COARSE = 0.7
F32 = jnp.float32
BF16 = jnp.bfloat16
VMEM = pl.BlockSpec(memory_space=pltpu.VMEM)
IX, PARITY, X_LOW, X_HIGH, Y_LOW, Y_HIGH, Z_LOW, Z_HIGH = range(8)


def places():
    (ix, n_x), (iy, n_y), (iz, n_z) = ((lax.axis_index(a), lax.axis_size(a)) for a in ("gx", "gy", "gz"))
    flags = [ix, iy % 2, ix > 0, ix < n_x - 1, iy > 0, iy < n_y - 1, iz > 0, iz < n_z - 1]
    return [jnp.asarray(flag, jnp.int32) for flag in flags]


def call(kernel, outs, scratch=(), limit=16, flops=10**6, in_specs=None, aliases=None, out_specs=None):
    def placed(*refs):
        kernel(places(), *refs)

    def run(*arrays):
        return pl.pallas_call(
            placed,
            out_shape=outs,
            in_specs=in_specs or [VMEM] * len(arrays),
            out_specs=out_specs or jax.tree.map(lambda _: VMEM, outs),
            scratch_shapes=list(scratch),
            input_output_aliases=aliases or {},
            compiler_params=pltpu.CompilerParams(vmem_limit_bytes=limit * 2**20),
            cost_estimate=pl.CostEstimate(flops=flops, bytes_accessed=10**5, transcendentals=0),
        )(*arrays)

    return run


def shaped(*shape):
    return jax.ShapeDtypeStruct(shape, F32)


def lane_no(shape):
    return lax.broadcasted_iota(jnp.int32, shape, len(shape) - 1)


def row_no(shape):
    return lax.broadcasted_iota(jnp.int32, shape, len(shape) - 2)


def turned(values, shift, axis):
    if isinstance(shift, int):
        shift = shift % values.shape[axis]
        if shift == 0:
            return values
    return pltpu.roll(values, shift, axis)


def batched(low, high, step, carry, size=6):
    def some(i, carry):
        return step([low + i * size + k for k in range(size)], carry)

    carry = lax.fori_loop(0, (high - low) // size, some, carry)
    rest = (high - low) % size
    return step(list(range(high - rest, high)), carry) if rest else carry


def picked(values, index):
    return jnp.take_along_axis(values, index, axis=1, mode="promise_in_bounds")


class Frame:
    def __init__(self, nx, ny):
        self.nx, self.ny = nx, ny
        self.wide, self.tall = nx + 2 * HALO, ny + 2 * HALO
        self.rows = self.tall + 2 * SUB
        self.span = pl.ds(SUB, self.tall)
        self.own = SUB + HALO
        self.main = (self.wide, self.rows, LANES)
        self.ends = (2, self.rows, LANES)


def bases(widths):
    return [sum(widths[:f]) for f in range(len(widths) + 1)]


def copied(pairs, sems):
    copies = [pltpu.make_async_copy(src, dst, sems.at[n]) for n, (src, dst) in enumerate(pairs)]
    for copy in copies:
        copy.start()
    return copies


def pack_kernel(count, widths, flags, *refs):
    fields = len(widths)
    n_x = 1 if count == 2 else 2
    ins, kept = refs[: fields + 1], refs[fields + 1 : 2 * fields + 2]
    outs, sems = refs[2 * fields + 2 : -1], refs[-1]
    x_outs, y_outs, corner_outs = outs[:n_x], outs[n_x : n_x + 2], outs[n_x + 2 :]
    nx, ny = ins[0].shape[0], ins[0].shape[1]
    nb, half, width = ins[-1].shape
    thirds = 3
    copies = []
    for ref, out in zip(ins, kept):
        for t in range(thirds):
            size = ref.shape[0] // thirds
            rows = pl.ds(t * size, size)
            copies.append(pltpu.make_async_copy(ref.at[rows], out.at[rows], sems.at[len(copies)]))
    for copy in copies:
        copy.start()
    for out in (*x_outs, *y_outs):
        out[...] = jnp.zeros(out.shape, F32)
    for copy in copies:
        copy.wait()
    base = bases(widths)
    labels = kept[-1]
    for s, out in enumerate(x_outs):

        def place(size, thick, s=s):
            if count == 2:
                return jnp.where(flags[IX] == 0, size - thick, 0)
            return (size - thick, 0)[s]

        for f, thick in enumerate(widths):
            at = place(nx, thick)
            for k in range(thick):
                slab = kept[f][at + k]
                out[base[f] + k] = slab
                row = (sum(w * w for w in widths[:f])) + k * thick
                corner_outs[2 * s][row : row + thick] = slab[ny - thick :]
                corner_outs[2 * s + 1][row : row + thick] = slab[:thick]
        out[base[-1], :half, :width] = labels[place(nb, 1)].astype(F32)
    for out, high in zip(y_outs, (True, False)):
        for f, thick in enumerate(widths):
            for x in range(nx):
                row = base[f] * nx + x * thick
                out[row : row + thick] = kept[f][x, ny - thick :] if high else kept[f][x, :thick]
        row = base[-1] * nx
        for b in range(nb):
            line = labels[b, half - 1 :] if high else labels[b, :1]
            out[row + b : row + b + 1, :width] = line.astype(F32)


def slab_of(own, low, high, base, width, x):
    nx = own.shape[0]
    if HALO <= x < HALO + nx:
        return own[x - HALO]
    if x < HALO:
        at = x - (HALO - width)
        return low[base + at] if at >= 0 else None
    at = x - HALO - nx
    return high[base + at] if at < width else None


def pack_y_kernel(fields, flags, *refs):
    ins, rider = refs[:fields], refs[fields]
    low, high, to_high, to_low = refs[fields + 1 :]
    nx, ny = ins[0].shape[0], ins[0].shape[1]
    wide = nx + 2 * HALO
    for f in range(fields):
        for x in range(wide):
            slab = slab_of(ins[f], low, high, HALO * f, HALO, x)
            at = (f * wide + x) * HALO
            to_high[at : at + HALO] = slab[ny - HALO :]
            to_low[at : at + HALO] = slab[:HALO]
    at = fields * wide * HALO
    to_high[at:], to_low[at:] = rider[...], rider[...]


def packed_lanes(wide_ref, f, frame, rows, to_high, to_low):
    group = lane_no((1, LANES)) // HALO
    nothing = jnp.ones((rows.size, LANES), F32)
    high, low = nothing, nothing
    for x in range(frame.wide):
        moved = turned(wide_ref[f, x, rows], HALO * (x + 1), 1)
        high = jnp.where(group == x, moved, high)
        low = jnp.where(group == (x + 1) % frame.wide, moved, low)
    at = pl.ds(f * frame.tall + rows.start - SUB, rows.size)
    to_high[at] = high
    to_low[at] = turned(low, -HALO, 1)


def first_frame_kernel(count, widths, flags, *refs):
    fields = len(widths)
    ins, labels, refs = refs[:fields], refs[fields], refs[fields + 1 :]
    x_low, x_high, y_low, y_high = refs[:4]
    corners = refs[4:6] * 2 if count == 2 else refs[4:8]
    wide_ref, send_forth, send_back, to_high, to_low = refs[-5:]
    nx, ny = ins[0].shape[0], ins[0].shape[1]
    frame = Frame(nx, ny)
    base = bases(widths)
    tall, own = frame.tall, frame.own
    even = flags[PARITY] == 0
    ones = jnp.ones((frame.rows, LANES), F32)
    for f, thick in enumerate(widths):
        for x in range(frame.wide):
            slab = slab_of(ins[f], x_low, x_high, base[f], thick, x)
            if slab is None:
                wide_ref[f, x] = ones
                continue
            edge = ones[: SUB + HALO]
            wide_ref[f, x, :own] = edge
            wide_ref[f, x, own + ny :] = edge
            wide_ref[f, x, own : own + ny] = slab
            if HALO <= x < HALO + nx:
                low, high, row = y_low, y_high, base[f] * nx + (x - HALO) * thick
            else:
                above = x >= HALO
                low, high = corners[2 * above : 2 * above + 2]
                at = x - HALO - nx if above else x - (HALO - thick)
                row = sum(w * w for w in widths[:f]) + at * thick
            wide_ref[f, x, own - thick : own] = low[row : row + thick]
            wide_ref[f, x, own + ny : own + ny + thick] = high[row : row + thick]
        packed_lanes(wide_ref, f, frame, pl.ds(SUB, tall), to_high, to_low)
    high, low = to_high[...], to_low[...]
    size = fields * tall
    send_forth[:size], send_back[:size] = jnp.where(even, high, low), jnp.where(even, low, high)
    nb, rows, width = labels.shape
    lane = lane_no((rows, LANES))
    high = low = jnp.zeros((rows, LANES), F32)
    for b in range(nb):
        slab = labels[b].astype(F32)
        high = jnp.where(lane == b, slab[:, width - 1 :], high)
        low = jnp.where(lane == b, slab[:, :1], low)
    send_forth[size:], send_back[size:] = jnp.where(even, high, low), jnp.where(even, low, high)


def frame_kernel(fields, flags, *refs):
    ins = refs[:fields]
    x_low, x_high, _ = refs[fields : fields + 3]
    wide_ref, to_high, to_low = refs[fields + 3 :]
    nx, ny = ins[0].shape[0], ins[0].shape[1]
    frame = Frame(nx, ny)
    spare = jnp.ones((SUB, LANES), F32)
    for f in range(fields):
        for x in range(frame.wide):
            wide_ref[f, x, frame.own : frame.own + ny] = slab_of(ins[f], x_low, x_high, HALO * f, HALO, x)
            wide_ref[f, x, :SUB] = spare
            wide_ref[f, x, SUB + frame.tall :] = spare
        packed_lanes(wide_ref, f, frame, pl.ds(2 * SUB, frame.tall - 2 * SUB), to_high, to_low)


def pack_z_kernel(fields, flags, wide_in, high_in, low_in, from_low, from_high, rider, *refs):
    wide_ref, send_forth, send_back, to_high, to_low = refs
    frame = Frame(wide_ref.shape[1] - 2 * HALO, wide_ref.shape[2] - 2 * (SUB + HALO))
    ny, tall, own = frame.ny, frame.tall, frame.own
    even = flags[PARITY] == 0
    for f in range(fields):
        for x in range(frame.wide):
            at = (f * frame.wide + x) * HALO
            wide_ref[f, x, SUB:own] = from_low[at : at + HALO]
            wide_ref[f, x, own + ny : own + ny + HALO] = from_high[at : at + HALO]
    size = fields * tall
    to_high[...], to_low[...] = high_in[...], low_in[...]
    for f in range(fields):
        for start in (SUB, tall):
            packed_lanes(wide_ref, f, frame, pl.ds(start, SUB), to_high, to_low)
    high, low = to_high[...], to_low[...]
    send_forth[:size], send_back[:size] = jnp.where(even, high, low), jnp.where(even, low, high)
    send_forth[size:], send_back[size:] = rider[...], rider[...]


class Links:
    def __init__(self, mesh):
        self.sizes = [mesh.shape[a] for a in ("gx", "gy", "gz")]
        n_x, n_y, n_z = self.sizes

        def at(i, j, k):
            return (i % n_x * n_y + j % n_y) * n_z + k

        every = [(i, j, k) for i in range(n_x) for j in range(n_y) for k in range(n_z)]
        self.ring_x = [(i, (i + 1) % n_x) for i in range(n_x)]
        self.corner = {d: [(at(i, j, k), at(i + d, j + 1, k)) for i, j, k in every] for d in (1, -1)}
        self.snake = []
        for i in range(n_x):
            for j in range(0, n_y, 2):
                nodes = [at(i, j, k) for k in range(n_z)] + [at(i, j + 1, k) for k in reversed(range(n_z))]
                self.snake += [(nodes[m], nodes[(m + 1) % len(nodes)]) for m in range(len(nodes))]

    @staticmethod
    def back(pairs):
        return [(b, a) for a, b in pairs]

    @staticmethod
    def send(values, pairs):
        return lax.ppermute(values, ("gx", "gy", "gz"), pairs)

    def x(self, sends):
        if self.sizes[0] == 2:
            return (lax.ppermute(sends[0], "gx", self.ring_x),)
        return lax.ppermute(sends[0], "gx", self.ring_x), lax.ppermute(sends[1], "gx", self.back(self.ring_x))

    def near(self, values, x=None, y=None, z=None):
        forth, back = self.z(*(z or (values, values)))
        from_x = self.x(x or (values, values))
        return (forth, back, *from_x, *self.ring_y(*(y or (values, values))))

    def ring_y(self, to_high, to_low):
        ring = [(j, (j + 1) % self.sizes[1]) for j in range(self.sizes[1])]
        return lax.ppermute(to_high, "gy", ring), lax.ppermute(to_low, "gy", self.back(ring))

    def corners(self, sends):
        if self.sizes[0] == 2:
            return self.send(sends[0], self.corner[1]), self.send(sends[1], self.back(self.corner[1]))
        return (
            self.send(sends[0], self.corner[1]),
            self.send(sends[1], self.back(self.corner[-1])),
            self.send(sends[2], self.corner[-1]),
            self.send(sends[3], self.back(self.corner[1])),
        )

    def z(self, forth, back):
        return self.send(forth, self.snake), self.send(back, self.back(self.snake))


def send_y(arrays, rider, from_x):
    nx, ny, nz = arrays[0].shape
    rows = len(arrays) * Frame(nx, ny).wide * HALO + SUB
    kernel = functools.partial(pack_y_kernel, len(arrays))
    return call(kernel, [shaped(rows, nz)] * 2)(*arrays, rider, from_x[0], from_x[-1])


def framed(arrays, from_x, sent):
    nx, ny, nz = arrays[0].shape
    frame, fields = Frame(nx, ny), len(arrays)
    outs = [shaped(fields, *frame.main)] + [shaped(fields * frame.tall, nz)] * 2
    return call(functools.partial(frame_kernel, fields), outs)(*arrays, from_x[0], from_x[-1], sent)


def send_z(frames, from_y, rider):
    wide, high, _ = frames
    return call(
        functools.partial(pack_z_kernel, wide.shape[0]),
        [shaped(*wide.shape)] + [shaped(high.shape[0] + SUB, LANES)] * 2,
        [pltpu.VMEM(high.shape, F32)] * 2,
        aliases={0: 0},
    )(*frames, *from_y, rider)


def sides(flags, forth, back):
    even = flags[PARITY] == 0
    return jnp.where(even, forth, back), jnp.where(even, back, forth)


def weight(one, two):
    return 2.0 * (one * two) / (one + two)


def lane_mask(x):
    return ((lane_no((1, LANES)) - (HALO * x + HALO - 1)) & (LANES - 1)) < 2


def edge_step(here, x, edges):
    return jnp.where(lane_mask(x), turned(here, HALO * x + HALO, 1), edges)


def joined(below, above):
    lane = lane_no((1, LANES))
    return jnp.where(lane % HALO == HALO - 1, turned(above, HALO - 1, 1), turned(below, 1, 1))


def at_edges(join, x):
    lane = lane_no((1, LANES))
    return jnp.where((lane == 0) | (lane == LANES - 1), turned(join, (LANES - HALO) - HALO * x, 1), 0.0)


def ends_near(below, above, edges):
    layer = lane_no((1, LANES)) % HALO
    return (
        jnp.where(layer == HALO - 1, turned(edges, -1, 1), turned(below, -1, 1)),
        turned(below, 1, 1),
        turned(above, -1, 1),
        jnp.where(layer == 0, turned(edges, 1 - HALO, 1), turned(above, 1, 1)),
    )


def main_sums(frame, field, xs, join, wx, wy, wz):
    span = frame.span
    slabs = [field[xs[0] - 1 + k, span] for k in range(len(xs) + 2)]
    faces = [wx[xs[0] - 1 + k, span] for k in range(len(xs) + 1)]
    totals = []
    for k, x in enumerate(xs):
        here, face_y, face_z = slabs[k + 1], wy[x, span], wz[x, span]
        total = faces[k + 1] * slabs[k + 2] + faces[k] * slabs[k]
        total = total + face_y * turned(here, -1, 0) + turned(face_y * here, 1, 0)
        total = total + face_z * turned(here, -1, 1) + turned(face_z * here, 1, 1)
        totals.append(total + at_edges(join, x))
    return slabs[1:-1], totals


def ends_sum(frame, ends, s, upper, lower, wx, wy, wz_up, wz_low):
    span, down = frame.span, pl.ds(SUB - 1, frame.tall)
    here = ends[s, span]
    total = wx[s, span] * turned(here, -HALO, 1) + turned(wx[s, span] * here, HALO, 1)
    total = total + wy[s, span] * ends[s, pl.ds(SUB + 1, frame.tall)] + wy[s, down] * ends[s, down]
    return total + wz_up[s, span] * upper + wz_low[s, span] * lower


def clear_spares(ref, frame):
    for x in range(ref.shape[0]):
        ref[x, :SUB] = jnp.zeros((SUB, LANES), F32)
        ref[x, SUB + frame.tall :] = jnp.zeros((SUB, LANES), F32)


def pack_rows(values):
    half = values.shape[0] // 2
    lane = lane_no((half, LANES))
    return jnp.where(lane < LANES // 2, values[:half], turned(values[half:], LANES // 2, 1))


def lane_total(values):
    return jnp.broadcast_to(jnp.sum(values.T, axis=0, keepdims=True), (SUB, LANES))


def paired(values):
    even = 2 * (lane_no(values.shape) % (LANES // 2))
    return picked(values + turned(values, -1, 1), even)


def faces_y_kept(flags, frame):
    row = row_no((frame.tall, LANES))
    at_low, at_high = row == HALO - 1, row == HALO + frame.ny - 1
    return jnp.where(at_low, flags[Y_LOW], jnp.where(at_high, flags[Y_HIGH], 1)).astype(F32)


def face_rows(count, flags, nb):
    x = [(jnp.where(flags[IX] == 0, 1, 0), SUB)] if count == 2 else [(0, SUB), (1, SUB)]
    return x + [(2, nb // 2), (3, nb // 2), (4, 2), (5, 2)]


def add_rows(total, labels, b, values, c, rows=SUB):
    iota = row_no((AGG, LANES)).astype(F32)
    for r in range(rows):
        row = pl.ds(r, 1)
        total = total + jnp.where(labels[b, row] == iota, values[c, row], 0.0)
    return total


def pack_lanes(values):
    lane = lane_no((2, LANES))
    packed = values[:2]
    for g in range(1, SUB):
        packed = jnp.where(lane // 16 == g, turned(values[2 * g : 2 * g + 2], 16 * g, 1), packed)
    return packed


def fields_kernel(count, flags, wide_ref, block_label, inner, face_label, wx, wy, wz, partial, cond_edges, face_weight, diag):
    frame = Frame(wx.shape[0] - 2 * HALO, wx.shape[1] - 2 * (SUB + HALO))
    wide, tall, span = frame.wide, frame.tall, frame.span
    last = HALO + frame.nx
    keep_y = faces_y_kept(flags, frame)
    inside = jnp.where(lane_no((1, LANES)) == LANES - 1, 0.0, 1.0)

    def fields(xs, carry):
        before, edges = carry
        stores = []
        for x in xs:
            here = wide_ref[0, x, span]
            keep = jnp.where(x == HALO - 1, flags[X_LOW], jnp.where(x == last - 1, flags[X_HIGH], 1)).astype(F32)
            face_x = keep * weight(here, wide_ref[0, jnp.minimum(x + 1, wide - 1), span])
            face_y = keep_y * weight(here, wide_ref[0, x, pl.ds(SUB + 1, tall)])
            face_z = inside * weight(here, turned(here, -1, 1))
            total = wide_ref[2, x, span] + face_x + before + face_y + turned(face_y, 1, 0)
            total = total + face_z + turned(face_z, 1, 1)
            stores.append((x, (face_x, face_y, face_z, total)))
            edges = edge_step(here, x, edges)
            before = face_x
        for x, values in stores:
            for ref, value in zip((wx, wy, wz, partial), values):
                ref[x, span] = value
        return before, edges

    nothing = jnp.zeros((tall, LANES), F32)
    cond_edges[...] = batched(0, wide, fields, (nothing, nothing + 1.0), 8)[1]
    nb, ny = frame.nx // 2, frame.ny
    for s, x in enumerate((HALO - 1, last - 1)):
        rows = [wx[x, pl.ds(frame.own + c, ny // 2, stride=2)] for c in range(2)]
        face_weight[s] = pack_rows(paired(rows[0] + rows[1]))
    for s, at in ((2, frame.own - 1), (3, frame.own + ny - 1)):
        lines = [wy[HALO + 2 * b, at : at + 1] + wy[HALO + 2 * b + 1, at : at + 1] for b in range(nb)]
        face_weight[s, : nb // 2] = pack_rows(paired(jnp.concatenate(lines, axis=0)))
    around = jnp.zeros((AGG, LANES), F32)
    around = lax.fori_loop(0, nb, lambda b, around: add_rows(around, block_label, b, inner, b), around)
    for s, rows in face_rows(count, flags, nb)[:-2]:
        around = add_rows(around, face_label, s, face_weight, s, rows)
    diag[...] = lane_total(around)


def fine_kernel(flags, wide_ref, forth, back, wx, wy, wz, partial, cond_edges, block_label, face_label, some_diag,
                *refs):
    inv_diag, start = refs[:2]
    ends = refs[2:8]
    pre, face_weight, scaled_rhs, scale, once, once_ends, res, diag, block_res = refs[8:]
    ex, ey, ez_up, ez_low, inv_ends, start_ends = ends
    nx, ny = pre.shape[0], pre.shape[1]
    frame = Frame(nx, ny)
    wide, tall, span = frame.wide, frame.tall, frame.span
    last = HALO + nx
    got = [sides(flags, forth[f * tall : (f + 1) * tall], back[f * tall : (f + 1) * tall]) for f in range(3)]
    (cond_below, cond_above), rhs_ends, absorb_ends = got
    for ref in (ey, start_ends, once_ends):
        clear_spares(ref, frame)

    lane = lane_no((1, LANES))
    keep_y = faces_y_kept(flags, frame)
    keep_low, keep_high = flags[Z_LOW].astype(F32), flags[Z_HIGH].astype(F32)
    near = ends_near(cond_below, cond_above, cond_edges[...])
    slab = lane // HALO
    keep_x = jnp.where(
        slab == HALO - 1, flags[X_LOW], jnp.where(slab == last - 1, flags[X_HIGH], 1)
    ).astype(F32)
    layer = lane % HALO
    for s, here in enumerate((cond_below, cond_above)):
        up, low = weight(here, near[2 * s]), weight(here, near[2 * s + 1])
        if s == 0:
            up = up * jnp.where(layer == HALO - 1, keep_low, 1.0)
        else:
            low = low * jnp.where(layer == 0, keep_high, 1.0)
        face_x = keep_x * weight(here, turned(here, -HALO, 1))
        face_y = keep_y * weight(here, turned(here, -1, 0))
        ex[s, span], ey[s, span], ez_up[s, span], ez_low[s, span] = face_x, face_y, up, low
        total = absorb_ends[s] + face_x + turned(face_x, HALO, 1) + face_y + turned(face_y, 1, 0) + up + low
        inverse = OMEGA_FINE / total
        inv_ends[s, span] = inverse
        start_ends[s, span] = inverse * rhs_ends[s]

    end_low, end_high = ez_up[0, span], ez_low[1, span]
    join_faces = joined(end_low, end_high)

    def first_sweep(xs, edges):
        stores = []
        for x in xs:
            total = partial[x, span] + at_edges(join_faces, x)
            inverse = OMEGA_FINE / total
            begin = inverse * wide_ref[1, x, span]
            stores.append((x, (total, inverse, begin)))
            edges = edge_step(begin, x, edges)
        for x, values in stores:
            for ref, value in zip((diag, inv_diag, start), values):
                ref[x, span] = value
        return edges

    edges = batched(0, wide, first_sweep, jnp.zeros((tall, LANES), F32), 8)

    join = joined(end_low * start_ends[0, span], end_high * start_ends[1, span])
    near = ends_near(start_ends[0, span], start_ends[1, span], edges)
    for s in range(2):
        total = ends_sum(frame, start_ends, s, near[2 * s], near[2 * s + 1], ex, ey, ez_up, ez_low)
        once_ends[s, span] = (2.0 - OMEGA_FINE) * start_ends[s, span] + inv_ends[s, span] * total

    def second(xs, carry):
        news = []
        for x, here, total in zip(xs, *main_sums(frame, start, xs, join, wx, wy, wz)):
            news.append((2.0 - OMEGA_FINE) * here + inv_diag[x, span] * total)
        for x, new in zip(xs, news):
            once[x, span] = new
        return carry

    batched(HALO - 1, last + 1, second, 0, 13 if (nx + 2) % 13 == 0 else 6)
    join2 = joined(end_low * once_ends[0, span], end_high * once_ends[1, span])

    def remainder(xs, carry):
        news = []
        for x, here, total in zip(xs, *main_sums(frame, once, xs, join2, wx, wy, wz)):
            news.append(wide_ref[1, x, span] - diag[x, span] * here + total)
        for x, new in zip(xs, news):
            res[x - HALO, span] = new
        for x in xs:
            pre[x - HALO] = once[x, pl.ds(frame.own, ny)]
        return carry

    batched(HALO, last, remainder, 0, 8)

    nb, half = nx // 2, ny // 2

    def rows_at(ref, x, off):
        return ref[x, pl.ds(frame.own + off, half, stride=2)]

    def to_blocks(bs, carry):
        for b in bs:
            four = sum(rows_at(res, 2 * b + a, c) for a in range(2) for c in range(2))
            block_res[b] = pack_rows(paired(four))
        return carry

    batched(0, nb, to_blocks, 0)
    zeros = jnp.zeros((AGG, LANES), F32)
    sums = lax.fori_loop(0, nb, lambda b, total: add_rows(total, block_label, b, block_res, b), zeros)

    lane = lane_no((half, LANES))
    around = zeros
    for s, (ref, side, layer_at) in enumerate(((ez_up, 0, HALO - 1), (ez_low, 1, 0))):
        values = rows_at(ref, side, 0) + rows_at(ref, side, 1)
        values = values + turned(values, -HALO, 1)
        spot = jnp.minimum(2 * HALO * lane + HALO * HALO + layer_at, LANES - 1)
        face_weight[s, :2] = pack_lanes(jnp.where(lane < nb, picked(values, spot), 0.0))
        around = add_rows(around, face_label, 4 + s, face_weight, s, 2)
    scale[...] = OMEGA_COARSE / (some_diag[...] + lane_total(around))
    scaled_rhs[...] = scale[...] * lane_total(sums)


def tile_sum(tile, rows, label_at, pairs_at, group=4):
    iota = row_no((AGG, LANES)).astype(F32)
    for first in range(0, rows, group):
        places, highs, lows = [], [], []
        for r in range(first, min(first + group, rows)):
            places.append(jnp.where(label_at(r) == iota, 1.0, 0.0).astype(BF16))
            held = sum(jnp.where(near == iota, w, 0.0) for near, w in pairs_at(r))
            highs.append(held.astype(BF16))
            lows.append((held - highs[-1].astype(F32)).astype(BF16))
        left = jnp.concatenate(places, axis=1)
        right = jnp.concatenate([jnp.concatenate(highs, axis=1), jnp.concatenate(lows, axis=1)], axis=0)
        tile = tile + lax.dot_general(left, right, (((1,), (1,)), ((), ())), preferred_element_type=F32)
    return tile


def both_halves(tile):
    return tile[:, :AGG] + tile[:, AGG:]


def keep_tile(out, t, tile):
    high = tile.astype(BF16)
    rows = pl.ds(t * AGG, AGG)
    out[rows, :AGG] = high
    out[rows, AGG:] = (tile - high.astype(F32)).astype(BF16)


def blocks_kernel(flags, cond, absorb, block_agg, _, block_label, near, weights, inner, part):
    nx, ny = cond.shape[0], cond.shape[1]
    nb, half, width = nx // 2, ny // 2, LANES // 2
    lane, row = lane_no((half, LANES)), row_no((half, LANES))

    def halves(values, slot):
        part[slot] = values
        return part[slot, pl.ds(0, half, stride=2)], part[slot, pl.ds(1, half, stride=2)]

    def label_at(b):
        values = block_agg[b].astype(F32)
        return jnp.concatenate([values, values], axis=1)

    def upper_x(b, slot):
        x = jnp.maximum(2 * b, 0)
        faces = weight(cond[x + 1], cond[jnp.minimum(x + 2, nx - 1)])
        return jnp.where((b == nb - 1) | (b < 0), 0.0, paired(sum(halves(faces, slot))))

    def step(bs, carry):
        low_x = upper_x(bs[0] - 1, 0)
        for k, b in enumerate(bs):
            x = 2 * b
            slot = 4 * k + 1
            one, two = cond[x], cond[x + 1]
            both_y = weight(one, turned(one, -1, 0)) + weight(two, turned(two, -1, 0))
            both_z = weight(one, turned(one, -1, 1)) + weight(two, turned(two, -1, 1))
            high_x = upper_x(b, slot)
            high_y = jnp.where(row == half - 1, 0.0, paired(halves(both_y, slot + 1)[1]))
            high_z = picked(sum(halves(both_z, slot + 2)), 2 * (lane % width) + 1)
            high_z = jnp.where(lane % width == width - 1, 0.0, high_z)
            low_y, low_z = turned(high_y, 1, 0), turned(high_z, 1, 1)
            own = label_at(b)
            near_x, past_x = label_at(jnp.minimum(b + 1, nb - 1)), label_at(jnp.maximum(b - 1, 0))
            near_y, past_y = turned(own, -1, 0), turned(own, 1, 0)
            near_z, past_z = turned(own, -1, 1), turned(own, 1, 1)
            total = paired(sum(halves(absorb[x] + absorb[x + 1], slot + 3)))
            for d, (beside, values) in enumerate((
                (near_x, high_x), (past_x, low_x), (near_y, high_y), (past_y, low_y), (near_z, high_z), (past_z, low_z)
            )):
                leaving = jnp.where(beside != own, values, 0.0)
                total = total + leaving
                near[d, b], weights[d, b] = pack_rows(beside).astype(jnp.int32), pack_rows(leaving)
            block_label[b] = pack_rows(own)
            inner[b] = pack_rows(total)
            low_x = high_x
        return carry

    batched(0, nb, step, 0, 4)


def labels_kernel(flags, block_agg, block_label, _, face_label, fine_label, line):
    nb, half, width = block_agg.shape
    lane = lane_no((half, LANES))
    line[...] = jnp.zeros(line.shape, F32)
    low, high = jnp.zeros((half, LANES), F32), jnp.zeros((half, LANES), F32)
    for b in range(nb):
        own = block_agg[b].astype(F32)
        own = jnp.concatenate([own, own], axis=1)
        line[0, b : b + 1], line[1, b : b + 1] = own[:1], own[half - 1 :]
        low = jnp.where(lane == b, own[:, :1], low)
        high = jnp.where(lane == b, own[:, width - 1 : width], high)
        spread = picked(own, lane // 2)
        for a in range(2):
            for c in range(2):
                fine_label[2 * b + a, pl.ds(c, half, stride=2)] = spread
    face_label[0], face_label[1] = block_label[0], block_label[nb - 1]
    for s in range(2):
        face_label[2 + s, : nb // 2] = pack_rows(line[s, :nb])
        face_label[4 + s, :2] = pack_lanes((low, high)[s])


def own_turn_kernel(flags, block_label, near, weights, coarse, out, values):
    table = jnp.broadcast_to(coarse[:1], (SUB, LANES))
    nb = block_label.shape[0]

    def sums(bs, carry):
        news = [sum(weights[d, b] * picked(table, near[d, b]) for d in range(6)) for b in bs]
        for b, new in zip(bs, news):
            values[b] = new
        return carry

    batched(0, nb, sums, 0)
    total = jnp.zeros((AGG, LANES), F32)
    total = lax.fori_loop(0, nb, lambda b, total: add_rows(total, block_label, b, values, b), total)
    out[...] = lane_total(total)


def faces_kernel(count, nb, flags, face_label, weight_xy, weight_z, x_low, x_high, y_low, y_high, forth, back, out,
                 near, weights):
    at, half = x_low.shape[0] - 1, x_low.shape[1] // 2
    near[0], near[1] = pack_rows(x_low[at, :half]), pack_rows(x_high[at, :half])
    at = sum(WIDTHS) * 2 * nb
    for s, ref in enumerate((y_low, y_high)):
        near[2 + s, : nb // 2] = pack_rows(ref[at : at + nb])
    at = forth.shape[0] - half
    for s, values in enumerate(sides(flags, forth[at:], back[at:])):
        near[4 + s, :2] = pack_lanes(values)
    weights[:4], weights[4:] = weight_xy[...], weight_z[...]
    for t, (s, rows) in enumerate(face_rows(count, flags, nb)):
        tile = tile_sum(
            jnp.zeros((AGG, 2 * AGG), F32),
            rows,
            lambda r, s=s: near[s, pl.ds(r, 1)],
            lambda r, s=s: [(face_label[s, pl.ds(r, 1)], weights[s, pl.ds(r, 1)])],
        )
        keep_tile(out, t, both_halves(tile))


def turn_kernel(flags, tiles, scaled_rhs, scale, own, inside, *refs):
    forth, back, *others, out = refs
    got = [ref[ref.shape[0] - 1, :SUB] if len(ref.shape) == 3 else ref[ref.shape[0] - SUB :] for ref in (*others, forth, back)]
    vectors = [*got[:-2], *sides(flags, *got[-2:])]
    row = row_no((SUB, AGG))
    parts = []
    for v in vectors:
        high = v.astype(BF16).astype(F32)
        parts.append(jnp.where(row == 0, high, jnp.where(row == 1, v - high, 0.0)).astype(BF16))
    got = jnp.dot(jnp.concatenate(parts, axis=1), tiles[...], preferred_element_type=F32)
    applied = jnp.sum(got[:, :AGG] + got[:, AGG:], axis=0, keepdims=True)
    out[...] = (1.0 - OMEGA_COARSE) * own[...] + scaled_rhs[...] + scale[...] * (inside[...] + applied)


def ride_kernel(count, flags, pre, fine_label, coarse, *outs):
    nx = pre.shape[0]
    for s, out in enumerate(outs):
        at = jnp.where(flags[IX] == 0, nx - HALO, 0) if count == 2 else (nx - HALO, 0)[s]
        for f, field in enumerate((pre, fine_label)):
            for x in range(HALO):
                out[HALO * f + x] = field[at + x]
        out[2 * HALO] = jnp.zeros(out.shape[1:], F32)
        out[2 * HALO, :SUB] = coarse[...]


def three_kernel(flags, low, mid, high, out):
    row = row_no(out.shape)
    out[...] = jnp.where(row == 0, low[...], jnp.where(row == 1, mid[...], high[...]))


def nine_kernel(flags, low, mid, high, out):
    out[...] = jnp.zeros(out.shape, F32)
    for n, ref in enumerate((low, mid, high)):
        out[3 * n : 3 * n + 3] = ref[:3]


def lift_kernel(flags, wide_ref, forth, back, main, ends):
    frame = Frame(wide_ref.shape[1] - 2 * HALO, wide_ref.shape[2] - 2 * (SUB + HALO))
    tall = frame.tall
    for b in range(frame.wide // 2):
        main[b] = wide_ref[1, 2 * b, frame.span].astype(jnp.int32)
    rows = pl.ds(tall, tall)
    for s, values in enumerate(sides(flags, forth[rows], back[rows])):
        ends[s] = values.astype(jnp.int32)


def rows_of(frame, table, dx):
    row = row_no((frame.tall, LANES))
    low, mid, high = (table[3 * n + dx + 1 : 3 * n + dx + 2] for n in range(3))
    return jnp.where(row < HALO, low, jnp.where(row < HALO + frame.ny, mid, high))


def lift_main_kernel(flags, table, labels, wide_ref, lifted):
    frame = Frame(wide_ref.shape[1] - 2 * HALO, wide_ref.shape[2] - 2 * (SUB + HALO))
    last = HALO + frame.nx
    for first, stop, dx in ((0, HALO, -1), (HALO, last, 0), (last, frame.wide, 1)):
        values = rows_of(frame, table[...], dx)

        def lift(bs, carry, values=values):
            news = [picked(values, labels[b]) for b in bs]
            for b, new in zip(bs, news):
                for a in range(2):
                    lifted[2 * b + a, frame.span] = wide_ref[0, 2 * b + a, frame.span] + new
            return carry

        batched(first // 2, stop // 2, lift, 0, 6)


def post_kernel(flags, lifted, table_forth, table_back, end_labels, forth, back, *refs):
    (wx, wy, wz, inv_diag, start), ends = refs[:5], refs[5:11]
    out, one, two, one_ends, two_ends, kept_out, sems = refs[11:]
    nx, ny = out.shape[0], out.shape[1]
    frame = Frame(nx, ny)
    wide, tall, span = frame.wide, frame.tall, frame.span
    ex, ey, ez_up, ez_low, inv_ends, start_ends = ends
    for ref in (one_ends, two_ends):
        clear_spares(ref, frame)
    lane = lane_no((tall, LANES))
    tables = sides(flags, table_forth[...], table_back[...])
    for s, (table, base) in enumerate(zip(tables, sides(flags, forth[:tall], back[:tall]))):
        below, inside, above = (picked(rows_of(frame, table, dx), end_labels[s]) for dx in (-1, 0, 1))
        spot = lane // HALO
        two_ends[s, span] = base + jnp.where(spot < HALO, below, jnp.where(spot < HALO + nx, inside, above))
    kept = 1.0 - OMEGA_FINE

    def result(at, count):
        rows = pl.ds(at, count)
        return pltpu.make_async_copy(kept_out.at[rows], out.at[rows], sems.at[at // count])

    buffers = ((lifted, two_ends), (one, one_ends), (two, two_ends), (one, one_ends))
    for s in range(POST):
        src, src_ends = buffers[s]
        join = joined(ez_up[0, span] * src_ends[0, span], ez_low[1, span] * src_ends[1, span])
        final = s == POST - 1
        dst, dst_ends = (None, None) if final else buffers[s + 1]

        def step(xs, edges, src=src, join=join, dst=dst, final=final):
            news = []
            for x, here, total in zip(xs, *main_sums(frame, src, xs, join, wx, wy, wz)):
                news.append(kept * here + start[x, span] + inv_diag[x, span] * total)
                if not final:
                    edges = edge_step(here, x, edges)
            for x, new in zip(xs, news):
                if final:
                    kept_out[x - HALO] = new[HALO : HALO + ny]
                else:
                    dst[x, span] = new
            if final:
                result(xs[0] - HALO, len(xs)).start()
            return edges

        size = 8 if final else 10
        edges = batched(s + 1, wide - s - 1, step, jnp.zeros((tall, LANES), F32), size)
        if not final:
            near = ends_near(src_ends[0, span], src_ends[1, span], edges)
            news = []
            for e in range(2):
                total = ends_sum(frame, src_ends, e, near[2 * e], near[2 * e + 1], ex, ey, ez_up, ez_low)
                news.append(kept * src_ends[e, span] + start_ends[e, span] + inv_ends[e, span] * total)
            dst_ends[0, span], dst_ends[1, span] = news
    for n in range(nx // 8):
        result(8 * n, 8).wait()


def body(links, right_side, conductance, absorption, block_agg):
    nx, ny, nz = right_side.shape
    frame = Frame(nx, ny)
    nb = nx // 2
    n_x = links.sizes[0]
    arrays = (conductance, right_side, absorption, block_agg)
    n_send = 1 if n_x == 2 else 2
    pinned = [pltpu.with_memory_space_constraint(a, pltpu.HBM) for a in arrays]
    outs = [jax.ShapeDtypeStruct(a.shape, a.dtype) for a in arrays]
    outs += [shaped(sum(WIDTHS) + 1, ny, nz)] * n_send + [shaped(sum(WIDTHS) * nx + 16, nz)] * 2
    outs += [shaped(-(-sum(w * w for w in WIDTHS) // SUB) * SUB, nz)] * (2 * n_send)
    got = call(
        functools.partial(pack_kernel, n_x, WIDTHS),
        outs,
        [pltpu.SemaphoreType.DMA((3 * 4,))],
        in_specs=[pl.BlockSpec(memory_space=pltpu.HBM)] * 4,
    )(*pinned)
    arrays, sends = got[:4], got[4:]
    from_x = links.x(sends[:n_send])
    from_y = links.ring_y(*sends[n_send : n_send + 2])
    from_corners = links.corners(sends[n_send + 2 :])
    blocks = (nb, SUB, LANES)
    outs = [shaped(*blocks), jax.ShapeDtypeStruct((6, *blocks), jnp.int32), shaped(6, *blocks), shaped(*blocks)]
    *rows, inner = call(blocks_kernel, outs, [pltpu.VMEM((17, ny, LANES), F32)])(
        arrays[0], arrays[2], arrays[3], sends[0]
    )
    got = lax.optimization_barrier((*from_x, *from_y, *from_corners, inner))
    from_x, from_y, from_corners, inner = got[:n_send], got[n_send : n_send + 2], got[n_send + 2 : -1], got[-1]
    block_label = rows[0]
    size = len(WIDTHS) * frame.tall
    wide, *sends = call(
        functools.partial(first_frame_kernel, n_x, WIDTHS),
        [shaped(len(WIDTHS), *frame.main)] + [shaped(size + ny // 2, nz)] * 2,
        [pltpu.VMEM((size, nz), F32)] * 2,
    )(*arrays, from_x[0], from_x[-1], *from_y, *from_corners)
    outs = [shaped(6, SUB, LANES), shaped(nx, ny, nz)]
    face_label, fine_label = call(labels_kernel, outs, [pltpu.VMEM((2, ny // 2, LANES), F32)])(
        arrays[3], block_label, sends[0]
    )
    outs = [shaped(*frame.main)] * 4 + [shaped(frame.tall, nz), shaped(4, SUB, LANES), shaped(SUB, AGG)]
    *fields, weight_xy, some_diag = call(functools.partial(fields_kernel, n_x), outs, limit=24)(
        wide, block_label, inner, face_label
    )
    halo = (wide, *links.z(*sends))
    outs = [shaped(*frame.main)] * 2 + [shaped(*frame.ends)] * 6 + [shaped(nx, ny, nz)]
    outs += [shaped(2, SUB, LANES)] + [shaped(SUB, AGG)] * 2
    scratch = [pltpu.VMEM(frame.main, F32), pltpu.VMEM(frame.ends, F32), pltpu.VMEM((nx, frame.rows, LANES), F32)]
    scratch += [pltpu.VMEM(frame.main, F32), pltpu.VMEM(blocks, F32)]
    got = call(fine_kernel, outs, scratch, limit=28)(
        *halo, *fields, block_label, face_label, some_diag
    )
    fields, pre = (*fields[:3], *got[:8]), got[8]
    weight_z, scaled_rhs, scale = got[9:]
    tiles = call(
        functools.partial(faces_kernel, n_x, nb),
        jax.ShapeDtypeStruct(((n_send + 4) * AGG, 2 * AGG), BF16),
        [pltpu.VMEM((6, SUB, LANES), F32)] * 2,
    )(face_label, weight_xy, weight_z, from_x[0], from_x[-1], *from_y, *halo[1:])
    coarse = scaled_rhs

    def turn(**more):
        near = links.near(coarse, **more)
        inside = call(own_turn_kernel, shaped(SUB, AGG), [pltpu.VMEM(blocks, F32)])(*rows, coarse)
        return call(turn_kernel, shaped(SUB, AGG))(tiles, scaled_rhs, scale, coarse, inside, *near), near

    both = (pre, fine_label)
    rides = call(functools.partial(ride_kernel, n_x), [shaped(2 * HALO + 1, ny, nz)] * n_send)(*both, coarse)
    coarse, near = turn(x=rides)
    from_x = near[2:-2]
    rides = send_y(both, coarse, from_x)
    frames = framed(both, from_x, rides[0])
    coarse, near = turn(y=rides)
    wide, *rides = send_z(frames, near[-2:], coarse)
    coarse, near = turn(z=rides)
    halo = (wide, *near[:2])
    outs = [jax.ShapeDtypeStruct((frame.wide // 2, frame.tall, nz), jnp.int32)]
    outs += [jax.ShapeDtypeStruct((2, frame.tall, nz), jnp.int32)]
    lifts = call(lift_kernel, outs)(*halo)
    for _ in range(KC - 4):
        coarse, _ = turn()
    from_x = links.x([coarse] * n_send)
    three = call(three_kernel, shaped(SUB, AGG))(from_x[0], coarse, from_x[-1])
    low, high = links.ring_y(three, three)
    nine = call(nine_kernel, shaped(2 * SUB, AGG))(low, three, high)
    tables = links.z(nine, nine)
    lifted = call(lift_main_kernel, shaped(*frame.main))(nine, lifts[0], halo[0])
    scratch = [pltpu.VMEM(frame.main, F32)] * 2 + [pltpu.VMEM(frame.ends, F32)] * 2
    scratch += [pltpu.VMEM((nx, ny, nz), F32), pltpu.SemaphoreType.DMA((nx // 8,))]
    return call(post_kernel, shaped(nx, ny, nz), scratch, limit=24, out_specs=pl.BlockSpec(memory_space=pl.ANY))(
        lifted, *tables, lifts[1], *halo[1:], *fields
    )


def solution(mesh):
    spec = P("gx", "gy", "gz")
    return jax.shard_map(
        functools.partial(body, Links(mesh)), mesh=mesh, in_specs=(spec,) * 4, out_specs=spec, check_vma=False
    )
```

```python
import functools

import jax
import jax.numpy as jnp
from jax import lax
from jax.experimental import pallas as pl
from jax.experimental.pallas import tpu as pltpu
from jax.sharding import PartitionSpec as P

AGG = 128
LANES = 128
SUB = 8
HALO = 4
WIDTHS = (4, 3, 3)
POST = 4
KC = 8
OMEGA_FINE = 0.8
OMEGA_COARSE = 0.7
F32 = jnp.float32
BF16 = jnp.bfloat16
VMEM = pl.BlockSpec(memory_space=pltpu.VMEM)
IX, PARITY, X_LOW, X_HIGH, Y_LOW, Y_HIGH, Z_LOW, Z_HIGH = range(8)


def places():
    (ix, n_x), (iy, n_y), (iz, n_z) = ((lax.axis_index(a), lax.axis_size(a)) for a in ("gx", "gy", "gz"))
    flags = [ix, iy % 2, ix > 0, ix < n_x - 1, iy > 0, iy < n_y - 1, iz > 0, iz < n_z - 1]
    return [jnp.asarray(flag, jnp.int32) for flag in flags]


def call(kernel, outs, scratch=(), limit=16, flops=10**6, in_specs=None, aliases=None, out_specs=None):
    def placed(*refs):
        kernel(places(), *refs)

    def run(*arrays):
        return pl.pallas_call(
            placed,
            out_shape=outs,
            in_specs=in_specs or [VMEM] * len(arrays),
            out_specs=out_specs or jax.tree.map(lambda _: VMEM, outs),
            scratch_shapes=list(scratch),
            input_output_aliases=aliases or {},
            compiler_params=pltpu.CompilerParams(vmem_limit_bytes=limit * 2**20),
            cost_estimate=pl.CostEstimate(flops=flops, bytes_accessed=10**5, transcendentals=0),
        )(*arrays)

    return run


def shaped(*shape):
    return jax.ShapeDtypeStruct(shape, F32)


def lane_no(shape):
    return lax.broadcasted_iota(jnp.int32, shape, len(shape) - 1)


def row_no(shape):
    return lax.broadcasted_iota(jnp.int32, shape, len(shape) - 2)


def turned(values, shift, axis):
    if isinstance(shift, int):
        shift = shift % values.shape[axis]
        if shift == 0:
            return values
    return pltpu.roll(values, shift, axis)


def batched(low, high, step, carry, size=6):
    def some(i, carry):
        return step([low + i * size + k for k in range(size)], carry)

    carry = lax.fori_loop(0, (high - low) // size, some, carry)
    rest = (high - low) % size
    return step(list(range(high - rest, high)), carry) if rest else carry


def picked(values, index):
    return jnp.take_along_axis(values, index, axis=1, mode="promise_in_bounds")


class Frame:
    def __init__(self, nx, ny):
        self.nx, self.ny = nx, ny
        self.wide, self.tall = nx + 2 * HALO, ny + 2 * HALO
        self.rows = self.tall + 2 * SUB
        self.span = pl.ds(SUB, self.tall)
        self.own = SUB + HALO
        self.main = (self.wide, self.rows, LANES)
        self.ends = (2, self.rows, LANES)


def bases(widths):
    return [sum(widths[:f]) for f in range(len(widths) + 1)]


def copied(pairs, sems):
    copies = [pltpu.make_async_copy(src, dst, sems.at[n]) for n, (src, dst) in enumerate(pairs)]
    for copy in copies:
        copy.start()
    return copies


def pack_kernel(count, widths, flags, *refs):
    fields = len(widths)
    n_x = 1 if count == 2 else 2
    ins, kept = refs[: fields + 1], refs[fields + 1 : 2 * fields + 2]
    outs, sems = refs[2 * fields + 2 : -1], refs[-1]
    x_outs, y_outs, corner_outs = outs[:n_x], outs[n_x : n_x + 2], outs[n_x + 2 :]
    nx, ny = ins[0].shape[0], ins[0].shape[1]
    nb, half, width = ins[-1].shape
    thirds = 3
    copies = []
    for ref, out in zip(ins, kept):
        for t in range(thirds):
            size = ref.shape[0] // thirds
            rows = pl.ds(t * size, size)
            copies.append(pltpu.make_async_copy(ref.at[rows], out.at[rows], sems.at[len(copies)]))
    for copy in copies:
        copy.start()
    for out in (*x_outs, *y_outs):
        out[...] = jnp.zeros(out.shape, F32)
    for copy in copies:
        copy.wait()
    base = bases(widths)
    labels = kept[-1]
    for s, out in enumerate(x_outs):

        def place(size, thick, s=s):
            if count == 2:
                return jnp.where(flags[IX] == 0, size - thick, 0)
            return (size - thick, 0)[s]

        for f, thick in enumerate(widths):
            at = place(nx, thick)
            for k in range(thick):
                slab = kept[f][at + k]
                out[base[f] + k] = slab
                row = (sum(w * w for w in widths[:f])) + k * thick
                corner_outs[2 * s][row : row + thick] = slab[ny - thick :]
                corner_outs[2 * s + 1][row : row + thick] = slab[:thick]
        out[base[-1], :half, :width] = labels[place(nb, 1)].astype(F32)
    for out, high in zip(y_outs, (True, False)):
        for f, thick in enumerate(widths):
            for x in range(nx):
                row = base[f] * nx + x * thick
                out[row : row + thick] = kept[f][x, ny - thick :] if high else kept[f][x, :thick]
        row = base[-1] * nx
        for b in range(nb):
            line = labels[b, half - 1 :] if high else labels[b, :1]
            out[row + b : row + b + 1, :width] = line.astype(F32)


def slab_of(own, low, high, base, width, x):
    nx = own.shape[0]
    if HALO <= x < HALO + nx:
        return own[x - HALO]
    if x < HALO:
        at = x - (HALO - width)
        return low[base + at] if at >= 0 else None
    at = x - HALO - nx
    return high[base + at] if at < width else None


def pack_y_kernel(fields, flags, *refs):
    ins, rider = refs[:fields], refs[fields]
    low, high, to_high, to_low = refs[fields + 1 :]
    nx, ny = ins[0].shape[0], ins[0].shape[1]
    wide = nx + 2 * HALO
    for f in range(fields):
        for x in range(wide):
            slab = slab_of(ins[f], low, high, HALO * f, HALO, x)
            at = (f * wide + x) * HALO
            to_high[at : at + HALO] = slab[ny - HALO :]
            to_low[at : at + HALO] = slab[:HALO]
    at = fields * wide * HALO
    to_high[at:], to_low[at:] = rider[...], rider[...]


def packed_lanes(wide_ref, f, frame, rows, to_high, to_low):
    group = lane_no((1, LANES)) // HALO
    nothing = jnp.ones((rows.size, LANES), F32)
    high, low = nothing, nothing
    for x in range(frame.wide):
        moved = turned(wide_ref[f, x, rows], HALO * (x + 1), 1)
        high = jnp.where(group == x, moved, high)
        low = jnp.where(group == (x + 1) % frame.wide, moved, low)
    at = pl.ds(f * frame.tall + rows.start - SUB, rows.size)
    to_high[at] = high
    to_low[at] = turned(low, -HALO, 1)


def first_frame_kernel(count, widths, flags, *refs):
    fields = len(widths)
    ins, labels, refs = refs[:fields], refs[fields], refs[fields + 1 :]
    x_low, x_high, y_low, y_high = refs[:4]
    corners = refs[4:6] * 2 if count == 2 else refs[4:8]
    wide_ref, send_forth, send_back, to_high, to_low = refs[-5:]
    nx, ny = ins[0].shape[0], ins[0].shape[1]
    frame = Frame(nx, ny)
    base = bases(widths)
    tall, own = frame.tall, frame.own
    even = flags[PARITY] == 0
    ones = jnp.ones((frame.rows, LANES), F32)
    for f, thick in enumerate(widths):
        for x in range(frame.wide):
            slab = slab_of(ins[f], x_low, x_high, base[f], thick, x)
            if slab is None:
                wide_ref[f, x] = ones
                continue
            edge = ones[: SUB + HALO]
            wide_ref[f, x, :own] = edge
            wide_ref[f, x, own + ny :] = edge
            wide_ref[f, x, own : own + ny] = slab
            if HALO <= x < HALO + nx:
                low, high, row = y_low, y_high, base[f] * nx + (x - HALO) * thick
            else:
                above = x >= HALO
                low, high = corners[2 * above : 2 * above + 2]
                at = x - HALO - nx if above else x - (HALO - thick)
                row = sum(w * w for w in widths[:f]) + at * thick
            wide_ref[f, x, own - thick : own] = low[row : row + thick]
            wide_ref[f, x, own + ny : own + ny + thick] = high[row : row + thick]
        packed_lanes(wide_ref, f, frame, pl.ds(SUB, tall), to_high, to_low)
    high, low = to_high[...], to_low[...]
    size = fields * tall
    send_forth[:size], send_back[:size] = jnp.where(even, high, low), jnp.where(even, low, high)
    nb, rows, width = labels.shape
    lane = lane_no((rows, LANES))
    high = low = jnp.zeros((rows, LANES), F32)
    for b in range(nb):
        slab = labels[b].astype(F32)
        high = jnp.where(lane == b, slab[:, width - 1 :], high)
        low = jnp.where(lane == b, slab[:, :1], low)
    send_forth[size:], send_back[size:] = jnp.where(even, high, low), jnp.where(even, low, high)


def frame_kernel(fields, flags, *refs):
    ins = refs[:fields]
    x_low, x_high, _ = refs[fields : fields + 3]
    wide_ref, to_high, to_low = refs[fields + 3 :]
    nx, ny = ins[0].shape[0], ins[0].shape[1]
    frame = Frame(nx, ny)
    spare = jnp.ones((SUB, LANES), F32)
    for f in range(fields):
        for x in range(frame.wide):
            wide_ref[f, x, frame.own : frame.own + ny] = slab_of(ins[f], x_low, x_high, HALO * f, HALO, x)
            wide_ref[f, x, :SUB] = spare
            wide_ref[f, x, SUB + frame.tall :] = spare
        packed_lanes(wide_ref, f, frame, pl.ds(2 * SUB, frame.tall - 2 * SUB), to_high, to_low)


def pack_z_kernel(fields, flags, wide_in, high_in, low_in, from_low, from_high, rider, *refs):
    wide_ref, send_forth, send_back, to_high, to_low = refs
    frame = Frame(wide_ref.shape[1] - 2 * HALO, wide_ref.shape[2] - 2 * (SUB + HALO))
    ny, tall, own = frame.ny, frame.tall, frame.own
    even = flags[PARITY] == 0
    for f in range(fields):
        for x in range(frame.wide):
            at = (f * frame.wide + x) * HALO
            wide_ref[f, x, SUB:own] = from_low[at : at + HALO]
            wide_ref[f, x, own + ny : own + ny + HALO] = from_high[at : at + HALO]
    size = fields * tall
    to_high[...], to_low[...] = high_in[...], low_in[...]
    for f in range(fields):
        for start in (SUB, tall):
            packed_lanes(wide_ref, f, frame, pl.ds(start, SUB), to_high, to_low)
    high, low = to_high[...], to_low[...]
    send_forth[:size], send_back[:size] = jnp.where(even, high, low), jnp.where(even, low, high)
    send_forth[size:], send_back[size:] = rider[...], rider[...]


class Links:
    def __init__(self, mesh):
        self.sizes = [mesh.shape[a] for a in ("gx", "gy", "gz")]
        n_x, n_y, n_z = self.sizes

        def at(i, j, k):
            return (i % n_x * n_y + j % n_y) * n_z + k

        every = [(i, j, k) for i in range(n_x) for j in range(n_y) for k in range(n_z)]
        self.ring_x = [(i, (i + 1) % n_x) for i in range(n_x)]
        self.corner = {d: [(at(i, j, k), at(i + d, j + 1, k)) for i, j, k in every] for d in (1, -1)}
        self.snake = []
        for i in range(n_x):
            for j in range(0, n_y, 2):
                nodes = [at(i, j, k) for k in range(n_z)] + [at(i, j + 1, k) for k in reversed(range(n_z))]
                self.snake += [(nodes[m], nodes[(m + 1) % len(nodes)]) for m in range(len(nodes))]

    @staticmethod
    def back(pairs):
        return [(b, a) for a, b in pairs]

    @staticmethod
    def send(values, pairs):
        return lax.ppermute(values, ("gx", "gy", "gz"), pairs)

    def x(self, sends):
        if self.sizes[0] == 2:
            return (lax.ppermute(sends[0], "gx", self.ring_x),)
        return lax.ppermute(sends[0], "gx", self.ring_x), lax.ppermute(sends[1], "gx", self.back(self.ring_x))

    def near(self, values, x=None, y=None, z=None):
        forth, back = self.z(*(z or (values, values)))
        from_x = self.x(x or (values, values))
        return (forth, back, *from_x, *self.ring_y(*(y or (values, values))))

    def ring_y(self, to_high, to_low):
        ring = [(j, (j + 1) % self.sizes[1]) for j in range(self.sizes[1])]
        return lax.ppermute(to_high, "gy", ring), lax.ppermute(to_low, "gy", self.back(ring))

    def corners(self, sends):
        if self.sizes[0] == 2:
            return self.send(sends[0], self.corner[1]), self.send(sends[1], self.back(self.corner[1]))
        return (
            self.send(sends[0], self.corner[1]),
            self.send(sends[1], self.back(self.corner[-1])),
            self.send(sends[2], self.corner[-1]),
            self.send(sends[3], self.back(self.corner[1])),
        )

    def z(self, forth, back):
        return self.send(forth, self.snake), self.send(back, self.back(self.snake))


def send_y(arrays, rider, from_x):
    nx, ny, nz = arrays[0].shape
    rows = len(arrays) * Frame(nx, ny).wide * HALO + SUB
    kernel = functools.partial(pack_y_kernel, len(arrays))
    return call(kernel, [shaped(rows, nz)] * 2)(*arrays, rider, from_x[0], from_x[-1])


def framed(arrays, from_x, sent):
    nx, ny, nz = arrays[0].shape
    frame, fields = Frame(nx, ny), len(arrays)
    outs = [shaped(fields, *frame.main)] + [shaped(fields * frame.tall, nz)] * 2
    return call(functools.partial(frame_kernel, fields), outs)(*arrays, from_x[0], from_x[-1], sent)


def send_z(frames, from_y, rider):
    wide, high, _ = frames
    return call(
        functools.partial(pack_z_kernel, wide.shape[0]),
        [shaped(*wide.shape)] + [shaped(high.shape[0] + SUB, LANES)] * 2,
        [pltpu.VMEM(high.shape, F32)] * 2,
        aliases={0: 0},
    )(*frames, *from_y, rider)


def sides(flags, forth, back):
    even = flags[PARITY] == 0
    return jnp.where(even, forth, back), jnp.where(even, back, forth)


def weight(one, two):
    return 2.0 * (one * two) / (one + two)


def lane_mask(x):
    return ((lane_no((1, LANES)) - (HALO * x + HALO - 1)) & (LANES - 1)) < 2


def edge_step(here, x, edges):
    return jnp.where(lane_mask(x), turned(here, HALO * x + HALO, 1), edges)


def joined(below, above):
    lane = lane_no((1, LANES))
    return jnp.where(lane % HALO == HALO - 1, turned(above, HALO - 1, 1), turned(below, 1, 1))


def at_edges(join, x):
    lane = lane_no((1, LANES))
    return jnp.where((lane == 0) | (lane == LANES - 1), turned(join, (LANES - HALO) - HALO * x, 1), 0.0)


def ends_near(below, above, edges):
    layer = lane_no((1, LANES)) % HALO
    return (
        jnp.where(layer == HALO - 1, turned(edges, -1, 1), turned(below, -1, 1)),
        turned(below, 1, 1),
        turned(above, -1, 1),
        jnp.where(layer == 0, turned(edges, 1 - HALO, 1), turned(above, 1, 1)),
    )


def main_sums(frame, field, xs, join, wx, wy, wz):
    span = frame.span
    slabs = [field[xs[0] - 1 + k, span] for k in range(len(xs) + 2)]
    faces = [wx[xs[0] - 1 + k, span] for k in range(len(xs) + 1)]
    totals = []
    for k, x in enumerate(xs):
        here, face_y, face_z = slabs[k + 1], wy[x, span], wz[x, span]
        total = faces[k + 1] * slabs[k + 2] + faces[k] * slabs[k]
        total = total + face_y * turned(here, -1, 0) + turned(face_y * here, 1, 0)
        total = total + face_z * turned(here, -1, 1) + turned(face_z * here, 1, 1)
        totals.append(total + at_edges(join, x))
    return slabs[1:-1], totals


def ends_sum(frame, ends, s, upper, lower, wx, wy, wz_up, wz_low):
    span, down = frame.span, pl.ds(SUB - 1, frame.tall)
    here = ends[s, span]
    total = wx[s, span] * turned(here, -HALO, 1) + turned(wx[s, span] * here, HALO, 1)
    total = total + wy[s, span] * ends[s, pl.ds(SUB + 1, frame.tall)] + wy[s, down] * ends[s, down]
    return total + wz_up[s, span] * upper + wz_low[s, span] * lower


def clear_spares(ref, frame):
    for x in range(ref.shape[0]):
        ref[x, :SUB] = jnp.zeros((SUB, LANES), F32)
        ref[x, SUB + frame.tall :] = jnp.zeros((SUB, LANES), F32)


def pack_rows(values):
    half = values.shape[0] // 2
    lane = lane_no((half, LANES))
    return jnp.where(lane < LANES // 2, values[:half], turned(values[half:], LANES // 2, 1))


def lane_total(values):
    return jnp.broadcast_to(jnp.sum(values.T, axis=0, keepdims=True), (SUB, LANES))


def paired(values):
    even = 2 * (lane_no(values.shape) % (LANES // 2))
    return picked(values + turned(values, -1, 1), even)


def faces_y_kept(flags, frame):
    row = row_no((frame.tall, LANES))
    at_low, at_high = row == HALO - 1, row == HALO + frame.ny - 1
    return jnp.where(at_low, flags[Y_LOW], jnp.where(at_high, flags[Y_HIGH], 1)).astype(F32)


def face_rows(count, flags, nb):
    x = [(jnp.where(flags[IX] == 0, 1, 0), SUB)] if count == 2 else [(0, SUB), (1, SUB)]
    return x + [(2, nb // 2), (3, nb // 2), (4, 2), (5, 2)]


def add_rows(total, labels, b, values, c, rows=SUB):
    iota = row_no((AGG, LANES)).astype(F32)
    for r in range(rows):
        row = pl.ds(r, 1)
        total = total + jnp.where(labels[b, row] == iota, values[c, row], 0.0)
    return total


def pack_lanes(values):
    lane = lane_no((2, LANES))
    packed = values[:2]
    for g in range(1, SUB):
        packed = jnp.where(lane // 16 == g, turned(values[2 * g : 2 * g + 2], 16 * g, 1), packed)
    return packed


def fields_kernel(count, flags, wide_ref, block_label, inner, face_label, wx, wy, wz, partial, cond_edges, face_weight, diag):
    frame = Frame(wx.shape[0] - 2 * HALO, wx.shape[1] - 2 * (SUB + HALO))
    wide, tall, span = frame.wide, frame.tall, frame.span
    last = HALO + frame.nx
    keep_y = faces_y_kept(flags, frame)
    inside = jnp.where(lane_no((1, LANES)) == LANES - 1, 0.0, 1.0)

    def fields(xs, carry):
        before, edges = carry
        stores = []
        for x in xs:
            here = wide_ref[0, x, span]
            keep = jnp.where(x == HALO - 1, flags[X_LOW], jnp.where(x == last - 1, flags[X_HIGH], 1)).astype(F32)
            face_x = keep * weight(here, wide_ref[0, jnp.minimum(x + 1, wide - 1), span])
            face_y = keep_y * weight(here, wide_ref[0, x, pl.ds(SUB + 1, tall)])
            face_z = inside * weight(here, turned(here, -1, 1))
            total = wide_ref[2, x, span] + face_x + before + face_y + turned(face_y, 1, 0)
            total = total + face_z + turned(face_z, 1, 1)
            stores.append((x, (face_x, face_y, face_z, total)))
            edges = edge_step(here, x, edges)
            before = face_x
        for x, values in stores:
            for ref, value in zip((wx, wy, wz, partial), values):
                ref[x, span] = value
        return before, edges

    nothing = jnp.zeros((tall, LANES), F32)
    cond_edges[...] = batched(0, wide, fields, (nothing, nothing + 1.0), 4)[1]
    nb, ny = frame.nx // 2, frame.ny
    for s, x in enumerate((HALO - 1, last - 1)):
        rows = [wx[x, pl.ds(frame.own + c, ny // 2, stride=2)] for c in range(2)]
        face_weight[s] = pack_rows(paired(rows[0] + rows[1]))
    for s, at in ((2, frame.own - 1), (3, frame.own + ny - 1)):
        lines = [wy[HALO + 2 * b, at : at + 1] + wy[HALO + 2 * b + 1, at : at + 1] for b in range(nb)]
        face_weight[s, : nb // 2] = pack_rows(paired(jnp.concatenate(lines, axis=0)))
    around = jnp.zeros((AGG, LANES), F32)
    around = lax.fori_loop(0, nb, lambda b, around: add_rows(around, block_label, b, inner, b), around)
    for s, rows in face_rows(count, flags, nb)[:-2]:
        around = add_rows(around, face_label, s, face_weight, s, rows)
    diag[...] = lane_total(around)


def fine_kernel(flags, wide_ref, forth, back, wx, wy, wz, partial, cond_edges, block_label, face_label, some_diag,
                *refs):
    inv_diag, start = refs[:2]
    ends = refs[2:8]
    pre, face_weight, scaled_rhs, scale, once, once_ends, res, diag, block_res = refs[8:]
    ex, ey, ez_up, ez_low, inv_ends, start_ends = ends
    nx, ny = pre.shape[0], pre.shape[1]
    frame = Frame(nx, ny)
    wide, tall, span = frame.wide, frame.tall, frame.span
    last = HALO + nx
    got = [sides(flags, forth[f * tall : (f + 1) * tall], back[f * tall : (f + 1) * tall]) for f in range(3)]
    (cond_below, cond_above), rhs_ends, absorb_ends = got
    for ref in (ey, start_ends, once_ends):
        clear_spares(ref, frame)

    lane = lane_no((1, LANES))
    keep_y = faces_y_kept(flags, frame)
    keep_low, keep_high = flags[Z_LOW].astype(F32), flags[Z_HIGH].astype(F32)
    near = ends_near(cond_below, cond_above, cond_edges[...])
    slab = lane // HALO
    keep_x = jnp.where(
        slab == HALO - 1, flags[X_LOW], jnp.where(slab == last - 1, flags[X_HIGH], 1)
    ).astype(F32)
    layer = lane % HALO
    for s, here in enumerate((cond_below, cond_above)):
        up, low = weight(here, near[2 * s]), weight(here, near[2 * s + 1])
        if s == 0:
            up = up * jnp.where(layer == HALO - 1, keep_low, 1.0)
        else:
            low = low * jnp.where(layer == 0, keep_high, 1.0)
        face_x = keep_x * weight(here, turned(here, -HALO, 1))
        face_y = keep_y * weight(here, turned(here, -1, 0))
        ex[s, span], ey[s, span], ez_up[s, span], ez_low[s, span] = face_x, face_y, up, low
        total = absorb_ends[s] + face_x + turned(face_x, HALO, 1) + face_y + turned(face_y, 1, 0) + up + low
        inverse = OMEGA_FINE / total
        inv_ends[s, span] = inverse
        start_ends[s, span] = inverse * rhs_ends[s]

    end_low, end_high = ez_up[0, span], ez_low[1, span]
    join_faces = joined(end_low, end_high)

    def first_sweep(xs, edges):
        stores = []
        for x in xs:
            total = partial[x, span] + at_edges(join_faces, x)
            inverse = OMEGA_FINE / total
            begin = inverse * wide_ref[1, x, span]
            stores.append((x, (total, inverse, begin)))
            edges = edge_step(begin, x, edges)
        for x, values in stores:
            for ref, value in zip((diag, inv_diag, start), values):
                ref[x, span] = value
        return edges

    edges = batched(0, wide, first_sweep, jnp.zeros((tall, LANES), F32), 8)

    join = joined(end_low * start_ends[0, span], end_high * start_ends[1, span])
    near = ends_near(start_ends[0, span], start_ends[1, span], edges)
    for s in range(2):
        total = ends_sum(frame, start_ends, s, near[2 * s], near[2 * s + 1], ex, ey, ez_up, ez_low)
        once_ends[s, span] = (2.0 - OMEGA_FINE) * start_ends[s, span] + inv_ends[s, span] * total

    def second(xs, carry):
        news = []
        for x, here, total in zip(xs, *main_sums(frame, start, xs, join, wx, wy, wz)):
            news.append((2.0 - OMEGA_FINE) * here + inv_diag[x, span] * total)
        for x, new in zip(xs, news):
            once[x, span] = new
        return carry

    batched(HALO - 1, last + 1, second, 0, 13 if (nx + 2) % 13 == 0 else 6)
    join2 = joined(end_low * once_ends[0, span], end_high * once_ends[1, span])

    def remainder(xs, carry):
        news = []
        for x, here, total in zip(xs, *main_sums(frame, once, xs, join2, wx, wy, wz)):
            news.append(wide_ref[1, x, span] - diag[x, span] * here + total)
        for x, new in zip(xs, news):
            res[x - HALO, span] = new
        for x in xs:
            pre[x - HALO] = once[x, pl.ds(frame.own, ny)]
        return carry

    batched(HALO, last, remainder, 0, 8)

    nb, half = nx // 2, ny // 2

    def rows_at(ref, x, off):
        return ref[x, pl.ds(frame.own + off, half, stride=2)]

    def to_blocks(bs, carry):
        for b in bs:
            four = sum(rows_at(res, 2 * b + a, c) for a in range(2) for c in range(2))
            block_res[b] = pack_rows(paired(four))
        return carry

    batched(0, nb, to_blocks, 0)
    zeros = jnp.zeros((AGG, LANES), F32)
    sums = lax.fori_loop(0, nb, lambda b, total: add_rows(total, block_label, b, block_res, b), zeros)

    lane = lane_no((half, LANES))
    around = zeros
    for s, (ref, side, layer_at) in enumerate(((ez_up, 0, HALO - 1), (ez_low, 1, 0))):
        values = rows_at(ref, side, 0) + rows_at(ref, side, 1)
        values = values + turned(values, -HALO, 1)
        spot = jnp.minimum(2 * HALO * lane + HALO * HALO + layer_at, LANES - 1)
        face_weight[s, :2] = pack_lanes(jnp.where(lane < nb, picked(values, spot), 0.0))
        around = add_rows(around, face_label, 4 + s, face_weight, s, 2)
    scale[...] = OMEGA_COARSE / (some_diag[...] + lane_total(around))
    scaled_rhs[...] = scale[...] * lane_total(sums)


def tile_sum(tile, rows, label_at, pairs_at, group=4):
    iota = row_no((AGG, LANES)).astype(F32)
    for first in range(0, rows, group):
        places, highs, lows = [], [], []
        for r in range(first, min(first + group, rows)):
            places.append(jnp.where(label_at(r) == iota, 1.0, 0.0).astype(BF16))
            held = sum(jnp.where(near == iota, w, 0.0) for near, w in pairs_at(r))
            highs.append(held.astype(BF16))
            lows.append((held - highs[-1].astype(F32)).astype(BF16))
        left = jnp.concatenate(places, axis=1)
        right = jnp.concatenate([jnp.concatenate(highs, axis=1), jnp.concatenate(lows, axis=1)], axis=0)
        tile = tile + lax.dot_general(left, right, (((1,), (1,)), ((), ())), preferred_element_type=F32)
    return tile


def both_halves(tile):
    return tile[:, :AGG] + tile[:, AGG:]


def keep_tile(out, t, tile):
    high = tile.astype(BF16)
    rows = pl.ds(t * AGG, AGG)
    out[rows, :AGG] = high
    out[rows, AGG:] = (tile - high.astype(F32)).astype(BF16)


def blocks_kernel(flags, cond, absorb, block_agg, _, block_label, near, weights, inner, face_label, fine_label,
                  part, line):
    nx, ny = cond.shape[0], cond.shape[1]
    nb, half, width = nx // 2, ny // 2, LANES // 2
    lane, row = lane_no((half, LANES)), row_no((half, LANES))

    def halves(values, slot):
        part[slot] = values
        return part[slot, pl.ds(0, half, stride=2)], part[slot, pl.ds(1, half, stride=2)]

    def label_at(b):
        values = block_agg[b].astype(F32)
        return jnp.concatenate([values, values], axis=1)

    def upper_x(b, slot):
        x = jnp.maximum(2 * b, 0)
        faces = weight(cond[x + 1], cond[jnp.minimum(x + 2, nx - 1)])
        return jnp.where((b == nb - 1) | (b < 0), 0.0, paired(sum(halves(faces, slot))))

    def step(bs, carry):
        low_x = upper_x(bs[0] - 1, 0)
        for k, b in enumerate(bs):
            x = 2 * b
            slot = 4 * k + 1
            one, two = cond[x], cond[x + 1]
            both_y = weight(one, turned(one, -1, 0)) + weight(two, turned(two, -1, 0))
            both_z = weight(one, turned(one, -1, 1)) + weight(two, turned(two, -1, 1))
            high_x = upper_x(b, slot)
            high_y = jnp.where(row == half - 1, 0.0, paired(halves(both_y, slot + 1)[1]))
            high_z = picked(sum(halves(both_z, slot + 2)), 2 * (lane % width) + 1)
            high_z = jnp.where(lane % width == width - 1, 0.0, high_z)
            low_y, low_z = turned(high_y, 1, 0), turned(high_z, 1, 1)
            own = label_at(b)
            near_x, past_x = label_at(jnp.minimum(b + 1, nb - 1)), label_at(jnp.maximum(b - 1, 0))
            near_y, past_y = turned(own, -1, 0), turned(own, 1, 0)
            near_z, past_z = turned(own, -1, 1), turned(own, 1, 1)
            total = paired(sum(halves(absorb[x] + absorb[x + 1], slot + 3)))
            for d, (beside, values) in enumerate((
                (near_x, high_x), (past_x, low_x), (near_y, high_y), (past_y, low_y), (near_z, high_z), (past_z, low_z)
            )):
                leaving = jnp.where(beside != own, values, 0.0)
                total = total + leaving
                near[d, b], weights[d, b] = pack_rows(beside).astype(jnp.int32), pack_rows(leaving)
            block_label[b] = pack_rows(own)
            inner[b] = pack_rows(total)
            spread = picked(own, lane // 2)
            for a in range(2):
                for c in range(2):
                    fine_label[x + a, pl.ds(c, half, stride=2)] = spread
            low_x = high_x
        return carry

    batched(0, nb, step, 0, 4)
    line[...] = jnp.zeros(line.shape, F32)
    low, high = jnp.zeros((half, LANES), F32), jnp.zeros((half, LANES), F32)
    for b in range(nb):
        own = label_at(b)
        line[0, b : b + 1], line[1, b : b + 1] = own[:1], own[half - 1 :]
        low = jnp.where(lane == b, own[:, :1], low)
        high = jnp.where(lane == b, own[:, width - 1 : width], high)
    face_label[0], face_label[1] = block_label[0], block_label[nb - 1]
    for s in range(2):
        face_label[2 + s, : nb // 2] = pack_rows(line[s, :nb])
        face_label[4 + s, :2] = pack_lanes((low, high)[s])


def own_turn_kernel(flags, block_label, near, weights, coarse, out, values):
    table = jnp.broadcast_to(coarse[:1], (SUB, LANES))
    nb = block_label.shape[0]

    def sums(bs, carry):
        news = [sum(weights[d, b] * picked(table, near[d, b]) for d in range(6)) for b in bs]
        for b, new in zip(bs, news):
            values[b] = new
        return carry

    batched(0, nb, sums, 0)
    total = jnp.zeros((AGG, LANES), F32)
    total = lax.fori_loop(0, nb, lambda b, total: add_rows(total, block_label, b, values, b), total)
    out[...] = lane_total(total)


def faces_kernel(count, nb, flags, face_label, weight_xy, weight_z, x_low, x_high, y_low, y_high, forth, back, out,
                 near, weights):
    at, half = x_low.shape[0] - 1, x_low.shape[1] // 2
    near[0], near[1] = pack_rows(x_low[at, :half]), pack_rows(x_high[at, :half])
    at = sum(WIDTHS) * 2 * nb
    for s, ref in enumerate((y_low, y_high)):
        near[2 + s, : nb // 2] = pack_rows(ref[at : at + nb])
    at = forth.shape[0] - half
    for s, values in enumerate(sides(flags, forth[at:], back[at:])):
        near[4 + s, :2] = pack_lanes(values)
    weights[:4], weights[4:] = weight_xy[...], weight_z[...]
    for t, (s, rows) in enumerate(face_rows(count, flags, nb)):
        tile = tile_sum(
            jnp.zeros((AGG, 2 * AGG), F32),
            rows,
            lambda r, s=s: near[s, pl.ds(r, 1)],
            lambda r, s=s: [(face_label[s, pl.ds(r, 1)], weights[s, pl.ds(r, 1)])],
        )
        keep_tile(out, t, both_halves(tile))


def turn_kernel(flags, tiles, scaled_rhs, scale, own, inside, *refs):
    forth, back, *others, out = refs
    got = [ref[ref.shape[0] - 1, :SUB] if len(ref.shape) == 3 else ref[ref.shape[0] - SUB :] for ref in (*others, forth, back)]
    vectors = [*got[:-2], *sides(flags, *got[-2:])]
    row = row_no((SUB, AGG))
    parts = []
    for v in vectors:
        high = v.astype(BF16).astype(F32)
        parts.append(jnp.where(row == 0, high, jnp.where(row == 1, v - high, 0.0)).astype(BF16))
    got = jnp.dot(jnp.concatenate(parts, axis=1), tiles[...], preferred_element_type=F32)
    applied = jnp.sum(got[:, :AGG] + got[:, AGG:], axis=0, keepdims=True)
    out[...] = (1.0 - OMEGA_COARSE) * own[...] + scaled_rhs[...] + scale[...] * (inside[...] + applied)


def ride_kernel(count, flags, pre, fine_label, coarse, *outs):
    nx = pre.shape[0]
    for s, out in enumerate(outs):
        at = jnp.where(flags[IX] == 0, nx - HALO, 0) if count == 2 else (nx - HALO, 0)[s]
        for f, field in enumerate((pre, fine_label)):
            for x in range(HALO):
                out[HALO * f + x] = field[at + x]
        out[2 * HALO] = jnp.zeros(out.shape[1:], F32)
        out[2 * HALO, :SUB] = coarse[...]


def three_kernel(flags, low, mid, high, out):
    row = row_no(out.shape)
    out[...] = jnp.where(row == 0, low[...], jnp.where(row == 1, mid[...], high[...]))


def nine_kernel(flags, low, mid, high, out):
    out[...] = jnp.zeros(out.shape, F32)
    for n, ref in enumerate((low, mid, high)):
        out[3 * n : 3 * n + 3] = ref[:3]


def lift_kernel(flags, wide_ref, forth, back, main, ends):
    frame = Frame(wide_ref.shape[1] - 2 * HALO, wide_ref.shape[2] - 2 * (SUB + HALO))
    tall = frame.tall
    for b in range(frame.wide // 2):
        main[b] = wide_ref[1, 2 * b, frame.span].astype(jnp.int32)
    rows = pl.ds(tall, tall)
    for s, values in enumerate(sides(flags, forth[rows], back[rows])):
        ends[s] = values.astype(jnp.int32)


def rows_of(frame, table, dx):
    row = row_no((frame.tall, LANES))
    low, mid, high = (table[3 * n + dx + 1 : 3 * n + dx + 2] for n in range(3))
    return jnp.where(row < HALO, low, jnp.where(row < HALO + frame.ny, mid, high))


def lift_main_kernel(flags, table, labels, wide_ref, lifted):
    frame = Frame(wide_ref.shape[1] - 2 * HALO, wide_ref.shape[2] - 2 * (SUB + HALO))
    last = HALO + frame.nx
    for first, stop, dx in ((0, HALO, -1), (HALO, last, 0), (last, frame.wide, 1)):
        values = rows_of(frame, table[...], dx)

        def lift(bs, carry, values=values):
            news = [picked(values, labels[b]) for b in bs]
            for b, new in zip(bs, news):
                for a in range(2):
                    lifted[2 * b + a, frame.span] = wide_ref[0, 2 * b + a, frame.span] + new
            return carry

        batched(first // 2, stop // 2, lift, 0, 6)


def post_kernel(flags, lifted, table_forth, table_back, end_labels, forth, back, *refs):
    (wx, wy, wz, inv_diag, start), ends = refs[:5], refs[5:11]
    out, one, two, one_ends, two_ends, kept_out, sems = refs[11:]
    nx, ny = out.shape[0], out.shape[1]
    frame = Frame(nx, ny)
    wide, tall, span = frame.wide, frame.tall, frame.span
    ex, ey, ez_up, ez_low, inv_ends, start_ends = ends
    for ref in (one_ends, two_ends):
        clear_spares(ref, frame)
    lane = lane_no((tall, LANES))
    tables = sides(flags, table_forth[...], table_back[...])
    for s, (table, base) in enumerate(zip(tables, sides(flags, forth[:tall], back[:tall]))):
        below, inside, above = (picked(rows_of(frame, table, dx), end_labels[s]) for dx in (-1, 0, 1))
        spot = lane // HALO
        two_ends[s, span] = base + jnp.where(spot < HALO, below, jnp.where(spot < HALO + nx, inside, above))
    kept = 1.0 - OMEGA_FINE

    def result(at, count):
        rows = pl.ds(at, count)
        return pltpu.make_async_copy(kept_out.at[rows], out.at[rows], sems.at[at // count])

    buffers = ((lifted, two_ends), (one, one_ends), (two, two_ends), (one, one_ends))
    for s in range(POST):
        src, src_ends = buffers[s]
        join = joined(ez_up[0, span] * src_ends[0, span], ez_low[1, span] * src_ends[1, span])
        final = s == POST - 1
        dst, dst_ends = (None, None) if final else buffers[s + 1]

        def step(xs, edges, src=src, join=join, dst=dst, final=final):
            news = []
            for x, here, total in zip(xs, *main_sums(frame, src, xs, join, wx, wy, wz)):
                news.append(kept * here + start[x, span] + inv_diag[x, span] * total)
                if not final:
                    edges = edge_step(here, x, edges)
            for x, new in zip(xs, news):
                if final:
                    kept_out[x - HALO] = new[HALO : HALO + ny]
                else:
                    dst[x, span] = new
            if final:
                result(xs[0] - HALO, len(xs)).start()
            return edges

        size = 8 if final else 15
        edges = batched(s + 1, wide - s - 1, step, jnp.zeros((tall, LANES), F32), size)
        if not final:
            near = ends_near(src_ends[0, span], src_ends[1, span], edges)
            news = []
            for e in range(2):
                total = ends_sum(frame, src_ends, e, near[2 * e], near[2 * e + 1], ex, ey, ez_up, ez_low)
                news.append(kept * src_ends[e, span] + start_ends[e, span] + inv_ends[e, span] * total)
            dst_ends[0, span], dst_ends[1, span] = news
    for n in range(nx // 8):
        result(8 * n, 8).wait()


def body(links, right_side, conductance, absorption, block_agg):
    nx, ny, nz = right_side.shape
    frame = Frame(nx, ny)
    nb = nx // 2
    n_x = links.sizes[0]
    arrays = (conductance, right_side, absorption, block_agg)
    n_send = 1 if n_x == 2 else 2
    pinned = [pltpu.with_memory_space_constraint(a, pltpu.HBM) for a in arrays]
    outs = [jax.ShapeDtypeStruct(a.shape, a.dtype) for a in arrays]
    outs += [shaped(sum(WIDTHS) + 1, ny, nz)] * n_send + [shaped(sum(WIDTHS) * nx + 16, nz)] * 2
    outs += [shaped(-(-sum(w * w for w in WIDTHS) // SUB) * SUB, nz)] * (2 * n_send)
    got = call(
        functools.partial(pack_kernel, n_x, WIDTHS),
        outs,
        [pltpu.SemaphoreType.DMA((3 * 4,))],
        in_specs=[pl.BlockSpec(memory_space=pltpu.HBM)] * 4,
    )(*pinned)
    arrays, sends = got[:4], got[4:]
    from_x = links.x(sends[:n_send])
    from_y = links.ring_y(*sends[n_send : n_send + 2])
    from_corners = links.corners(sends[n_send + 2 :])
    blocks = (nb, SUB, LANES)
    outs = [shaped(*blocks), jax.ShapeDtypeStruct((6, *blocks), jnp.int32), shaped(6, *blocks), shaped(*blocks)]
    outs += [shaped(6, SUB, LANES), shaped(nx, ny, nz)]
    scratch = [pltpu.VMEM((17, ny, LANES), F32), pltpu.VMEM((2, ny // 2, LANES), F32)]
    *rows, inner, face_label, fine_label = call(blocks_kernel, outs, scratch)(
        arrays[0], arrays[2], arrays[3], sends[0]
    )
    got = lax.optimization_barrier((*from_x, *from_y, *from_corners, inner))
    from_x, from_y, from_corners, inner = got[:n_send], got[n_send : n_send + 2], got[n_send + 2 : -1], got[-1]
    block_label = rows[0]
    size = len(WIDTHS) * frame.tall
    wide, *sends = call(
        functools.partial(first_frame_kernel, n_x, WIDTHS),
        [shaped(len(WIDTHS), *frame.main)] + [shaped(size + ny // 2, nz)] * 2,
        [pltpu.VMEM((size, nz), F32)] * 2,
    )(*arrays, from_x[0], from_x[-1], *from_y, *from_corners)
    outs = [shaped(*frame.main)] * 4 + [shaped(frame.tall, nz), shaped(4, SUB, LANES), shaped(SUB, AGG)]
    *fields, weight_xy, some_diag = call(functools.partial(fields_kernel, n_x), outs, limit=24)(
        wide, block_label, inner, face_label
    )
    halo = (wide, *links.z(*sends))
    outs = [shaped(*frame.main)] * 2 + [shaped(*frame.ends)] * 6 + [shaped(nx, ny, nz)]
    outs += [shaped(2, SUB, LANES)] + [shaped(SUB, AGG)] * 2
    scratch = [pltpu.VMEM(frame.main, F32), pltpu.VMEM(frame.ends, F32), pltpu.VMEM((nx, frame.rows, LANES), F32)]
    scratch += [pltpu.VMEM(frame.main, F32), pltpu.VMEM(blocks, F32)]
    got = call(fine_kernel, outs, scratch, limit=28)(
        *halo, *fields, block_label, face_label, some_diag
    )
    fields, pre = (*fields[:3], *got[:8]), got[8]
    weight_z, scaled_rhs, scale = got[9:]
    tiles = call(
        functools.partial(faces_kernel, n_x, nb),
        jax.ShapeDtypeStruct(((n_send + 4) * AGG, 2 * AGG), BF16),
        [pltpu.VMEM((6, SUB, LANES), F32)] * 2,
    )(face_label, weight_xy, weight_z, from_x[0], from_x[-1], *from_y, *halo[1:])
    coarse = scaled_rhs

    def turn(**more):
        near = links.near(coarse, **more)
        inside = call(own_turn_kernel, shaped(SUB, AGG), [pltpu.VMEM(blocks, F32)])(*rows, coarse)
        return call(turn_kernel, shaped(SUB, AGG))(tiles, scaled_rhs, scale, coarse, inside, *near), near

    both = (pre, fine_label)
    rides = call(functools.partial(ride_kernel, n_x), [shaped(2 * HALO + 1, ny, nz)] * n_send)(*both, coarse)
    coarse, near = turn(x=rides)
    from_x = near[2:-2]
    rides = send_y(both, coarse, from_x)
    frames = framed(both, from_x, rides[0])
    coarse, near = turn(y=rides)
    wide, *rides = send_z(frames, near[-2:], coarse)
    coarse, near = turn(z=rides)
    halo = (wide, *near[:2])
    outs = [jax.ShapeDtypeStruct((frame.wide // 2, frame.tall, nz), jnp.int32)]
    outs += [jax.ShapeDtypeStruct((2, frame.tall, nz), jnp.int32)]
    lifts = call(lift_kernel, outs)(*halo)
    for _ in range(KC - 4):
        coarse, _ = turn()
    from_x = links.x([coarse] * n_send)
    three = call(three_kernel, shaped(SUB, AGG))(from_x[0], coarse, from_x[-1])
    low, high = links.ring_y(three, three)
    nine = call(nine_kernel, shaped(2 * SUB, AGG))(low, three, high)
    tables = links.z(nine, nine)
    lifted = call(lift_main_kernel, shaped(*frame.main))(nine, lifts[0], halo[0])
    scratch = [pltpu.VMEM(frame.main, F32)] * 2 + [pltpu.VMEM(frame.ends, F32)] * 2
    scratch += [pltpu.VMEM((nx, ny, nz), F32), pltpu.SemaphoreType.DMA((nx // 8,))]
    return call(post_kernel, shaped(nx, ny, nz), scratch, limit=24, out_specs=pl.BlockSpec(memory_space=pl.ANY))(
        lifted, *tables, lifts[1], *halo[1:], *fields
    )


def solution(mesh):
    spec = P("gx", "gy", "gz")
    return jax.shard_map(
        functools.partial(body, Links(mesh)), mesh=mesh, in_specs=(spec,) * 4, out_specs=spec, check_vma=False
    )
```
